32 devices in a mesh: grp: 2 (over y), ctx: 4 (over z), head: 2 (over x), sub: 2 (over core).
Axes of the slice: x: 2, y: 2, z: 4, core: 2. Of those that a mesh axis runs over, the one named last changes fastest.
Arguments:
- queries: bfloat16 [512, 16384], P(('grp', 'ctx', 'head', 'sub')), parts along dimension 0, may hold values from -400 to 400
- kv_cache: bfloat16 [2, 8192, 1024], P(None, ('grp', 'ctx', 'sub'), 'head'), parts along dimension 1, may hold values from -6 to 6
- page_counts: int32 [8], P('grp'), parts along dimension 0, may hold values from 1 to 4, as said below
Outputs:
- attended: bfloat16 [512, 16384], P(('grp', 'ctx', 'head', 'sub')), parts along dimension 0
The draws below stay inside these ranges and needn't reach their ends.
There are 2 independent parts, one for each index of `grp`. The reference program is written for one: setup_inputs(seed, part) draws one part's arguments, and reference() takes and returns one part's arrays. A program takes and returns all parts, laid end to end along the dimension named above; each array names one. Nothing has to cross between parts.
Inputs may be any that keep to these rules, and one draw needn't show every extreme that they name: `page_counts`: each count is at least 1, the counts sum to exactly 8, and one request has exactly 4 pages.
All inputs are finite; a program needn't handle non-finite values.
Results may differ from the reference program's by a relative error of at most 0.014.
Values may be sent and summed in bfloat16 or wider, within the bound.
No kernel may reach another device: no remote copies, remote signals or barrier semaphores. Data moves between devices by JAX's collectives and lax.ppermute only.
A program may use at most 64 MiB of HBM per device.

```python
import jax
import jax.numpy as jnp
from jax import lax

HQ = 128
KVH = 8
HD = 128
REQS = 4
QR = 64
PAGE = 256
SPAN = 256
CTX = 4096
LIVE_PAGES = 8


def page_split(key):
    largest = LIVE_PAGES // 2
    first_key, second_key, shuffle_key = jax.random.split(jax.random.fold_in(key, 11), 3)
    first_cut = jax.random.randint(first_key, (), 1, largest - 1)
    second_cut = jax.random.randint(second_key, (), 1, largest - first_cut)
    counts = jnp.stack([jnp.int32(largest), first_cut, second_cut, largest - first_cut - second_cut]).astype(jnp.int32)
    shuffle = jax.random.permutation(shuffle_key, REQS)
    return counts[shuffle]


def cache_field(key):
    field_values = jax.random.normal(jax.random.fold_in(key, 23), (2, CTX, KVH * HD), jnp.float32)
    field_values = jnp.clip(field_values, -6.0, 6.0)
    return field_values


def draw_page_counts(key, part):
    return page_split(key)


def draw_kv_cache(key, part):
    return cache_field(key).astype(jnp.bfloat16)


def draw_queries(key, part):
    drawn = jax.random.normal(jax.random.fold_in(key, 37), (SPAN, HQ * HD), jnp.float32)
    field_values = 2.5 * jnp.clip(drawn, -6.0, 6.0)
    return field_values.astype(jnp.bfloat16)


def setup_inputs(seed: int = 0, part: int = 0) -> dict:
    streams_of = jax.random.split(jax.random.key(seed), 4)
    own_keys = jax.random.split(jax.random.fold_in(streams_of[3], part), 4)
    return {
        "queries": draw_queries(jax.random.fold_in(jax.random.fold_in(streams_of[3], part), 71), part),
        "kv_cache": draw_kv_cache(jax.random.fold_in(jax.random.fold_in(streams_of[3], part), 71), part),
        "page_counts": draw_page_counts(jax.random.fold_in(jax.random.fold_in(streams_of[3], part), 71), part),
    }


NEG = -1e30


def reference(queries, kv_cache, page_counts):
    per_group = HQ // KVH
    live = LIVE_PAGES * PAGE
    base = CTX - live
    page_ends = jnp.cumsum(page_counts).astype(jnp.int32) * PAGE
    page_starts = page_ends - page_counts.astype(jnp.int32) * PAGE
    cache_keys = kv_cache[0, base:].astype(jnp.float32).reshape(live, KVH, HD)
    cache_values = kv_cache[1, base:].astype(jnp.float32).reshape(live, KVH, HD)
    grouped = queries.astype(jnp.float32).reshape(REQS, QR, KVH, per_group, HD)
    places = jnp.arange(live, dtype=jnp.int32)
    offsets = jnp.arange(QR, dtype=jnp.int32)
    score_scale = HD ** -0.5

    def one_request(request):
        query_pos = page_ends[request] - QR + offsets
        visible = (places[None, :] >= page_starts[request]) & (places[None, :] <= query_pos[:, None])
        request_rows = grouped[request]

        def one_head(head_id):
            query_head = request_rows[:, head_id]
            key_head = cache_keys[:, head_id]
            value_head = cache_values[:, head_id]
            scores = jnp.einsum('qgd,pd->qgp', query_head, key_head) * score_scale
            scores = jnp.where(visible[:, None, :], scores, NEG)
            top_score = jnp.max(scores, axis=2, keepdims=True)
            numerators = jnp.exp(scores - top_score)
            totals = jnp.sum(numerators, axis=2)
            weights = numerators.astype(jnp.bfloat16).astype(jnp.float32)
            return jnp.einsum('qgp,pd->qgd', weights, value_head) / totals[..., None]

        heads_out = lax.map(one_head, jnp.arange(KVH, dtype=jnp.int32))
        return jnp.transpose(heads_out, (1, 0, 2, 3))

    result = lax.map(one_request, jnp.arange(REQS, dtype=jnp.int32))
    return result.reshape(SPAN, HQ * HD).astype(jnp.bfloat16)
```

```python
import functools

import jax
import jax.numpy as jnp
from jax import lax
from jax.experimental import pallas as pl
from jax.experimental.pallas import tpu as pltpu
from jax.sharding import PartitionSpec as P

HQ = 128
KVH = 8
HD = 128
REQS = 4
QR = 64
PAGE = 256
SPAN = 256


NEG = -1e30
EXP2_SCALE = HD ** (-0.5) * 1.4426950408889634
PARTNERS = ((0, 1), (1, 0), (1, 1))


def moved(array, axes, pairs):
    return lax.ppermute(array, axes, pairs)


def split_kernel(head_axis_and_sub, queries, kv, kv_same, kv_cross, q0, q1, q2, sems):
    head_count, sub_count = head_axis_and_sub
    head, sub = lax.axis_index("head"), lax.axis_index("sub")
    width = kv.shape[2] // sub_count
    copies = []
    for out, there in ((kv_same, sub), (kv_cross, 1 - sub)):
        columns = pl.ds(pl.multiple_of(there * width, width), width)
        copies.append((kv.at[:, :, columns], out))
    width = queries.shape[1] // (head_count * sub_count)
    for out, (step_head, step_sub) in zip((q0, q1, q2), PARTNERS):
        there = (head ^ step_head) * sub_count + (sub ^ step_sub)
        columns = pl.ds(pl.multiple_of(there * width, width), width)
        copies.append((queries.at[:, columns], out))
    copies = [pltpu.make_async_copy(a, b, sems.at[i]) for i, (a, b) in enumerate(copies)]
    for copy in copies:
        copy.start()
    for copy in copies:
        copy.wait()


def join_kernel(head_axis_and_sub, o_own, o0, o1, o2, out, sems):
    head_count, sub_count = head_axis_and_sub
    head, sub = lax.axis_index("head"), lax.axis_index("sub")
    width = o_own.shape[1]
    copies = []
    for i, (piece, (step_head, step_sub)) in enumerate(zip((o_own, o0, o1, o2), ((0, 0),) + PARTNERS)):
        there = (head ^ step_head) * sub_count + (sub ^ step_sub)
        columns = pl.ds(pl.multiple_of(there * width, width), width)
        copies.append(pltpu.make_async_copy(piece, out.at[:, columns], sems.at[i]))
    for copy in copies:
        copy.start()
    for copy in copies:
        copy.wait()


def attend_kernel(
    head_axis_and_sub, most_pages,
    counts, queries, q0, q1, q2, own, paired, p_same, p_cross, x_same, x_cross, r_same, r_cross,
    o_own, o0, o1, o2,
    q_all, kv_all, o_all, q_sems, kv_sems, o_sems,
):
    head_count, sub_count = head_axis_and_sub
    ctx, head, sub = lax.axis_index("ctx"), lax.axis_index("head"), lax.axis_index("sub")
    tokens = queries.shape[0]
    width = q0.shape[1]
    local_kv = own.shape[2] // HD
    per_group = width // HD // local_kv
    place = head * sub_count + sub
    start = jnp.int32(0)
    for r in range(REQS):
        start = start + jnp.where(r < ctx, counts[r], 0)
    count = counts[ctx]

    columns = pl.ds(pl.multiple_of(place * width, width), width)
    q_copies = [pltpu.make_async_copy(queries.at[:, columns], q_all.at[0], q_sems.at[0])]
    for i, ref in enumerate((q0, q1, q2)):
        q_copies.append(pltpu.make_async_copy(ref, q_all.at[i + 1], q_sems.at[i + 1]))
    for copy in q_copies:
        copy.start()

    sources = (own, paired, p_same, p_cross, x_same, x_cross, r_same, r_cross)
    lower = sub == 0

    def either(first, second):
        return jnp.where(lower, first, second)

    table = (
        (either(2, 3), either(5, 4), -1, -1),
        (either(4, 5), either(3, 2), either(2, 3), -1),
        (either(0, 1), either(1, 0), either(6, 7), either(3, 2)),
        (-1, -1, either(0, 1), either(1, 0)),
    )

    def source_of(pair):
        found = jnp.int32(-1)
        for c in range(4):
            for n in range(4):
                found = jnp.where((ctx == c) & (pair == n), table[c][n], found)
        return found

    for p in range(most_pages):
        @pl.when(p < count)
        def _():
            page = start + p
            which = source_of(page // 2)
            rows = pl.ds(pl.multiple_of(lax.rem(page, 2) * PAGE, PAGE), PAGE)
            for i, ref in enumerate(sources):
                @pl.when(which == i)
                def _():
                    pltpu.make_async_copy(ref.at[:, rows, :], kv_all.at[p], kv_sems.at[p]).start()

    for copy in q_copies:
        copy.wait()
    for p in range(most_pages):
        @pl.when(p < count)
        def _():
            pltpu.make_async_copy(own.at[:, pl.ds(0, PAGE), :], kv_all.at[p], kv_sems.at[p]).wait()

    rows = per_group * tokens
    span = per_group * HD

    def attend(pages):
        def block(turn, carry):
            piece = turn // local_kv
            group = lax.rem(turn, local_kv)
            step = jnp.where(piece == 0, 0, jnp.where(piece == 1, 1, jnp.where(piece == 2, sub_count, sub_count + 1)))
            first_token = (place ^ step) * tokens
            q_cols = pl.ds(pl.multiple_of(group * span, span), span)
            kv_cols = pl.ds(pl.multiple_of(group * HD, HD), HD)
            q_block = q_all[piece, :, q_cols]
            q_rows = jnp.concatenate([q_block[:, j * HD:(j + 1) * HD] for j in range(per_group)], axis=0)
            scores = [
                lax.dot_general(
                    q_rows, kv_all[p, 0, :, kv_cols], (((1,), (1,)), ((), ())), preferred_element_type=jnp.float32
                )
                for p in range(pages)
            ]
            token = lax.rem(lax.broadcasted_iota(jnp.int32, (rows, PAGE), 0), tokens)
            column = lax.broadcasted_iota(jnp.int32, (rows, PAGE), 1)
            visible = column <= PAGE - QR + first_token + token
            scores[-1] = jnp.where(visible, scores[-1], NEG)
            top = functools.reduce(jnp.maximum, scores)
            top = jnp.max(top, axis=1, keepdims=True)
            numerators = [jnp.exp2((s - top) * EXP2_SCALE) for s in scores]
            totals = jnp.sum(functools.reduce(jnp.add, numerators), axis=1, keepdims=True)
            product = functools.reduce(
                jnp.add,
                [
                    jnp.dot(n.astype(jnp.bfloat16), kv_all[p, 1, :, kv_cols], preferred_element_type=jnp.float32)
                    for p, n in enumerate(numerators)
                ],
            )
            done = (product / totals).astype(jnp.bfloat16)
            done = jnp.concatenate([done[j * tokens:(j + 1) * tokens] for j in range(per_group)], axis=1)
            o_all[piece, :, q_cols] = done
            return carry

        lax.fori_loop(0, 4 * local_kv, block, 0)

    for pages in range(1, most_pages + 1):
        @pl.when(count == pages)
        def _():
            attend(pages)

    o_copies = [
        pltpu.make_async_copy(o_all.at[i], ref, o_sems.at[i]) for i, ref in enumerate((o_own, o0, o1, o2))
    ]
    for copy in o_copies:
        copy.start()
    for copy in o_copies:
        copy.wait()


def pages_to_queries(queries, kv_cache, page_counts):
    ctx_size, sub_size = lax.axis_size("ctx"), lax.axis_size("sub")
    head_count = lax.axis_size("head")
    most_pages = kv_cache.shape[1] // PAGE * ctx_size * sub_size // 4
    tokens, width = queries.shape[0], queries.shape[1] // (head_count * sub_size)
    half = kv_cache.shape[:2] + (kv_cache.shape[2] // sub_size,)
    anywhere = pl.BlockSpec(memory_space=pl.ANY)
    q_piece = jax.ShapeDtypeStruct((tokens, width), queries.dtype)
    kv_piece = jax.ShapeDtypeStruct(half, kv_cache.dtype)
    sizes = (head_count, sub_size)

    kv_same, kv_cross, q0, q1, q2 = pl.pallas_call(
        functools.partial(split_kernel, sizes),
        out_shape=[kv_piece, kv_piece, q_piece, q_piece, q_piece],
        in_specs=[anywhere] * 2,
        out_specs=[anywhere] * 5,
        scratch_shapes=[pltpu.SemaphoreType.DMA((5,))],
        name="split",
    )(queries, kv_cache)

    def at(ctx, sub):
        return ctx * sub_size + sub

    line = ("ctx", "sub")
    p_same = moved(kv_same, line, [(at(2, 0), at(0, 0)), (at(2, 1), at(1, 1)), (at(3, 0), at(1, 0)), (at(3, 1), at(2, 1))])
    p_cross = moved(kv_cross, line, [(at(2, 0), at(0, 1)), (at(2, 1), at(1, 0)), (at(3, 0), at(1, 1)), (at(3, 1), at(2, 0))])
    q_in = []
    for piece, (step_head, step_sub) in zip((q0, q1, q2), PARTNERS):
        pairs = [
            (h * sub_size + s, (h ^ step_head) * sub_size + (s ^ step_sub))
            for h in range(head_count) for s in range(sub_size)
        ]
        q_in.append(moved(piece, ("head", "sub"), pairs))
    paired = moved(kv_cross, line, [(at(c, s), at(c, 1 - s)) for c in (2, 3) for s in (0, 1)])
    r_same = moved(kv_same, line, [(at(3, 0), at(2, 0))])
    r_cross = moved(kv_cross, line, [(at(3, 0), at(2, 1))])
    x_same = moved(p_same, line, [(at(0, 0), at(1, 0)), (at(1, 1), at(0, 1))])
    x_cross = moved(p_cross, line, [(at(0, 1), at(1, 1)), (at(1, 0), at(0, 0))])

    outs = pl.pallas_call(
        functools.partial(attend_kernel, sizes, most_pages),
        out_shape=[q_piece] * 4,
        in_specs=[pl.BlockSpec(memory_space=pltpu.SMEM)] + [anywhere] * 12,
        out_specs=[anywhere] * 4,
        scratch_shapes=[
            pltpu.VMEM((4, tokens, width), queries.dtype),
            pltpu.VMEM((most_pages, 2, PAGE, half[2]), kv_cache.dtype),
            pltpu.VMEM((4, tokens, width), queries.dtype),
            pltpu.SemaphoreType.DMA((4,)),
            pltpu.SemaphoreType.DMA((most_pages,)),
            pltpu.SemaphoreType.DMA((4,)),
        ],
        compiler_params=pltpu.CompilerParams(vmem_limit_bytes=32 * 1024 * 1024),
        name="attend",
    )(page_counts, queries, *q_in, kv_same, paired, p_same, p_cross, x_same, x_cross, r_same, r_cross)

    back = [outs[0]]
    for piece, (step_head, step_sub) in zip(outs[1:], PARTNERS):
        pairs = [
            (h * sub_size + s, (h ^ step_head) * sub_size + (s ^ step_sub))
            for h in range(head_count) for s in range(sub_size)
        ]
        back.append(moved(piece, ("head", "sub"), pairs))
    return pl.pallas_call(
        functools.partial(join_kernel, sizes),
        out_shape=jax.ShapeDtypeStruct(queries.shape, queries.dtype),
        in_specs=[anywhere] * 4,
        out_specs=anywhere,
        scratch_shapes=[pltpu.SemaphoreType.DMA((4,))],
        name="join",
    )(*back)


def from_behind(array, axis, by):
    count = lax.axis_size(axis)
    pairs = [(i, i + by) for i in range(count) if 0 <= i + by < count]
    return lax.ppermute(array, axis, pairs)


def queries_to_pages(queries, kv_cache, page_counts):
    per_group = HQ // KVH
    local_heads = kv_cache.shape[2] // HD
    ctx_size = lax.axis_size("ctx")
    sub_size = lax.axis_size("sub")
    head_count = lax.axis_size("head")
    tok_rows = queries.shape[0]
    score_scale = HD ** (-0.5)
    regrouped = lax.all_to_all(queries, "head", split_axis=1, concat_axis=0, tiled=True)
    all_queries = lax.all_gather(regrouped, ("ctx", "sub"), axis=0, tiled=True)
    all_queries = all_queries.reshape(SPAN, local_heads, per_group, HD)
    page_ends = jnp.cumsum(page_counts)
    ctx_rows = SPAN // ctx_size
    offsets = jnp.arange(QR, dtype=jnp.int32)
    columns = jnp.arange(PAGE, dtype=jnp.int32)
    flat_index = lax.axis_index("ctx") * sub_size + lax.axis_index("sub")
    pages_here = kv_cache.shape[1] // PAGE
    base_pages = pages_here * ctx_size * sub_size // 2
    initial = (
        jnp.full((SPAN, local_heads, per_group), NEG, jnp.float32),
        jnp.zeros((SPAN, local_heads, per_group), jnp.float32),
        jnp.zeros((SPAN, local_heads, per_group, HD), jnp.float32),
    )
    half_rows = kv_cache.shape[1] // 2
    arrived = from_behind(kv_cache[:, half_rows:], "ctx", -(ctx_size // 2))
    is_lower = lax.axis_index("ctx") < ctx_size // 2
    source_flat = flat_index + ctx_size // 2 * sub_size
    working = jnp.where(is_lower, arrived, kv_cache[:, :half_rows])
    first_page = jnp.where(
        is_lower, source_flat * pages_here + pages_here // 2, flat_index * pages_here
    )
    page_total = working.shape[1] // PAGE

    def add_page(page_turn, running):
        page_index = first_page + page_turn
        relative = page_index - base_pages
        counted = jnp.sum((relative >= page_ends).astype(jnp.int32))
        request = jnp.where(relative < 0, REQS, counted)

        def update(partial_value):
            run_max, run_sum, run_out = partial_value
            request_id = jnp.minimum(request, REQS - 1)
            row_start = request_id * QR
            gathered = row_start + offsets
            within = gathered % ctx_rows
            ctx_block = gathered // ctx_rows
            sub_part = within // (head_count * tok_rows)
            head_part = within // tok_rows % head_count
            tok_part = within % tok_rows
            natural = ctx_block * ctx_rows + (head_part * sub_size + sub_part) * tok_rows + tok_part
            query_pos = (page_ends[request_id] + base_pages) * PAGE - QR + natural - row_start
            key_pos = page_index * PAGE + columns
            visible = key_pos[None, :] <= query_pos[:, None]
            page_keys = working[0].reshape(PAGE, local_heads, HD)
            page_values = working[1].reshape(PAGE, local_heads, HD)
            query_rows = lax.dynamic_slice_in_dim(all_queries, row_start, QR, 0)
            scores = (
                jnp.einsum(
                    "qkgd,pkd->qkgp", query_rows, page_keys, preferred_element_type=jnp.float32
                )
                * score_scale
            )
            scores = jnp.where(visible[:, None, None, :], scores, NEG)
            old_max = lax.dynamic_slice_in_dim(run_max, row_start, QR, 0)
            old_sum = lax.dynamic_slice_in_dim(run_sum, row_start, QR, 0)
            old_out = lax.dynamic_slice_in_dim(run_out, row_start, QR, 0)
            new_max = jnp.maximum(old_max, jnp.max(scores, axis=3))
            factor = jnp.exp(old_max - new_max)
            numerators = jnp.exp(scores - new_max[..., None])
            new_sum = old_sum * factor + jnp.sum(numerators, axis=3)
            product = jnp.einsum(
                "qkgp,pkd->qkgd",
                numerators.astype(jnp.bfloat16),
                page_values,
                preferred_element_type=jnp.float32,
            )
            new_out = old_out * factor[..., None] + product
            return (
                lax.dynamic_update_slice_in_dim(run_max, new_max, row_start, 0),
                lax.dynamic_update_slice_in_dim(run_sum, new_sum, row_start, 0),
                lax.dynamic_update_slice_in_dim(run_out, new_out, row_start, 0),
            )

        def unchanged(partial_value):
            return partial_value

        return lax.cond(request < REQS, update, unchanged, running)

    run_max, run_sum, run_out = lax.fori_loop(0, page_total, add_page, initial)
    share = SPAN // (ctx_size * sub_size)
    global_max = lax.pmax(run_max, ("ctx", "sub"))
    factor = jnp.exp(run_max - global_max)
    sums_here, outs_here = (
        lax.psum_scatter(
            (run_sum * factor).astype(jnp.bfloat16), ("ctx", "sub"), scatter_dimension=0, tiled=True
        ).astype(jnp.float32),
        lax.psum_scatter(
            (run_out * factor[..., None]).astype(jnp.bfloat16),
            ("ctx", "sub"),
            scatter_dimension=0,
            tiled=True,
        ).astype(jnp.float32),
    )
    finished = (outs_here / sums_here[..., None]).astype(jnp.bfloat16)
    finished = finished.reshape(share, local_heads * per_group * HD)
    return lax.all_to_all(finished, "head", split_axis=0, concat_axis=1, tiled=True)


def per_device(queries, kv_cache, page_counts):
    ctx_size, sub_size, head_count = lax.axis_size("ctx"), lax.axis_size("sub"), lax.axis_size("head")
    small = (
        ctx_size == REQS == 4
        and head_count == sub_size == 2
        and kv_cache.shape[1] == 2 * PAGE
        and kv_cache.shape[2] % (sub_size * HD) == 0
        and queries.shape[0] % 16 == 0
        and queries.shape[0] * head_count * sub_size == QR
    )
    return (pages_to_queries if small else queries_to_pages)(queries, kv_cache, page_counts)


def solution(mesh):
    return jax.shard_map(
        per_device,
        mesh=mesh,
        in_specs=(
            P(("grp", "ctx", "head", "sub"), None),
            P(None, ("grp", "ctx", "sub"), "head"),
            P("grp"),
        ),
        out_specs=P(("grp", "ctx", "head", "sub"), None),
        check_vma=False,
    )
```

```python
import functools

import jax
import jax.numpy as jnp
from jax import lax
from jax.experimental import pallas as pl
from jax.experimental.pallas import tpu as pltpu
from jax.sharding import PartitionSpec as P

HQ = 128
KVH = 8
HD = 128
REQS = 4
QR = 64
PAGE = 256
SPAN = 256


NEG = -1e30
EXP2_SCALE = HD ** (-0.5) * 1.4426950408889634
PARTNERS = ((0, 1), (1, 0), (1, 1))


def moved(array, axes, pairs):
    return lax.ppermute(array, axes, pairs)


def staged(copies, sems):
    inward = [pltpu.make_async_copy(a, m, sems.at[0, i]) for i, (a, m, _) in enumerate(copies)]
    outward = [pltpu.make_async_copy(m, b, sems.at[1, i]) for i, (_, m, b) in enumerate(copies)]
    for copy in inward:
        copy.start()
    for first, second in zip(inward, outward):
        first.wait()
        second.start()
    for copy in outward:
        copy.wait()


def split_pages_kernel(kv, kv_same, kv_cross, stage, sems):
    sub = lax.axis_index("sub")
    width = kv_same.shape[2]
    copies = []
    for i, (out, there) in enumerate(((kv_same, sub), (kv_cross, 1 - sub))):
        columns = pl.ds(pl.multiple_of(there * width, width), width)
        copies.append((kv.at[:, :, columns], stage.at[i], out))
    staged(copies, sems)


def split_queries_kernel(sizes, queries, q0, q1, q2, stage, sems):
    head, sub = lax.axis_index("head"), lax.axis_index("sub")
    width = q0.shape[1]
    copies = []
    for i, (out, (step_head, step_sub)) in enumerate(zip((q0, q1, q2), PARTNERS)):
        there = (head ^ step_head) * sizes[1] + (sub ^ step_sub)
        columns = pl.ds(pl.multiple_of(there * width, width), width)
        copies.append((queries.at[:, columns], stage.at[i], out))
    staged(copies, sems)


def join_kernel(sizes, o_own, o0, o1, o2, out, sems):
    head, sub = lax.axis_index("head"), lax.axis_index("sub")
    width = o_own.shape[1]
    copies = []
    for i, (piece, (step_head, step_sub)) in enumerate(zip((o_own, o0, o1, o2), ((0, 0),) + PARTNERS)):
        there = (head ^ step_head) * sizes[1] + (sub ^ step_sub)
        columns = pl.ds(pl.multiple_of(there * width, width), width)
        copies.append(pltpu.make_async_copy(piece, out.at[:, columns], sems.at[i]))
    for copy in copies:
        copy.start()
    for copy in copies:
        copy.wait()


def attend_kernel(
    sizes, most_pages,
    counts, queries, q0, q1, q2, own, paired, p_same, p_cross, x_same, x_cross, r_same, r_cross,
    o_own, o0, o1, o2,
    q_all, kv_all, o_all, q_sems, kv_sems, o_sems,
):
    head_count, sub_count = sizes
    ctx, head, sub = lax.axis_index("ctx"), lax.axis_index("head"), lax.axis_index("sub")
    tokens = queries.shape[0]
    width = q0.shape[1]
    local_kv = own.shape[2] // HD
    per_group = width // HD // local_kv
    place = head * sub_count + sub
    start = jnp.int32(0)
    for r in range(REQS):
        start = start + jnp.where(r < ctx, counts[r], 0)
    count = counts[ctx]

    columns = pl.ds(pl.multiple_of(place * width, width), width)
    q_copies = [pltpu.make_async_copy(queries.at[:, columns], q_all.at[0], q_sems.at[0])]
    for i, ref in enumerate((q0, q1, q2)):
        q_copies.append(pltpu.make_async_copy(ref, q_all.at[i + 1], q_sems.at[i + 1]))
    for copy in q_copies:
        copy.start()

    sources = (own, paired, p_same, p_cross, x_same, x_cross, r_same, r_cross)
    lower = sub == 0

    def either(first, second):
        return jnp.where(lower, first, second)

    table = (
        (either(2, 3), either(5, 4), -1, -1),
        (either(4, 5), either(3, 2), either(6, 7), -1),
        (either(0, 1), either(1, 0), either(2, 3), either(3, 2)),
        (-1, -1, either(0, 1), either(1, 0)),
    )

    def source_of(pair):
        found = jnp.int32(-1)
        for c in range(4):
            for n in range(4):
                found = jnp.where((ctx == c) & (pair == n), table[c][n], found)
        return found

    for p in range(most_pages):
        @pl.when(p < count)
        def _():
            page = start + p
            which = source_of(page // 2)
            rows = pl.ds(pl.multiple_of(lax.rem(page, 2) * PAGE, PAGE), PAGE)
            for i, ref in enumerate(sources):
                @pl.when(which == i)
                def _():
                    pltpu.make_async_copy(ref.at[:, rows, :], kv_all.at[p], kv_sems.at[p]).start()

    for copy in q_copies:
        copy.wait()
    for p in range(most_pages):
        @pl.when(p < count)
        def _():
            pltpu.make_async_copy(own.at[:, pl.ds(0, PAGE), :], kv_all.at[p], kv_sems.at[p]).wait()

    rows = per_group * tokens
    span = per_group * HD

    def attend(pages):
        def block(turn, carry):
            piece = turn // local_kv
            group = lax.rem(turn, local_kv)
            step = jnp.where(piece == 0, 0, jnp.where(piece == 1, 1, jnp.where(piece == 2, sub_count, sub_count + 1)))
            first_token = (place ^ step) * tokens
            q_cols = pl.ds(pl.multiple_of(group * span, span), span)
            kv_cols = pl.ds(pl.multiple_of(group * HD, HD), HD)
            q_block = q_all[piece, :, q_cols]
            q_rows = jnp.concatenate([q_block[:, j * HD:(j + 1) * HD] for j in range(per_group)], axis=0)
            scores = [
                lax.dot_general(
                    q_rows, kv_all[p, 0, :, kv_cols], (((1,), (1,)), ((), ())), preferred_element_type=jnp.float32
                )
                for p in range(pages)
            ]
            token = lax.rem(lax.broadcasted_iota(jnp.int32, (rows, PAGE), 0), tokens)
            column = lax.broadcasted_iota(jnp.int32, (rows, PAGE), 1)
            visible = column <= PAGE - QR + first_token + token
            scores[-1] = jnp.where(visible, scores[-1], NEG)
            top = functools.reduce(jnp.maximum, scores)
            top = jnp.max(top, axis=1, keepdims=True)
            numerators = [jnp.exp2((s - top) * EXP2_SCALE) for s in scores]
            totals = jnp.sum(functools.reduce(jnp.add, numerators), axis=1, keepdims=True)
            product = functools.reduce(
                jnp.add,
                [
                    jnp.dot(n.astype(jnp.bfloat16), kv_all[p, 1, :, kv_cols], preferred_element_type=jnp.float32)
                    for p, n in enumerate(numerators)
                ],
            )
            done = (product / totals).astype(jnp.bfloat16)
            done = jnp.concatenate([done[j * tokens:(j + 1) * tokens] for j in range(per_group)], axis=1)
            o_all[piece, :, q_cols] = done
            return carry

        lax.fori_loop(0, 4 * local_kv, block, 0)

    for pages in range(1, most_pages + 1):
        @pl.when(count == pages)
        def _():
            attend(pages)

    o_copies = [
        pltpu.make_async_copy(o_all.at[i], ref, o_sems.at[i]) for i, ref in enumerate((o_own, o0, o1, o2))
    ]
    for copy in o_copies:
        copy.start()
    for copy in o_copies:
        copy.wait()


def pages_to_queries(queries, kv_cache, page_counts):
    ctx_size, sub_size = lax.axis_size("ctx"), lax.axis_size("sub")
    head_count = lax.axis_size("head")
    most_pages = kv_cache.shape[1] // PAGE * ctx_size * sub_size // 4
    tokens, width = queries.shape[0], queries.shape[1] // (head_count * sub_size)
    half = kv_cache.shape[:2] + (kv_cache.shape[2] // sub_size,)
    anywhere = pl.BlockSpec(memory_space=pl.ANY)
    q_piece = jax.ShapeDtypeStruct((tokens, width), queries.dtype)
    kv_piece = jax.ShapeDtypeStruct(half, kv_cache.dtype)
    sizes = (head_count, sub_size)

    kv_same, kv_cross = pl.pallas_call(
        split_pages_kernel,
        out_shape=[kv_piece, kv_piece],
        in_specs=[anywhere],
        out_specs=[anywhere] * 2,
        scratch_shapes=[pltpu.VMEM((2,) + half, kv_cache.dtype), pltpu.SemaphoreType.DMA((2, 2))],
        name="split_pages",
    )(kv_cache)
    q_out = pl.pallas_call(
        functools.partial(split_queries_kernel, sizes),
        out_shape=[q_piece] * 3,
        in_specs=[anywhere],
        out_specs=[anywhere] * 3,
        scratch_shapes=[pltpu.VMEM((3, tokens, width), queries.dtype), pltpu.SemaphoreType.DMA((2, 3))],
        name="split_queries",
    )(queries)

    def at(ctx, sub):
        return ctx * sub_size + sub

    line = ("ctx", "sub")
    p_same = moved(kv_same, line, [(at(2, 0), at(0, 0)), (at(2, 1), at(1, 1)), (at(3, 0), at(2, 0)), (at(3, 1), at(2, 1))])
    p_cross = moved(kv_cross, line, [(at(2, 0), at(0, 1)), (at(2, 1), at(1, 0)), (at(3, 0), at(2, 1)), (at(3, 1), at(2, 0))])
    r_same = moved(kv_same, line, [(at(3, 0), at(1, 0))])
    r_cross = moved(kv_cross, line, [(at(3, 0), at(1, 1))])
    q_in = []
    for piece, (step_head, step_sub) in zip(q_out, PARTNERS):
        pairs = [
            (h * sub_size + s, (h ^ step_head) * sub_size + (s ^ step_sub))
            for h in range(head_count) for s in range(sub_size)
        ]
        q_in.append(moved(piece, ("head", "sub"), pairs))
    paired = moved(kv_cross, line, [(at(c, s), at(c, 1 - s)) for c in (2, 3) for s in (0, 1)])
    x_same = moved(p_same, line, [(at(0, 0), at(1, 0)), (at(1, 1), at(0, 1))])
    x_cross = moved(p_cross, line, [(at(0, 1), at(1, 1)), (at(1, 0), at(0, 0))])

    outs = pl.pallas_call(
        functools.partial(attend_kernel, sizes, most_pages),
        out_shape=[q_piece] * 4,
        in_specs=[pl.BlockSpec(memory_space=pltpu.SMEM)] + [anywhere] * 12,
        out_specs=[anywhere] * 4,
        scratch_shapes=[
            pltpu.VMEM((4, tokens, width), queries.dtype),
            pltpu.VMEM((most_pages, 2, PAGE, half[2]), kv_cache.dtype),
            pltpu.VMEM((4, tokens, width), queries.dtype),
            pltpu.SemaphoreType.DMA((4,)),
            pltpu.SemaphoreType.DMA((most_pages,)),
            pltpu.SemaphoreType.DMA((4,)),
        ],
        compiler_params=pltpu.CompilerParams(vmem_limit_bytes=32 * 1024 * 1024),
        name="attend",
    )(page_counts, queries, *q_in, kv_same, paired, p_same, p_cross, x_same, x_cross, r_same, r_cross)

    back = [outs[0]]
    for piece, (step_head, step_sub) in zip(outs[1:], PARTNERS):
        pairs = [
            (h * sub_size + s, (h ^ step_head) * sub_size + (s ^ step_sub))
            for h in range(head_count) for s in range(sub_size)
        ]
        back.append(moved(piece, ("head", "sub"), pairs))
    return pl.pallas_call(
        functools.partial(join_kernel, sizes),
        out_shape=jax.ShapeDtypeStruct(queries.shape, queries.dtype),
        in_specs=[anywhere] * 4,
        out_specs=pl.BlockSpec(memory_space=pltpu.VMEM),
        scratch_shapes=[pltpu.SemaphoreType.DMA((4,))],
        name="join",
    )(*back)


def from_behind(array, axis, by):
    count = lax.axis_size(axis)
    pairs = [(i, i + by) for i in range(count) if 0 <= i + by < count]
    return lax.ppermute(array, axis, pairs)


def queries_to_pages(queries, kv_cache, page_counts):
    per_group = HQ // KVH
    local_heads = kv_cache.shape[2] // HD
    ctx_size = lax.axis_size("ctx")
    sub_size = lax.axis_size("sub")
    head_count = lax.axis_size("head")
    tok_rows = queries.shape[0]
    score_scale = HD ** (-0.5)
    regrouped = lax.all_to_all(queries, "head", split_axis=1, concat_axis=0, tiled=True)
    all_queries = lax.all_gather(regrouped, ("ctx", "sub"), axis=0, tiled=True)
    all_queries = all_queries.reshape(SPAN, local_heads, per_group, HD)
    page_ends = jnp.cumsum(page_counts)
    ctx_rows = SPAN // ctx_size
    offsets = jnp.arange(QR, dtype=jnp.int32)
    columns = jnp.arange(PAGE, dtype=jnp.int32)
    flat_index = lax.axis_index("ctx") * sub_size + lax.axis_index("sub")
    pages_here = kv_cache.shape[1] // PAGE
    base_pages = pages_here * ctx_size * sub_size // 2
    initial = (
        jnp.full((SPAN, local_heads, per_group), NEG, jnp.float32),
        jnp.zeros((SPAN, local_heads, per_group), jnp.float32),
        jnp.zeros((SPAN, local_heads, per_group, HD), jnp.float32),
    )
    half_rows = kv_cache.shape[1] // 2
    arrived = from_behind(kv_cache[:, half_rows:], "ctx", -(ctx_size // 2))
    is_lower = lax.axis_index("ctx") < ctx_size // 2
    source_flat = flat_index + ctx_size // 2 * sub_size
    working = jnp.where(is_lower, arrived, kv_cache[:, :half_rows])
    first_page = jnp.where(
        is_lower, source_flat * pages_here + pages_here // 2, flat_index * pages_here
    )
    page_total = working.shape[1] // PAGE

    def add_page(page_turn, running):
        page_index = first_page + page_turn
        relative = page_index - base_pages
        counted = jnp.sum((relative >= page_ends).astype(jnp.int32))
        request = jnp.where(relative < 0, REQS, counted)

        def update(partial_value):
            run_max, run_sum, run_out = partial_value
            request_id = jnp.minimum(request, REQS - 1)
            row_start = request_id * QR
            gathered = row_start + offsets
            within = gathered % ctx_rows
            ctx_block = gathered // ctx_rows
            sub_part = within // (head_count * tok_rows)
            head_part = within // tok_rows % head_count
            tok_part = within % tok_rows
            natural = ctx_block * ctx_rows + (head_part * sub_size + sub_part) * tok_rows + tok_part
            query_pos = (page_ends[request_id] + base_pages) * PAGE - QR + natural - row_start
            key_pos = page_index * PAGE + columns
            visible = key_pos[None, :] <= query_pos[:, None]
            page_keys = working[0].reshape(PAGE, local_heads, HD)
            page_values = working[1].reshape(PAGE, local_heads, HD)
            query_rows = lax.dynamic_slice_in_dim(all_queries, row_start, QR, 0)
            scores = (
                jnp.einsum(
                    "qkgd,pkd->qkgp", query_rows, page_keys, preferred_element_type=jnp.float32
                )
                * score_scale
            )
            scores = jnp.where(visible[:, None, None, :], scores, NEG)
            old_max = lax.dynamic_slice_in_dim(run_max, row_start, QR, 0)
            old_sum = lax.dynamic_slice_in_dim(run_sum, row_start, QR, 0)
            old_out = lax.dynamic_slice_in_dim(run_out, row_start, QR, 0)
            new_max = jnp.maximum(old_max, jnp.max(scores, axis=3))
            factor = jnp.exp(old_max - new_max)
            numerators = jnp.exp(scores - new_max[..., None])
            new_sum = old_sum * factor + jnp.sum(numerators, axis=3)
            product = jnp.einsum(
                "qkgp,pkd->qkgd",
                numerators.astype(jnp.bfloat16),
                page_values,
                preferred_element_type=jnp.float32,
            )
            new_out = old_out * factor[..., None] + product
            return (
                lax.dynamic_update_slice_in_dim(run_max, new_max, row_start, 0),
                lax.dynamic_update_slice_in_dim(run_sum, new_sum, row_start, 0),
                lax.dynamic_update_slice_in_dim(run_out, new_out, row_start, 0),
            )

        def unchanged(partial_value):
            return partial_value

        return lax.cond(request < REQS, update, unchanged, running)

    run_max, run_sum, run_out = lax.fori_loop(0, page_total, add_page, initial)
    share = SPAN // (ctx_size * sub_size)
    global_max = lax.pmax(run_max, ("ctx", "sub"))
    factor = jnp.exp(run_max - global_max)
    sums_here, outs_here = (
        lax.psum_scatter(
            (run_sum * factor).astype(jnp.bfloat16), ("ctx", "sub"), scatter_dimension=0, tiled=True
        ).astype(jnp.float32),
        lax.psum_scatter(
            (run_out * factor[..., None]).astype(jnp.bfloat16),
            ("ctx", "sub"),
            scatter_dimension=0,
            tiled=True,
        ).astype(jnp.float32),
    )
    finished = (outs_here / sums_here[..., None]).astype(jnp.bfloat16)
    finished = finished.reshape(share, local_heads * per_group * HD)
    return lax.all_to_all(finished, "head", split_axis=0, concat_axis=1, tiled=True)


def per_device(queries, kv_cache, page_counts):
    ctx_size, sub_size, head_count = lax.axis_size("ctx"), lax.axis_size("sub"), lax.axis_size("head")
    small = (
        ctx_size == REQS == 4
        and head_count == sub_size == 2
        and kv_cache.shape[1] == 2 * PAGE
        and kv_cache.shape[2] % (sub_size * HD) == 0
        and queries.shape[0] % 16 == 0
        and queries.shape[0] * head_count * sub_size == QR
    )
    return (pages_to_queries if small else queries_to_pages)(queries, kv_cache, page_counts)


def solution(mesh):
    return jax.shard_map(
        per_device,
        mesh=mesh,
        in_specs=(
            P(("grp", "ctx", "head", "sub"), None),
            P(None, ("grp", "ctx", "sub"), "head"),
            P("grp"),
        ),
        out_specs=P(("grp", "ctx", "head", "sub"), None),
        check_vma=False,
    )
```

```python
import functools

import jax
import jax.numpy as jnp
from jax import lax
from jax.experimental import pallas as pl
from jax.experimental.pallas import tpu as pltpu
from jax.sharding import PartitionSpec as P

HQ = 128
KVH = 8
HD = 128
REQS = 4
QR = 64
PAGE = 256
SPAN = 256


NEG = -1e30
EXP2_SCALE = HD ** (-0.5) * 1.4426950408889634
STEPS = ((0, 0), (0, 1), (1, 0), (1, 1))


def staged(copies, sems):
    inward = [pltpu.make_async_copy(a, m, sems.at[0, i]) for i, (a, m, _) in enumerate(copies)]
    outward = [pltpu.make_async_copy(m, b, sems.at[1, i]) for i, (_, m, b) in enumerate(copies)]
    for copy in inward:
        copy.start()
    for first, second in zip(inward, outward):
        first.wait()
        second.start()
    for copy in outward:
        copy.wait()


def place_of(step, sizes):
    head, sub = lax.axis_index("head"), lax.axis_index("sub")
    return (head ^ step[0]) * sizes[1] + (sub ^ step[1])


def part_of(place, width):
    return pl.ds(pl.multiple_of(place * width, width), width)


def split_pages_kernel(kv, after, kv_same, kv_cross, stage, sems):
    sub = lax.axis_index("sub")
    width = kv_same.shape[2]
    copies = [
        (kv.at[:, :, part_of(there, width)], stage.at[i], out)
        for i, (out, there) in enumerate(((kv_same, sub), (kv_cross, 1 - sub)))
    ]
    staged(copies, sems)


def split_queries_kernel(sizes, queries, *refs):
    outs, (stage, sems) = refs[:4], refs[4:]
    width = outs[0].shape[1]
    copies = [
        (queries.at[:, part_of(place_of(step, sizes), width)], stage.at[i], out)
        for i, (out, step) in enumerate(zip(outs, STEPS))
    ]
    staged(copies, sems)


def join_kernel(sizes, low_ctx, *refs):
    sources, (out, sems) = refs[:-2], refs[-2:]
    width = sources[0].shape[1]
    ctx = lax.axis_index("ctx")
    for group in range(low_ctx + 1):
        @pl.when(ctx == group if group < low_ctx else ctx >= low_ctx)
        def _():
            for i, step in enumerate(STEPS):
                part = part_of(place_of(step, sizes), width)
                pltpu.make_async_copy(sources[group * 4 + i], out.at[:, part], sems.at[i]).start()
    for i, step in enumerate(STEPS):
        part = part_of(place_of(step, sizes), width)
        pltpu.make_async_copy(sources[i], out.at[:, part], sems.at[i]).wait()


def attend_kernel(sizes, low_ctx, slots, most_pages, piece, waits, counts, *refs):
    items = low_ctx if piece is not None else 4
    q_in, (own, paired, r_same, r_cross) = refs[:items], refs[items:items + 4]
    o_out = refs[items + 4 + waits:2 * items + 4 + waits]
    q_all, kv_all, o_all, q_sems, kv_sems, o_sems = refs[2 * items + 4 + waits:]
    ctx, sub = lax.axis_index("ctx"), lax.axis_index("sub")
    tokens, width = q_all.shape[1:]
    local_kv = own.shape[2] // HD
    per_group = width // HD // local_kv
    rows = per_group * tokens
    span = per_group * HD

    def start_of(request):
        start = jnp.int32(0)
        for r in range(REQS):
            start = start + jnp.where(r < request, counts[r], 0)
        return start

    if piece is None:
        first_slot = start_of(ctx)
        used = counts[ctx]
    else:
        first_slot = jnp.int32(0)
        used = start_of(low_ctx)

    def work():
        q_copies = [pltpu.make_async_copy(ref, q_all.at[i], q_sems.at[i]) for i, ref in enumerate(q_in)]
        for copy in q_copies:
            copy.start()
        here = jnp.where(ctx == low_ctx, 0, 2)
        for p in range(slots):
            @pl.when(p < used)
            def _():
                page = first_slot + p
                pair = page // 2
                odd = lax.rem(pair, 2) != sub
                which = jnp.where(pair // 2 * 2 == here, 0, 2) + odd.astype(jnp.int32)
                page_rows = pl.ds(pl.multiple_of(lax.rem(page, 2) * PAGE, PAGE), PAGE)
                for i, ref in enumerate((own, paired, r_same, r_cross)):
                    @pl.when(which == i)
                    def _():
                        pltpu.make_async_copy(ref.at[:, page_rows, :], kv_all.at[p], kv_sems.at[p]).start()
        for copy in q_copies:
            copy.wait()
        for p in range(slots):
            @pl.when(p < used)
            def _():
                pltpu.make_async_copy(own.at[:, pl.ds(0, PAGE), :], kv_all.at[p], kv_sems.at[p]).wait()

        def attend(item, request_slot, first_token, pages):
            def block(group, carry):
                q_cols = pl.ds(pl.multiple_of(group * span, span), span)
                kv_cols = pl.ds(pl.multiple_of(group * HD, HD), HD)
                q_block = q_all[item, :, q_cols]
                q_rows = jnp.concatenate([q_block[:, j * HD:(j + 1) * HD] for j in range(per_group)], axis=0)
                scores = [
                    lax.dot_general(
                        q_rows, kv_all[request_slot + p, 0, :, kv_cols], (((1,), (1,)), ((), ())),
                        preferred_element_type=jnp.float32,
                    )
                    for p in range(pages)
                ]
                token = lax.rem(lax.broadcasted_iota(jnp.int32, (rows, PAGE), 0), tokens)
                column = lax.broadcasted_iota(jnp.int32, (rows, PAGE), 1)
                visible = column <= PAGE - QR + first_token + token
                scores[-1] = jnp.where(visible, scores[-1], NEG)
                top = functools.reduce(jnp.maximum, scores)
                top = jnp.max(top, axis=1, keepdims=True)
                numerators = [jnp.exp2((s - top) * EXP2_SCALE) for s in scores]
                totals = jnp.sum(functools.reduce(jnp.add, numerators), axis=1, keepdims=True)
                product = functools.reduce(
                    jnp.add,
                    [
                        jnp.dot(
                            n.astype(jnp.bfloat16), kv_all[request_slot + p, 1, :, kv_cols],
                            preferred_element_type=jnp.float32,
                        )
                        for p, n in enumerate(numerators)
                    ],
                )
                done = (product / totals).astype(jnp.bfloat16)
                done = jnp.concatenate([done[j * tokens:(j + 1) * tokens] for j in range(per_group)], axis=1)
                o_all[item, :, q_cols] = done
                return carry

            lax.fori_loop(0, local_kv, block, 0)

        def one_item(item, carry):
            if piece is None:
                request, request_slot = ctx, jnp.int32(0)
                place = place_of((item // 2, lax.rem(item, 2)), sizes)
            else:
                request, request_slot = item, start_of(item)
                place = place_of(STEPS[piece], sizes)
            count = counts[request]
            for pages in range(1, most_pages + 1):
                @pl.when(count == pages)
                def _():
                    attend(item, request_slot, place * tokens, pages)
            for i, ref in enumerate(o_out):
                @pl.when(item == i)
                def _():
                    pltpu.make_async_copy(o_all.at[i], ref, o_sems.at[i]).start()
            return carry

        lax.fori_loop(0, items, one_item, 0)
        for i, ref in enumerate(o_out):
            pltpu.make_async_copy(o_all.at[i], ref, o_sems.at[i]).wait()

    pl.when(ctx >= low_ctx if piece is None else ctx == low_ctx)(work)


def queries_up(queries, kv_cache, page_counts):
    ctx_size, sub_size = lax.axis_size("ctx"), lax.axis_size("sub")
    head_count = lax.axis_size("head")
    low_ctx = ctx_size // 2
    live_pages = kv_cache.shape[1] // PAGE * ctx_size * sub_size // 2
    most_pages = live_pages // 2
    tokens, width = queries.shape[0], queries.shape[1] // (head_count * sub_size)
    half = kv_cache.shape[:2] + (kv_cache.shape[2] // sub_size,)
    anywhere = pl.BlockSpec(memory_space=pl.ANY)
    q_piece = jax.ShapeDtypeStruct((tokens, width), queries.dtype)
    kv_piece = jax.ShapeDtypeStruct(half, kv_cache.dtype)
    sizes = (head_count, sub_size)

    q_out = pl.pallas_call(
        functools.partial(split_queries_kernel, sizes),
        out_shape=[q_piece] * 4,
        in_specs=[anywhere],
        out_specs=[anywhere] * 4,
        scratch_shapes=[pltpu.VMEM((4, tokens, width), queries.dtype), pltpu.SemaphoreType.DMA((2, 4))],
        name="split_queries",
    )(queries)
    kv_same, kv_cross = pl.pallas_call(
        split_pages_kernel,
        out_shape=[kv_piece, kv_piece],
        in_specs=[anywhere] * 2,
        out_specs=[anywhere] * 2,
        scratch_shapes=[pltpu.VMEM((2,) + half, kv_cache.dtype), pltpu.SemaphoreType.DMA((2, 2))],
        name="split_pages",
    )(kv_cache, q_out[0])

    everything = ("ctx", "head", "sub")

    def moved(array, step, routes):
        pairs = [
            ((a * head_count + h) * sub_size + s, (b * head_count + (h ^ step[0])) * sub_size + (s ^ step[1]))
            for a, b in routes for h in range(head_count) for s in range(sub_size)
        ]
        return lax.ppermute(array, everything, pairs)

    upper = [(c, c) for c in range(low_ctx, ctx_size)]
    order = (3, 2, 1, 0)
    q_up = {}
    for i in order:
        for r in range(low_ctx):
            q_up[r, i] = moved(q_out[i], STEPS[i], [(r, low_ctx)])
    r_same = moved(kv_same, (0, 0), [(low_ctx + 1, low_ctx)])
    r_cross = moved(kv_cross, (0, 1), [(low_ctx + 1, low_ctx)])
    paired = moved(kv_cross, (0, 1), upper)
    q_own = [q_out[0]] + [moved(q_out[i], STEPS[i], upper) for i in (1, 2, 3)]

    def attended(piece, pieces, after):
        items = len(pieces)
        slots = most_pages if piece is None else live_pages - (REQS - low_ctx)
        return pl.pallas_call(
            functools.partial(attend_kernel, sizes, low_ctx, slots, most_pages, piece, len(after)),
            out_shape=[q_piece] * items,
            in_specs=[pl.BlockSpec(memory_space=pltpu.SMEM)] + [anywhere] * (items + 4 + len(after)),
            out_specs=[anywhere] * items,
            scratch_shapes=[
                pltpu.VMEM((items, tokens, width), queries.dtype),
                pltpu.VMEM((slots, 2, PAGE, half[2]), kv_cache.dtype),
                pltpu.VMEM((items, tokens, width), queries.dtype),
                pltpu.SemaphoreType.DMA((items,)),
                pltpu.SemaphoreType.DMA((slots,)),
                pltpu.SemaphoreType.DMA((items,)),
            ],
            compiler_params=pltpu.CompilerParams(vmem_limit_bytes=24 * 1024 * 1024),
            cost_estimate=pl.CostEstimate(flops=10**9, bytes_accessed=2**21, transcendentals=10**6),
            name="attend_own" if piece is None else f"attend_{piece}",
        )(page_counts, *pieces, kv_same, paired, r_same, r_cross, *after)

    back = {}
    last = []
    for turn, i in enumerate(order):
        ahead = [back[r, order[turn - 2]] for r in range(low_ctx)] if turn >= 2 else []
        outs = attended(i, [q_up[r, i] for r in range(low_ctx)], last + ahead)
        for r in range(low_ctx):
            back[r, i] = moved(outs[r], STEPS[i], [(low_ctx, r)])
        last = [outs[0]]
        if turn == 1:
            outs = attended(None, q_own, last)
            last = [outs[0]]
            back[low_ctx, 0] = outs[0]
            for j in (1, 2, 3):
                back[low_ctx, j] = moved(outs[j], STEPS[j], upper)

    return pl.pallas_call(
        functools.partial(join_kernel, sizes, low_ctx),
        out_shape=jax.ShapeDtypeStruct(queries.shape, queries.dtype),
        in_specs=[anywhere] * (4 * (low_ctx + 1)),
        out_specs=pl.BlockSpec(memory_space=pltpu.VMEM),
        scratch_shapes=[pltpu.SemaphoreType.DMA((4,))],
        name="join",
    )(*[back[r, i] for r in range(low_ctx + 1) for i in range(4)])


def from_behind(array, axis, by):
    count = lax.axis_size(axis)
    pairs = [(i, i + by) for i in range(count) if 0 <= i + by < count]
    return lax.ppermute(array, axis, pairs)


def queries_to_pages(queries, kv_cache, page_counts):
    per_group = HQ // KVH
    local_heads = kv_cache.shape[2] // HD
    ctx_size = lax.axis_size("ctx")
    sub_size = lax.axis_size("sub")
    head_count = lax.axis_size("head")
    tok_rows = queries.shape[0]
    score_scale = HD ** (-0.5)
    regrouped = lax.all_to_all(queries, "head", split_axis=1, concat_axis=0, tiled=True)
    all_queries = lax.all_gather(regrouped, ("ctx", "sub"), axis=0, tiled=True)
    all_queries = all_queries.reshape(SPAN, local_heads, per_group, HD)
    page_ends = jnp.cumsum(page_counts)
    ctx_rows = SPAN // ctx_size
    offsets = jnp.arange(QR, dtype=jnp.int32)
    columns = jnp.arange(PAGE, dtype=jnp.int32)
    flat_index = lax.axis_index("ctx") * sub_size + lax.axis_index("sub")
    pages_here = kv_cache.shape[1] // PAGE
    base_pages = pages_here * ctx_size * sub_size // 2
    initial = (
        jnp.full((SPAN, local_heads, per_group), NEG, jnp.float32),
        jnp.zeros((SPAN, local_heads, per_group), jnp.float32),
        jnp.zeros((SPAN, local_heads, per_group, HD), jnp.float32),
    )
    half_rows = kv_cache.shape[1] // 2
    arrived = from_behind(kv_cache[:, half_rows:], "ctx", -(ctx_size // 2))
    is_lower = lax.axis_index("ctx") < ctx_size // 2
    source_flat = flat_index + ctx_size // 2 * sub_size
    working = jnp.where(is_lower, arrived, kv_cache[:, :half_rows])
    first_page = jnp.where(
        is_lower, source_flat * pages_here + pages_here // 2, flat_index * pages_here
    )
    page_total = working.shape[1] // PAGE

    def add_page(page_turn, running):
        page_index = first_page + page_turn
        relative = page_index - base_pages
        counted = jnp.sum((relative >= page_ends).astype(jnp.int32))
        request = jnp.where(relative < 0, REQS, counted)

        def update(partial_value):
            run_max, run_sum, run_out = partial_value
            request_id = jnp.minimum(request, REQS - 1)
            row_start = request_id * QR
            gathered = row_start + offsets
            within = gathered % ctx_rows
            ctx_block = gathered // ctx_rows
            sub_part = within // (head_count * tok_rows)
            head_part = within // tok_rows % head_count
            tok_part = within % tok_rows
            natural = ctx_block * ctx_rows + (head_part * sub_size + sub_part) * tok_rows + tok_part
            query_pos = (page_ends[request_id] + base_pages) * PAGE - QR + natural - row_start
            key_pos = page_index * PAGE + columns
            visible = key_pos[None, :] <= query_pos[:, None]
            page_keys = working[0].reshape(PAGE, local_heads, HD)
            page_values = working[1].reshape(PAGE, local_heads, HD)
            query_rows = lax.dynamic_slice_in_dim(all_queries, row_start, QR, 0)
            scores = (
                jnp.einsum(
                    "qkgd,pkd->qkgp", query_rows, page_keys, preferred_element_type=jnp.float32
                )
                * score_scale
            )
            scores = jnp.where(visible[:, None, None, :], scores, NEG)
            old_max = lax.dynamic_slice_in_dim(run_max, row_start, QR, 0)
            old_sum = lax.dynamic_slice_in_dim(run_sum, row_start, QR, 0)
            old_out = lax.dynamic_slice_in_dim(run_out, row_start, QR, 0)
            new_max = jnp.maximum(old_max, jnp.max(scores, axis=3))
            factor = jnp.exp(old_max - new_max)
            numerators = jnp.exp(scores - new_max[..., None])
            new_sum = old_sum * factor + jnp.sum(numerators, axis=3)
            product = jnp.einsum(
                "qkgp,pkd->qkgd",
                numerators.astype(jnp.bfloat16),
                page_values,
                preferred_element_type=jnp.float32,
            )
            new_out = old_out * factor[..., None] + product
            return (
                lax.dynamic_update_slice_in_dim(run_max, new_max, row_start, 0),
                lax.dynamic_update_slice_in_dim(run_sum, new_sum, row_start, 0),
                lax.dynamic_update_slice_in_dim(run_out, new_out, row_start, 0),
            )

        def unchanged(partial_value):
            return partial_value

        return lax.cond(request < REQS, update, unchanged, running)

    run_max, run_sum, run_out = lax.fori_loop(0, page_total, add_page, initial)
    share = SPAN // (ctx_size * sub_size)
    global_max = lax.pmax(run_max, ("ctx", "sub"))
    factor = jnp.exp(run_max - global_max)
    sums_here, outs_here = (
        lax.psum_scatter(
            (run_sum * factor).astype(jnp.bfloat16), ("ctx", "sub"), scatter_dimension=0, tiled=True
        ).astype(jnp.float32),
        lax.psum_scatter(
            (run_out * factor[..., None]).astype(jnp.bfloat16),
            ("ctx", "sub"),
            scatter_dimension=0,
            tiled=True,
        ).astype(jnp.float32),
    )
    finished = (outs_here / sums_here[..., None]).astype(jnp.bfloat16)
    finished = finished.reshape(share, local_heads * per_group * HD)
    return lax.all_to_all(finished, "head", split_axis=0, concat_axis=1, tiled=True)


def per_device(queries, kv_cache, page_counts):
    ctx_size, sub_size, head_count = lax.axis_size("ctx"), lax.axis_size("sub"), lax.axis_size("head")
    small = (
        ctx_size == REQS == 4
        and head_count == sub_size == 2
        and kv_cache.shape[1] == 2 * PAGE
        and kv_cache.shape[2] % (sub_size * HD) == 0
        and queries.shape[0] % 16 == 0
        and queries.shape[0] * head_count * sub_size == QR
    )
    return (queries_up if small else queries_to_pages)(queries, kv_cache, page_counts)


def solution(mesh):
    return jax.shard_map(
        per_device,
        mesh=mesh,
        in_specs=(
            P(("grp", "ctx", "head", "sub"), None),
            P(None, ("grp", "ctx", "sub"), "head"),
            P("grp"),
        ),
        out_specs=P(("grp", "ctx", "head", "sub"), None),
        check_vma=False,
    )
```

```python
import functools

import jax
import jax.numpy as jnp
from jax import lax
from jax.experimental import pallas as pl
from jax.experimental.pallas import tpu as pltpu
from jax.sharding import PartitionSpec as P

HQ = 128
KVH = 8
HD = 128
REQS = 4
QR = 64
PAGE = 256
SPAN = 256


NEG = -1e30
EXP2_SCALE = HD ** (-0.5) * 1.4426950408889634
STEPS = ((0, 0), (0, 1), (1, 0), (1, 1))


def place_of(step, sizes):
    head, sub = lax.axis_index("head"), lax.axis_index("sub")
    return (head ^ step[0]) * sizes[1] + (sub ^ step[1])


def part_of(place, width):
    return pl.ds(pl.multiple_of(place * width, width), width)


def run(copies):
    for copy in copies:
        copy.start()
    for copy in copies:
        copy.wait()


def split_pages_kernel(kv, *refs):
    outs, sems = refs[:-1], refs[-1]
    local_kv = len(outs) // 2
    sub = lax.axis_index("sub")
    run([
        pltpu.make_async_copy(
            kv.at[:, :, part_of((sub ^ (i // local_kv)) * local_kv + i % local_kv, HD)], out, sems.at[i]
        )
        for i, out in enumerate(outs)
    ])


def split_queries_kernel(sizes, queries, after, *refs):
    outs, sems = refs[:-1], refs[-1]
    run([
        pltpu.make_async_copy(
            queries.at[:, part_of(place_of(step, sizes), out.shape[1])], out, sems.at[i]
        )
        for i, (out, step) in enumerate(zip(outs, STEPS[1:]))
    ])


def join_kernel(sizes, local_kv, *refs):
    pieces, (out, sems) = refs[:-2], refs[-2:]
    run([
        pltpu.make_async_copy(
            piece,
            out.at[:, part_of(place_of(STEPS[i // local_kv], sizes) * local_kv + i % local_kv, piece.shape[1])],
            sems.at[i],
        )
        for i, piece in enumerate(pieces)
    ])


def attend_kernel(
    sizes, most_pages, kv_head,
    counts, queries, q0, q1, q2, kv, paired, p_same, p_cross, x_same, x_cross, r_same, r_cross,
    o_own, o0, o1, o2,
    q_all, kv_all, o_all, q_sems, kv_sems, o_sems,
):
    ctx, sub = lax.axis_index("ctx"), lax.axis_index("sub")
    pieces, tokens, span = q_all.shape
    per_group = span // HD
    rows = per_group * tokens
    local_kv = q0.shape[1] // span
    start = jnp.int32(0)
    for r in range(REQS):
        start = start + jnp.where(r < ctx, counts[r], 0)
    count = counts[ctx]

    own_head = part_of(place_of((0, 0), sizes) * local_kv + kv_head, span)
    q_copies = [pltpu.make_async_copy(queries.at[:, own_head], q_all.at[0], q_sems.at[0])]
    for i, ref in enumerate((q0, q1, q2)):
        piece = ref.at[:, pl.ds(kv_head * span, span)]
        q_copies.append(pltpu.make_async_copy(piece, q_all.at[i + 1], q_sems.at[i + 1]))
    for copy in q_copies:
        copy.start()

    own = kv.at[:, :, part_of(sub * local_kv + kv_head, HD)]
    sources = (own, paired, p_same, p_cross, x_same, x_cross, r_same, r_cross)

    def either(first, second):
        return jnp.where(sub == 0, first, second)

    table = (
        (either(2, 3), either(5, 4), -1, -1),
        (either(4, 5), either(3, 2), either(6, 7), -1),
        (either(0, 1), either(1, 0), either(2, 3), either(3, 2)),
        (-1, -1, either(0, 1), either(1, 0)),
    )

    def source_of(pair):
        found = jnp.int32(-1)
        for c in range(4):
            for n in range(4):
                found = jnp.where((ctx == c) & (pair == n), table[c][n], found)
        return found

    for p in range(most_pages):
        @pl.when(p < count)
        def _():
            page = start + p
            which = source_of(page // 2)
            page_rows = pl.ds(pl.multiple_of(lax.rem(page, 2) * PAGE, PAGE), PAGE)
            for i, ref in enumerate(sources):
                @pl.when(which == i)
                def _():
                    pltpu.make_async_copy(ref.at[:, page_rows, :], kv_all.at[p], kv_sems.at[p]).start()

    for copy in q_copies:
        copy.wait()
    for p in range(most_pages):
        @pl.when(p < count)
        def _():
            pltpu.make_async_copy(paired.at[:, pl.ds(0, PAGE), :], kv_all.at[p], kv_sems.at[p]).wait()

    def attend(pages):
        def block(piece, carry):
            place = place_of((piece // 2, lax.rem(piece, 2)), sizes)
            q_block = q_all[piece]
            q_rows = jnp.concatenate([q_block[:, j * HD:(j + 1) * HD] for j in range(per_group)], axis=0)
            scores = [
                lax.dot_general(q_rows, kv_all[p, 0], (((1,), (1,)), ((), ())), preferred_element_type=jnp.float32)
                for p in range(pages)
            ]
            token = lax.rem(lax.broadcasted_iota(jnp.int32, (rows, PAGE), 0), tokens)
            column = lax.broadcasted_iota(jnp.int32, (rows, PAGE), 1)
            visible = column <= PAGE - QR + place * tokens + token
            scores[-1] = jnp.where(visible, scores[-1], NEG)
            top = functools.reduce(jnp.maximum, scores)
            top = jnp.max(top, axis=1, keepdims=True)
            numerators = [jnp.exp2((s - top) * EXP2_SCALE) for s in scores]
            totals = jnp.sum(functools.reduce(jnp.add, numerators), axis=1, keepdims=True)
            product = functools.reduce(
                jnp.add,
                [
                    jnp.dot(n.astype(jnp.bfloat16), kv_all[p, 1], preferred_element_type=jnp.float32)
                    for p, n in enumerate(numerators)
                ],
            )
            done = (product / totals).astype(jnp.bfloat16)
            o_all[piece] = jnp.concatenate([done[j * tokens:(j + 1) * tokens] for j in range(per_group)], axis=1)
            for i, ref in enumerate((o_own, o0, o1, o2)):
                @pl.when(piece == i)
                def _():
                    pltpu.make_async_copy(o_all.at[i], ref, o_sems.at[i]).start()
            return carry

        lax.fori_loop(0, pieces, block, 0)

    for pages in range(1, most_pages + 1):
        @pl.when(count == pages)
        def _():
            attend(pages)

    for i, ref in enumerate((o_own, o0, o1, o2)):
        pltpu.make_async_copy(o_all.at[i], ref, o_sems.at[i]).wait()


def pages_to_queries(queries, kv_cache, page_counts):
    ctx_size, sub_size = lax.axis_size("ctx"), lax.axis_size("sub")
    head_count = lax.axis_size("head")
    sizes = (head_count, sub_size)
    most_pages = kv_cache.shape[1] // PAGE * ctx_size * sub_size // 4
    local_kv = kv_cache.shape[2] // HD // sub_size
    tokens, width = queries.shape[0], queries.shape[1] // (head_count * sub_size)
    span = width // local_kv
    anywhere = pl.BlockSpec(memory_space=pl.ANY)
    in_hbm = pl.BlockSpec(memory_space=pltpu.HBM)
    kv_piece = pltpu.VMEM(kv_cache.shape[:2] + (HD,), kv_cache.dtype)
    q_piece = pltpu.VMEM((tokens, width), queries.dtype)
    o_piece = pltpu.VMEM((tokens, span), queries.dtype)

    queries = pltpu.with_memory_space_constraint(queries, pltpu.HBM)
    kv_cache = pltpu.with_memory_space_constraint(kv_cache, pltpu.HBM)
    kv_parts = pl.pallas_call(
        split_pages_kernel,
        out_shape=[kv_piece] * (2 * local_kv),
        in_specs=[in_hbm],
        out_specs=[anywhere] * (2 * local_kv),
        scratch_shapes=[pltpu.SemaphoreType.DMA((2 * local_kv,))],
        name="split_pages",
    )(kv_cache)
    def at(ctx, sub):
        return ctx * sub_size + sub

    def along(array, routes):
        return lax.ppermute(array, ("ctx", "sub"), [(at(*a), at(*b)) for a, b in routes])

    def across(array, step):
        pairs = [
            (h * sub_size + s, (h ^ step[0]) * sub_size + (s ^ step[1]))
            for h in range(head_count) for s in range(sub_size)
        ]
        return lax.ppermute(array, ("head", "sub"), pairs)

    same, cross = kv_parts[:local_kv], kv_parts[local_kv:]
    p_same, p_cross, r_same, r_cross, x_same, x_cross, paired = ([None] * local_kv for _ in range(7))
    for j in range(local_kv):
        p_same[j] = along(same[j], [((2, 0), (0, 0)), ((2, 1), (1, 1)), ((3, 0), (2, 0)), ((3, 1), (2, 1))])
        p_cross[j] = along(cross[j], [((2, 0), (0, 1)), ((2, 1), (1, 0)), ((3, 0), (2, 1)), ((3, 1), (2, 0))])
        r_same[j] = along(same[j], [((3, 0), (1, 0))])
        r_cross[j] = along(cross[j], [((3, 0), (1, 1))])
        x_same[j] = along(p_same[j], [((0, 0), (1, 0)), ((1, 1), (0, 1))])
        x_cross[j] = along(p_cross[j], [((0, 1), (1, 1)), ((1, 0), (0, 0))])
        paired[j] = along(cross[j], [((c, s), (c, 1 - s)) for c in (2, 3) for s in (0, 1)])

    q_out = pl.pallas_call(
        functools.partial(split_queries_kernel, sizes),
        out_shape=[q_piece] * 3,
        in_specs=[in_hbm, anywhere],
        out_specs=[anywhere] * 3,
        scratch_shapes=[pltpu.SemaphoreType.DMA((3,))],
        name="split_queries",
    )(queries, paired[0])

    q_in = [across(piece, step) for piece, step in zip(q_out, STEPS[1:])]

    pieces = {}
    for j in range(local_kv):
        outs = pl.pallas_call(
            functools.partial(attend_kernel, sizes, most_pages, j),
            out_shape=[o_piece] * 4,
            in_specs=[pl.BlockSpec(memory_space=pltpu.SMEM), in_hbm] + [anywhere] * 3 + [in_hbm] + [anywhere] * 7,
            out_specs=[anywhere] * 4,
            scratch_shapes=[
                pltpu.VMEM((4, tokens, span), queries.dtype),
                pltpu.VMEM((most_pages, 2, PAGE, HD), kv_cache.dtype),
                pltpu.VMEM((4, tokens, span), queries.dtype),
                pltpu.SemaphoreType.DMA((4,)),
                pltpu.SemaphoreType.DMA((most_pages,)),
                pltpu.SemaphoreType.DMA((4,)),
            ],
            compiler_params=pltpu.CompilerParams(vmem_limit_bytes=24 * 1024 * 1024),
            name=f"attend_{j}",
        )(
            page_counts, queries, *q_in, kv_cache, paired[j], p_same[j], p_cross[j], x_same[j], x_cross[j],
            r_same[j], r_cross[j],
        )
        pieces[0, j] = outs[0]
        for i in (1, 2, 3):
            pieces[i, j] = across(outs[i], STEPS[i])

    return pl.pallas_call(
        functools.partial(join_kernel, sizes, local_kv),
        out_shape=jax.ShapeDtypeStruct(queries.shape, queries.dtype),
        in_specs=[pl.BlockSpec(memory_space=pltpu.VMEM)] * (4 * local_kv),
        out_specs=in_hbm,
        scratch_shapes=[pltpu.SemaphoreType.DMA((4 * local_kv,))],
        name="join",
    )(*[pieces[i, j] for i in range(4) for j in range(local_kv)])


def from_behind(array, axis, by):
    count = lax.axis_size(axis)
    pairs = [(i, i + by) for i in range(count) if 0 <= i + by < count]
    return lax.ppermute(array, axis, pairs)


def queries_to_pages(queries, kv_cache, page_counts):
    per_group = HQ // KVH
    local_heads = kv_cache.shape[2] // HD
    ctx_size = lax.axis_size("ctx")
    sub_size = lax.axis_size("sub")
    head_count = lax.axis_size("head")
    tok_rows = queries.shape[0]
    score_scale = HD ** (-0.5)
    regrouped = lax.all_to_all(queries, "head", split_axis=1, concat_axis=0, tiled=True)
    all_queries = lax.all_gather(regrouped, ("ctx", "sub"), axis=0, tiled=True)
    all_queries = all_queries.reshape(SPAN, local_heads, per_group, HD)
    page_ends = jnp.cumsum(page_counts)
    ctx_rows = SPAN // ctx_size
    offsets = jnp.arange(QR, dtype=jnp.int32)
    columns = jnp.arange(PAGE, dtype=jnp.int32)
    flat_index = lax.axis_index("ctx") * sub_size + lax.axis_index("sub")
    pages_here = kv_cache.shape[1] // PAGE
    base_pages = pages_here * ctx_size * sub_size // 2
    initial = (
        jnp.full((SPAN, local_heads, per_group), NEG, jnp.float32),
        jnp.zeros((SPAN, local_heads, per_group), jnp.float32),
        jnp.zeros((SPAN, local_heads, per_group, HD), jnp.float32),
    )
    half_rows = kv_cache.shape[1] // 2
    arrived = from_behind(kv_cache[:, half_rows:], "ctx", -(ctx_size // 2))
    is_lower = lax.axis_index("ctx") < ctx_size // 2
    source_flat = flat_index + ctx_size // 2 * sub_size
    working = jnp.where(is_lower, arrived, kv_cache[:, :half_rows])
    first_page = jnp.where(
        is_lower, source_flat * pages_here + pages_here // 2, flat_index * pages_here
    )
    page_total = working.shape[1] // PAGE

    def add_page(page_turn, running):
        page_index = first_page + page_turn
        relative = page_index - base_pages
        counted = jnp.sum((relative >= page_ends).astype(jnp.int32))
        request = jnp.where(relative < 0, REQS, counted)

        def update(partial_value):
            run_max, run_sum, run_out = partial_value
            request_id = jnp.minimum(request, REQS - 1)
            row_start = request_id * QR
            gathered = row_start + offsets
            within = gathered % ctx_rows
            ctx_block = gathered // ctx_rows
            sub_part = within // (head_count * tok_rows)
            head_part = within // tok_rows % head_count
            tok_part = within % tok_rows
            natural = ctx_block * ctx_rows + (head_part * sub_size + sub_part) * tok_rows + tok_part
            query_pos = (page_ends[request_id] + base_pages) * PAGE - QR + natural - row_start
            key_pos = page_index * PAGE + columns
            visible = key_pos[None, :] <= query_pos[:, None]
            page_keys = working[0].reshape(PAGE, local_heads, HD)
            page_values = working[1].reshape(PAGE, local_heads, HD)
            query_rows = lax.dynamic_slice_in_dim(all_queries, row_start, QR, 0)
            scores = (
                jnp.einsum(
                    "qkgd,pkd->qkgp", query_rows, page_keys, preferred_element_type=jnp.float32
                )
                * score_scale
            )
            scores = jnp.where(visible[:, None, None, :], scores, NEG)
            old_max = lax.dynamic_slice_in_dim(run_max, row_start, QR, 0)
            old_sum = lax.dynamic_slice_in_dim(run_sum, row_start, QR, 0)
            old_out = lax.dynamic_slice_in_dim(run_out, row_start, QR, 0)
            new_max = jnp.maximum(old_max, jnp.max(scores, axis=3))
            factor = jnp.exp(old_max - new_max)
            numerators = jnp.exp(scores - new_max[..., None])
            new_sum = old_sum * factor + jnp.sum(numerators, axis=3)
            product = jnp.einsum(
                "qkgp,pkd->qkgd",
                numerators.astype(jnp.bfloat16),
                page_values,
                preferred_element_type=jnp.float32,
            )
            new_out = old_out * factor[..., None] + product
            return (
                lax.dynamic_update_slice_in_dim(run_max, new_max, row_start, 0),
                lax.dynamic_update_slice_in_dim(run_sum, new_sum, row_start, 0),
                lax.dynamic_update_slice_in_dim(run_out, new_out, row_start, 0),
            )

        def unchanged(partial_value):
            return partial_value

        return lax.cond(request < REQS, update, unchanged, running)

    run_max, run_sum, run_out = lax.fori_loop(0, page_total, add_page, initial)
    share = SPAN // (ctx_size * sub_size)
    global_max = lax.pmax(run_max, ("ctx", "sub"))
    factor = jnp.exp(run_max - global_max)
    sums_here, outs_here = (
        lax.psum_scatter(
            (run_sum * factor).astype(jnp.bfloat16), ("ctx", "sub"), scatter_dimension=0, tiled=True
        ).astype(jnp.float32),
        lax.psum_scatter(
            (run_out * factor[..., None]).astype(jnp.bfloat16),
            ("ctx", "sub"),
            scatter_dimension=0,
            tiled=True,
        ).astype(jnp.float32),
    )
    finished = (outs_here / sums_here[..., None]).astype(jnp.bfloat16)
    finished = finished.reshape(share, local_heads * per_group * HD)
    return lax.all_to_all(finished, "head", split_axis=0, concat_axis=1, tiled=True)


def per_device(queries, kv_cache, page_counts):
    ctx_size, sub_size, head_count = lax.axis_size("ctx"), lax.axis_size("sub"), lax.axis_size("head")
    small = (
        ctx_size == REQS == 4
        and head_count == sub_size == 2
        and kv_cache.shape[1] == 2 * PAGE
        and kv_cache.shape[2] % (sub_size * HD) == 0
        and queries.shape[0] % 16 == 0
        and queries.shape[0] * head_count * sub_size == QR
    )
    return (pages_to_queries if small else queries_to_pages)(queries, kv_cache, page_counts)


def solution(mesh):
    return jax.shard_map(
        per_device,
        mesh=mesh,
        in_specs=(
            P(("grp", "ctx", "head", "sub"), None),
            P(None, ("grp", "ctx", "sub"), "head"),
            P("grp"),
        ),
        out_specs=P(("grp", "ctx", "head", "sub"), None),
        check_vma=False,
    )
```

```python
import functools

import jax
import jax.numpy as jnp
from jax import lax
from jax.experimental import pallas as pl
from jax.experimental.pallas import tpu as pltpu
from jax.sharding import PartitionSpec as P

HQ = 128
KVH = 8
HD = 128
REQS = 4
QR = 64
PAGE = 256
SPAN = 256


NEG = -1e30
EXP2_SCALE = HD ** (-0.5) * 1.4426950408889634


def run(copies):
    for copy in copies:
        copy.start()
    for copy in copies:
        copy.wait()


def head_part(step, width):
    return pl.ds(pl.multiple_of((lax.axis_index("head") ^ step) * width, width), width)


def split_kernel(queries, *refs):
    outs, sems = refs[:-1], refs[-1]
    run([
        pltpu.make_async_copy(queries.at[:, head_part(step, out.shape[1])], out, sems.at[step])
        for step, out in enumerate(outs)
    ])


def join_kernel(sub_count, *refs):
    pieces, (out, sems) = refs[:-2], refs[-2:]
    sub = lax.axis_index("sub")
    for source in range(sub_count):
        @pl.when(sub == source)
        def _():
            run([
                pltpu.make_async_copy(
                    pieces[step * sub_count + source], out.at[:, head_part(step, pieces[0].shape[1])], sems.at[step]
                )
                for step in range(len(pieces) // sub_count)
            ])


def attend_kernel(low_ctx, sub_count, step, source_sub, waits, counts, queries, own, paired, far, *refs):
    out, kv_all, kv_sems = refs[waits:]
    ctx, head, sub = lax.axis_index("ctx"), lax.axis_index("head"), lax.axis_index("sub")
    tokens, width = queries.shape
    local_kv, most_pages = kv_all.shape[:2]
    span = width // local_kv
    per_group = span // HD
    rows = per_group * tokens
    own_pair = (ctx - low_ctx) * sub_count + sub
    first_token = ((head ^ step) * sub_count + source_sub) * tokens

    def work():
        request = own_pair
        start = jnp.int32(0)
        for r in range(REQS):
            start = start + jnp.where(r < request, counts[r], 0)
        count = counts[request]

        for g in range(local_kv):
            for p in range(most_pages):
                @pl.when(p < count)
                def _():
                    page = start + p
                    apart = page // 2 - own_pair
                    page_rows = pl.ds(pl.multiple_of(lax.rem(page, 2) * PAGE, PAGE), PAGE)
                    which = jnp.where(apart == 0, 0, jnp.where(apart == 1 - 2 * sub, 1, 2))
                    for i, ref in enumerate((own, paired, far)):
                        @pl.when(which == i)
                        def _():
                            pltpu.make_async_copy(
                                ref.at[:, page_rows, pl.ds(g * HD, HD)], kv_all.at[g, p], kv_sems.at[g, p]
                            ).start()

        def attend(pages):
            token = lax.rem(lax.broadcasted_iota(jnp.int32, (rows, PAGE), 0), tokens)
            column = lax.broadcasted_iota(jnp.int32, (rows, PAGE), 1)
            visible = column <= PAGE - QR + first_token + token

            def block(g, carry):
                for p in range(pages):
                    pltpu.make_async_copy(
                        own.at[:, pl.ds(0, PAGE), pl.ds(0, HD)], kv_all.at[g, p], kv_sems.at[g, p]
                    ).wait()
                part = pl.ds(pl.multiple_of(g * span, span), span)
                q_block = queries[:, part]
                q_rows = jnp.concatenate([q_block[:, j * HD:(j + 1) * HD] for j in range(per_group)], axis=0)
                scores = [
                    lax.dot_general(
                        q_rows, kv_all[g, p, 0], (((1,), (1,)), ((), ())), preferred_element_type=jnp.float32
                    )
                    for p in range(pages)
                ]
                scores[-1] = jnp.where(visible, scores[-1], NEG)
                top = functools.reduce(jnp.maximum, scores)
                top = jnp.max(top, axis=1, keepdims=True)
                numerators = [jnp.exp2((s - top) * EXP2_SCALE) for s in scores]
                totals = jnp.sum(functools.reduce(jnp.add, numerators), axis=1, keepdims=True)
                product = functools.reduce(
                    jnp.add,
                    [
                        jnp.dot(n.astype(jnp.bfloat16), kv_all[g, p, 1], preferred_element_type=jnp.float32)
                        for p, n in enumerate(numerators)
                    ],
                )
                done = (product / totals).astype(jnp.bfloat16)
                out[:, part] = jnp.concatenate([done[j * tokens:(j + 1) * tokens] for j in range(per_group)], axis=1)
                return carry

            lax.fori_loop(0, local_kv, block, 0)

        for pages in range(1, most_pages + 1):
            @pl.when(count == pages)
            def _():
                attend(pages)

    pl.when(ctx >= low_ctx)(work)


def one_request_each(queries, kv_cache, page_counts):
    ctx_size, sub_size = lax.axis_size("ctx"), lax.axis_size("sub")
    head_count = lax.axis_size("head")
    low_ctx = ctx_size // 2
    most_pages = kv_cache.shape[1] // PAGE * ctx_size * sub_size // 4
    local_kv = kv_cache.shape[2] // HD
    tokens, width = queries.shape[0], queries.shape[1] // head_count
    anywhere = pl.BlockSpec(memory_space=pl.ANY)
    in_vmem = pl.BlockSpec(memory_space=pltpu.VMEM)
    q_piece = pltpu.VMEM((tokens, width), queries.dtype)

    def vmem(array):
        return pltpu.with_memory_space_constraint(array, pltpu.VMEM)

    def hbm(array):
        return pltpu.with_memory_space_constraint(array, pltpu.HBM)

    def moved(array, routes):
        def flat(place):
            return (place[0] * head_count + place[1]) * sub_size + place[2]

        return lax.ppermute(array, ("ctx", "head", "sub"), [(flat(a), flat(b)) for a, b in routes])

    def worker(request, head):
        return low_ctx + request // sub_size, head, request % sub_size

    heads = range(head_count)
    paired = moved(
        kv_cache, [((c, h, s), (c, h, 1 - s)) for c in range(low_ctx, ctx_size) for h in heads for s in range(sub_size)]
    )
    middle = [(low_ctx, sub_size - 1), (low_ctx + 1, 0)]
    far = moved(
        kv_cache, [((a[0], h, a[1]), (b[0], h, b[1])) for a, b in (middle, middle[::-1]) for h in heads]
    )

    q_out = pl.pallas_call(
        split_kernel,
        out_shape=[q_piece] * head_count,
        in_specs=[anywhere],
        out_specs=[anywhere] * head_count,
        scratch_shapes=[pltpu.SemaphoreType.DMA((head_count,))],
        name="split",
    )(hbm(queries))

    routes = {
        (step, s): [((r, h, s), worker(r, h ^ step)) for r in range(ctx_size) for h in heads]
        for step in heads for s in range(sub_size)
    }
    q_in = {key: moved(q_out[key[0]], pairs) for key, pairs in routes.items()}

    back = {}
    after = []
    for step, s in routes:
        if (step, s) == (head_count - 1, sub_size - 1):
            after += [back[key] for key in routes if key[0] == 0]
        out = pl.pallas_call(
            functools.partial(attend_kernel, low_ctx, sub_size, step, s, len(after)),
            out_shape=q_piece,
            in_specs=[pl.BlockSpec(memory_space=pltpu.SMEM), in_vmem] + [anywhere] * (3 + len(after)),
            out_specs=in_vmem,
            scratch_shapes=[
                pltpu.VMEM((local_kv, most_pages, 2, PAGE, HD), kv_cache.dtype),
                pltpu.SemaphoreType.DMA((local_kv, most_pages)),
            ],
            compiler_params=pltpu.CompilerParams(vmem_limit_bytes=24 * 1024 * 1024),
            cost_estimate=pl.CostEstimate(flops=6 * 10**9, bytes_accessed=2**22, transcendentals=10**6),
            name=f"attend_{step}{s}",
        )(page_counts, vmem(q_in[step, s]), hbm(kv_cache), paired, far, *after)
        back[step, s] = moved(out, [(b, a) for a, b in routes[step, s]])
        after = [out]

    return pl.pallas_call(
        functools.partial(join_kernel, sub_size),
        out_shape=pltpu.HBM(queries.shape, queries.dtype),
        in_specs=[anywhere] * len(back),
        out_specs=anywhere,
        scratch_shapes=[pltpu.SemaphoreType.DMA((head_count,))],
        name="join",
    )(*[vmem(back[key]) for key in routes])


def from_behind(array, axis, by):
    count = lax.axis_size(axis)
    pairs = [(i, i + by) for i in range(count) if 0 <= i + by < count]
    return lax.ppermute(array, axis, pairs)


def queries_to_pages(queries, kv_cache, page_counts):
    per_group = HQ // KVH
    local_heads = kv_cache.shape[2] // HD
    ctx_size = lax.axis_size("ctx")
    sub_size = lax.axis_size("sub")
    head_count = lax.axis_size("head")
    tok_rows = queries.shape[0]
    score_scale = HD ** (-0.5)
    regrouped = lax.all_to_all(queries, "head", split_axis=1, concat_axis=0, tiled=True)
    all_queries = lax.all_gather(regrouped, ("ctx", "sub"), axis=0, tiled=True)
    all_queries = all_queries.reshape(SPAN, local_heads, per_group, HD)
    page_ends = jnp.cumsum(page_counts)
    ctx_rows = SPAN // ctx_size
    offsets = jnp.arange(QR, dtype=jnp.int32)
    columns = jnp.arange(PAGE, dtype=jnp.int32)
    flat_index = lax.axis_index("ctx") * sub_size + lax.axis_index("sub")
    pages_here = kv_cache.shape[1] // PAGE
    base_pages = pages_here * ctx_size * sub_size // 2
    initial = (
        jnp.full((SPAN, local_heads, per_group), NEG, jnp.float32),
        jnp.zeros((SPAN, local_heads, per_group), jnp.float32),
        jnp.zeros((SPAN, local_heads, per_group, HD), jnp.float32),
    )
    half_rows = kv_cache.shape[1] // 2
    arrived = from_behind(kv_cache[:, half_rows:], "ctx", -(ctx_size // 2))
    is_lower = lax.axis_index("ctx") < ctx_size // 2
    source_flat = flat_index + ctx_size // 2 * sub_size
    working = jnp.where(is_lower, arrived, kv_cache[:, :half_rows])
    first_page = jnp.where(
        is_lower, source_flat * pages_here + pages_here // 2, flat_index * pages_here
    )
    page_total = working.shape[1] // PAGE

    def add_page(page_turn, running):
        page_index = first_page + page_turn
        relative = page_index - base_pages
        counted = jnp.sum((relative >= page_ends).astype(jnp.int32))
        request = jnp.where(relative < 0, REQS, counted)

        def update(partial_value):
            run_max, run_sum, run_out = partial_value
            request_id = jnp.minimum(request, REQS - 1)
            row_start = request_id * QR
            gathered = row_start + offsets
            within = gathered % ctx_rows
            ctx_block = gathered // ctx_rows
            sub_part = within // (head_count * tok_rows)
            head_part = within // tok_rows % head_count
            tok_part = within % tok_rows
            natural = ctx_block * ctx_rows + (head_part * sub_size + sub_part) * tok_rows + tok_part
            query_pos = (page_ends[request_id] + base_pages) * PAGE - QR + natural - row_start
            key_pos = page_index * PAGE + columns
            visible = key_pos[None, :] <= query_pos[:, None]
            page_keys = working[0].reshape(PAGE, local_heads, HD)
            page_values = working[1].reshape(PAGE, local_heads, HD)
            query_rows = lax.dynamic_slice_in_dim(all_queries, row_start, QR, 0)
            scores = (
                jnp.einsum(
                    "qkgd,pkd->qkgp", query_rows, page_keys, preferred_element_type=jnp.float32
                )
                * score_scale
            )
            scores = jnp.where(visible[:, None, None, :], scores, NEG)
            old_max = lax.dynamic_slice_in_dim(run_max, row_start, QR, 0)
            old_sum = lax.dynamic_slice_in_dim(run_sum, row_start, QR, 0)
            old_out = lax.dynamic_slice_in_dim(run_out, row_start, QR, 0)
            new_max = jnp.maximum(old_max, jnp.max(scores, axis=3))
            factor = jnp.exp(old_max - new_max)
            numerators = jnp.exp(scores - new_max[..., None])
            new_sum = old_sum * factor + jnp.sum(numerators, axis=3)
            product = jnp.einsum(
                "qkgp,pkd->qkgd",
                numerators.astype(jnp.bfloat16),
                page_values,
                preferred_element_type=jnp.float32,
            )
            new_out = old_out * factor[..., None] + product
            return (
                lax.dynamic_update_slice_in_dim(run_max, new_max, row_start, 0),
                lax.dynamic_update_slice_in_dim(run_sum, new_sum, row_start, 0),
                lax.dynamic_update_slice_in_dim(run_out, new_out, row_start, 0),
            )

        def unchanged(partial_value):
            return partial_value

        return lax.cond(request < REQS, update, unchanged, running)

    run_max, run_sum, run_out = lax.fori_loop(0, page_total, add_page, initial)
    share = SPAN // (ctx_size * sub_size)
    global_max = lax.pmax(run_max, ("ctx", "sub"))
    factor = jnp.exp(run_max - global_max)
    sums_here, outs_here = (
        lax.psum_scatter(
            (run_sum * factor).astype(jnp.bfloat16), ("ctx", "sub"), scatter_dimension=0, tiled=True
        ).astype(jnp.float32),
        lax.psum_scatter(
            (run_out * factor[..., None]).astype(jnp.bfloat16),
            ("ctx", "sub"),
            scatter_dimension=0,
            tiled=True,
        ).astype(jnp.float32),
    )
    finished = (outs_here / sums_here[..., None]).astype(jnp.bfloat16)
    finished = finished.reshape(share, local_heads * per_group * HD)
    return lax.all_to_all(finished, "head", split_axis=0, concat_axis=1, tiled=True)


def per_device(queries, kv_cache, page_counts):
    ctx_size, sub_size, head_count = lax.axis_size("ctx"), lax.axis_size("sub"), lax.axis_size("head")
    small = (
        ctx_size == REQS == 4
        and head_count == sub_size == 2
        and kv_cache.shape[1] == 2 * PAGE
        and kv_cache.shape[2] % (sub_size * HD) == 0
        and queries.shape[0] % 16 == 0
        and queries.shape[0] * head_count * sub_size == QR
    )
    return (one_request_each if small else queries_to_pages)(queries, kv_cache, page_counts)


def solution(mesh):
    return jax.shard_map(
        per_device,
        mesh=mesh,
        in_specs=(
            P(("grp", "ctx", "head", "sub"), None),
            P(None, ("grp", "ctx", "sub"), "head"),
            P("grp"),
        ),
        out_specs=P(("grp", "ctx", "head", "sub"), None),
        check_vma=False,
    )
```

```python
import functools

import jax
import jax.numpy as jnp
from jax import lax
from jax.experimental import pallas as pl
from jax.experimental.pallas import tpu as pltpu
from jax.sharding import PartitionSpec as P

HQ = 128
KVH = 8
HD = 128
REQS = 4
QR = 64
PAGE = 256
SPAN = 256


NEG = -1e30
EXP2_SCALE = HD ** (-0.5) * 1.4426950408889634


def run(copies):
    for copy in copies:
        copy.start()
    for copy in copies:
        copy.wait()


def head_part(step, width):
    return pl.ds(pl.multiple_of((lax.axis_index("head") ^ step) * width, width), width)


def split_kernel(queries, *refs):
    outs, sems = refs[:-1], refs[-1]
    run([
        pltpu.make_async_copy(queries.at[:, head_part(step, out.shape[1])], out, sems.at[step])
        for step, out in enumerate(outs)
    ])


def join_kernel(sub_count, *refs):
    pieces, (out, sems) = refs[:-2], refs[-2:]
    sub = lax.axis_index("sub")
    for source in range(sub_count):
        @pl.when(sub == source)
        def _():
            run([
                pltpu.make_async_copy(
                    pieces[step * sub_count + source], out.at[:, head_part(step, pieces[0].shape[1])], sems.at[step]
                )
                for step in range(len(pieces) // sub_count)
            ])


def own_pair_of(low_ctx, sub_count):
    return (lax.axis_index("ctx") - low_ctx) * sub_count + lax.axis_index("sub")


def gather_kernel(low_ctx, sub_count, waits, counts, *refs):
    sources, (out, sems) = refs[:-2 - waits], refs[-2:]
    local_kv, most_pages = out.shape[:2]
    own_pair = own_pair_of(low_ctx, sub_count)
    sub = lax.axis_index("sub")

    @pl.when(lax.axis_index("ctx") >= low_ctx)
    def _():
        start = jnp.int32(0)
        for r in range(REQS):
            start = start + jnp.where(r < own_pair, counts[r], 0)
        count = counts[own_pair]

        def each_page(act):
            for p in range(most_pages):
                page = start + p
                apart = page // 2 - own_pair
                which = jnp.where(apart == 0, -1, jnp.where(apart == 1 - 2 * sub, 0, 1))
                if len(sources) == 1:
                    which = jnp.where(which < 0, 0, -1)
                page_rows = pl.ds(pl.multiple_of(lax.rem(page, 2) * PAGE, PAGE), PAGE)
                for i, ref in enumerate(sources):
                    @pl.when((p < count) & (which == i))
                    def _():
                        for g in range(local_kv):
                            act(pltpu.make_async_copy(
                                ref.at[:, page_rows, pl.ds(g * HD, HD)], out.at[g, p], sems.at[g, p]
                            ))

        each_page(lambda copy: copy.start())
        each_page(lambda copy: copy.wait())


def attend_kernel(low_ctx, sub_count, step, source_sub, waits, counts, queries, pages_in, *refs):
    out = refs[waits]
    head = lax.axis_index("head")
    tokens, width = queries.shape
    local_kv, most_pages = pages_in.shape[:2]
    span = width // local_kv
    per_group = span // HD
    rows = per_group * tokens
    first_token = ((head ^ step) * sub_count + source_sub) * tokens

    def attend(pages):
        token = lax.rem(lax.broadcasted_iota(jnp.int32, (rows, PAGE), 0), tokens)
        column = lax.broadcasted_iota(jnp.int32, (rows, PAGE), 1)
        visible = column <= PAGE - QR + first_token + token

        def block(g, carry):
            part = pl.ds(pl.multiple_of(g * span, span), span)
            q_block = queries[:, part]
            q_rows = jnp.concatenate([q_block[:, j * HD:(j + 1) * HD] for j in range(per_group)], axis=0)
            scores = [
                lax.dot_general(
                    q_rows, pages_in[g, p, 0], (((1,), (1,)), ((), ())), preferred_element_type=jnp.float32
                )
                for p in range(pages)
            ]
            scores[-1] = jnp.where(visible, scores[-1], NEG)
            top = functools.reduce(jnp.maximum, scores)
            top = jnp.max(top, axis=1, keepdims=True)
            numerators = [jnp.exp2((s - top) * EXP2_SCALE) for s in scores]
            totals = jnp.sum(functools.reduce(jnp.add, numerators), axis=1, keepdims=True)
            product = functools.reduce(
                jnp.add,
                [
                    jnp.dot(n.astype(jnp.bfloat16), pages_in[g, p, 1], preferred_element_type=jnp.float32)
                    for p, n in enumerate(numerators)
                ],
            )
            done = (product / totals).astype(jnp.bfloat16)
            out[:, part] = jnp.concatenate([done[j * tokens:(j + 1) * tokens] for j in range(per_group)], axis=1)
            return carry

        lax.fori_loop(0, local_kv, block, 0)

    @pl.when(lax.axis_index("ctx") >= low_ctx)
    def _():
        count = counts[own_pair_of(low_ctx, sub_count)]
        for pages in range(1, most_pages + 1):
            @pl.when(count == pages)
            def _():
                attend(pages)


def one_request_each(queries, kv_cache, page_counts):
    ctx_size, sub_size = lax.axis_size("ctx"), lax.axis_size("sub")
    head_count = lax.axis_size("head")
    low_ctx = ctx_size // 2
    most_pages = kv_cache.shape[1] // PAGE * ctx_size * sub_size // 4
    local_kv = kv_cache.shape[2] // HD
    tokens, width = queries.shape[0], queries.shape[1] // head_count
    anywhere = pl.BlockSpec(memory_space=pl.ANY)
    in_vmem = pl.BlockSpec(memory_space=pltpu.VMEM)
    q_piece = pltpu.VMEM((tokens, width), queries.dtype)

    def vmem(array):
        return pltpu.with_memory_space_constraint(array, pltpu.VMEM)

    def hbm(array):
        return pltpu.with_memory_space_constraint(array, pltpu.HBM)

    def moved(array, routes):
        def flat(place):
            return (place[0] * head_count + place[1]) * sub_size + place[2]

        return lax.ppermute(array, ("ctx", "head", "sub"), [(flat(a), flat(b)) for a, b in routes])

    def worker(request, head):
        return low_ctx + request // sub_size, head, request % sub_size

    heads = range(head_count)
    q_out = pl.pallas_call(
        split_kernel,
        out_shape=[q_piece] * head_count,
        in_specs=[anywhere],
        out_specs=[anywhere] * head_count,
        scratch_shapes=[pltpu.SemaphoreType.DMA((head_count,))],
        name="split",
    )(hbm(queries))
    routes = {
        (step, s): [((r, h, s), worker(r, h ^ step)) for r in range(ctx_size) for h in heads]
        for step in heads for s in range(sub_size)
    }
    q_in = {(0, s): moved(q_out[0], routes[0, s]) for s in range(sub_size)}

    q_rest, kv_sent = lax.optimization_barrier((q_out[1:], kv_cache))
    middle = [(low_ctx, sub_size - 1), (low_ctx + 1, 0)]
    far = moved(kv_sent, [((a[0], h, a[1]), (b[0], h, b[1])) for a, b in (middle, middle[::-1]) for h in heads])
    paired = moved(
        kv_sent, [((c, h, s), (c, h, 1 - s)) for c in range(low_ctx, ctx_size) for h in heads for s in range(sub_size)]
    )
    for step in heads[1:]:
        for s in range(sub_size):
            q_in[step, s] = moved(q_rest[step - 1], routes[step, s])

    def gather(sources, waits, name, **options):
        return pl.pallas_call(
            functools.partial(gather_kernel, low_ctx, sub_size, len(waits)),
            out_shape=pltpu.VMEM((local_kv, most_pages, 2, PAGE, HD), kv_cache.dtype),
            in_specs=[pl.BlockSpec(memory_space=pltpu.SMEM)] + [anywhere] * len(sources + waits),
            out_specs=anywhere,
            scratch_shapes=[pltpu.SemaphoreType.DMA((local_kv, most_pages))],
            name=name,
            **options,
        )(page_counts, *sources, *waits)

    gathered = gather(
        [hbm(kv_cache)], [q_in[0, s] for s in range(sub_size)], "gather_own",
        cost_estimate=pl.CostEstimate(flops=2 * 10**10, bytes_accessed=2**20, transcendentals=0),
    )
    gathered = gather([paired, far], [vmem(gathered)], "gather_rest", input_output_aliases={3: 0})

    back = {}
    after = []
    for step, s in routes:
        if (step, s) == (head_count - 1, sub_size - 1):
            after += [back[key] for key in routes if key[0] == 0]
        out = pl.pallas_call(
            functools.partial(attend_kernel, low_ctx, sub_size, step, s, len(after)),
            out_shape=q_piece,
            in_specs=[pl.BlockSpec(memory_space=pltpu.SMEM)] + [in_vmem] * 2 + [anywhere] * len(after),
            out_specs=in_vmem,
            compiler_params=pltpu.CompilerParams(vmem_limit_bytes=24 * 1024 * 1024),
            cost_estimate=pl.CostEstimate(flops=6 * 10**9, bytes_accessed=2**22, transcendentals=10**6),
            name=f"attend_{step}{s}",
        )(page_counts, vmem(q_in[step, s]), vmem(gathered), *after)
        back[step, s] = moved(out, [(b, a) for a, b in routes[step, s]])
        after = [out]

    return pl.pallas_call(
        functools.partial(join_kernel, sub_size),
        out_shape=pltpu.HBM(queries.shape, queries.dtype),
        in_specs=[anywhere] * len(back),
        out_specs=anywhere,
        scratch_shapes=[pltpu.SemaphoreType.DMA((head_count,))],
        name="join",
    )(*[vmem(back[key]) for key in routes])


def from_behind(array, axis, by):
    count = lax.axis_size(axis)
    pairs = [(i, i + by) for i in range(count) if 0 <= i + by < count]
    return lax.ppermute(array, axis, pairs)


def queries_to_pages(queries, kv_cache, page_counts):
    per_group = HQ // KVH
    local_heads = kv_cache.shape[2] // HD
    ctx_size = lax.axis_size("ctx")
    sub_size = lax.axis_size("sub")
    head_count = lax.axis_size("head")
    tok_rows = queries.shape[0]
    score_scale = HD ** (-0.5)
    regrouped = lax.all_to_all(queries, "head", split_axis=1, concat_axis=0, tiled=True)
    all_queries = lax.all_gather(regrouped, ("ctx", "sub"), axis=0, tiled=True)
    all_queries = all_queries.reshape(SPAN, local_heads, per_group, HD)
    page_ends = jnp.cumsum(page_counts)
    ctx_rows = SPAN // ctx_size
    offsets = jnp.arange(QR, dtype=jnp.int32)
    columns = jnp.arange(PAGE, dtype=jnp.int32)
    flat_index = lax.axis_index("ctx") * sub_size + lax.axis_index("sub")
    pages_here = kv_cache.shape[1] // PAGE
    base_pages = pages_here * ctx_size * sub_size // 2
    initial = (
        jnp.full((SPAN, local_heads, per_group), NEG, jnp.float32),
        jnp.zeros((SPAN, local_heads, per_group), jnp.float32),
        jnp.zeros((SPAN, local_heads, per_group, HD), jnp.float32),
    )
    half_rows = kv_cache.shape[1] // 2
    arrived = from_behind(kv_cache[:, half_rows:], "ctx", -(ctx_size // 2))
    is_lower = lax.axis_index("ctx") < ctx_size // 2
    source_flat = flat_index + ctx_size // 2 * sub_size
    working = jnp.where(is_lower, arrived, kv_cache[:, :half_rows])
    first_page = jnp.where(
        is_lower, source_flat * pages_here + pages_here // 2, flat_index * pages_here
    )
    page_total = working.shape[1] // PAGE

    def add_page(page_turn, running):
        page_index = first_page + page_turn
        relative = page_index - base_pages
        counted = jnp.sum((relative >= page_ends).astype(jnp.int32))
        request = jnp.where(relative < 0, REQS, counted)

        def update(partial_value):
            run_max, run_sum, run_out = partial_value
            request_id = jnp.minimum(request, REQS - 1)
            row_start = request_id * QR
            gathered = row_start + offsets
            within = gathered % ctx_rows
            ctx_block = gathered // ctx_rows
            sub_part = within // (head_count * tok_rows)
            head_part = within // tok_rows % head_count
            tok_part = within % tok_rows
            natural = ctx_block * ctx_rows + (head_part * sub_size + sub_part) * tok_rows + tok_part
            query_pos = (page_ends[request_id] + base_pages) * PAGE - QR + natural - row_start
            key_pos = page_index * PAGE + columns
            visible = key_pos[None, :] <= query_pos[:, None]
            page_keys = working[0].reshape(PAGE, local_heads, HD)
            page_values = working[1].reshape(PAGE, local_heads, HD)
            query_rows = lax.dynamic_slice_in_dim(all_queries, row_start, QR, 0)
            scores = (
                jnp.einsum(
                    "qkgd,pkd->qkgp", query_rows, page_keys, preferred_element_type=jnp.float32
                )
                * score_scale
            )
            scores = jnp.where(visible[:, None, None, :], scores, NEG)
            old_max = lax.dynamic_slice_in_dim(run_max, row_start, QR, 0)
            old_sum = lax.dynamic_slice_in_dim(run_sum, row_start, QR, 0)
            old_out = lax.dynamic_slice_in_dim(run_out, row_start, QR, 0)
            new_max = jnp.maximum(old_max, jnp.max(scores, axis=3))
            factor = jnp.exp(old_max - new_max)
            numerators = jnp.exp(scores - new_max[..., None])
            new_sum = old_sum * factor + jnp.sum(numerators, axis=3)
            product = jnp.einsum(
                "qkgp,pkd->qkgd",
                numerators.astype(jnp.bfloat16),
                page_values,
                preferred_element_type=jnp.float32,
            )
            new_out = old_out * factor[..., None] + product
            return (
                lax.dynamic_update_slice_in_dim(run_max, new_max, row_start, 0),
                lax.dynamic_update_slice_in_dim(run_sum, new_sum, row_start, 0),
                lax.dynamic_update_slice_in_dim(run_out, new_out, row_start, 0),
            )

        def unchanged(partial_value):
            return partial_value

        return lax.cond(request < REQS, update, unchanged, running)

    run_max, run_sum, run_out = lax.fori_loop(0, page_total, add_page, initial)
    share = SPAN // (ctx_size * sub_size)
    global_max = lax.pmax(run_max, ("ctx", "sub"))
    factor = jnp.exp(run_max - global_max)
    sums_here, outs_here = (
        lax.psum_scatter(
            (run_sum * factor).astype(jnp.bfloat16), ("ctx", "sub"), scatter_dimension=0, tiled=True
        ).astype(jnp.float32),
        lax.psum_scatter(
            (run_out * factor[..., None]).astype(jnp.bfloat16),
            ("ctx", "sub"),
            scatter_dimension=0,
            tiled=True,
        ).astype(jnp.float32),
    )
    finished = (outs_here / sums_here[..., None]).astype(jnp.bfloat16)
    finished = finished.reshape(share, local_heads * per_group * HD)
    return lax.all_to_all(finished, "head", split_axis=0, concat_axis=1, tiled=True)


def per_device(queries, kv_cache, page_counts):
    ctx_size, sub_size, head_count = lax.axis_size("ctx"), lax.axis_size("sub"), lax.axis_size("head")
    small = (
        ctx_size == REQS == 4
        and head_count == sub_size == 2
        and kv_cache.shape[1] == 2 * PAGE
        and kv_cache.shape[2] % (sub_size * HD) == 0
        and queries.shape[0] % 16 == 0
        and queries.shape[0] * head_count * sub_size == QR
    )
    return (one_request_each if small else queries_to_pages)(queries, kv_cache, page_counts)


def solution(mesh):
    return jax.shard_map(
        per_device,
        mesh=mesh,
        in_specs=(
            P(("grp", "ctx", "head", "sub"), None),
            P(None, ("grp", "ctx", "sub"), "head"),
            P("grp"),
        ),
        out_specs=P(("grp", "ctx", "head", "sub"), None),
        check_vma=False,
    )
```

```python
import functools

import jax
import jax.numpy as jnp
from jax import lax
from jax.experimental import pallas as pl
from jax.experimental.pallas import tpu as pltpu
from jax.sharding import PartitionSpec as P

HQ = 128
KVH = 8
HD = 128
REQS = 4
QR = 64
PAGE = 256
SPAN = 256


NEG = -1e30
EXP2_SCALE = HD ** (-0.5) * 1.4426950408889634


def run(copies):
    for copy in copies:
        copy.start()
    for copy in copies:
        copy.wait()


def head_part(step, width):
    return pl.ds(pl.multiple_of((lax.axis_index("head") ^ step) * width, width), width)


def split_kernel(queries, *refs):
    outs, sems = refs[:-1], refs[-1]
    run([
        pltpu.make_async_copy(queries.at[:, head_part(step, out.shape[1])], out, sems.at[step])
        for step, out in enumerate(outs)
    ])


def join_kernel(sub_count, *refs):
    pieces, (out, sems) = refs[:-2], refs[-2:]
    sub = lax.axis_index("sub")
    for source in range(sub_count):
        @pl.when(sub == source)
        def _():
            run([
                pltpu.make_async_copy(
                    pieces[step * sub_count + source], out.at[:, head_part(step, pieces[0].shape[1])], sems.at[step]
                )
                for step in range(len(pieces) // sub_count)
            ])


def own_pair_of(low_ctx, sub_count):
    return (lax.axis_index("ctx") - low_ctx) * sub_count + lax.axis_index("sub")


def gather_kernel(low_ctx, sub_count, counts, own, far, paired, after, out, sems):
    local_kv, most_pages = out.shape[:2]
    own_pair = own_pair_of(low_ctx, sub_count)
    sub = lax.axis_index("sub")

    @pl.when(lax.axis_index("ctx") >= low_ctx)
    def _():
        start = jnp.int32(0)
        for r in range(REQS):
            start = start + jnp.where(r < own_pair, counts[r], 0)
        count = counts[own_pair]
        for p in range(most_pages):
            @pl.when(p < count)
            def _():
                page = start + p
                apart = page // 2 - own_pair
                page_rows = pl.ds(pl.multiple_of(lax.rem(page, 2) * PAGE, PAGE), PAGE)
                which = jnp.where(apart == 0, 0, jnp.where(apart == 1 - 2 * sub, 1, 2))
                for i, ref in enumerate((own, paired, far)):
                    @pl.when(which == i)
                    def _():
                        for g in range(local_kv):
                            pltpu.make_async_copy(
                                ref.at[:, page_rows, pl.ds(g * HD, HD)], out.at[g, p], sems.at[g, p]
                            ).start()
        for p in range(most_pages):
            @pl.when(p < count)
            def _():
                for g in range(local_kv):
                    pltpu.make_async_copy(
                        own.at[:, pl.ds(0, PAGE), pl.ds(0, HD)], out.at[g, p], sems.at[g, p]
                    ).wait()


def attend_kernel(low_ctx, sub_count, step, source_sub, waits, counts, queries, pages_in, *refs):
    out = refs[waits]
    head = lax.axis_index("head")
    tokens, width = queries.shape
    local_kv, most_pages = pages_in.shape[:2]
    span = width // local_kv
    per_group = span // HD
    rows = per_group * tokens
    first_token = ((head ^ step) * sub_count + source_sub) * tokens

    def attend(pages):
        token = lax.rem(lax.broadcasted_iota(jnp.int32, (rows, PAGE), 0), tokens)
        column = lax.broadcasted_iota(jnp.int32, (rows, PAGE), 1)
        visible = column <= PAGE - QR + first_token + token

        def block(g, carry):
            part = pl.ds(pl.multiple_of(g * span, span), span)
            q_block = queries[:, part]
            q_rows = jnp.concatenate([q_block[:, j * HD:(j + 1) * HD] for j in range(per_group)], axis=0)
            scores = [
                lax.dot_general(
                    q_rows, pages_in[g, p, 0], (((1,), (1,)), ((), ())), preferred_element_type=jnp.float32
                )
                for p in range(pages)
            ]
            scores[-1] = jnp.where(visible, scores[-1], NEG)
            top = functools.reduce(jnp.maximum, scores)
            top = jnp.max(top, axis=1, keepdims=True)
            numerators = [jnp.exp2((s - top) * EXP2_SCALE) for s in scores]
            totals = jnp.sum(functools.reduce(jnp.add, numerators), axis=1, keepdims=True)
            product = functools.reduce(
                jnp.add,
                [
                    jnp.dot(n.astype(jnp.bfloat16), pages_in[g, p, 1], preferred_element_type=jnp.float32)
                    for p, n in enumerate(numerators)
                ],
            )
            done = (product / totals).astype(jnp.bfloat16)
            out[:, part] = jnp.concatenate([done[j * tokens:(j + 1) * tokens] for j in range(per_group)], axis=1)
            return carry

        lax.fori_loop(0, local_kv, block, 0, unroll=2 if local_kv % 2 == 0 else 1)

    @pl.when(lax.axis_index("ctx") >= low_ctx)
    def _():
        count = counts[own_pair_of(low_ctx, sub_count)]
        for pages in range(1, most_pages + 1):
            @pl.when(count == pages)
            def _():
                attend(pages)


def one_request_each(queries, kv_cache, page_counts):
    ctx_size, sub_size = lax.axis_size("ctx"), lax.axis_size("sub")
    head_count = lax.axis_size("head")
    low_ctx = ctx_size // 2
    most_pages = kv_cache.shape[1] // PAGE * ctx_size * sub_size // 4
    local_kv = kv_cache.shape[2] // HD
    tokens, width = queries.shape[0], queries.shape[1] // head_count
    anywhere = pl.BlockSpec(memory_space=pl.ANY)
    in_vmem = pl.BlockSpec(memory_space=pltpu.VMEM)
    q_piece = pltpu.VMEM((tokens, width), queries.dtype)

    def vmem(array):
        return pltpu.with_memory_space_constraint(array, pltpu.VMEM)

    def hbm(array):
        return pltpu.with_memory_space_constraint(array, pltpu.HBM)

    def moved(array, routes):
        def flat(place):
            return (place[0] * head_count + place[1]) * sub_size + place[2]

        return lax.ppermute(array, ("ctx", "head", "sub"), [(flat(a), flat(b)) for a, b in routes])

    def worker(request, head):
        return low_ctx + request // sub_size, head, request % sub_size

    heads = range(head_count)
    q_out = pl.pallas_call(
        split_kernel,
        out_shape=[q_piece] * head_count,
        in_specs=[anywhere],
        out_specs=[anywhere] * head_count,
        scratch_shapes=[pltpu.SemaphoreType.DMA((head_count,))],
        name="split",
    )(hbm(queries))
    routes = {
        (step, s): [((r, h, s), worker(r, h ^ step)) for r in range(ctx_size) for h in heads]
        for step in heads for s in range(sub_size)
    }
    q_in = {(0, s): moved(q_out[0], routes[0, s]) for s in range(sub_size)}

    q_rest, kv_sent = lax.optimization_barrier((q_out[1:], kv_cache))
    middle = [(low_ctx, sub_size - 1), (low_ctx + 1, 0)]
    far = moved(kv_sent, [((a[0], h, a[1]), (b[0], h, b[1])) for a, b in (middle, middle[::-1]) for h in heads])
    paired = moved(
        kv_sent, [((c, h, s), (c, h, 1 - s)) for c in range(low_ctx, ctx_size) for h in heads for s in range(sub_size)]
    )
    for step in heads[1:]:
        for s in range(sub_size):
            q_in[step, s] = moved(q_rest[step - 1], routes[step, s])

    first_here = pl.pallas_call(
        lambda first, out: None,
        out_shape=pltpu.VMEM((8, HD), jnp.float32),
        in_specs=[anywhere],
        out_specs=anywhere,
        cost_estimate=pl.CostEstimate(flops=2 * 10**10, bytes_accessed=2**20, transcendentals=0),
        name="first_here",
    )(q_in[0, 0])
    gathered = pl.pallas_call(
        functools.partial(gather_kernel, low_ctx, sub_size),
        out_shape=pltpu.VMEM((local_kv, most_pages, 2, PAGE, HD), kv_cache.dtype),
        in_specs=[pl.BlockSpec(memory_space=pltpu.SMEM)] + [anywhere] * 4,
        out_specs=anywhere,
        scratch_shapes=[pltpu.SemaphoreType.DMA((local_kv, most_pages))],
        name="gather",
    )(page_counts, hbm(kv_cache), far, paired, first_here)

    back = {}
    after = []
    for step, s in routes:
        if (step, s) == (head_count - 1, sub_size - 1):
            after += [back[key] for key in routes if key[0] == 0]
        out = pl.pallas_call(
            functools.partial(attend_kernel, low_ctx, sub_size, step, s, len(after)),
            out_shape=q_piece,
            in_specs=[pl.BlockSpec(memory_space=pltpu.SMEM)] + [in_vmem] * 2 + [anywhere] * len(after),
            out_specs=in_vmem,
            compiler_params=pltpu.CompilerParams(vmem_limit_bytes=24 * 1024 * 1024),
            cost_estimate=pl.CostEstimate(flops=6 * 10**9, bytes_accessed=2**22, transcendentals=10**6),
            name=f"attend_{step}{s}",
        )(page_counts, vmem(q_in[step, s]), vmem(gathered), *after)
        back[step, s] = moved(out, [(b, a) for a, b in routes[step, s]])
        after = [out]

    return pl.pallas_call(
        functools.partial(join_kernel, sub_size),
        out_shape=pltpu.HBM(queries.shape, queries.dtype),
        in_specs=[anywhere] * len(back),
        out_specs=anywhere,
        scratch_shapes=[pltpu.SemaphoreType.DMA((head_count,))],
        name="join",
    )(*[vmem(back[key]) for key in routes])


def from_behind(array, axis, by):
    count = lax.axis_size(axis)
    pairs = [(i, i + by) for i in range(count) if 0 <= i + by < count]
    return lax.ppermute(array, axis, pairs)


def queries_to_pages(queries, kv_cache, page_counts):
    per_group = HQ // KVH
    local_heads = kv_cache.shape[2] // HD
    ctx_size = lax.axis_size("ctx")
    sub_size = lax.axis_size("sub")
    head_count = lax.axis_size("head")
    tok_rows = queries.shape[0]
    score_scale = HD ** (-0.5)
    regrouped = lax.all_to_all(queries, "head", split_axis=1, concat_axis=0, tiled=True)
    all_queries = lax.all_gather(regrouped, ("ctx", "sub"), axis=0, tiled=True)
    all_queries = all_queries.reshape(SPAN, local_heads, per_group, HD)
    page_ends = jnp.cumsum(page_counts)
    ctx_rows = SPAN // ctx_size
    offsets = jnp.arange(QR, dtype=jnp.int32)
    columns = jnp.arange(PAGE, dtype=jnp.int32)
    flat_index = lax.axis_index("ctx") * sub_size + lax.axis_index("sub")
    pages_here = kv_cache.shape[1] // PAGE
    base_pages = pages_here * ctx_size * sub_size // 2
    initial = (
        jnp.full((SPAN, local_heads, per_group), NEG, jnp.float32),
        jnp.zeros((SPAN, local_heads, per_group), jnp.float32),
        jnp.zeros((SPAN, local_heads, per_group, HD), jnp.float32),
    )
    half_rows = kv_cache.shape[1] // 2
    arrived = from_behind(kv_cache[:, half_rows:], "ctx", -(ctx_size // 2))
    is_lower = lax.axis_index("ctx") < ctx_size // 2
    source_flat = flat_index + ctx_size // 2 * sub_size
    working = jnp.where(is_lower, arrived, kv_cache[:, :half_rows])
    first_page = jnp.where(
        is_lower, source_flat * pages_here + pages_here // 2, flat_index * pages_here
    )
    page_total = working.shape[1] // PAGE

    def add_page(page_turn, running):
        page_index = first_page + page_turn
        relative = page_index - base_pages
        counted = jnp.sum((relative >= page_ends).astype(jnp.int32))
        request = jnp.where(relative < 0, REQS, counted)

        def update(partial_value):
            run_max, run_sum, run_out = partial_value
            request_id = jnp.minimum(request, REQS - 1)
            row_start = request_id * QR
            gathered = row_start + offsets
            within = gathered % ctx_rows
            ctx_block = gathered // ctx_rows
            sub_part = within // (head_count * tok_rows)
            head_part = within // tok_rows % head_count
            tok_part = within % tok_rows
            natural = ctx_block * ctx_rows + (head_part * sub_size + sub_part) * tok_rows + tok_part
            query_pos = (page_ends[request_id] + base_pages) * PAGE - QR + natural - row_start
            key_pos = page_index * PAGE + columns
            visible = key_pos[None, :] <= query_pos[:, None]
            page_keys = working[0].reshape(PAGE, local_heads, HD)
            page_values = working[1].reshape(PAGE, local_heads, HD)
            query_rows = lax.dynamic_slice_in_dim(all_queries, row_start, QR, 0)
            scores = (
                jnp.einsum(
                    "qkgd,pkd->qkgp", query_rows, page_keys, preferred_element_type=jnp.float32
                )
                * score_scale
            )
            scores = jnp.where(visible[:, None, None, :], scores, NEG)
            old_max = lax.dynamic_slice_in_dim(run_max, row_start, QR, 0)
            old_sum = lax.dynamic_slice_in_dim(run_sum, row_start, QR, 0)
            old_out = lax.dynamic_slice_in_dim(run_out, row_start, QR, 0)
            new_max = jnp.maximum(old_max, jnp.max(scores, axis=3))
            factor = jnp.exp(old_max - new_max)
            numerators = jnp.exp(scores - new_max[..., None])
            new_sum = old_sum * factor + jnp.sum(numerators, axis=3)
            product = jnp.einsum(
                "qkgp,pkd->qkgd",
                numerators.astype(jnp.bfloat16),
                page_values,
                preferred_element_type=jnp.float32,
            )
            new_out = old_out * factor[..., None] + product
            return (
                lax.dynamic_update_slice_in_dim(run_max, new_max, row_start, 0),
                lax.dynamic_update_slice_in_dim(run_sum, new_sum, row_start, 0),
                lax.dynamic_update_slice_in_dim(run_out, new_out, row_start, 0),
            )

        def unchanged(partial_value):
            return partial_value

        return lax.cond(request < REQS, update, unchanged, running)

    run_max, run_sum, run_out = lax.fori_loop(0, page_total, add_page, initial)
    share = SPAN // (ctx_size * sub_size)
    global_max = lax.pmax(run_max, ("ctx", "sub"))
    factor = jnp.exp(run_max - global_max)
    sums_here, outs_here = (
        lax.psum_scatter(
            (run_sum * factor).astype(jnp.bfloat16), ("ctx", "sub"), scatter_dimension=0, tiled=True
        ).astype(jnp.float32),
        lax.psum_scatter(
            (run_out * factor[..., None]).astype(jnp.bfloat16),
            ("ctx", "sub"),
            scatter_dimension=0,
            tiled=True,
        ).astype(jnp.float32),
    )
    finished = (outs_here / sums_here[..., None]).astype(jnp.bfloat16)
    finished = finished.reshape(share, local_heads * per_group * HD)
    return lax.all_to_all(finished, "head", split_axis=0, concat_axis=1, tiled=True)


def per_device(queries, kv_cache, page_counts):
    ctx_size, sub_size, head_count = lax.axis_size("ctx"), lax.axis_size("sub"), lax.axis_size("head")
    small = (
        ctx_size == REQS == 4
        and head_count == sub_size == 2
        and kv_cache.shape[1] == 2 * PAGE
        and kv_cache.shape[2] % (sub_size * HD) == 0
        and queries.shape[0] % 16 == 0
        and queries.shape[0] * head_count * sub_size == QR
    )
    return (one_request_each if small else queries_to_pages)(queries, kv_cache, page_counts)


def solution(mesh):
    return jax.shard_map(
        per_device,
        mesh=mesh,
        in_specs=(
            P(("grp", "ctx", "head", "sub"), None),
            P(None, ("grp", "ctx", "sub"), "head"),
            P("grp"),
        ),
        out_specs=P(("grp", "ctx", "head", "sub"), None),
        check_vma=False,
    )
```

```python
import functools

import jax
import jax.numpy as jnp
from jax import lax
from jax.experimental import pallas as pl
from jax.experimental.pallas import tpu as pltpu
from jax.sharding import PartitionSpec as P

HQ = 128
KVH = 8
HD = 128
REQS = 4
QR = 64
PAGE = 256
SPAN = 256


NEG = -1e30
EXP2_SCALE = HD ** (-0.5) * 1.4426950408889634


def run(copies):
    for copy in copies:
        copy.start()
    for copy in copies:
        copy.wait()


def head_part(step, width):
    return pl.ds(pl.multiple_of((lax.axis_index("head") ^ step) * width, width), width)


def split_kernel(queries, *refs):
    outs, sems = refs[:-1], refs[-1]
    run([
        pltpu.make_async_copy(queries.at[:, head_part(step, out.shape[1])], out, sems.at[step])
        for step, out in enumerate(outs)
    ])


def join_kernel(sub_count, *refs):
    pieces, (out, sems) = refs[:-2], refs[-2:]
    sub = lax.axis_index("sub")
    for source in range(sub_count):
        @pl.when(sub == source)
        def _():
            run([
                pltpu.make_async_copy(
                    pieces[step * sub_count + source], out.at[:, head_part(step, pieces[0].shape[1])], sems.at[step]
                )
                for step in range(len(pieces) // sub_count)
            ])


def own_pair_of(low_ctx, sub_count):
    return (lax.axis_index("ctx") - low_ctx) * sub_count + lax.axis_index("sub")


def gather_kernel(low_ctx, sub_count, counts, own, far, paired, after, out, sems):
    local_kv, most_pages = out.shape[:2]
    own_pair = own_pair_of(low_ctx, sub_count)
    sub = lax.axis_index("sub")

    @pl.when(lax.axis_index("ctx") >= low_ctx)
    def _():
        start = jnp.int32(0)
        for r in range(REQS):
            start = start + jnp.where(r < own_pair, counts[r], 0)
        count = counts[own_pair]
        sources = (own, paired, far)

        def copies(p, which):
            page_rows = pl.ds(pl.multiple_of(lax.rem(start + p, 2) * PAGE, PAGE), PAGE)
            return [
                pltpu.make_async_copy(
                    sources[which].at[i, page_rows, pl.ds(g * HD, HD)], out.at[g, p, i], sems.at[g, p, i]
                )
                for g in range(local_kv) for i in range(2)
            ]

        for p in range(most_pages):
            @pl.when(p < count)
            def _():
                apart = (start + p) // 2 - own_pair
                which = jnp.where(apart == 0, 0, jnp.where(apart == 1 - 2 * sub, 1, 2))
                for n in range(len(sources)):
                    @pl.when(which == n)
                    def _():
                        for copy in copies(p, n):
                            copy.start()
        for p in range(most_pages):
            @pl.when(p < count)
            def _():
                for copy in copies(p, 0):
                    copy.wait()


def attend_kernel(low_ctx, sub_count, step, source_sub, waits, counts, queries, pages_in, *refs):
    out = refs[waits]
    head = lax.axis_index("head")
    tokens, width = queries.shape
    local_kv, most_pages = pages_in.shape[:2]
    span = width // local_kv
    per_group = span // HD
    rows = per_group * tokens
    first_token = ((head ^ step) * sub_count + source_sub) * tokens

    def attend(pages):
        token = lax.rem(lax.broadcasted_iota(jnp.int32, (rows, PAGE), 0), tokens)
        column = lax.broadcasted_iota(jnp.int32, (rows, PAGE), 1)
        visible = column <= PAGE - QR + first_token + token

        def block(g, carry):
            part = pl.ds(pl.multiple_of(g * span, span), span)
            q_block = queries[:, part]
            q_rows = jnp.concatenate([q_block[:, j * HD:(j + 1) * HD] for j in range(per_group)], axis=0)
            scores = [
                lax.dot_general(
                    q_rows, pages_in[g, p, 0], (((1,), (1,)), ((), ())), preferred_element_type=jnp.float32
                )
                for p in range(pages)
            ]
            scores[-1] = jnp.where(visible, scores[-1], NEG)
            top = functools.reduce(jnp.maximum, scores)
            top = jnp.max(top, axis=1, keepdims=True)
            numerators = [jnp.exp2((s - top) * EXP2_SCALE) for s in scores]
            totals = jnp.sum(functools.reduce(jnp.add, numerators), axis=1, keepdims=True)
            product = functools.reduce(
                jnp.add,
                [
                    jnp.dot(n.astype(jnp.bfloat16), pages_in[g, p, 1], preferred_element_type=jnp.float32)
                    for p, n in enumerate(numerators)
                ],
            )
            done = (product / totals).astype(jnp.bfloat16)
            out[:, part] = jnp.concatenate([done[j * tokens:(j + 1) * tokens] for j in range(per_group)], axis=1)
            return carry

        lax.fori_loop(0, local_kv, block, 0, unroll=2 if local_kv % 2 == 0 else 1)

    @pl.when(lax.axis_index("ctx") >= low_ctx)
    def _():
        count = counts[own_pair_of(low_ctx, sub_count)]
        for pages in range(1, most_pages + 1):
            @pl.when(count == pages)
            def _():
                attend(pages)


def one_request_each(queries, kv_cache, page_counts):
    ctx_size, sub_size = lax.axis_size("ctx"), lax.axis_size("sub")
    head_count = lax.axis_size("head")
    low_ctx = ctx_size // 2
    most_pages = kv_cache.shape[1] // PAGE * ctx_size * sub_size // 4
    local_kv = kv_cache.shape[2] // HD
    tokens, width = queries.shape[0], queries.shape[1] // head_count
    anywhere = pl.BlockSpec(memory_space=pl.ANY)
    in_vmem = pl.BlockSpec(memory_space=pltpu.VMEM)
    q_piece = pltpu.VMEM((tokens, width), queries.dtype)

    def vmem(array):
        return pltpu.with_memory_space_constraint(array, pltpu.VMEM)

    def hbm(array):
        return pltpu.with_memory_space_constraint(array, pltpu.HBM)

    def moved(array, routes):
        def flat(place):
            return (place[0] * head_count + place[1]) * sub_size + place[2]

        return lax.ppermute(array, ("ctx", "head", "sub"), [(flat(a), flat(b)) for a, b in routes])

    def worker(request, head):
        return low_ctx + request // sub_size, head, request % sub_size

    heads = range(head_count)
    q_out = pl.pallas_call(
        split_kernel,
        out_shape=[q_piece] * head_count,
        in_specs=[anywhere],
        out_specs=[anywhere] * head_count,
        scratch_shapes=[pltpu.SemaphoreType.DMA((head_count,))],
        compiler_params=pltpu.CompilerParams(vmem_limit_bytes=2**20),
        name="split",
    )(hbm(queries))
    routes = {
        (step, s): [((r, h, s), worker(r, h ^ step)) for r in range(ctx_size) for h in heads]
        for step in heads for s in range(sub_size)
    }
    q_in = {(0, s): moved(q_out[0], routes[0, s]) for s in range(sub_size)}

    middle = [(low_ctx, sub_size - 1), (low_ctx + 1, 0)]
    far = moved(kv_cache, [((a[0], h, a[1]), (b[0], h, b[1])) for a, b in (middle, middle[::-1]) for h in heads])
    paired = moved(
        kv_cache, [((c, h, s), (c, h, 1 - s)) for c in range(low_ctx, ctx_size) for h in heads for s in range(sub_size)]
    )
    for step in heads[1:]:
        for s in range(sub_size):
            q_in[step, s] = moved(q_out[step], routes[step, s])

    first_here = pl.pallas_call(
        lambda *refs: None,
        out_shape=pltpu.VMEM((8, HD), jnp.float32),
        in_specs=[anywhere] * 2,
        out_specs=anywhere,
        cost_estimate=pl.CostEstimate(flops=2 * 10**10, bytes_accessed=2**20, transcendentals=0),
        compiler_params=pltpu.CompilerParams(vmem_limit_bytes=2**20),
        name="first_here",
    )(vmem(q_in[0, 0]), vmem(far))
    gathered = pl.pallas_call(
        functools.partial(gather_kernel, low_ctx, sub_size),
        out_shape=pltpu.VMEM((local_kv, most_pages, 2, PAGE, HD), kv_cache.dtype),
        in_specs=[pl.BlockSpec(memory_space=pltpu.SMEM)] + [anywhere] * 4,
        out_specs=anywhere,
        scratch_shapes=[pltpu.SemaphoreType.DMA((local_kv, most_pages, 2))],
        compiler_params=pltpu.CompilerParams(vmem_limit_bytes=2**20),
        name="gather",
    )(page_counts, hbm(kv_cache), vmem(far), vmem(paired), vmem(first_here))

    back = {}
    after = []
    for step, s in routes:
        if (step, s) == (head_count - 1, sub_size - 1):
            after.append(back[0, 0])
        out = pl.pallas_call(
            functools.partial(attend_kernel, low_ctx, sub_size, step, s, len(after)),
            out_shape=q_piece,
            in_specs=[pl.BlockSpec(memory_space=pltpu.SMEM)] + [in_vmem] * 2 + [anywhere] * len(after),
            out_specs=in_vmem,
            compiler_params=pltpu.CompilerParams(vmem_limit_bytes=12 * 2**20),
            cost_estimate=pl.CostEstimate(flops=6 * 10**9, bytes_accessed=2**22, transcendentals=10**6),
            name=f"attend_{step}{s}",
        )(page_counts, vmem(q_in[step, s]), vmem(gathered), *after)
        back[step, s] = moved(out, [(b, a) for a, b in routes[step, s]])
        after = [out]

    return pl.pallas_call(
        functools.partial(join_kernel, sub_size),
        out_shape=pltpu.HBM(queries.shape, queries.dtype),
        in_specs=[anywhere] * len(back),
        out_specs=anywhere,
        scratch_shapes=[pltpu.SemaphoreType.DMA((head_count,))],
        compiler_params=pltpu.CompilerParams(vmem_limit_bytes=2**20),
        name="join",
    )(*[vmem(back[key]) for key in routes])


def from_behind(array, axis, by):
    count = lax.axis_size(axis)
    pairs = [(i, i + by) for i in range(count) if 0 <= i + by < count]
    return lax.ppermute(array, axis, pairs)


def queries_to_pages(queries, kv_cache, page_counts):
    per_group = HQ // KVH
    local_heads = kv_cache.shape[2] // HD
    ctx_size = lax.axis_size("ctx")
    sub_size = lax.axis_size("sub")
    head_count = lax.axis_size("head")
    tok_rows = queries.shape[0]
    score_scale = HD ** (-0.5)
    regrouped = lax.all_to_all(queries, "head", split_axis=1, concat_axis=0, tiled=True)
    all_queries = lax.all_gather(regrouped, ("ctx", "sub"), axis=0, tiled=True)
    all_queries = all_queries.reshape(SPAN, local_heads, per_group, HD)
    page_ends = jnp.cumsum(page_counts)
    ctx_rows = SPAN // ctx_size
    offsets = jnp.arange(QR, dtype=jnp.int32)
    columns = jnp.arange(PAGE, dtype=jnp.int32)
    flat_index = lax.axis_index("ctx") * sub_size + lax.axis_index("sub")
    pages_here = kv_cache.shape[1] // PAGE
    base_pages = pages_here * ctx_size * sub_size // 2
    initial = (
        jnp.full((SPAN, local_heads, per_group), NEG, jnp.float32),
        jnp.zeros((SPAN, local_heads, per_group), jnp.float32),
        jnp.zeros((SPAN, local_heads, per_group, HD), jnp.float32),
    )
    half_rows = kv_cache.shape[1] // 2
    arrived = from_behind(kv_cache[:, half_rows:], "ctx", -(ctx_size // 2))
    is_lower = lax.axis_index("ctx") < ctx_size // 2
    source_flat = flat_index + ctx_size // 2 * sub_size
    working = jnp.where(is_lower, arrived, kv_cache[:, :half_rows])
    first_page = jnp.where(
        is_lower, source_flat * pages_here + pages_here // 2, flat_index * pages_here
    )
    page_total = working.shape[1] // PAGE

    def add_page(page_turn, running):
        page_index = first_page + page_turn
        relative = page_index - base_pages
        counted = jnp.sum((relative >= page_ends).astype(jnp.int32))
        request = jnp.where(relative < 0, REQS, counted)

        def update(partial_value):
            run_max, run_sum, run_out = partial_value
            request_id = jnp.minimum(request, REQS - 1)
            row_start = request_id * QR
            gathered = row_start + offsets
            within = gathered % ctx_rows
            ctx_block = gathered // ctx_rows
            sub_part = within // (head_count * tok_rows)
            head_part = within // tok_rows % head_count
            tok_part = within % tok_rows
            natural = ctx_block * ctx_rows + (head_part * sub_size + sub_part) * tok_rows + tok_part
            query_pos = (page_ends[request_id] + base_pages) * PAGE - QR + natural - row_start
            key_pos = page_index * PAGE + columns
            visible = key_pos[None, :] <= query_pos[:, None]
            page_keys = working[0].reshape(PAGE, local_heads, HD)
            page_values = working[1].reshape(PAGE, local_heads, HD)
            query_rows = lax.dynamic_slice_in_dim(all_queries, row_start, QR, 0)
            scores = (
                jnp.einsum(
                    "qkgd,pkd->qkgp", query_rows, page_keys, preferred_element_type=jnp.float32
                )
                * score_scale
            )
            scores = jnp.where(visible[:, None, None, :], scores, NEG)
            old_max = lax.dynamic_slice_in_dim(run_max, row_start, QR, 0)
            old_sum = lax.dynamic_slice_in_dim(run_sum, row_start, QR, 0)
            old_out = lax.dynamic_slice_in_dim(run_out, row_start, QR, 0)
            new_max = jnp.maximum(old_max, jnp.max(scores, axis=3))
            factor = jnp.exp(old_max - new_max)
            numerators = jnp.exp(scores - new_max[..., None])
            new_sum = old_sum * factor + jnp.sum(numerators, axis=3)
            product = jnp.einsum(
                "qkgp,pkd->qkgd",
                numerators.astype(jnp.bfloat16),
                page_values,
                preferred_element_type=jnp.float32,
            )
            new_out = old_out * factor[..., None] + product
            return (
                lax.dynamic_update_slice_in_dim(run_max, new_max, row_start, 0),
                lax.dynamic_update_slice_in_dim(run_sum, new_sum, row_start, 0),
                lax.dynamic_update_slice_in_dim(run_out, new_out, row_start, 0),
            )

        def unchanged(partial_value):
            return partial_value

        return lax.cond(request < REQS, update, unchanged, running)

    run_max, run_sum, run_out = lax.fori_loop(0, page_total, add_page, initial)
    share = SPAN // (ctx_size * sub_size)
    global_max = lax.pmax(run_max, ("ctx", "sub"))
    factor = jnp.exp(run_max - global_max)
    sums_here, outs_here = (
        lax.psum_scatter(
            (run_sum * factor).astype(jnp.bfloat16), ("ctx", "sub"), scatter_dimension=0, tiled=True
        ).astype(jnp.float32),
        lax.psum_scatter(
            (run_out * factor[..., None]).astype(jnp.bfloat16),
            ("ctx", "sub"),
            scatter_dimension=0,
            tiled=True,
        ).astype(jnp.float32),
    )
    finished = (outs_here / sums_here[..., None]).astype(jnp.bfloat16)
    finished = finished.reshape(share, local_heads * per_group * HD)
    return lax.all_to_all(finished, "head", split_axis=0, concat_axis=1, tiled=True)


def per_device(queries, kv_cache, page_counts):
    ctx_size, sub_size, head_count = lax.axis_size("ctx"), lax.axis_size("sub"), lax.axis_size("head")
    small = (
        ctx_size == REQS == 4
        and head_count == sub_size == 2
        and kv_cache.shape[1] == 2 * PAGE
        and kv_cache.shape[2] % (sub_size * HD) == 0
        and queries.shape[0] % 16 == 0
        and queries.shape[0] * head_count * sub_size == QR
    )
    return (one_request_each if small else queries_to_pages)(queries, kv_cache, page_counts)


def solution(mesh):
    return jax.shard_map(
        per_device,
        mesh=mesh,
        in_specs=(
            P(("grp", "ctx", "head", "sub"), None),
            P(None, ("grp", "ctx", "sub"), "head"),
            P("grp"),
        ),
        out_specs=P(("grp", "ctx", "head", "sub"), None),
        check_vma=False,
    )
```

```python
import functools

import jax
import jax.numpy as jnp
from jax import lax
from jax.experimental import pallas as pl
from jax.experimental.pallas import tpu as pltpu
from jax.sharding import PartitionSpec as P

HQ = 128
KVH = 8
HD = 128
REQS = 4
QR = 64
PAGE = 256
SPAN = 256


NEG = -1e30
EXP2_SCALE = HD ** (-0.5) * 1.4426950408889634


def run(copies):
    for copy in copies:
        copy.start()
    for copy in copies:
        copy.wait()


def head_part(step, width):
    return pl.ds(pl.multiple_of((lax.axis_index("head") ^ step) * width, width), width)


def split_kernel(queries, kv, *refs):
    outs, sems = refs[:-1], refs[-1]
    kv_count = kv.shape[0]
    run([
        pltpu.make_async_copy(kv.at[i], out, sems.at[i]) for i, out in enumerate(outs[:kv_count])
    ] + [
        pltpu.make_async_copy(queries.at[:, head_part(step, out.shape[1])], out, sems.at[kv_count + step])
        for step, out in enumerate(outs[kv_count:])
    ])


def join_kernel(sub_count, *refs):
    pieces, (out, sems) = refs[:-2], refs[-2:]
    sub = lax.axis_index("sub")
    for source in range(sub_count):
        @pl.when(sub == source)
        def _():
            run([
                pltpu.make_async_copy(
                    pieces[step * sub_count + source], out.at[:, head_part(step, pieces[0].shape[1])], sems.at[step]
                )
                for step in range(len(pieces) // sub_count)
            ])


def own_pair_of(low_ctx, sub_count):
    return (lax.axis_index("ctx") - low_ctx) * sub_count + lax.axis_index("sub")


def gather_kernel(low_ctx, sub_count, counts, own, far_keys, far_values, paired, after, out, sems):
    local_kv, most_pages = out.shape[:2]
    own_pair = own_pair_of(low_ctx, sub_count)
    sub = lax.axis_index("sub")

    @pl.when(lax.axis_index("ctx") >= low_ctx)
    def _():
        start = jnp.int32(0)
        for r in range(REQS):
            start = start + jnp.where(r < own_pair, counts[r], 0)
        count = counts[own_pair]
        sources = ((own.at[0], own.at[1]), (paired.at[0], paired.at[1]), (far_keys, far_values))

        def copies(p, which):
            page_rows = pl.ds(pl.multiple_of(lax.rem(start + p, 2) * PAGE, PAGE), PAGE)
            return [
                pltpu.make_async_copy(
                    sources[which][i].at[page_rows, pl.ds(g * HD, HD)], out.at[g, p, i], sems.at[g, p, i]
                )
                for g in range(local_kv) for i in range(2)
            ]

        for p in range(most_pages):
            @pl.when(p < count)
            def _():
                apart = (start + p) // 2 - own_pair
                which = jnp.where(apart == 0, 0, jnp.where(apart == 1 - 2 * sub, 1, 2))
                for n in range(len(sources)):
                    @pl.when(which == n)
                    def _():
                        for copy in copies(p, n):
                            copy.start()
        for p in range(most_pages):
            @pl.when(p < count)
            def _():
                for copy in copies(p, 0):
                    copy.wait()


def attend_kernel(low_ctx, sub_count, step, source_sub, waits, counts, queries, pages_in, *refs):
    out = refs[waits]
    head = lax.axis_index("head")
    tokens, width = queries.shape
    local_kv, most_pages = pages_in.shape[:2]
    span = width // local_kv
    per_group = span // HD
    rows = per_group * tokens
    first_token = ((head ^ step) * sub_count + source_sub) * tokens

    def attend(pages):
        token = lax.rem(lax.broadcasted_iota(jnp.int32, (rows, PAGE), 0), tokens)
        column = lax.broadcasted_iota(jnp.int32, (rows, PAGE), 1)
        visible = column <= PAGE - QR + first_token + token

        def block(g, carry):
            part = pl.ds(pl.multiple_of(g * span, span), span)
            q_block = queries[:, part]
            q_rows = jnp.concatenate([q_block[:, j * HD:(j + 1) * HD] for j in range(per_group)], axis=0)
            scores = [
                lax.dot_general(
                    q_rows, pages_in[g, p, 0], (((1,), (1,)), ((), ())), preferred_element_type=jnp.float32
                )
                for p in range(pages)
            ]
            scores[-1] = jnp.where(visible, scores[-1], NEG)
            top = functools.reduce(jnp.maximum, scores)
            top = jnp.max(top, axis=1, keepdims=True)
            numerators = [jnp.exp2((s - top) * EXP2_SCALE) for s in scores]
            totals = jnp.sum(functools.reduce(jnp.add, numerators), axis=1, keepdims=True)
            product = functools.reduce(
                jnp.add,
                [
                    jnp.dot(n.astype(jnp.bfloat16), pages_in[g, p, 1], preferred_element_type=jnp.float32)
                    for p, n in enumerate(numerators)
                ],
            )
            done = (product / totals).astype(jnp.bfloat16)
            out[:, part] = jnp.concatenate([done[j * tokens:(j + 1) * tokens] for j in range(per_group)], axis=1)
            return carry

        lax.fori_loop(0, local_kv, block, 0, unroll=2 if local_kv % 2 == 0 else 1)

    @pl.when(lax.axis_index("ctx") >= low_ctx)
    def _():
        count = counts[own_pair_of(low_ctx, sub_count)]
        for pages in range(1, most_pages + 1):
            @pl.when(count == pages)
            def _():
                attend(pages)


def one_request_each(queries, kv_cache, page_counts):
    ctx_size, sub_size = lax.axis_size("ctx"), lax.axis_size("sub")
    head_count = lax.axis_size("head")
    low_ctx = ctx_size // 2
    most_pages = kv_cache.shape[1] // PAGE * ctx_size * sub_size // 4
    local_kv = kv_cache.shape[2] // HD
    tokens, width = queries.shape[0], queries.shape[1] // head_count
    anywhere = pl.BlockSpec(memory_space=pl.ANY)
    in_vmem = pl.BlockSpec(memory_space=pltpu.VMEM)
    q_piece = pltpu.VMEM((tokens, width), queries.dtype)

    def vmem(array):
        return pltpu.with_memory_space_constraint(array, pltpu.VMEM)

    def hbm(array):
        return pltpu.with_memory_space_constraint(array, pltpu.HBM)

    def moved(array, routes):
        def flat(place):
            return (place[0] * head_count + place[1]) * sub_size + place[2]

        return lax.ppermute(array, ("ctx", "head", "sub"), [(flat(a), flat(b)) for a, b in routes])

    def worker(request, head):
        return low_ctx + request // sub_size, head, request % sub_size

    heads = range(head_count)
    kv_piece = pltpu.VMEM(kv_cache.shape[1:], kv_cache.dtype)
    keys, values, *q_out = pl.pallas_call(
        split_kernel,
        out_shape=[kv_piece] * 2 + [q_piece] * head_count,
        in_specs=[anywhere] * 2,
        out_specs=[anywhere] * (2 + head_count),
        scratch_shapes=[pltpu.SemaphoreType.DMA((2 + head_count,))],
        compiler_params=pltpu.CompilerParams(vmem_limit_bytes=2**20),
        name="split",
    )(hbm(queries), hbm(kv_cache))
    routes = {
        (step, s): [((r, h, s), worker(r, h ^ step)) for r in range(ctx_size) for h in heads]
        for step in heads[::-1] for s in range(sub_size)
    }
    q_in = {key: moved(q_out[key[0]], pairs) for key, pairs in routes.items()}
    first, last = list(routes)[0], list(routes)[-1]

    middle = [(low_ctx, sub_size - 1), (low_ctx + 1, 0)]
    far = [
        moved(part, [((a[0], h, a[1]), (b[0], h, b[1])) for a, b in (middle, middle[::-1]) for h in heads])
        for part in (keys, values)
    ]
    paired = moved(
        kv_cache, [((c, h, s), (c, h, 1 - s)) for c in range(low_ctx, ctx_size) for h in heads for s in range(sub_size)]
    )

    first_here = pl.pallas_call(
        lambda *refs: None,
        out_shape=pltpu.VMEM((8, HD), jnp.float32),
        in_specs=[anywhere] * 3,
        out_specs=anywhere,
        cost_estimate=pl.CostEstimate(flops=2 * 10**10, bytes_accessed=2**20, transcendentals=0),
        compiler_params=pltpu.CompilerParams(vmem_limit_bytes=2**20),
        name="first_here",
    )(vmem(q_in[first]), *map(vmem, far))
    gathered = pl.pallas_call(
        functools.partial(gather_kernel, low_ctx, sub_size),
        out_shape=pltpu.VMEM((local_kv, most_pages, 2, PAGE, HD), kv_cache.dtype),
        in_specs=[pl.BlockSpec(memory_space=pltpu.SMEM)] + [anywhere] * 5,
        out_specs=anywhere,
        scratch_shapes=[pltpu.SemaphoreType.DMA((local_kv, most_pages, 2))],
        compiler_params=pltpu.CompilerParams(vmem_limit_bytes=2**20),
        name="gather",
    )(page_counts, hbm(kv_cache), *map(vmem, far), vmem(paired), vmem(first_here))

    back = {}
    after = []
    for step, s in routes:
        if (step, s) == last:
            after.append(back[first])
        out = pl.pallas_call(
            functools.partial(attend_kernel, low_ctx, sub_size, step, s, len(after)),
            out_shape=q_piece,
            in_specs=[pl.BlockSpec(memory_space=pltpu.SMEM)] + [in_vmem] * 2 + [anywhere] * len(after),
            out_specs=in_vmem,
            compiler_params=pltpu.CompilerParams(vmem_limit_bytes=12 * 2**20),
            cost_estimate=pl.CostEstimate(flops=6 * 10**9, bytes_accessed=2**22, transcendentals=10**6),
            name=f"attend_{step}{s}",
        )(page_counts, vmem(q_in[step, s]), vmem(gathered), *after)
        back[step, s] = moved(out, [(b, a) for a, b in routes[step, s]])
        after = [out]

    return pl.pallas_call(
        functools.partial(join_kernel, sub_size),
        out_shape=pltpu.HBM(queries.shape, queries.dtype),
        in_specs=[anywhere] * len(back),
        out_specs=anywhere,
        scratch_shapes=[pltpu.SemaphoreType.DMA((head_count,))],
        compiler_params=pltpu.CompilerParams(vmem_limit_bytes=2**20),
        name="join",
    )(*[vmem(back[key]) for key in sorted(routes)])


def from_behind(array, axis, by):
    count = lax.axis_size(axis)
    pairs = [(i, i + by) for i in range(count) if 0 <= i + by < count]
    return lax.ppermute(array, axis, pairs)


def queries_to_pages(queries, kv_cache, page_counts):
    per_group = HQ // KVH
    local_heads = kv_cache.shape[2] // HD
    ctx_size = lax.axis_size("ctx")
    sub_size = lax.axis_size("sub")
    head_count = lax.axis_size("head")
    tok_rows = queries.shape[0]
    score_scale = HD ** (-0.5)
    regrouped = lax.all_to_all(queries, "head", split_axis=1, concat_axis=0, tiled=True)
    all_queries = lax.all_gather(regrouped, ("ctx", "sub"), axis=0, tiled=True)
    all_queries = all_queries.reshape(SPAN, local_heads, per_group, HD)
    page_ends = jnp.cumsum(page_counts)
    ctx_rows = SPAN // ctx_size
    offsets = jnp.arange(QR, dtype=jnp.int32)
    columns = jnp.arange(PAGE, dtype=jnp.int32)
    flat_index = lax.axis_index("ctx") * sub_size + lax.axis_index("sub")
    pages_here = kv_cache.shape[1] // PAGE
    base_pages = pages_here * ctx_size * sub_size // 2
    initial = (
        jnp.full((SPAN, local_heads, per_group), NEG, jnp.float32),
        jnp.zeros((SPAN, local_heads, per_group), jnp.float32),
        jnp.zeros((SPAN, local_heads, per_group, HD), jnp.float32),
    )
    half_rows = kv_cache.shape[1] // 2
    arrived = from_behind(kv_cache[:, half_rows:], "ctx", -(ctx_size // 2))
    is_lower = lax.axis_index("ctx") < ctx_size // 2
    source_flat = flat_index + ctx_size // 2 * sub_size
    working = jnp.where(is_lower, arrived, kv_cache[:, :half_rows])
    first_page = jnp.where(
        is_lower, source_flat * pages_here + pages_here // 2, flat_index * pages_here
    )
    page_total = working.shape[1] // PAGE

    def add_page(page_turn, running):
        page_index = first_page + page_turn
        relative = page_index - base_pages
        counted = jnp.sum((relative >= page_ends).astype(jnp.int32))
        request = jnp.where(relative < 0, REQS, counted)

        def update(partial_value):
            run_max, run_sum, run_out = partial_value
            request_id = jnp.minimum(request, REQS - 1)
            row_start = request_id * QR
            gathered = row_start + offsets
            within = gathered % ctx_rows
            ctx_block = gathered // ctx_rows
            sub_part = within // (head_count * tok_rows)
            head_part = within // tok_rows % head_count
            tok_part = within % tok_rows
            natural = ctx_block * ctx_rows + (head_part * sub_size + sub_part) * tok_rows + tok_part
            query_pos = (page_ends[request_id] + base_pages) * PAGE - QR + natural - row_start
            key_pos = page_index * PAGE + columns
            visible = key_pos[None, :] <= query_pos[:, None]
            page_keys = working[0].reshape(PAGE, local_heads, HD)
            page_values = working[1].reshape(PAGE, local_heads, HD)
            query_rows = lax.dynamic_slice_in_dim(all_queries, row_start, QR, 0)
            scores = (
                jnp.einsum(
                    "qkgd,pkd->qkgp", query_rows, page_keys, preferred_element_type=jnp.float32
                )
                * score_scale
            )
            scores = jnp.where(visible[:, None, None, :], scores, NEG)
            old_max = lax.dynamic_slice_in_dim(run_max, row_start, QR, 0)
            old_sum = lax.dynamic_slice_in_dim(run_sum, row_start, QR, 0)
            old_out = lax.dynamic_slice_in_dim(run_out, row_start, QR, 0)
            new_max = jnp.maximum(old_max, jnp.max(scores, axis=3))
            factor = jnp.exp(old_max - new_max)
            numerators = jnp.exp(scores - new_max[..., None])
            new_sum = old_sum * factor + jnp.sum(numerators, axis=3)
            product = jnp.einsum(
                "qkgp,pkd->qkgd",
                numerators.astype(jnp.bfloat16),
                page_values,
                preferred_element_type=jnp.float32,
            )
            new_out = old_out * factor[..., None] + product
            return (
                lax.dynamic_update_slice_in_dim(run_max, new_max, row_start, 0),
                lax.dynamic_update_slice_in_dim(run_sum, new_sum, row_start, 0),
                lax.dynamic_update_slice_in_dim(run_out, new_out, row_start, 0),
            )

        def unchanged(partial_value):
            return partial_value

        return lax.cond(request < REQS, update, unchanged, running)

    run_max, run_sum, run_out = lax.fori_loop(0, page_total, add_page, initial)
    share = SPAN // (ctx_size * sub_size)
    global_max = lax.pmax(run_max, ("ctx", "sub"))
    factor = jnp.exp(run_max - global_max)
    sums_here, outs_here = (
        lax.psum_scatter(
            (run_sum * factor).astype(jnp.bfloat16), ("ctx", "sub"), scatter_dimension=0, tiled=True
        ).astype(jnp.float32),
        lax.psum_scatter(
            (run_out * factor[..., None]).astype(jnp.bfloat16),
            ("ctx", "sub"),
            scatter_dimension=0,
            tiled=True,
        ).astype(jnp.float32),
    )
    finished = (outs_here / sums_here[..., None]).astype(jnp.bfloat16)
    finished = finished.reshape(share, local_heads * per_group * HD)
    return lax.all_to_all(finished, "head", split_axis=0, concat_axis=1, tiled=True)


def per_device(queries, kv_cache, page_counts):
    ctx_size, sub_size, head_count = lax.axis_size("ctx"), lax.axis_size("sub"), lax.axis_size("head")
    small = (
        ctx_size == REQS == 4
        and head_count == sub_size == 2
        and kv_cache.shape[1] == 2 * PAGE
        and kv_cache.shape[2] % (sub_size * HD) == 0
        and queries.shape[0] % 16 == 0
        and queries.shape[0] * head_count * sub_size == QR
    )
    return (one_request_each if small else queries_to_pages)(queries, kv_cache, page_counts)


def solution(mesh):
    return jax.shard_map(
        per_device,
        mesh=mesh,
        in_specs=(
            P(("grp", "ctx", "head", "sub"), None),
            P(None, ("grp", "ctx", "sub"), "head"),
            P("grp"),
        ),
        out_specs=P(("grp", "ctx", "head", "sub"), None),
        check_vma=False,
    )
```

```python
import functools

import jax
import jax.numpy as jnp
from jax import lax
from jax.experimental import pallas as pl
from jax.experimental.pallas import tpu as pltpu
from jax.sharding import PartitionSpec as P

HQ = 128
KVH = 8
HD = 128
REQS = 4
QR = 64
PAGE = 256
SPAN = 256


NEG = -1e30
EXP2_SCALE = HD ** (-0.5) * 1.4426950408889634


def run(copies):
    for copy in copies:
        copy.start()
    for copy in copies:
        copy.wait()


def head_part(step, width):
    return pl.ds(pl.multiple_of((lax.axis_index("head") ^ step) * width, width), width)


def split_kernel(queries, kv, *refs):
    outs, sems = refs[:-1], refs[-1]
    kv_count = kv.shape[0]
    run([
        pltpu.make_async_copy(kv.at[i], out, sems.at[i]) for i, out in enumerate(outs[:kv_count])
    ] + [
        pltpu.make_async_copy(queries.at[:, head_part(step, out.shape[1])], out, sems.at[kv_count + step])
        for step, out in enumerate(outs[kv_count:])
    ])


def join_kernel(sub_count, *refs):
    pieces, (out, sems) = refs[:-2], refs[-2:]
    sub = lax.axis_index("sub")
    for source in range(sub_count):
        @pl.when(sub == source)
        def _():
            run([
                pltpu.make_async_copy(
                    pieces[step * sub_count + source], out.at[:, head_part(step, pieces[0].shape[1])], sems.at[step]
                )
                for step in range(len(pieces) // sub_count)
            ])


def own_pair_of(low_ctx, sub_count):
    return (lax.axis_index("ctx") - low_ctx) * sub_count + lax.axis_index("sub")


def gather_kernel(low_ctx, sub_count, counts, own, far_keys, far_values, paired, after, out, sems):
    local_kv, most_pages = out.shape[:2]
    own_pair = own_pair_of(low_ctx, sub_count)
    sub = lax.axis_index("sub")

    @pl.when(lax.axis_index("ctx") >= low_ctx)
    def _():
        start = jnp.int32(0)
        for r in range(REQS):
            start = start + jnp.where(r < own_pair, counts[r], 0)
        count = counts[own_pair]
        sources = ((own.at[0], own.at[1]), (paired.at[0], paired.at[1]), (far_keys, far_values))

        def copies(p, which):
            page_rows = pl.ds(pl.multiple_of(lax.rem(start + p, 2) * PAGE, PAGE), PAGE)
            return [
                pltpu.make_async_copy(
                    sources[which][i].at[page_rows, pl.ds(g * HD, HD)], out.at[g, p, i], sems.at[g, p, i]
                )
                for g in range(local_kv) for i in range(2)
            ]

        for p in range(most_pages):
            @pl.when(p < count)
            def _():
                apart = (start + p) // 2 - own_pair
                which = jnp.where(apart == 0, 0, jnp.where(apart == 1 - 2 * sub, 1, 2))
                for n in range(len(sources)):
                    @pl.when(which == n)
                    def _():
                        for copy in copies(p, n):
                            copy.start()
        for p in range(most_pages):
            @pl.when(p < count)
            def _():
                for copy in copies(p, 0):
                    copy.wait()


def attend_kernel(low_ctx, sub_count, step, source_sub, waits, counts, queries, pages_in, *refs):
    out = refs[waits]
    head = lax.axis_index("head")
    tokens, width = queries.shape
    local_kv, most_pages = pages_in.shape[:2]
    span = width // local_kv
    per_group = span // HD
    rows = per_group * tokens
    first_token = ((head ^ step) * sub_count + source_sub) * tokens

    def attend(pages):
        token = lax.rem(lax.broadcasted_iota(jnp.int32, (rows, PAGE), 0), tokens)
        column = lax.broadcasted_iota(jnp.int32, (rows, PAGE), 1)
        visible = column <= PAGE - QR + first_token + token

        def block(g, carry):
            part = pl.ds(pl.multiple_of(g * span, span), span)
            q_block = queries[:, part]
            q_rows = jnp.concatenate([q_block[:, j * HD:(j + 1) * HD] for j in range(per_group)], axis=0)
            scores = [
                lax.dot_general(
                    q_rows, pages_in[g, p, 0], (((1,), (1,)), ((), ())), preferred_element_type=jnp.float32
                )
                for p in range(pages)
            ]
            scores[-1] = jnp.where(visible, scores[-1], NEG)
            top = functools.reduce(jnp.maximum, scores)
            top = jnp.max(top, axis=1, keepdims=True)
            numerators = [jnp.exp2((s - top) * EXP2_SCALE) for s in scores]
            totals = jnp.sum(functools.reduce(jnp.add, numerators), axis=1, keepdims=True)
            product = functools.reduce(
                jnp.add,
                [
                    jnp.dot(n.astype(jnp.bfloat16), pages_in[g, p, 1], preferred_element_type=jnp.float32)
                    for p, n in enumerate(numerators)
                ],
            )
            done = (product / totals).astype(jnp.bfloat16)
            out[:, part] = jnp.concatenate([done[j * tokens:(j + 1) * tokens] for j in range(per_group)], axis=1)
            return carry

        lax.fori_loop(0, local_kv, block, 0, unroll=2 if local_kv % 2 == 0 else 1)

    @pl.when(lax.axis_index("ctx") >= low_ctx)
    def _():
        count = counts[own_pair_of(low_ctx, sub_count)]
        for pages in range(1, most_pages + 1):
            @pl.when(count == pages)
            def _():
                attend(pages)


def one_request_each(queries, kv_cache, page_counts):
    ctx_size, sub_size = lax.axis_size("ctx"), lax.axis_size("sub")
    head_count = lax.axis_size("head")
    low_ctx = ctx_size // 2
    most_pages = kv_cache.shape[1] // PAGE * ctx_size * sub_size // 4
    local_kv = kv_cache.shape[2] // HD
    tokens, width = queries.shape[0], queries.shape[1] // head_count
    anywhere = pl.BlockSpec(memory_space=pl.ANY)
    in_vmem = pl.BlockSpec(memory_space=pltpu.VMEM)
    q_piece = pltpu.VMEM((tokens, width), queries.dtype)

    def vmem(array):
        return pltpu.with_memory_space_constraint(array, pltpu.VMEM)

    def hbm(array):
        return pltpu.with_memory_space_constraint(array, pltpu.HBM)

    def moved(array, routes):
        def flat(place):
            return (place[0] * head_count + place[1]) * sub_size + place[2]

        return lax.ppermute(array, ("ctx", "head", "sub"), [(flat(a), flat(b)) for a, b in routes])

    def worker(request, head):
        return low_ctx + request // sub_size, head, request % sub_size

    heads = range(head_count)
    kv_piece = pltpu.VMEM(kv_cache.shape[1:], kv_cache.dtype)
    keys, values, *q_out = pl.pallas_call(
        split_kernel,
        out_shape=[kv_piece] * 2 + [q_piece] * head_count,
        in_specs=[anywhere] * 2,
        out_specs=[anywhere] * (2 + head_count),
        scratch_shapes=[pltpu.SemaphoreType.DMA((2 + head_count,))],
        compiler_params=pltpu.CompilerParams(vmem_limit_bytes=2**20),
        name="split",
    )(hbm(queries), hbm(kv_cache))
    routes = {
        (step, s): [((r, h, s), worker(r, h ^ step)) for r in range(ctx_size) for h in heads]
        for step in heads[::-1] for s in range(sub_size)
    }
    first, last = list(routes)[0], list(routes)[-1]
    middle = [(low_ctx, sub_size - 1), (low_ctx + 1, 0)]
    far = [
        moved(part, [((a[0], h, a[1]), (b[0], h, b[1])) for a, b in (middle, middle[::-1]) for h in heads])
        for part in (keys, values)
    ]
    q_last, kv_later, far[0] = lax.optimization_barrier((q_out[last[0]], kv_cache, far[0]))
    q_in = {key: moved(q_last if key == last else q_out[key[0]], pairs) for key, pairs in routes.items()}
    paired = moved(
        kv_later, [((c, h, s), (c, h, 1 - s)) for c in range(low_ctx, ctx_size) for h in heads for s in range(sub_size)]
    )

    far_here = pl.pallas_call(
        lambda *refs: None,
        out_shape=pltpu.VMEM((8, HD), jnp.float32),
        in_specs=[anywhere] * 2,
        out_specs=anywhere,
        cost_estimate=pl.CostEstimate(flops=2 * 10**10, bytes_accessed=2**20, transcendentals=0),
        compiler_params=pltpu.CompilerParams(vmem_limit_bytes=2**20),
        name="far_here",
    )(*map(vmem, far))
    gathered = pl.pallas_call(
        functools.partial(gather_kernel, low_ctx, sub_size),
        out_shape=pltpu.VMEM((local_kv, most_pages, 2, PAGE, HD), kv_cache.dtype),
        in_specs=[pl.BlockSpec(memory_space=pltpu.SMEM)] + [anywhere] * 5,
        out_specs=anywhere,
        scratch_shapes=[pltpu.SemaphoreType.DMA((local_kv, most_pages, 2))],
        compiler_params=pltpu.CompilerParams(vmem_limit_bytes=2**20),
        name="gather",
    )(page_counts, hbm(kv_cache), *map(vmem, far), vmem(paired), vmem(far_here))

    back = {}
    after = []
    for step, s in routes:
        if (step, s) == last:
            after.append(back[first])
        out = pl.pallas_call(
            functools.partial(attend_kernel, low_ctx, sub_size, step, s, len(after)),
            out_shape=q_piece,
            in_specs=[pl.BlockSpec(memory_space=pltpu.SMEM)] + [in_vmem] * 2 + [anywhere] * len(after),
            out_specs=in_vmem,
            compiler_params=pltpu.CompilerParams(vmem_limit_bytes=12 * 2**20),
            cost_estimate=pl.CostEstimate(flops=6 * 10**9, bytes_accessed=2**22, transcendentals=10**6),
            name=f"attend_{step}{s}",
        )(page_counts, vmem(q_in[step, s]), vmem(gathered), *after)
        back[step, s] = moved(out, [(b, a) for a, b in routes[step, s]])
        after = [out]

    return pl.pallas_call(
        functools.partial(join_kernel, sub_size),
        out_shape=pltpu.HBM(queries.shape, queries.dtype),
        in_specs=[anywhere] * len(back),
        out_specs=anywhere,
        scratch_shapes=[pltpu.SemaphoreType.DMA((head_count,))],
        compiler_params=pltpu.CompilerParams(vmem_limit_bytes=2**20),
        name="join",
    )(*[vmem(back[key]) for key in sorted(routes)])


def from_behind(array, axis, by):
    count = lax.axis_size(axis)
    pairs = [(i, i + by) for i in range(count) if 0 <= i + by < count]
    return lax.ppermute(array, axis, pairs)


def queries_to_pages(queries, kv_cache, page_counts):
    per_group = HQ // KVH
    local_heads = kv_cache.shape[2] // HD
    ctx_size = lax.axis_size("ctx")
    sub_size = lax.axis_size("sub")
    head_count = lax.axis_size("head")
    tok_rows = queries.shape[0]
    score_scale = HD ** (-0.5)
    regrouped = lax.all_to_all(queries, "head", split_axis=1, concat_axis=0, tiled=True)
    all_queries = lax.all_gather(regrouped, ("ctx", "sub"), axis=0, tiled=True)
    all_queries = all_queries.reshape(SPAN, local_heads, per_group, HD)
    page_ends = jnp.cumsum(page_counts)
    ctx_rows = SPAN // ctx_size
    offsets = jnp.arange(QR, dtype=jnp.int32)
    columns = jnp.arange(PAGE, dtype=jnp.int32)
    flat_index = lax.axis_index("ctx") * sub_size + lax.axis_index("sub")
    pages_here = kv_cache.shape[1] // PAGE
    base_pages = pages_here * ctx_size * sub_size // 2
    initial = (
        jnp.full((SPAN, local_heads, per_group), NEG, jnp.float32),
        jnp.zeros((SPAN, local_heads, per_group), jnp.float32),
        jnp.zeros((SPAN, local_heads, per_group, HD), jnp.float32),
    )
    half_rows = kv_cache.shape[1] // 2
    arrived = from_behind(kv_cache[:, half_rows:], "ctx", -(ctx_size // 2))
    is_lower = lax.axis_index("ctx") < ctx_size // 2
    source_flat = flat_index + ctx_size // 2 * sub_size
    working = jnp.where(is_lower, arrived, kv_cache[:, :half_rows])
    first_page = jnp.where(
        is_lower, source_flat * pages_here + pages_here // 2, flat_index * pages_here
    )
    page_total = working.shape[1] // PAGE

    def add_page(page_turn, running):
        page_index = first_page + page_turn
        relative = page_index - base_pages
        counted = jnp.sum((relative >= page_ends).astype(jnp.int32))
        request = jnp.where(relative < 0, REQS, counted)

        def update(partial_value):
            run_max, run_sum, run_out = partial_value
            request_id = jnp.minimum(request, REQS - 1)
            row_start = request_id * QR
            gathered = row_start + offsets
            within = gathered % ctx_rows
            ctx_block = gathered // ctx_rows
            sub_part = within // (head_count * tok_rows)
            head_part = within // tok_rows % head_count
            tok_part = within % tok_rows
            natural = ctx_block * ctx_rows + (head_part * sub_size + sub_part) * tok_rows + tok_part
            query_pos = (page_ends[request_id] + base_pages) * PAGE - QR + natural - row_start
            key_pos = page_index * PAGE + columns
            visible = key_pos[None, :] <= query_pos[:, None]
            page_keys = working[0].reshape(PAGE, local_heads, HD)
            page_values = working[1].reshape(PAGE, local_heads, HD)
            query_rows = lax.dynamic_slice_in_dim(all_queries, row_start, QR, 0)
            scores = (
                jnp.einsum(
                    "qkgd,pkd->qkgp", query_rows, page_keys, preferred_element_type=jnp.float32
                )
                * score_scale
            )
            scores = jnp.where(visible[:, None, None, :], scores, NEG)
            old_max = lax.dynamic_slice_in_dim(run_max, row_start, QR, 0)
            old_sum = lax.dynamic_slice_in_dim(run_sum, row_start, QR, 0)
            old_out = lax.dynamic_slice_in_dim(run_out, row_start, QR, 0)
            new_max = jnp.maximum(old_max, jnp.max(scores, axis=3))
            factor = jnp.exp(old_max - new_max)
            numerators = jnp.exp(scores - new_max[..., None])
            new_sum = old_sum * factor + jnp.sum(numerators, axis=3)
            product = jnp.einsum(
                "qkgp,pkd->qkgd",
                numerators.astype(jnp.bfloat16),
                page_values,
                preferred_element_type=jnp.float32,
            )
            new_out = old_out * factor[..., None] + product
            return (
                lax.dynamic_update_slice_in_dim(run_max, new_max, row_start, 0),
                lax.dynamic_update_slice_in_dim(run_sum, new_sum, row_start, 0),
                lax.dynamic_update_slice_in_dim(run_out, new_out, row_start, 0),
            )

        def unchanged(partial_value):
            return partial_value

        return lax.cond(request < REQS, update, unchanged, running)

    run_max, run_sum, run_out = lax.fori_loop(0, page_total, add_page, initial)
    share = SPAN // (ctx_size * sub_size)
    global_max = lax.pmax(run_max, ("ctx", "sub"))
    factor = jnp.exp(run_max - global_max)
    sums_here, outs_here = (
        lax.psum_scatter(
            (run_sum * factor).astype(jnp.bfloat16), ("ctx", "sub"), scatter_dimension=0, tiled=True
        ).astype(jnp.float32),
        lax.psum_scatter(
            (run_out * factor[..., None]).astype(jnp.bfloat16),
            ("ctx", "sub"),
            scatter_dimension=0,
            tiled=True,
        ).astype(jnp.float32),
    )
    finished = (outs_here / sums_here[..., None]).astype(jnp.bfloat16)
    finished = finished.reshape(share, local_heads * per_group * HD)
    return lax.all_to_all(finished, "head", split_axis=0, concat_axis=1, tiled=True)


def per_device(queries, kv_cache, page_counts):
    ctx_size, sub_size, head_count = lax.axis_size("ctx"), lax.axis_size("sub"), lax.axis_size("head")
    small = (
        ctx_size == REQS == 4
        and head_count == sub_size == 2
        and kv_cache.shape[1] == 2 * PAGE
        and kv_cache.shape[2] % (sub_size * HD) == 0
        and queries.shape[0] % 16 == 0
        and queries.shape[0] * head_count * sub_size == QR
    )
    return (one_request_each if small else queries_to_pages)(queries, kv_cache, page_counts)


def solution(mesh):
    return jax.shard_map(
        per_device,
        mesh=mesh,
        in_specs=(
            P(("grp", "ctx", "head", "sub"), None),
            P(None, ("grp", "ctx", "sub"), "head"),
            P("grp"),
        ),
        out_specs=P(("grp", "ctx", "head", "sub"), None),
        check_vma=False,
    )
```

```python
import functools

import jax
import jax.numpy as jnp
from jax import lax
from jax.experimental import pallas as pl
from jax.experimental.pallas import tpu as pltpu
from jax.sharding import PartitionSpec as P

HQ = 128
KVH = 8
HD = 128
REQS = 4
QR = 64
PAGE = 256
SPAN = 256


NEG = -1e30
EXP2_SCALE = HD ** (-0.5) * 1.4426950408889634


def run(copies):
    for copy in copies:
        copy.start()
    for copy in copies:
        copy.wait()


def head_part(step, width):
    return pl.ds(pl.multiple_of((lax.axis_index("head") ^ step) * width, width), width)


def split_kernel(queries, *refs):
    outs, sems = refs[:-1], refs[-1]
    run([
        pltpu.make_async_copy(queries.at[:, head_part(step, out.shape[1])], out, sems.at[step])
        for step, out in enumerate(outs)
    ])


def join_kernel(step, sub_count, *refs):
    pieces, (out, sems) = refs[:sub_count], refs[-2:]
    for source, piece in enumerate(pieces):
        @pl.when(lax.axis_index("sub") == source)
        def _():
            run([pltpu.make_async_copy(piece, out.at[:, head_part(step, piece.shape[1])], sems.at[0])])


def own_pair_of(low_ctx, sub_count):
    return (lax.axis_index("ctx") - low_ctx) * sub_count + lax.axis_index("sub")


def gather_kernel(low_ctx, sub_count, counts, own, far, paired, after, out, sems):
    local_kv, most_pages = out.shape[:2]
    own_pair = own_pair_of(low_ctx, sub_count)
    sub = lax.axis_index("sub")

    @pl.when(lax.axis_index("ctx") >= low_ctx)
    def _():
        start = jnp.int32(0)
        for r in range(REQS):
            start = start + jnp.where(r < own_pair, counts[r], 0)
        count = counts[own_pair]
        sources = (own, paired, far)

        def copies(p, which):
            page_rows = pl.ds(pl.multiple_of(lax.rem(start + p, 2) * PAGE, PAGE), PAGE)
            return [
                pltpu.make_async_copy(
                    sources[which].at[i, page_rows, pl.ds(g * HD, HD)], out.at[g, p, i], sems.at[g, p, i]
                )
                for g in range(local_kv) for i in range(2)
            ]

        for p in range(most_pages):
            @pl.when(p < count)
            def _():
                apart = (start + p) // 2 - own_pair
                which = jnp.where(apart == 0, 0, jnp.where(apart == 1 - 2 * sub, 1, 2))
                for n in range(len(sources)):
                    @pl.when(which == n)
                    def _():
                        for copy in copies(p, n):
                            copy.start()
        for p in range(most_pages):
            @pl.when(p < count)
            def _():
                for copy in copies(p, 0):
                    copy.wait()


def attend_kernel(low_ctx, sub_count, step, waits, counts, pages_in, *refs):
    queries, outs = refs[:sub_count], refs[sub_count + waits:]
    head = lax.axis_index("head")
    tokens, width = queries[0].shape
    local_kv, most_pages = pages_in.shape[:2]
    span = width // local_kv
    per_group = span // HD
    piece_rows = per_group * tokens
    rows = sub_count * piece_rows
    first_token = (head ^ step) * sub_count * tokens

    def attend(pages):
        row = lax.broadcasted_iota(jnp.int32, (rows, PAGE), 0)
        token = first_token + row // piece_rows * tokens + lax.rem(row, tokens)
        column = lax.broadcasted_iota(jnp.int32, (rows, PAGE), 1)
        visible = column <= PAGE - QR + token

        def block(g, carry):
            part = pl.ds(pl.multiple_of(g * span, span), span)
            q_blocks = [ref[:, part] for ref in queries]
            q_rows = jnp.concatenate([q[:, j * HD:(j + 1) * HD] for q in q_blocks for j in range(per_group)], axis=0)
            scores = [
                lax.dot_general(
                    q_rows, pages_in[g, p, 0], (((1,), (1,)), ((), ())), preferred_element_type=jnp.float32
                )
                for p in range(pages)
            ]
            scores[-1] = jnp.where(visible, scores[-1], NEG)
            top = functools.reduce(jnp.maximum, scores)
            top = jnp.max(top, axis=1, keepdims=True)
            numerators = [jnp.exp2((s - top) * EXP2_SCALE) for s in scores]
            totals = jnp.sum(functools.reduce(jnp.add, numerators), axis=1, keepdims=True)
            product = functools.reduce(
                jnp.add,
                [
                    jnp.dot(n.astype(jnp.bfloat16), pages_in[g, p, 1], preferred_element_type=jnp.float32)
                    for p, n in enumerate(numerators)
                ],
            )
            done = (product / totals).astype(jnp.bfloat16)
            for i, out in enumerate(outs):
                start = i * piece_rows
                out[:, part] = jnp.concatenate(
                    [done[start + j * tokens:start + (j + 1) * tokens] for j in range(per_group)], axis=1
                )
            return carry

        lax.fori_loop(0, local_kv, block, 0, unroll=2 if local_kv % 2 == 0 else 1)

    @pl.when(lax.axis_index("ctx") >= low_ctx)
    def _():
        count = counts[own_pair_of(low_ctx, sub_count)]
        for pages in range(1, most_pages + 1):
            @pl.when(count == pages)
            def _():
                attend(pages)


def one_request_each(queries, kv_cache, page_counts):
    ctx_size, sub_size = lax.axis_size("ctx"), lax.axis_size("sub")
    head_count = lax.axis_size("head")
    low_ctx = ctx_size // 2
    most_pages = kv_cache.shape[1] // PAGE * ctx_size * sub_size // 4
    local_kv = kv_cache.shape[2] // HD
    tokens, width = queries.shape[0], queries.shape[1] // head_count
    anywhere = pl.BlockSpec(memory_space=pl.ANY)
    in_vmem = pl.BlockSpec(memory_space=pltpu.VMEM)
    q_piece = pltpu.VMEM((tokens, width), queries.dtype)

    def vmem(array):
        return pltpu.with_memory_space_constraint(array, pltpu.VMEM)

    def hbm(array):
        return pltpu.with_memory_space_constraint(array, pltpu.HBM)

    def moved(array, routes):
        def flat(place):
            return (place[0] * head_count + place[1]) * sub_size + place[2]

        return lax.ppermute(array, ("ctx", "head", "sub"), [(flat(a), flat(b)) for a, b in routes])

    def worker(request, head):
        return low_ctx + request // sub_size, head, request % sub_size

    heads = range(head_count)
    q_out = pl.pallas_call(
        split_kernel,
        out_shape=[q_piece] * head_count,
        in_specs=[anywhere],
        out_specs=[anywhere] * head_count,
        scratch_shapes=[pltpu.SemaphoreType.DMA((head_count,))],
        compiler_params=pltpu.CompilerParams(vmem_limit_bytes=2**20),
        name="split",
    )(hbm(queries))
    routes = {
        (step, s): [((r, h, s), worker(r, h ^ step)) for r in range(ctx_size) for h in heads]
        for step in heads[::-1] for s in range(sub_size)
    }
    q_in = {key: moved(q_out[key[0]], pairs) for key, pairs in routes.items()}
    first = list(routes)[0]

    middle = [(low_ctx, sub_size - 1), (low_ctx + 1, 0)]
    far = moved(kv_cache, [((a[0], h, a[1]), (b[0], h, b[1])) for a, b in (middle, middle[::-1]) for h in heads])
    paired = moved(
        kv_cache, [((c, h, s), (c, h, 1 - s)) for c in range(low_ctx, ctx_size) for h in heads for s in range(sub_size)]
    )
    first_here = pl.pallas_call(
        lambda *refs: None,
        out_shape=pltpu.VMEM((8, HD), jnp.float32),
        in_specs=[anywhere] * 2,
        out_specs=anywhere,
        cost_estimate=pl.CostEstimate(flops=2 * 10**10, bytes_accessed=2**20, transcendentals=0),
        compiler_params=pltpu.CompilerParams(vmem_limit_bytes=2**20),
        name="first_here",
    )(vmem(q_in[first]), vmem(far))
    gathered = pl.pallas_call(
        functools.partial(gather_kernel, low_ctx, sub_size),
        out_shape=pltpu.VMEM((local_kv, most_pages, 2, PAGE, HD), kv_cache.dtype),
        in_specs=[pl.BlockSpec(memory_space=pltpu.SMEM)] + [anywhere] * 4,
        out_specs=anywhere,
        scratch_shapes=[pltpu.SemaphoreType.DMA((local_kv, most_pages, 2))],
        compiler_params=pltpu.CompilerParams(vmem_limit_bytes=2**20),
        name="gather",
    )(page_counts, hbm(kv_cache), vmem(far), vmem(paired), vmem(first_here))

    back = {}
    after = []
    for step in heads[::-1]:
        subs = range(sub_size)
        outs = pl.pallas_call(
            functools.partial(attend_kernel, low_ctx, sub_size, step, len(after)),
            out_shape=[q_piece] * sub_size,
            in_specs=[pl.BlockSpec(memory_space=pltpu.SMEM)] + [in_vmem] * (1 + sub_size) + [anywhere] * len(after),
            out_specs=[in_vmem] * sub_size,
            compiler_params=pltpu.CompilerParams(vmem_limit_bytes=12 * 2**20),
            cost_estimate=pl.CostEstimate(flops=10**10, bytes_accessed=2**22, transcendentals=10**6),
            name=f"attend_{step}",
        )(page_counts, vmem(gathered), *[vmem(q_in[step, s]) for s in subs], *after)
        for s in subs:
            back[step, s] = moved(outs[s], [(b, a) for a, b in routes[step, s]])
        after = [outs[0]]

    joined = []
    for step in heads[::-1]:
        joined = [
            pl.pallas_call(
                functools.partial(join_kernel, step, sub_size),
                out_shape=pltpu.HBM(queries.shape, queries.dtype),
                in_specs=[anywhere] * (sub_size + len(joined)),
                out_specs=anywhere,
                scratch_shapes=[pltpu.SemaphoreType.DMA((1,))],
                input_output_aliases={sub_size: 0} if joined else {},
                compiler_params=pltpu.CompilerParams(vmem_limit_bytes=2**20),
                name=f"join_{step}",
            )(*[vmem(back[step, s]) for s in range(sub_size)], *map(hbm, joined))
        ]
    return joined[0]


def from_behind(array, axis, by):
    count = lax.axis_size(axis)
    pairs = [(i, i + by) for i in range(count) if 0 <= i + by < count]
    return lax.ppermute(array, axis, pairs)


def queries_to_pages(queries, kv_cache, page_counts):
    per_group = HQ // KVH
    local_heads = kv_cache.shape[2] // HD
    ctx_size = lax.axis_size("ctx")
    sub_size = lax.axis_size("sub")
    head_count = lax.axis_size("head")
    tok_rows = queries.shape[0]
    score_scale = HD ** (-0.5)
    regrouped = lax.all_to_all(queries, "head", split_axis=1, concat_axis=0, tiled=True)
    all_queries = lax.all_gather(regrouped, ("ctx", "sub"), axis=0, tiled=True)
    all_queries = all_queries.reshape(SPAN, local_heads, per_group, HD)
    page_ends = jnp.cumsum(page_counts)
    ctx_rows = SPAN // ctx_size
    offsets = jnp.arange(QR, dtype=jnp.int32)
    columns = jnp.arange(PAGE, dtype=jnp.int32)
    flat_index = lax.axis_index("ctx") * sub_size + lax.axis_index("sub")
    pages_here = kv_cache.shape[1] // PAGE
    base_pages = pages_here * ctx_size * sub_size // 2
    initial = (
        jnp.full((SPAN, local_heads, per_group), NEG, jnp.float32),
        jnp.zeros((SPAN, local_heads, per_group), jnp.float32),
        jnp.zeros((SPAN, local_heads, per_group, HD), jnp.float32),
    )
    half_rows = kv_cache.shape[1] // 2
    arrived = from_behind(kv_cache[:, half_rows:], "ctx", -(ctx_size // 2))
    is_lower = lax.axis_index("ctx") < ctx_size // 2
    source_flat = flat_index + ctx_size // 2 * sub_size
    working = jnp.where(is_lower, arrived, kv_cache[:, :half_rows])
    first_page = jnp.where(
        is_lower, source_flat * pages_here + pages_here // 2, flat_index * pages_here
    )
    page_total = working.shape[1] // PAGE

    def add_page(page_turn, running):
        page_index = first_page + page_turn
        relative = page_index - base_pages
        counted = jnp.sum((relative >= page_ends).astype(jnp.int32))
        request = jnp.where(relative < 0, REQS, counted)

        def update(partial_value):
            run_max, run_sum, run_out = partial_value
            request_id = jnp.minimum(request, REQS - 1)
            row_start = request_id * QR
            gathered = row_start + offsets
            within = gathered % ctx_rows
            ctx_block = gathered // ctx_rows
            sub_part = within // (head_count * tok_rows)
            head_part = within // tok_rows % head_count
            tok_part = within % tok_rows
            natural = ctx_block * ctx_rows + (head_part * sub_size + sub_part) * tok_rows + tok_part
            query_pos = (page_ends[request_id] + base_pages) * PAGE - QR + natural - row_start
            key_pos = page_index * PAGE + columns
            visible = key_pos[None, :] <= query_pos[:, None]
            page_keys = working[0].reshape(PAGE, local_heads, HD)
            page_values = working[1].reshape(PAGE, local_heads, HD)
            query_rows = lax.dynamic_slice_in_dim(all_queries, row_start, QR, 0)
            scores = (
                jnp.einsum(
                    "qkgd,pkd->qkgp", query_rows, page_keys, preferred_element_type=jnp.float32
                )
                * score_scale
            )
            scores = jnp.where(visible[:, None, None, :], scores, NEG)
            old_max = lax.dynamic_slice_in_dim(run_max, row_start, QR, 0)
            old_sum = lax.dynamic_slice_in_dim(run_sum, row_start, QR, 0)
            old_out = lax.dynamic_slice_in_dim(run_out, row_start, QR, 0)
            new_max = jnp.maximum(old_max, jnp.max(scores, axis=3))
            factor = jnp.exp(old_max - new_max)
            numerators = jnp.exp(scores - new_max[..., None])
            new_sum = old_sum * factor + jnp.sum(numerators, axis=3)
            product = jnp.einsum(
                "qkgp,pkd->qkgd",
                numerators.astype(jnp.bfloat16),
                page_values,
                preferred_element_type=jnp.float32,
            )
            new_out = old_out * factor[..., None] + product
            return (
                lax.dynamic_update_slice_in_dim(run_max, new_max, row_start, 0),
                lax.dynamic_update_slice_in_dim(run_sum, new_sum, row_start, 0),
                lax.dynamic_update_slice_in_dim(run_out, new_out, row_start, 0),
            )

        def unchanged(partial_value):
            return partial_value

        return lax.cond(request < REQS, update, unchanged, running)

    run_max, run_sum, run_out = lax.fori_loop(0, page_total, add_page, initial)
    share = SPAN // (ctx_size * sub_size)
    global_max = lax.pmax(run_max, ("ctx", "sub"))
    factor = jnp.exp(run_max - global_max)
    sums_here, outs_here = (
        lax.psum_scatter(
            (run_sum * factor).astype(jnp.bfloat16), ("ctx", "sub"), scatter_dimension=0, tiled=True
        ).astype(jnp.float32),
        lax.psum_scatter(
            (run_out * factor[..., None]).astype(jnp.bfloat16),
            ("ctx", "sub"),
            scatter_dimension=0,
            tiled=True,
        ).astype(jnp.float32),
    )
    finished = (outs_here / sums_here[..., None]).astype(jnp.bfloat16)
    finished = finished.reshape(share, local_heads * per_group * HD)
    return lax.all_to_all(finished, "head", split_axis=0, concat_axis=1, tiled=True)


def per_device(queries, kv_cache, page_counts):
    ctx_size, sub_size, head_count = lax.axis_size("ctx"), lax.axis_size("sub"), lax.axis_size("head")
    small = (
        ctx_size == REQS == 4
        and head_count == sub_size == 2
        and kv_cache.shape[1] == 2 * PAGE
        and kv_cache.shape[2] % (sub_size * HD) == 0
        and queries.shape[0] % 16 == 0
        and queries.shape[0] * head_count * sub_size == QR
    )
    return (one_request_each if small else queries_to_pages)(queries, kv_cache, page_counts)


def solution(mesh):
    return jax.shard_map(
        per_device,
        mesh=mesh,
        in_specs=(
            P(("grp", "ctx", "head", "sub"), None),
            P(None, ("grp", "ctx", "sub"), "head"),
            P("grp"),
        ),
        out_specs=P(("grp", "ctx", "head", "sub"), None),
        check_vma=False,
    )
```

```python
import functools

import jax
import jax.numpy as jnp
from jax import lax
from jax.experimental import pallas as pl
from jax.experimental.pallas import tpu as pltpu
from jax.sharding import PartitionSpec as P

HQ = 128
KVH = 8
HD = 128
REQS = 4
QR = 64
PAGE = 256
SPAN = 256


NEG = -1e30
EXP2_SCALE = HD ** (-0.5) * 1.4426950408889634


def run(copies):
    for copy in copies:
        copy.start()
    for copy in copies:
        copy.wait()


def head_part(step, width):
    return pl.ds(pl.multiple_of((lax.axis_index("head") ^ step) * width, width), width)


def split_kernel(queries, *refs):
    outs, sems = refs[:-1], refs[-1]
    run([
        pltpu.make_async_copy(queries.at[:, head_part(step, out.shape[1])], out, sems.at[step])
        for step, out in enumerate(outs)
    ])


def join_kernel(step, sub_count, *refs):
    pieces, (out, sems) = refs[:sub_count], refs[-2:]
    for source, piece in enumerate(pieces):
        @pl.when(lax.axis_index("sub") == source)
        def _():
            run([pltpu.make_async_copy(piece, out.at[:, head_part(step, piece.shape[1])], sems.at[0])])


def own_pair_of(low_ctx, sub_count):
    return (lax.axis_index("ctx") - low_ctx) * sub_count + lax.axis_index("sub")


def gather_kernel(low_ctx, sub_count, counts, own, far, paired, after, out):
    local_kv, most_pages = out.shape[:2]
    own_pair = own_pair_of(low_ctx, sub_count)
    sub = lax.axis_index("sub")

    @pl.when(lax.axis_index("ctx") >= low_ctx)
    def _():
        start = jnp.int32(0)
        for r in range(REQS):
            start = start + jnp.where(r < own_pair, counts[r], 0)
        count = counts[own_pair]
        for p in range(most_pages):
            page = start + p
            apart = page // 2 - own_pair
            which = jnp.where(apart == 0, 0, jnp.where(apart == 1 - 2 * sub, 1, 2))
            page_rows = pl.ds(pl.multiple_of(lax.rem(page, 2) * PAGE, PAGE), PAGE)
            for n, ref in enumerate((own, paired, far)):
                @pl.when((p < count) & (which == n))
                def _():
                    for g in range(local_kv):
                        for i in range(2):
                            out[g, p, i] = ref[i, page_rows, g * HD:(g + 1) * HD]


def attend_kernel(low_ctx, sub_count, step, waits, counts, pages_in, *refs):
    queries, outs = refs[:sub_count], refs[sub_count + waits:]
    head = lax.axis_index("head")
    tokens, width = queries[0].shape
    local_kv, most_pages = pages_in.shape[:2]
    span = width // local_kv
    per_group = span // HD
    piece_rows = per_group * tokens
    rows = sub_count * piece_rows
    first_token = (head ^ step) * sub_count * tokens

    def attend(pages):
        row = lax.broadcasted_iota(jnp.int32, (rows, PAGE), 0)
        token = first_token + row // piece_rows * tokens + lax.rem(row, tokens)
        column = lax.broadcasted_iota(jnp.int32, (rows, PAGE), 1)
        visible = column <= PAGE - QR + token

        def scores_of(g):
            q_blocks = [ref[:, g * span:(g + 1) * span] for ref in queries]
            q_rows = jnp.concatenate([q[:, j * HD:(j + 1) * HD] for q in q_blocks for j in range(per_group)], axis=0)
            for p in range(pages):
                scores = lax.dot_general(
                    q_rows, pages_in[g, p, 0], (((1,), (1,)), ((), ())), preferred_element_type=jnp.float32
                )
                yield jnp.where(visible, scores, NEG) if p == pages - 1 else scores

        scores = list(scores_of(0))
        for g in range(local_kv):
            following = scores_of(g + 1) if g + 1 < local_kv else iter(())
            later = []
            top = jnp.max(functools.reduce(jnp.maximum, scores), axis=1, keepdims=True)
            totals, product = None, None
            for p in range(pages):
                later += [s for _, s in zip(range(1), following)]
                numerators = jnp.exp2((scores[p] - top) * EXP2_SCALE)
                part = jnp.dot(
                    numerators.astype(jnp.bfloat16), pages_in[g, p, 1], preferred_element_type=jnp.float32
                )
                totals = numerators if p == 0 else totals + numerators
                product = part if p == 0 else product + part
            totals = jnp.sum(totals, axis=1, keepdims=True)
            done = (product / totals).astype(jnp.bfloat16)
            for i, out in enumerate(outs):
                start = i * piece_rows
                out[:, g * span:(g + 1) * span] = jnp.concatenate(
                    [done[start + j * tokens:start + (j + 1) * tokens] for j in range(per_group)], axis=1
                )
            scores = later

    @pl.when(lax.axis_index("ctx") >= low_ctx)
    def _():
        count = counts[own_pair_of(low_ctx, sub_count)]
        for pages in [*range(1, most_pages - REQS + 3), most_pages]:
            @pl.when(count == pages)
            def _():
                attend(pages)


def one_request_each(queries, kv_cache, page_counts):
    ctx_size, sub_size = lax.axis_size("ctx"), lax.axis_size("sub")
    head_count = lax.axis_size("head")
    low_ctx = ctx_size // 2
    most_pages = kv_cache.shape[1] // PAGE * ctx_size * sub_size // 4
    local_kv = kv_cache.shape[2] // HD
    tokens, width = queries.shape[0], queries.shape[1] // head_count
    anywhere = pl.BlockSpec(memory_space=pl.ANY)
    in_vmem = pl.BlockSpec(memory_space=pltpu.VMEM)
    q_piece = pltpu.VMEM((tokens, width), queries.dtype)

    def vmem(array):
        return pltpu.with_memory_space_constraint(array, pltpu.VMEM)

    def hbm(array):
        return pltpu.with_memory_space_constraint(array, pltpu.HBM)

    def moved(array, routes):
        def flat(place):
            return (place[0] * head_count + place[1]) * sub_size + place[2]

        return lax.ppermute(array, ("ctx", "head", "sub"), [(flat(a), flat(b)) for a, b in routes])

    def worker(request, head):
        return low_ctx + request // sub_size, head, request % sub_size

    heads = range(head_count)
    *q_out, = pl.pallas_call(
        split_kernel,
        out_shape=[q_piece] * head_count,
        in_specs=[anywhere],
        out_specs=[anywhere] * head_count,
        scratch_shapes=[pltpu.SemaphoreType.DMA((head_count,))],
        compiler_params=pltpu.CompilerParams(vmem_limit_bytes=2**20),
        name="split",
    )(hbm(queries))
    routes = {
        (step, s): [((r, h, s), worker(r, h ^ step)) for r in range(ctx_size) for h in heads]
        for step in heads[::-1] for s in range(sub_size)
    }
    q_in = {}
    for key, pairs in routes.items():
        q_in[key] = moved(q_out[key[0]], pairs)
        if len(q_in) == 1:
            *q_out[:-1], q_in[key] = lax.optimization_barrier((*q_out[:-1], q_in[key]))
    first = list(routes)[0]

    middle = [(low_ctx, sub_size - 1), (low_ctx + 1, 0)]
    far = moved(kv_cache, [((a[0], h, a[1]), (b[0], h, b[1])) for a, b in (middle, middle[::-1]) for h in heads])
    paired = moved(
        kv_cache, [((c, h, s), (c, h, 1 - s)) for c in range(low_ctx, ctx_size) for h in heads for s in range(sub_size)]
    )
    first_here = pl.pallas_call(
        lambda *refs: None,
        out_shape=pltpu.VMEM((8, HD), jnp.float32),
        in_specs=[anywhere] * 2,
        out_specs=anywhere,
        cost_estimate=pl.CostEstimate(flops=2 * 10**10, bytes_accessed=2**20, transcendentals=0),
        compiler_params=pltpu.CompilerParams(vmem_limit_bytes=2**20),
        name="first_here",
    )(vmem(q_in[first]), vmem(far))
    gathered = pl.pallas_call(
        functools.partial(gather_kernel, low_ctx, sub_size),
        out_shape=pltpu.VMEM((local_kv, most_pages, 2, PAGE, HD), kv_cache.dtype),
        in_specs=[pl.BlockSpec(memory_space=pltpu.SMEM)] + [in_vmem] * 3 + [anywhere],
        out_specs=in_vmem,
        compiler_params=pltpu.CompilerParams(vmem_limit_bytes=2**20),
        name="gather",
    )(page_counts, vmem(kv_cache), vmem(far), vmem(paired), vmem(first_here))

    back = {}
    after = []
    for step in heads[::-1]:
        subs = range(sub_size)
        outs = pl.pallas_call(
            functools.partial(attend_kernel, low_ctx, sub_size, step, len(after)),
            out_shape=[q_piece] * sub_size,
            in_specs=[pl.BlockSpec(memory_space=pltpu.SMEM)] + [in_vmem] * (1 + sub_size) + [anywhere] * len(after),
            out_specs=[in_vmem] * sub_size,
            compiler_params=pltpu.CompilerParams(vmem_limit_bytes=12 * 2**20),
            cost_estimate=pl.CostEstimate(flops=10**10, bytes_accessed=2**22, transcendentals=10**6),
            name=f"attend_{step}",
        )(page_counts, vmem(gathered), *[vmem(q_in[step, s]) for s in subs], *after)
        for s in subs:
            back[step, s] = moved(outs[s], [(b, a) for a, b in routes[step, s]])
        after = [outs[0]]

    joined = []
    for step in heads[::-1]:
        joined = [
            pl.pallas_call(
                functools.partial(join_kernel, step, sub_size),
                out_shape=pltpu.HBM(queries.shape, queries.dtype),
                in_specs=[anywhere] * (sub_size + len(joined)),
                out_specs=anywhere,
                scratch_shapes=[pltpu.SemaphoreType.DMA((1,))],
                input_output_aliases={sub_size: 0} if joined else {},
                compiler_params=pltpu.CompilerParams(vmem_limit_bytes=2**20),
                name=f"join_{step}",
            )(*[vmem(back[step, s]) for s in range(sub_size)], *map(hbm, joined))
        ]
    return joined[0]


def from_behind(array, axis, by):
    count = lax.axis_size(axis)
    pairs = [(i, i + by) for i in range(count) if 0 <= i + by < count]
    return lax.ppermute(array, axis, pairs)


def queries_to_pages(queries, kv_cache, page_counts):
    per_group = HQ // KVH
    local_heads = kv_cache.shape[2] // HD
    ctx_size = lax.axis_size("ctx")
    sub_size = lax.axis_size("sub")
    head_count = lax.axis_size("head")
    tok_rows = queries.shape[0]
    score_scale = HD ** (-0.5)
    regrouped = lax.all_to_all(queries, "head", split_axis=1, concat_axis=0, tiled=True)
    all_queries = lax.all_gather(regrouped, ("ctx", "sub"), axis=0, tiled=True)
    all_queries = all_queries.reshape(SPAN, local_heads, per_group, HD)
    page_ends = jnp.cumsum(page_counts)
    ctx_rows = SPAN // ctx_size
    offsets = jnp.arange(QR, dtype=jnp.int32)
    columns = jnp.arange(PAGE, dtype=jnp.int32)
    flat_index = lax.axis_index("ctx") * sub_size + lax.axis_index("sub")
    pages_here = kv_cache.shape[1] // PAGE
    base_pages = pages_here * ctx_size * sub_size // 2
    initial = (
        jnp.full((SPAN, local_heads, per_group), NEG, jnp.float32),
        jnp.zeros((SPAN, local_heads, per_group), jnp.float32),
        jnp.zeros((SPAN, local_heads, per_group, HD), jnp.float32),
    )
    half_rows = kv_cache.shape[1] // 2
    arrived = from_behind(kv_cache[:, half_rows:], "ctx", -(ctx_size // 2))
    is_lower = lax.axis_index("ctx") < ctx_size // 2
    source_flat = flat_index + ctx_size // 2 * sub_size
    working = jnp.where(is_lower, arrived, kv_cache[:, :half_rows])
    first_page = jnp.where(
        is_lower, source_flat * pages_here + pages_here // 2, flat_index * pages_here
    )
    page_total = working.shape[1] // PAGE

    def add_page(page_turn, running):
        page_index = first_page + page_turn
        relative = page_index - base_pages
        counted = jnp.sum((relative >= page_ends).astype(jnp.int32))
        request = jnp.where(relative < 0, REQS, counted)

        def update(partial_value):
            run_max, run_sum, run_out = partial_value
            request_id = jnp.minimum(request, REQS - 1)
            row_start = request_id * QR
            gathered = row_start + offsets
            within = gathered % ctx_rows
            ctx_block = gathered // ctx_rows
            sub_part = within // (head_count * tok_rows)
            head_part = within // tok_rows % head_count
            tok_part = within % tok_rows
            natural = ctx_block * ctx_rows + (head_part * sub_size + sub_part) * tok_rows + tok_part
            query_pos = (page_ends[request_id] + base_pages) * PAGE - QR + natural - row_start
            key_pos = page_index * PAGE + columns
            visible = key_pos[None, :] <= query_pos[:, None]
            page_keys = working[0].reshape(PAGE, local_heads, HD)
            page_values = working[1].reshape(PAGE, local_heads, HD)
            query_rows = lax.dynamic_slice_in_dim(all_queries, row_start, QR, 0)
            scores = (
                jnp.einsum(
                    "qkgd,pkd->qkgp", query_rows, page_keys, preferred_element_type=jnp.float32
                )
                * score_scale
            )
            scores = jnp.where(visible[:, None, None, :], scores, NEG)
            old_max = lax.dynamic_slice_in_dim(run_max, row_start, QR, 0)
            old_sum = lax.dynamic_slice_in_dim(run_sum, row_start, QR, 0)
            old_out = lax.dynamic_slice_in_dim(run_out, row_start, QR, 0)
            new_max = jnp.maximum(old_max, jnp.max(scores, axis=3))
            factor = jnp.exp(old_max - new_max)
            numerators = jnp.exp(scores - new_max[..., None])
            new_sum = old_sum * factor + jnp.sum(numerators, axis=3)
            product = jnp.einsum(
                "qkgp,pkd->qkgd",
                numerators.astype(jnp.bfloat16),
                page_values,
                preferred_element_type=jnp.float32,
            )
            new_out = old_out * factor[..., None] + product
            return (
                lax.dynamic_update_slice_in_dim(run_max, new_max, row_start, 0),
                lax.dynamic_update_slice_in_dim(run_sum, new_sum, row_start, 0),
                lax.dynamic_update_slice_in_dim(run_out, new_out, row_start, 0),
            )

        def unchanged(partial_value):
            return partial_value

        return lax.cond(request < REQS, update, unchanged, running)

    run_max, run_sum, run_out = lax.fori_loop(0, page_total, add_page, initial)
    share = SPAN // (ctx_size * sub_size)
    global_max = lax.pmax(run_max, ("ctx", "sub"))
    factor = jnp.exp(run_max - global_max)
    sums_here, outs_here = (
        lax.psum_scatter(
            (run_sum * factor).astype(jnp.bfloat16), ("ctx", "sub"), scatter_dimension=0, tiled=True
        ).astype(jnp.float32),
        lax.psum_scatter(
            (run_out * factor[..., None]).astype(jnp.bfloat16),
            ("ctx", "sub"),
            scatter_dimension=0,
            tiled=True,
        ).astype(jnp.float32),
    )
    finished = (outs_here / sums_here[..., None]).astype(jnp.bfloat16)
    finished = finished.reshape(share, local_heads * per_group * HD)
    return lax.all_to_all(finished, "head", split_axis=0, concat_axis=1, tiled=True)


def per_device(queries, kv_cache, page_counts):
    ctx_size, sub_size, head_count = lax.axis_size("ctx"), lax.axis_size("sub"), lax.axis_size("head")
    small = (
        ctx_size == REQS == 4
        and head_count == sub_size == 2
        and kv_cache.shape[1] == 2 * PAGE
        and kv_cache.shape[2] % (sub_size * HD) == 0
        and queries.shape[0] % 16 == 0
        and queries.shape[0] * head_count * sub_size == QR
    )
    return (one_request_each if small else queries_to_pages)(queries, kv_cache, page_counts)


def solution(mesh):
    return jax.shard_map(
        per_device,
        mesh=mesh,
        in_specs=(
            P(("grp", "ctx", "head", "sub"), None),
            P(None, ("grp", "ctx", "sub"), "head"),
            P("grp"),
        ),
        out_specs=P(("grp", "ctx", "head", "sub"), None),
        check_vma=False,
    )
```

```python
import functools

import jax
import jax.numpy as jnp
from jax import lax
from jax.experimental import pallas as pl
from jax.experimental.pallas import tpu as pltpu
from jax.sharding import PartitionSpec as P

HQ = 128
KVH = 8
HD = 128
REQS = 4
QR = 64
PAGE = 256
SPAN = 256


NEG = -1e30
EXP2_SCALE = HD ** (-0.5) * 1.4426950408889634


def run(copies):
    for copy in copies:
        copy.start()
    for copy in copies:
        copy.wait()


def head_part(step, width):
    return pl.ds(pl.multiple_of((lax.axis_index("head") ^ step) * width, width), width)


def split_kernel(queries, *refs):
    outs, sems = refs[:-1], refs[-1]
    run([
        pltpu.make_async_copy(queries.at[:, head_part(step, out.shape[1])], out, sems.at[step])
        for step, out in enumerate(outs)
    ])


def join_kernel(keys, *refs):
    out, sems = refs[-2:]
    for i, (step, source) in enumerate(keys):
        @pl.when(lax.axis_index("sub") == source)
        def _():
            run([pltpu.make_async_copy(refs[i], out.at[:, head_part(step, refs[i].shape[1])], sems.at[0])])


def own_pair_of(low_ctx, sub_count):
    return (lax.axis_index("ctx") - low_ctx) * sub_count + lax.axis_index("sub")


def gather_kernel(low_ctx, sub_count, counts, own, far, paired, after, out):
    local_kv, most_pages = out.shape[:2]
    own_pair = own_pair_of(low_ctx, sub_count)
    sub = lax.axis_index("sub")

    @pl.when(lax.axis_index("ctx") >= low_ctx)
    def _():
        start = jnp.int32(0)
        for r in range(REQS):
            start = start + jnp.where(r < own_pair, counts[r], 0)
        count = counts[own_pair]
        for p in range(most_pages):
            page = start + p
            apart = page // 2 - own_pair
            which = jnp.where(apart == 0, 0, jnp.where(apart == 1 - 2 * sub, 1, 2))
            page_rows = pl.ds(pl.multiple_of(lax.rem(page, 2) * PAGE, PAGE), PAGE)
            for n, ref in enumerate((own, paired, far)):
                @pl.when((p < count) & (which == n))
                def _():
                    for g in range(local_kv):
                        for i in range(2):
                            out[g, p, i] = ref[i, page_rows, g * HD:(g + 1) * HD]


def attend_kernel(low_ctx, sub_count, step, source_sub, waits, counts, pages_in, queries, *refs):
    out = refs[waits]
    head = lax.axis_index("head")
    tokens, width = queries.shape
    local_kv, most_pages = pages_in.shape[:2]
    span = width // local_kv
    per_group = span // HD
    rows = per_group * tokens
    first_token = ((head ^ step) * sub_count + source_sub) * tokens

    def attend(pages):
        token = lax.rem(lax.broadcasted_iota(jnp.int32, (rows, PAGE), 0), tokens)
        column = lax.broadcasted_iota(jnp.int32, (rows, PAGE), 1)
        visible = column <= PAGE - QR + first_token + token

        def scores_of(g):
            q_block = queries[:, g * span:(g + 1) * span]
            q_rows = jnp.concatenate([q_block[:, j * HD:(j + 1) * HD] for j in range(per_group)], axis=0)
            for p in range(pages):
                scores = lax.dot_general(
                    q_rows, pages_in[g, p, 0], (((1,), (1,)), ((), ())), preferred_element_type=jnp.float32
                )
                yield jnp.where(visible, scores, NEG) if p == pages - 1 else scores

        scores = list(scores_of(0))
        for g in range(local_kv):
            following = scores_of(g + 1) if g + 1 < local_kv else iter(())
            later = []
            top = jnp.max(functools.reduce(jnp.maximum, scores), axis=1, keepdims=True)
            totals, product = None, None
            for p in range(pages):
                later += [s for _, s in zip(range(1), following)]
                numerators = jnp.exp2((scores[p] - top) * EXP2_SCALE)
                part = jnp.dot(
                    numerators.astype(jnp.bfloat16), pages_in[g, p, 1], preferred_element_type=jnp.float32
                )
                totals = numerators if p == 0 else totals + numerators
                product = part if p == 0 else product + part
            totals = jnp.sum(totals, axis=1, keepdims=True)
            done = (product / totals).astype(jnp.bfloat16)
            out[:, g * span:(g + 1) * span] = jnp.concatenate(
                [done[j * tokens:(j + 1) * tokens] for j in range(per_group)], axis=1
            )
            scores = later

    @pl.when(lax.axis_index("ctx") >= low_ctx)
    def _():
        count = counts[own_pair_of(low_ctx, sub_count)]
        for pages in [*range(1, most_pages - REQS + 3), most_pages]:
            @pl.when(count == pages)
            def _():
                attend(pages)


def one_request_each(queries, kv_cache, page_counts):
    ctx_size, sub_size = lax.axis_size("ctx"), lax.axis_size("sub")
    head_count = lax.axis_size("head")
    low_ctx = ctx_size // 2
    most_pages = kv_cache.shape[1] // PAGE * ctx_size * sub_size // 4
    local_kv = kv_cache.shape[2] // HD
    tokens, width = queries.shape[0], queries.shape[1] // head_count
    anywhere = pl.BlockSpec(memory_space=pl.ANY)
    in_vmem = pl.BlockSpec(memory_space=pltpu.VMEM)
    q_piece = pltpu.VMEM((tokens, width), queries.dtype)

    def vmem(array):
        return pltpu.with_memory_space_constraint(array, pltpu.VMEM)

    def hbm(array):
        return pltpu.with_memory_space_constraint(array, pltpu.HBM)

    def moved(array, routes):
        def flat(place):
            return (place[0] * head_count + place[1]) * sub_size + place[2]

        return lax.ppermute(array, ("ctx", "head", "sub"), [(flat(a), flat(b)) for a, b in routes])

    def worker(request, head):
        return low_ctx + request // sub_size, head, request % sub_size

    heads = range(head_count)
    q_out = pl.pallas_call(
        split_kernel,
        out_shape=[q_piece] * head_count,
        in_specs=[anywhere],
        out_specs=[anywhere] * head_count,
        scratch_shapes=[pltpu.SemaphoreType.DMA((head_count,))],
        compiler_params=pltpu.CompilerParams(vmem_limit_bytes=2**20),
        name="split",
    )(hbm(queries))
    routes = {
        (step, s): [((r, h, s), worker(r, h ^ step)) for r in range(ctx_size) for h in heads]
        for step in heads[::-1] for s in range(sub_size)
    }
    q_in = {key: moved(q_out[key[0]], pairs) for key, pairs in routes.items()}
    first = list(routes)[0]

    middle = [(low_ctx, sub_size - 1), (low_ctx + 1, 0)]
    far = moved(kv_cache, [((a[0], h, a[1]), (b[0], h, b[1])) for a, b in (middle, middle[::-1]) for h in heads])
    paired = moved(
        kv_cache, [((c, h, s), (c, h, 1 - s)) for c in range(low_ctx, ctx_size) for h in heads for s in range(sub_size)]
    )
    first_here = pl.pallas_call(
        lambda *refs: None,
        out_shape=pltpu.VMEM((8, HD), jnp.float32),
        in_specs=[anywhere] * 2,
        out_specs=anywhere,
        cost_estimate=pl.CostEstimate(flops=2 * 10**10, bytes_accessed=2**20, transcendentals=0),
        compiler_params=pltpu.CompilerParams(vmem_limit_bytes=2**20),
        name="first_here",
    )(vmem(q_in[first]), vmem(far))
    gathered = pl.pallas_call(
        functools.partial(gather_kernel, low_ctx, sub_size),
        out_shape=pltpu.VMEM((local_kv, most_pages, 2, PAGE, HD), kv_cache.dtype),
        in_specs=[pl.BlockSpec(memory_space=pltpu.SMEM)] + [in_vmem] * 3 + [anywhere],
        out_specs=in_vmem,
        compiler_params=pltpu.CompilerParams(vmem_limit_bytes=2**20),
        name="gather",
    )(page_counts, vmem(kv_cache), vmem(far), vmem(paired), vmem(first_here))

    back = {}
    after = []
    for step, s in routes:
        out = pl.pallas_call(
            functools.partial(attend_kernel, low_ctx, sub_size, step, s, len(after)),
            out_shape=q_piece,
            in_specs=[pl.BlockSpec(memory_space=pltpu.SMEM)] + [in_vmem] * 2 + [anywhere] * len(after),
            out_specs=in_vmem,
            compiler_params=pltpu.CompilerParams(vmem_limit_bytes=12 * 2**20),
            cost_estimate=pl.CostEstimate(flops=6 * 10**9, bytes_accessed=2**22, transcendentals=10**6),
            name=f"attend_{step}{s}",
        )(page_counts, vmem(gathered), vmem(q_in[step, s]), *after)
        back[step, s] = moved(out, [(b, a) for a, b in routes[step, s]])
        after = [out]

    joined = []
    for keys in [[key for key in routes if key[0]]] + [[key] for key in routes if not key[0]]:
        joined = [
            pl.pallas_call(
                functools.partial(join_kernel, keys),
                out_shape=pltpu.HBM(queries.shape, queries.dtype),
                in_specs=[anywhere] * (len(keys) + len(joined)),
                out_specs=anywhere,
                scratch_shapes=[pltpu.SemaphoreType.DMA((1,))],
                input_output_aliases={len(keys): 0} if joined else {},
                compiler_params=pltpu.CompilerParams(vmem_limit_bytes=2**20),
                name="join",
            )(*[vmem(back[key]) for key in keys], *map(hbm, joined))
        ]
    return joined[0]


def from_behind(array, axis, by):
    count = lax.axis_size(axis)
    pairs = [(i, i + by) for i in range(count) if 0 <= i + by < count]
    return lax.ppermute(array, axis, pairs)


def queries_to_pages(queries, kv_cache, page_counts):
    per_group = HQ // KVH
    local_heads = kv_cache.shape[2] // HD
    ctx_size = lax.axis_size("ctx")
    sub_size = lax.axis_size("sub")
    head_count = lax.axis_size("head")
    tok_rows = queries.shape[0]
    score_scale = HD ** (-0.5)
    regrouped = lax.all_to_all(queries, "head", split_axis=1, concat_axis=0, tiled=True)
    all_queries = lax.all_gather(regrouped, ("ctx", "sub"), axis=0, tiled=True)
    all_queries = all_queries.reshape(SPAN, local_heads, per_group, HD)
    page_ends = jnp.cumsum(page_counts)
    ctx_rows = SPAN // ctx_size
    offsets = jnp.arange(QR, dtype=jnp.int32)
    columns = jnp.arange(PAGE, dtype=jnp.int32)
    flat_index = lax.axis_index("ctx") * sub_size + lax.axis_index("sub")
    pages_here = kv_cache.shape[1] // PAGE
    base_pages = pages_here * ctx_size * sub_size // 2
    initial = (
        jnp.full((SPAN, local_heads, per_group), NEG, jnp.float32),
        jnp.zeros((SPAN, local_heads, per_group), jnp.float32),
        jnp.zeros((SPAN, local_heads, per_group, HD), jnp.float32),
    )
    half_rows = kv_cache.shape[1] // 2
    arrived = from_behind(kv_cache[:, half_rows:], "ctx", -(ctx_size // 2))
    is_lower = lax.axis_index("ctx") < ctx_size // 2
    source_flat = flat_index + ctx_size // 2 * sub_size
    working = jnp.where(is_lower, arrived, kv_cache[:, :half_rows])
    first_page = jnp.where(
        is_lower, source_flat * pages_here + pages_here // 2, flat_index * pages_here
    )
    page_total = working.shape[1] // PAGE

    def add_page(page_turn, running):
        page_index = first_page + page_turn
        relative = page_index - base_pages
        counted = jnp.sum((relative >= page_ends).astype(jnp.int32))
        request = jnp.where(relative < 0, REQS, counted)

        def update(partial_value):
            run_max, run_sum, run_out = partial_value
            request_id = jnp.minimum(request, REQS - 1)
            row_start = request_id * QR
            gathered = row_start + offsets
            within = gathered % ctx_rows
            ctx_block = gathered // ctx_rows
            sub_part = within // (head_count * tok_rows)
            head_part = within // tok_rows % head_count
            tok_part = within % tok_rows
            natural = ctx_block * ctx_rows + (head_part * sub_size + sub_part) * tok_rows + tok_part
            query_pos = (page_ends[request_id] + base_pages) * PAGE - QR + natural - row_start
            key_pos = page_index * PAGE + columns
            visible = key_pos[None, :] <= query_pos[:, None]
            page_keys = working[0].reshape(PAGE, local_heads, HD)
            page_values = working[1].reshape(PAGE, local_heads, HD)
            query_rows = lax.dynamic_slice_in_dim(all_queries, row_start, QR, 0)
            scores = (
                jnp.einsum(
                    "qkgd,pkd->qkgp", query_rows, page_keys, preferred_element_type=jnp.float32
                )
                * score_scale
            )
            scores = jnp.where(visible[:, None, None, :], scores, NEG)
            old_max = lax.dynamic_slice_in_dim(run_max, row_start, QR, 0)
            old_sum = lax.dynamic_slice_in_dim(run_sum, row_start, QR, 0)
            old_out = lax.dynamic_slice_in_dim(run_out, row_start, QR, 0)
            new_max = jnp.maximum(old_max, jnp.max(scores, axis=3))
            factor = jnp.exp(old_max - new_max)
            numerators = jnp.exp(scores - new_max[..., None])
            new_sum = old_sum * factor + jnp.sum(numerators, axis=3)
            product = jnp.einsum(
                "qkgp,pkd->qkgd",
                numerators.astype(jnp.bfloat16),
                page_values,
                preferred_element_type=jnp.float32,
            )
            new_out = old_out * factor[..., None] + product
            return (
                lax.dynamic_update_slice_in_dim(run_max, new_max, row_start, 0),
                lax.dynamic_update_slice_in_dim(run_sum, new_sum, row_start, 0),
                lax.dynamic_update_slice_in_dim(run_out, new_out, row_start, 0),
            )

        def unchanged(partial_value):
            return partial_value

        return lax.cond(request < REQS, update, unchanged, running)

    run_max, run_sum, run_out = lax.fori_loop(0, page_total, add_page, initial)
    share = SPAN // (ctx_size * sub_size)
    global_max = lax.pmax(run_max, ("ctx", "sub"))
    factor = jnp.exp(run_max - global_max)
    sums_here, outs_here = (
        lax.psum_scatter(
            (run_sum * factor).astype(jnp.bfloat16), ("ctx", "sub"), scatter_dimension=0, tiled=True
        ).astype(jnp.float32),
        lax.psum_scatter(
            (run_out * factor[..., None]).astype(jnp.bfloat16),
            ("ctx", "sub"),
            scatter_dimension=0,
            tiled=True,
        ).astype(jnp.float32),
    )
    finished = (outs_here / sums_here[..., None]).astype(jnp.bfloat16)
    finished = finished.reshape(share, local_heads * per_group * HD)
    return lax.all_to_all(finished, "head", split_axis=0, concat_axis=1, tiled=True)


def per_device(queries, kv_cache, page_counts):
    ctx_size, sub_size, head_count = lax.axis_size("ctx"), lax.axis_size("sub"), lax.axis_size("head")
    small = (
        ctx_size == REQS == 4
        and head_count == sub_size == 2
        and kv_cache.shape[1] == 2 * PAGE
        and kv_cache.shape[2] % (sub_size * HD) == 0
        and queries.shape[0] % 16 == 0
        and queries.shape[0] * head_count * sub_size == QR
    )
    return (one_request_each if small else queries_to_pages)(queries, kv_cache, page_counts)


def solution(mesh):
    return jax.shard_map(
        per_device,
        mesh=mesh,
        in_specs=(
            P(("grp", "ctx", "head", "sub"), None),
            P(None, ("grp", "ctx", "sub"), "head"),
            P("grp"),
        ),
        out_specs=P(("grp", "ctx", "head", "sub"), None),
        check_vma=False,
    )
```

```python
import functools

import jax
import jax.numpy as jnp
from jax import lax
from jax.experimental import pallas as pl
from jax.experimental.pallas import tpu as pltpu
from jax.sharding import PartitionSpec as P

HQ = 128
KVH = 8
HD = 128
REQS = 4
QR = 64
PAGE = 256
SPAN = 256


NEG = -1e30
EXP2_SCALE = HD ** (-0.5) * 1.4426950408889634


def run(copies):
    for copy in copies:
        copy.start()
    for copy in copies:
        copy.wait()


def head_part(step, width):
    return pl.ds(pl.multiple_of((lax.axis_index("head") ^ step) * width, width), width)


def split_kernel(queries, *refs):
    outs, sems = refs[:-1], refs[-1]
    run([
        pltpu.make_async_copy(queries.at[:, head_part(step, out.shape[1])], out, sems.at[step])
        for step, out in enumerate(outs)
    ])


def join_kernel(keys, *refs):
    out, sems = refs[-2:]
    for i, (step, source) in enumerate(keys):
        @pl.when(lax.axis_index("sub") == source)
        def _():
            run([pltpu.make_async_copy(refs[i], out.at[:, head_part(step, refs[i].shape[1])], sems.at[0])])


def own_pair_of(low_ctx, sub_count):
    return (lax.axis_index("ctx") - low_ctx) * sub_count + lax.axis_index("sub")


def gather_kernel(low_ctx, sub_count, counts, own, far, paired, after, out):
    local_kv, most_pages = out.shape[:2]
    own_pair = own_pair_of(low_ctx, sub_count)
    sub = lax.axis_index("sub")

    @pl.when(lax.axis_index("ctx") >= low_ctx)
    def _():
        start = jnp.int32(0)
        for r in range(REQS):
            start = start + jnp.where(r < own_pair, counts[r], 0)
        count = counts[own_pair]
        for p in range(most_pages):
            page = start + p
            apart = page // 2 - own_pair
            which = jnp.where(apart == 0, 0, jnp.where(apart == 1 - 2 * sub, 1, 2))
            page_rows = pl.ds(pl.multiple_of(lax.rem(page, 2) * PAGE, PAGE), PAGE)
            for n, ref in enumerate((own, paired, far)):
                @pl.when((p < count) & (which == n))
                def _():
                    for g in range(local_kv):
                        for i in range(2):
                            out[g, p, i] = ref[i, page_rows, g * HD:(g + 1) * HD]


def attend_kernel(low_ctx, sub_count, step, source_sub, waits, counts, pages_in, queries, *refs):
    out = refs[waits]
    head = lax.axis_index("head")
    tokens, width = queries.shape
    local_kv, most_pages = pages_in.shape[:2]
    span = width // local_kv
    per_group = span // HD
    rows = per_group * tokens
    first_token = ((head ^ step) * sub_count + source_sub) * tokens

    def attend(pages):
        token = lax.rem(lax.broadcasted_iota(jnp.int32, (rows, PAGE), 0), tokens)
        column = lax.broadcasted_iota(jnp.int32, (rows, PAGE), 1)
        visible = column <= PAGE - QR + first_token + token

        def scores_of(g):
            q_block = queries[:, g * span:(g + 1) * span]
            q_rows = jnp.concatenate([q_block[:, j * HD:(j + 1) * HD] for j in range(per_group)], axis=0)
            for p in range(pages):
                scores = lax.dot_general(
                    q_rows, pages_in[g, p, 0], (((1,), (1,)), ((), ())), preferred_element_type=jnp.float32
                )
                yield jnp.where(visible, scores, NEG) if p == pages - 1 else scores

        scores = list(scores_of(0))
        for g in range(local_kv):
            following = scores_of(g + 1) if g + 1 < local_kv else iter(())
            later = []
            top = jnp.max(functools.reduce(jnp.maximum, scores), axis=1, keepdims=True)
            totals, product = None, None
            for p in range(pages):
                later += [s for _, s in zip(range(1), following)]
                numerators = jnp.exp2((scores[p] - top) * EXP2_SCALE)
                part = jnp.dot(
                    numerators.astype(jnp.bfloat16), pages_in[g, p, 1], preferred_element_type=jnp.float32
                )
                totals = numerators if p == 0 else totals + numerators
                product = part if p == 0 else product + part
            totals = jnp.sum(totals, axis=1, keepdims=True)
            done = (product / totals).astype(jnp.bfloat16)
            out[:, g * span:(g + 1) * span] = jnp.concatenate(
                [done[j * tokens:(j + 1) * tokens] for j in range(per_group)], axis=1
            )
            scores = later

    @pl.when(lax.axis_index("ctx") >= low_ctx)
    def _():
        count = counts[own_pair_of(low_ctx, sub_count)]
        for pages in [*range(1, most_pages - REQS + 3), most_pages]:
            @pl.when(count == pages)
            def _():
                attend(pages)


def one_request_each(queries, kv_cache, page_counts):
    ctx_size, sub_size = lax.axis_size("ctx"), lax.axis_size("sub")
    head_count = lax.axis_size("head")
    low_ctx = ctx_size // 2
    most_pages = kv_cache.shape[1] // PAGE * ctx_size * sub_size // 4
    local_kv = kv_cache.shape[2] // HD
    tokens, width = queries.shape[0], queries.shape[1] // head_count
    anywhere = pl.BlockSpec(memory_space=pl.ANY)
    in_vmem = pl.BlockSpec(memory_space=pltpu.VMEM)
    q_piece = pltpu.VMEM((tokens, width), queries.dtype)

    def vmem(array):
        return pltpu.with_memory_space_constraint(array, pltpu.VMEM)

    def hbm(array):
        return pltpu.with_memory_space_constraint(array, pltpu.HBM)

    def moved(array, routes):
        def flat(place):
            return (place[0] * head_count + place[1]) * sub_size + place[2]

        return lax.ppermute(array, ("ctx", "head", "sub"), [(flat(a), flat(b)) for a, b in routes])

    def worker(request, head):
        return low_ctx + request // sub_size, head, request % sub_size

    heads = range(head_count)
    q_out = pl.pallas_call(
        split_kernel,
        out_shape=[q_piece] * head_count,
        in_specs=[anywhere],
        out_specs=[anywhere] * head_count,
        scratch_shapes=[pltpu.SemaphoreType.DMA((head_count,))],
        compiler_params=pltpu.CompilerParams(vmem_limit_bytes=2**20),
        name="split",
    )(hbm(queries))
    routes = {
        (step, s): [((r, h, s), worker(r, h ^ step)) for r in range(ctx_size) for h in heads]
        for step in heads[::-1] for s in range(sub_size)
    }
    q_in = {key: moved(q_out[key[0]], pairs) for key, pairs in routes.items()}
    first = list(routes)[0]

    middle = [(low_ctx, sub_size - 1), (low_ctx + 1, 0)]
    far = moved(kv_cache, [((a[0], h, a[1]), (b[0], h, b[1])) for a, b in (middle, middle[::-1]) for h in heads])
    paired = moved(
        kv_cache, [((c, h, s), (c, h, 1 - s)) for c in range(low_ctx, ctx_size) for h in heads for s in range(sub_size)]
    )
    first_here = pl.pallas_call(
        lambda *refs: None,
        out_shape=pltpu.VMEM((8, HD), jnp.float32),
        in_specs=[anywhere],
        out_specs=anywhere,
        cost_estimate=pl.CostEstimate(flops=2 * 10**10, bytes_accessed=2**20, transcendentals=0),
        compiler_params=pltpu.CompilerParams(vmem_limit_bytes=2**20),
        name="first_here",
    )(vmem(q_in[first]))
    gathered = pl.pallas_call(
        functools.partial(gather_kernel, low_ctx, sub_size),
        out_shape=pltpu.VMEM((local_kv, most_pages, 2, PAGE, HD), kv_cache.dtype),
        in_specs=[pl.BlockSpec(memory_space=pltpu.SMEM)] + [in_vmem] * 3 + [anywhere],
        out_specs=in_vmem,
        compiler_params=pltpu.CompilerParams(vmem_limit_bytes=2**20),
        name="gather",
    )(page_counts, vmem(kv_cache), vmem(far), vmem(paired), vmem(first_here))

    back = {}
    after = []
    for step, s in routes:
        out = pl.pallas_call(
            functools.partial(attend_kernel, low_ctx, sub_size, step, s, len(after)),
            out_shape=q_piece,
            in_specs=[pl.BlockSpec(memory_space=pltpu.SMEM)] + [in_vmem] * 2 + [anywhere] * len(after),
            out_specs=in_vmem,
            compiler_params=pltpu.CompilerParams(vmem_limit_bytes=12 * 2**20),
            cost_estimate=pl.CostEstimate(flops=6 * 10**9, bytes_accessed=2**22, transcendentals=10**6),
            name=f"attend_{step}{s}",
        )(page_counts, vmem(gathered), vmem(q_in[step, s]), *after)
        back[step, s] = moved(out, [(b, a) for a, b in routes[step, s]])
        after = [out]

    joined = []
    for keys in [[key for key in routes if key[0]]] + [[key] for key in routes if not key[0]]:
        joined = [
            pl.pallas_call(
                functools.partial(join_kernel, keys),
                out_shape=pltpu.HBM(queries.shape, queries.dtype),
                in_specs=[anywhere] * (len(keys) + len(joined)),
                out_specs=anywhere,
                scratch_shapes=[pltpu.SemaphoreType.DMA((1,))],
                input_output_aliases={len(keys): 0} if joined else {},
                compiler_params=pltpu.CompilerParams(vmem_limit_bytes=2**20),
                name="join",
            )(*[vmem(back[key]) for key in keys], *map(hbm, joined))
        ]
    return joined[0]


def from_behind(array, axis, by):
    count = lax.axis_size(axis)
    pairs = [(i, i + by) for i in range(count) if 0 <= i + by < count]
    return lax.ppermute(array, axis, pairs)


def queries_to_pages(queries, kv_cache, page_counts):
    per_group = HQ // KVH
    local_heads = kv_cache.shape[2] // HD
    ctx_size = lax.axis_size("ctx")
    sub_size = lax.axis_size("sub")
    head_count = lax.axis_size("head")
    tok_rows = queries.shape[0]
    score_scale = HD ** (-0.5)
    regrouped = lax.all_to_all(queries, "head", split_axis=1, concat_axis=0, tiled=True)
    all_queries = lax.all_gather(regrouped, ("ctx", "sub"), axis=0, tiled=True)
    all_queries = all_queries.reshape(SPAN, local_heads, per_group, HD)
    page_ends = jnp.cumsum(page_counts)
    ctx_rows = SPAN // ctx_size
    offsets = jnp.arange(QR, dtype=jnp.int32)
    columns = jnp.arange(PAGE, dtype=jnp.int32)
    flat_index = lax.axis_index("ctx") * sub_size + lax.axis_index("sub")
    pages_here = kv_cache.shape[1] // PAGE
    base_pages = pages_here * ctx_size * sub_size // 2
    initial = (
        jnp.full((SPAN, local_heads, per_group), NEG, jnp.float32),
        jnp.zeros((SPAN, local_heads, per_group), jnp.float32),
        jnp.zeros((SPAN, local_heads, per_group, HD), jnp.float32),
    )
    half_rows = kv_cache.shape[1] // 2
    arrived = from_behind(kv_cache[:, half_rows:], "ctx", -(ctx_size // 2))
    is_lower = lax.axis_index("ctx") < ctx_size // 2
    source_flat = flat_index + ctx_size // 2 * sub_size
    working = jnp.where(is_lower, arrived, kv_cache[:, :half_rows])
    first_page = jnp.where(
        is_lower, source_flat * pages_here + pages_here // 2, flat_index * pages_here
    )
    page_total = working.shape[1] // PAGE

    def add_page(page_turn, running):
        page_index = first_page + page_turn
        relative = page_index - base_pages
        counted = jnp.sum((relative >= page_ends).astype(jnp.int32))
        request = jnp.where(relative < 0, REQS, counted)

        def update(partial_value):
            run_max, run_sum, run_out = partial_value
            request_id = jnp.minimum(request, REQS - 1)
            row_start = request_id * QR
            gathered = row_start + offsets
            within = gathered % ctx_rows
            ctx_block = gathered // ctx_rows
            sub_part = within // (head_count * tok_rows)
            head_part = within // tok_rows % head_count
            tok_part = within % tok_rows
            natural = ctx_block * ctx_rows + (head_part * sub_size + sub_part) * tok_rows + tok_part
            query_pos = (page_ends[request_id] + base_pages) * PAGE - QR + natural - row_start
            key_pos = page_index * PAGE + columns
            visible = key_pos[None, :] <= query_pos[:, None]
            page_keys = working[0].reshape(PAGE, local_heads, HD)
            page_values = working[1].reshape(PAGE, local_heads, HD)
            query_rows = lax.dynamic_slice_in_dim(all_queries, row_start, QR, 0)
            scores = (
                jnp.einsum(
                    "qkgd,pkd->qkgp", query_rows, page_keys, preferred_element_type=jnp.float32
                )
                * score_scale
            )
            scores = jnp.where(visible[:, None, None, :], scores, NEG)
            old_max = lax.dynamic_slice_in_dim(run_max, row_start, QR, 0)
            old_sum = lax.dynamic_slice_in_dim(run_sum, row_start, QR, 0)
            old_out = lax.dynamic_slice_in_dim(run_out, row_start, QR, 0)
            new_max = jnp.maximum(old_max, jnp.max(scores, axis=3))
            factor = jnp.exp(old_max - new_max)
            numerators = jnp.exp(scores - new_max[..., None])
            new_sum = old_sum * factor + jnp.sum(numerators, axis=3)
            product = jnp.einsum(
                "qkgp,pkd->qkgd",
                numerators.astype(jnp.bfloat16),
                page_values,
                preferred_element_type=jnp.float32,
            )
            new_out = old_out * factor[..., None] + product
            return (
                lax.dynamic_update_slice_in_dim(run_max, new_max, row_start, 0),
                lax.dynamic_update_slice_in_dim(run_sum, new_sum, row_start, 0),
                lax.dynamic_update_slice_in_dim(run_out, new_out, row_start, 0),
            )

        def unchanged(partial_value):
            return partial_value

        return lax.cond(request < REQS, update, unchanged, running)

    run_max, run_sum, run_out = lax.fori_loop(0, page_total, add_page, initial)
    share = SPAN // (ctx_size * sub_size)
    global_max = lax.pmax(run_max, ("ctx", "sub"))
    factor = jnp.exp(run_max - global_max)
    sums_here, outs_here = (
        lax.psum_scatter(
            (run_sum * factor).astype(jnp.bfloat16), ("ctx", "sub"), scatter_dimension=0, tiled=True
        ).astype(jnp.float32),
        lax.psum_scatter(
            (run_out * factor[..., None]).astype(jnp.bfloat16),
            ("ctx", "sub"),
            scatter_dimension=0,
            tiled=True,
        ).astype(jnp.float32),
    )
    finished = (outs_here / sums_here[..., None]).astype(jnp.bfloat16)
    finished = finished.reshape(share, local_heads * per_group * HD)
    return lax.all_to_all(finished, "head", split_axis=0, concat_axis=1, tiled=True)


def per_device(queries, kv_cache, page_counts):
    ctx_size, sub_size, head_count = lax.axis_size("ctx"), lax.axis_size("sub"), lax.axis_size("head")
    small = (
        ctx_size == REQS == 4
        and head_count == sub_size == 2
        and kv_cache.shape[1] == 2 * PAGE
        and kv_cache.shape[2] % (sub_size * HD) == 0
        and queries.shape[0] % 16 == 0
        and queries.shape[0] * head_count * sub_size == QR
    )
    return (one_request_each if small else queries_to_pages)(queries, kv_cache, page_counts)


def solution(mesh):
    return jax.shard_map(
        per_device,
        mesh=mesh,
        in_specs=(
            P(("grp", "ctx", "head", "sub"), None),
            P(None, ("grp", "ctx", "sub"), "head"),
            P("grp"),
        ),
        out_specs=P(("grp", "ctx", "head", "sub"), None),
        check_vma=False,
    )
```

```python
import functools

import jax
import jax.numpy as jnp
from jax import lax
from jax.experimental import pallas as pl
from jax.experimental.pallas import tpu as pltpu
from jax.sharding import PartitionSpec as P

HQ = 128
KVH = 8
HD = 128
REQS = 4
QR = 64
PAGE = 256
SPAN = 256


NEG = -1e30
EXP2_SCALE = HD ** (-0.5) * 1.4426950408889634


def run(copies):
    for copy in copies:
        copy.start()
    for copy in copies:
        copy.wait()


def head_part(step, width):
    return pl.ds(pl.multiple_of((lax.axis_index("head") ^ step) * width, width), width)


def split_kernel(queries, *refs):
    outs, sems = refs[:-1], refs[-1]
    run([
        pltpu.make_async_copy(queries.at[:, head_part(step, out.shape[1])], out, sems.at[step])
        for step, out in enumerate(outs)
    ])


def join_kernel(low_ctx, turns, *refs):
    out, sems = refs[-2:]
    is_lower = lax.axis_index("ctx") < low_ctx
    for piece, keys in zip(refs, turns):
        for key, here in zip(keys, (is_lower, jnp.logical_not(is_lower))):
            if key is not None:
                @pl.when(here & (lax.axis_index("sub") == key[1]))
                def _():
                    run([pltpu.make_async_copy(piece, out.at[:, head_part(key[0], piece.shape[1])], sems.at[0])])


def own_pair_of(low_ctx, sub_count):
    return (lax.axis_index("ctx") - low_ctx) * sub_count + lax.axis_index("sub")


def gather_kernel(low_ctx, sub_count, counts, own, far, paired, after, out):
    local_kv, most_pages = out.shape[:2]
    own_pair = own_pair_of(low_ctx, sub_count)
    sub = lax.axis_index("sub")

    @pl.when(lax.axis_index("ctx") >= low_ctx)
    def _():
        start = jnp.int32(0)
        for r in range(REQS):
            start = start + jnp.where(r < own_pair, counts[r], 0)
        count = counts[own_pair]
        for p in range(most_pages):
            page = start + p
            apart = page // 2 - own_pair
            which = jnp.where(apart == 0, 0, jnp.where(apart == 1 - 2 * sub, 1, 2))
            page_rows = pl.ds(pl.multiple_of(lax.rem(page, 2) * PAGE, PAGE), PAGE)
            for n, ref in enumerate((own, paired, far)):
                @pl.when((p < count) & (which == n))
                def _():
                    for g in range(local_kv):
                        for i in range(2):
                            out[g, p, i] = ref[i, page_rows, g * HD:(g + 1) * HD]


def attend_kernel(low_ctx, sub_count, turn, waits, counts, pages_in, queries, *refs):
    out = refs[waits]
    head = lax.axis_index("head")
    tokens, width = queries.shape
    local_kv, most_pages = pages_in.shape[:2]
    span = width // local_kv
    per_group = span // HD
    rows = per_group * tokens
    request = own_pair_of(low_ctx, sub_count)

    def token_of(key):
        return ((head ^ key[0]) * sub_count + key[1]) * tokens

    lower, upper = turn
    if lower is None or upper is None:
        first_token = token_of(lower or upper)
    else:
        first_token = jnp.where(request < low_ctx, token_of(lower), token_of(upper))
    works = (lax.axis_index("ctx") >= low_ctx)
    if lower is None:
        works = works & (request >= low_ctx)
    if upper is None:
        works = works & (request < low_ctx)

    def attend(pages):
        token = lax.rem(lax.broadcasted_iota(jnp.int32, (rows, PAGE), 0), tokens)
        column = lax.broadcasted_iota(jnp.int32, (rows, PAGE), 1)
        visible = column <= PAGE - QR + first_token + token

        def scores_of(g):
            q_block = queries[:, g * span:(g + 1) * span]
            q_rows = jnp.concatenate([q_block[:, j * HD:(j + 1) * HD] for j in range(per_group)], axis=0)
            for p in range(pages):
                scores = lax.dot_general(
                    q_rows, pages_in[g, p, 0], (((1,), (1,)), ((), ())), preferred_element_type=jnp.float32
                )
                yield jnp.where(visible, scores, NEG) if p == pages - 1 else scores

        scores = list(scores_of(0))
        for g in range(local_kv):
            following = scores_of(g + 1) if g + 1 < local_kv else iter(())
            later = []
            top = jnp.max(functools.reduce(jnp.maximum, scores), axis=1, keepdims=True)
            totals, product = None, None
            for p in range(pages):
                later += [s for _, s in zip(range(1), following)]
                numerators = jnp.exp2((scores[p] - top) * EXP2_SCALE)
                part = jnp.dot(
                    numerators.astype(jnp.bfloat16), pages_in[g, p, 1], preferred_element_type=jnp.float32
                )
                totals = numerators if p == 0 else totals + numerators
                product = part if p == 0 else product + part
            totals = jnp.sum(totals, axis=1, keepdims=True)
            done = (product / totals).astype(jnp.bfloat16)
            out[:, g * span:(g + 1) * span] = jnp.concatenate(
                [done[j * tokens:(j + 1) * tokens] for j in range(per_group)], axis=1
            )
            scores = later

    @pl.when(works)
    def _():
        count = counts[request]
        for pages in [*range(1, most_pages - REQS + 3), most_pages]:
            @pl.when(count == pages)
            def _():
                attend(pages)


def one_request_each(queries, kv_cache, page_counts):
    ctx_size, sub_size = lax.axis_size("ctx"), lax.axis_size("sub")
    head_count = lax.axis_size("head")
    low_ctx = ctx_size // 2
    most_pages = kv_cache.shape[1] // PAGE * ctx_size * sub_size // 4
    local_kv = kv_cache.shape[2] // HD
    tokens, width = queries.shape[0], queries.shape[1] // head_count
    anywhere = pl.BlockSpec(memory_space=pl.ANY)
    in_vmem = pl.BlockSpec(memory_space=pltpu.VMEM)
    q_piece = pltpu.VMEM((tokens, width), queries.dtype)

    def vmem(array):
        return pltpu.with_memory_space_constraint(array, pltpu.VMEM)

    def hbm(array):
        return pltpu.with_memory_space_constraint(array, pltpu.HBM)

    def moved(array, routes):
        def flat(place):
            return (place[0] * head_count + place[1]) * sub_size + place[2]

        return lax.ppermute(array, ("ctx", "head", "sub"), [(flat(a), flat(b)) for a, b in routes])

    def worker(request, head):
        return low_ctx + request // sub_size, head, request % sub_size

    heads = range(head_count)
    q_out = pl.pallas_call(
        split_kernel,
        out_shape=[q_piece] * head_count,
        in_specs=[anywhere],
        out_specs=[anywhere] * head_count,
        scratch_shapes=[pltpu.SemaphoreType.DMA((head_count,))],
        compiler_params=pltpu.CompilerParams(vmem_limit_bytes=2**20),
        name="split",
    )(hbm(queries))
    lower = [(step, s) for step in heads[::-1] for s in range(sub_size)]
    upper = [lower[0]] + lower[2:] + [lower[1]]
    turns = list(zip(lower + [None], [None] + upper))

    def routes_of(turn):
        return [
            ((r, h, key[1]), worker(r, h ^ key[0]))
            for key, requests in zip(turn, (range(low_ctx), range(low_ctx, ctx_size))) if key is not None
            for r in requests for h in heads
        ]

    q_in = [moved(q_out[(turn[0] or turn[1])[0]], routes_of(turn)) for turn in turns]

    middle = [(low_ctx, sub_size - 1), (low_ctx + 1, 0)]
    far = moved(kv_cache, [((a[0], h, a[1]), (b[0], h, b[1])) for a, b in (middle, middle[::-1]) for h in heads])
    paired = moved(
        kv_cache, [((c, h, s), (c, h, 1 - s)) for c in range(low_ctx, ctx_size) for h in heads for s in range(sub_size)]
    )
    first_here = pl.pallas_call(
        lambda *refs: None,
        out_shape=pltpu.VMEM((8, HD), jnp.float32),
        in_specs=[anywhere] * 2,
        out_specs=anywhere,
        cost_estimate=pl.CostEstimate(flops=2 * 10**10, bytes_accessed=2**20, transcendentals=0),
        compiler_params=pltpu.CompilerParams(vmem_limit_bytes=2**20),
        name="first_here",
    )(vmem(q_in[0]), vmem(far))
    gathered = pl.pallas_call(
        functools.partial(gather_kernel, low_ctx, sub_size),
        out_shape=pltpu.VMEM((local_kv, most_pages, 2, PAGE, HD), kv_cache.dtype),
        in_specs=[pl.BlockSpec(memory_space=pltpu.SMEM)] + [in_vmem] * 3 + [anywhere],
        out_specs=in_vmem,
        compiler_params=pltpu.CompilerParams(vmem_limit_bytes=2**20),
        name="gather",
    )(page_counts, vmem(kv_cache), vmem(far), vmem(paired), vmem(first_here))

    back = []
    after = []
    for turn, arrived in zip(turns, q_in):
        out = pl.pallas_call(
            functools.partial(attend_kernel, low_ctx, sub_size, turn, len(after)),
            out_shape=q_piece,
            in_specs=[pl.BlockSpec(memory_space=pltpu.SMEM)] + [in_vmem] * 2 + [anywhere] * len(after),
            out_specs=in_vmem,
            compiler_params=pltpu.CompilerParams(vmem_limit_bytes=12 * 2**20),
            cost_estimate=pl.CostEstimate(flops=6 * 10**9, bytes_accessed=2**22, transcendentals=10**6),
            name=f"attend_{len(back)}",
        )(page_counts, vmem(gathered), vmem(arrived), *after)
        back.append(moved(out, [(b, a) for a, b in routes_of(turn)]))
        after = [out]

    joined = []
    for chosen in [range(len(turns) - 2)] + [[i] for i in range(len(turns) - 2, len(turns))]:
        joined = [
            pl.pallas_call(
                functools.partial(join_kernel, low_ctx, [turns[i] for i in chosen]),
                out_shape=pltpu.HBM(queries.shape, queries.dtype),
                in_specs=[anywhere] * (len(chosen) + len(joined)),
                out_specs=anywhere,
                scratch_shapes=[pltpu.SemaphoreType.DMA((1,))],
                input_output_aliases={len(chosen): 0} if joined else {},
                compiler_params=pltpu.CompilerParams(vmem_limit_bytes=2**20),
                name="join",
            )(*[vmem(back[i]) for i in chosen], *map(hbm, joined))
        ]
    return joined[0]


def from_behind(array, axis, by):
    count = lax.axis_size(axis)
    pairs = [(i, i + by) for i in range(count) if 0 <= i + by < count]
    return lax.ppermute(array, axis, pairs)


def queries_to_pages(queries, kv_cache, page_counts):
    per_group = HQ // KVH
    local_heads = kv_cache.shape[2] // HD
    ctx_size = lax.axis_size("ctx")
    sub_size = lax.axis_size("sub")
    head_count = lax.axis_size("head")
    tok_rows = queries.shape[0]
    score_scale = HD ** (-0.5)
    regrouped = lax.all_to_all(queries, "head", split_axis=1, concat_axis=0, tiled=True)
    all_queries = lax.all_gather(regrouped, ("ctx", "sub"), axis=0, tiled=True)
    all_queries = all_queries.reshape(SPAN, local_heads, per_group, HD)
    page_ends = jnp.cumsum(page_counts)
    ctx_rows = SPAN // ctx_size
    offsets = jnp.arange(QR, dtype=jnp.int32)
    columns = jnp.arange(PAGE, dtype=jnp.int32)
    flat_index = lax.axis_index("ctx") * sub_size + lax.axis_index("sub")
    pages_here = kv_cache.shape[1] // PAGE
    base_pages = pages_here * ctx_size * sub_size // 2
    initial = (
        jnp.full((SPAN, local_heads, per_group), NEG, jnp.float32),
        jnp.zeros((SPAN, local_heads, per_group), jnp.float32),
        jnp.zeros((SPAN, local_heads, per_group, HD), jnp.float32),
    )
    half_rows = kv_cache.shape[1] // 2
    arrived = from_behind(kv_cache[:, half_rows:], "ctx", -(ctx_size // 2))
    is_lower = lax.axis_index("ctx") < ctx_size // 2
    source_flat = flat_index + ctx_size // 2 * sub_size
    working = jnp.where(is_lower, arrived, kv_cache[:, :half_rows])
    first_page = jnp.where(
        is_lower, source_flat * pages_here + pages_here // 2, flat_index * pages_here
    )
    page_total = working.shape[1] // PAGE

    def add_page(page_turn, running):
        page_index = first_page + page_turn
        relative = page_index - base_pages
        counted = jnp.sum((relative >= page_ends).astype(jnp.int32))
        request = jnp.where(relative < 0, REQS, counted)

        def update(partial_value):
            run_max, run_sum, run_out = partial_value
            request_id = jnp.minimum(request, REQS - 1)
            row_start = request_id * QR
            gathered = row_start + offsets
            within = gathered % ctx_rows
            ctx_block = gathered // ctx_rows
            sub_part = within // (head_count * tok_rows)
            head_part = within // tok_rows % head_count
            tok_part = within % tok_rows
            natural = ctx_block * ctx_rows + (head_part * sub_size + sub_part) * tok_rows + tok_part
            query_pos = (page_ends[request_id] + base_pages) * PAGE - QR + natural - row_start
            key_pos = page_index * PAGE + columns
            visible = key_pos[None, :] <= query_pos[:, None]
            page_keys = working[0].reshape(PAGE, local_heads, HD)
            page_values = working[1].reshape(PAGE, local_heads, HD)
            query_rows = lax.dynamic_slice_in_dim(all_queries, row_start, QR, 0)
            scores = (
                jnp.einsum(
                    "qkgd,pkd->qkgp", query_rows, page_keys, preferred_element_type=jnp.float32
                )
                * score_scale
            )
            scores = jnp.where(visible[:, None, None, :], scores, NEG)
            old_max = lax.dynamic_slice_in_dim(run_max, row_start, QR, 0)
            old_sum = lax.dynamic_slice_in_dim(run_sum, row_start, QR, 0)
            old_out = lax.dynamic_slice_in_dim(run_out, row_start, QR, 0)
            new_max = jnp.maximum(old_max, jnp.max(scores, axis=3))
            factor = jnp.exp(old_max - new_max)
            numerators = jnp.exp(scores - new_max[..., None])
            new_sum = old_sum * factor + jnp.sum(numerators, axis=3)
            product = jnp.einsum(
                "qkgp,pkd->qkgd",
                numerators.astype(jnp.bfloat16),
                page_values,
                preferred_element_type=jnp.float32,
            )
            new_out = old_out * factor[..., None] + product
            return (
                lax.dynamic_update_slice_in_dim(run_max, new_max, row_start, 0),
                lax.dynamic_update_slice_in_dim(run_sum, new_sum, row_start, 0),
                lax.dynamic_update_slice_in_dim(run_out, new_out, row_start, 0),
            )

        def unchanged(partial_value):
            return partial_value

        return lax.cond(request < REQS, update, unchanged, running)

    run_max, run_sum, run_out = lax.fori_loop(0, page_total, add_page, initial)
    share = SPAN // (ctx_size * sub_size)
    global_max = lax.pmax(run_max, ("ctx", "sub"))
    factor = jnp.exp(run_max - global_max)
    sums_here, outs_here = (
        lax.psum_scatter(
            (run_sum * factor).astype(jnp.bfloat16), ("ctx", "sub"), scatter_dimension=0, tiled=True
        ).astype(jnp.float32),
        lax.psum_scatter(
            (run_out * factor[..., None]).astype(jnp.bfloat16),
            ("ctx", "sub"),
            scatter_dimension=0,
            tiled=True,
        ).astype(jnp.float32),
    )
    finished = (outs_here / sums_here[..., None]).astype(jnp.bfloat16)
    finished = finished.reshape(share, local_heads * per_group * HD)
    return lax.all_to_all(finished, "head", split_axis=0, concat_axis=1, tiled=True)


def per_device(queries, kv_cache, page_counts):
    ctx_size, sub_size, head_count = lax.axis_size("ctx"), lax.axis_size("sub"), lax.axis_size("head")
    small = (
        ctx_size == REQS == 4
        and head_count == sub_size == 2
        and kv_cache.shape[1] == 2 * PAGE
        and kv_cache.shape[2] % (sub_size * HD) == 0
        and queries.shape[0] % 16 == 0
        and queries.shape[0] * head_count * sub_size == QR
    )
    return (one_request_each if small else queries_to_pages)(queries, kv_cache, page_counts)


def solution(mesh):
    return jax.shard_map(
        per_device,
        mesh=mesh,
        in_specs=(
            P(("grp", "ctx", "head", "sub"), None),
            P(None, ("grp", "ctx", "sub"), "head"),
            P("grp"),
        ),
        out_specs=P(("grp", "ctx", "head", "sub"), None),
        check_vma=False,
    )
```

```python
import functools

import jax
import jax.numpy as jnp
from jax import lax
from jax.experimental import pallas as pl
from jax.experimental.pallas import tpu as pltpu
from jax.sharding import PartitionSpec as P

HQ = 128
KVH = 8
HD = 128
REQS = 4
QR = 64
PAGE = 256
SPAN = 256


NEG = -1e30
EXP2_SCALE = HD ** (-0.5) * 1.4426950408889634


def run(copies):
    for copy in copies:
        copy.start()
    for copy in copies:
        copy.wait()


def head_part(step, width):
    return pl.ds(pl.multiple_of((lax.axis_index("head") ^ step) * width, width), width)


def split_kernel(queries, *refs):
    outs, sems = refs[:-1], refs[-1]
    run([
        pltpu.make_async_copy(queries.at[:, head_part(step, out.shape[1])], out, sems.at[step])
        for step, out in enumerate(outs)
    ])


def join_kernel(late_count, turns, *refs):
    out, sems = refs[-2:]
    is_late = lax.axis_index("ctx") < late_count
    for piece, keys in zip(refs, turns):
        for key, here in zip(keys, (jnp.logical_not(is_late), is_late)):
            if key is not None:
                @pl.when(here & (lax.axis_index("sub") == key[1]))
                def _():
                    run([pltpu.make_async_copy(piece, out.at[:, head_part(key[0], piece.shape[1])], sems.at[0])])


def own_pair_of(low_ctx, sub_count):
    return (lax.axis_index("ctx") - low_ctx) * sub_count + lax.axis_index("sub")


def gather_kernel(low_ctx, sub_count, counts, own, far, paired, after, out):
    local_kv, most_pages = out.shape[:2]
    own_pair = own_pair_of(low_ctx, sub_count)
    sub = lax.axis_index("sub")

    @pl.when(lax.axis_index("ctx") >= low_ctx)
    def _():
        start = jnp.int32(0)
        for r in range(REQS):
            start = start + jnp.where(r < own_pair, counts[r], 0)
        count = counts[own_pair]
        for p in range(most_pages):
            page = start + p
            apart = page // 2 - own_pair
            which = jnp.where(apart == 0, 0, jnp.where(apart == 1 - 2 * sub, 1, 2))
            page_rows = pl.ds(pl.multiple_of(lax.rem(page, 2) * PAGE, PAGE), PAGE)
            for n, ref in enumerate((own, paired, far)):
                @pl.when((p < count) & (which == n))
                def _():
                    for g in range(local_kv):
                        for i in range(2):
                            out[g, p, i] = ref[i, page_rows, g * HD:(g + 1) * HD]


def attend_kernel(low_ctx, sub_count, late_count, turn, waits, counts, pages_in, queries, *refs):
    out = refs[waits]
    head = lax.axis_index("head")
    tokens, width = queries.shape
    local_kv, most_pages = pages_in.shape[:2]
    span = width // local_kv
    per_group = span // HD
    rows = per_group * tokens
    request = own_pair_of(low_ctx, sub_count)

    def token_of(key):
        return ((head ^ key[0]) * sub_count + key[1]) * tokens

    early, late = turn
    is_late = request < late_count
    if early is None or late is None:
        first_token = token_of(early or late)
    else:
        first_token = jnp.where(is_late, token_of(late), token_of(early))
    works = lax.axis_index("ctx") >= low_ctx
    if early is None:
        works = works & is_late
    if late is None:
        works = works & jnp.logical_not(is_late)

    def attend(pages):
        token = lax.rem(lax.broadcasted_iota(jnp.int32, (rows, PAGE), 0), tokens)
        column = lax.broadcasted_iota(jnp.int32, (rows, PAGE), 1)
        visible = column <= PAGE - QR + first_token + token

        def scores_of(g):
            q_block = queries[:, g * span:(g + 1) * span]
            q_rows = jnp.concatenate([q_block[:, j * HD:(j + 1) * HD] for j in range(per_group)], axis=0)
            for p in range(pages):
                scores = lax.dot_general(
                    q_rows, pages_in[g, p, 0], (((1,), (1,)), ((), ())), preferred_element_type=jnp.float32
                )
                yield jnp.where(visible, scores, NEG) if p == pages - 1 else scores

        scores = list(scores_of(0))
        for g in range(local_kv):
            following = scores_of(g + 1) if g + 1 < local_kv else iter(())
            later = []
            top = jnp.max(functools.reduce(jnp.maximum, scores), axis=1, keepdims=True)
            totals, product = None, None
            for p in range(pages):
                later += [s for _, s in zip(range(1), following)]
                numerators = jnp.exp2((scores[p] - top) * EXP2_SCALE)
                part = jnp.dot(
                    numerators.astype(jnp.bfloat16), pages_in[g, p, 1], preferred_element_type=jnp.float32
                )
                totals = numerators if p == 0 else totals + numerators
                product = part if p == 0 else product + part
            totals = jnp.sum(totals, axis=1, keepdims=True)
            done = (product / totals).astype(jnp.bfloat16)
            out[:, g * span:(g + 1) * span] = jnp.concatenate(
                [done[j * tokens:(j + 1) * tokens] for j in range(per_group)], axis=1
            )
            scores = later

    @pl.when(works)
    def _():
        count = counts[request]
        for pages in [*range(1, most_pages - REQS + 3), most_pages]:
            @pl.when(count == pages)
            def _():
                attend(pages)


def one_request_each(queries, kv_cache, page_counts):
    ctx_size, sub_size = lax.axis_size("ctx"), lax.axis_size("sub")
    head_count = lax.axis_size("head")
    low_ctx = ctx_size // 2
    most_pages = kv_cache.shape[1] // PAGE * ctx_size * sub_size // 4
    local_kv = kv_cache.shape[2] // HD
    tokens, width = queries.shape[0], queries.shape[1] // head_count
    anywhere = pl.BlockSpec(memory_space=pl.ANY)
    in_vmem = pl.BlockSpec(memory_space=pltpu.VMEM)
    q_piece = pltpu.VMEM((tokens, width), queries.dtype)

    def vmem(array):
        return pltpu.with_memory_space_constraint(array, pltpu.VMEM)

    def hbm(array):
        return pltpu.with_memory_space_constraint(array, pltpu.HBM)

    def moved(array, routes):
        def flat(place):
            return (place[0] * head_count + place[1]) * sub_size + place[2]

        return lax.ppermute(array, ("ctx", "head", "sub"), [(flat(a), flat(b)) for a, b in routes])

    def worker(request, head):
        return low_ctx + request // sub_size, head, request % sub_size

    heads = range(head_count)
    q_out = pl.pallas_call(
        split_kernel,
        out_shape=[q_piece] * head_count,
        in_specs=[anywhere],
        out_specs=[anywhere] * head_count,
        scratch_shapes=[pltpu.SemaphoreType.DMA((head_count,))],
        compiler_params=pltpu.CompilerParams(vmem_limit_bytes=2**20),
        name="split",
    )(hbm(queries))
    late_count = 1
    early = [(step, s) for step in heads[::-1] for s in range(sub_size)]
    late = [early[0]] + early[2:] + [early[1]]
    turns = list(zip(early + [None], [None] + late))

    def routes_of(turn):
        return [
            ((r, h, key[1]), worker(r, h ^ key[0]))
            for key, requests in zip(turn, (range(late_count, ctx_size), range(late_count))) if key is not None
            for r in requests for h in heads
        ]

    q_in = [moved(q_out[(turn[0] or turn[1])[0]], routes_of(turn)) for turn in turns]

    middle = [(low_ctx, sub_size - 1), (low_ctx + 1, 0)]
    far = moved(kv_cache, [((a[0], h, a[1]), (b[0], h, b[1])) for a, b in (middle, middle[::-1]) for h in heads])
    paired = moved(
        kv_cache, [((c, h, s), (c, h, 1 - s)) for c in range(low_ctx, ctx_size) for h in heads for s in range(sub_size)]
    )
    first_here = pl.pallas_call(
        lambda *refs: None,
        out_shape=pltpu.VMEM((8, HD), jnp.float32),
        in_specs=[anywhere] * 2,
        out_specs=anywhere,
        cost_estimate=pl.CostEstimate(flops=2 * 10**10, bytes_accessed=2**20, transcendentals=0),
        compiler_params=pltpu.CompilerParams(vmem_limit_bytes=2**20),
        name="first_here",
    )(vmem(q_in[0]), vmem(far))
    gathered = pl.pallas_call(
        functools.partial(gather_kernel, low_ctx, sub_size),
        out_shape=pltpu.VMEM((local_kv, most_pages, 2, PAGE, HD), kv_cache.dtype),
        in_specs=[pl.BlockSpec(memory_space=pltpu.SMEM)] + [in_vmem] * 3 + [anywhere],
        out_specs=in_vmem,
        compiler_params=pltpu.CompilerParams(vmem_limit_bytes=2**20),
        name="gather",
    )(page_counts, vmem(kv_cache), vmem(far), vmem(paired), vmem(first_here))

    back = []
    after = []
    for turn, arrived in zip(turns, q_in):
        out = pl.pallas_call(
            functools.partial(attend_kernel, low_ctx, sub_size, late_count, turn, len(after)),
            out_shape=q_piece,
            in_specs=[pl.BlockSpec(memory_space=pltpu.SMEM)] + [in_vmem] * 2 + [anywhere] * len(after),
            out_specs=in_vmem,
            compiler_params=pltpu.CompilerParams(vmem_limit_bytes=12 * 2**20),
            cost_estimate=pl.CostEstimate(flops=6 * 10**9, bytes_accessed=2**22, transcendentals=10**6),
            name=f"attend_{len(back)}",
        )(page_counts, vmem(gathered), vmem(arrived), *after)
        back.append(moved(out, [(b, a) for a, b in routes_of(turn)]))
        after = [out]

    joined = []
    for chosen in [range(len(turns) - 2)] + [[i] for i in range(len(turns) - 2, len(turns))]:
        joined = [
            pl.pallas_call(
                functools.partial(join_kernel, late_count, [turns[i] for i in chosen]),
                out_shape=pltpu.HBM(queries.shape, queries.dtype),
                in_specs=[anywhere] * (len(chosen) + len(joined)),
                out_specs=anywhere,
                scratch_shapes=[pltpu.SemaphoreType.DMA((1,))],
                input_output_aliases={len(chosen): 0} if joined else {},
                compiler_params=pltpu.CompilerParams(vmem_limit_bytes=2**20),
                name="join",
            )(*[vmem(back[i]) for i in chosen], *map(hbm, joined))
        ]
    return joined[0]


def from_behind(array, axis, by):
    count = lax.axis_size(axis)
    pairs = [(i, i + by) for i in range(count) if 0 <= i + by < count]
    return lax.ppermute(array, axis, pairs)


def queries_to_pages(queries, kv_cache, page_counts):
    per_group = HQ // KVH
    local_heads = kv_cache.shape[2] // HD
    ctx_size = lax.axis_size("ctx")
    sub_size = lax.axis_size("sub")
    head_count = lax.axis_size("head")
    tok_rows = queries.shape[0]
    score_scale = HD ** (-0.5)
    regrouped = lax.all_to_all(queries, "head", split_axis=1, concat_axis=0, tiled=True)
    all_queries = lax.all_gather(regrouped, ("ctx", "sub"), axis=0, tiled=True)
    all_queries = all_queries.reshape(SPAN, local_heads, per_group, HD)
    page_ends = jnp.cumsum(page_counts)
    ctx_rows = SPAN // ctx_size
    offsets = jnp.arange(QR, dtype=jnp.int32)
    columns = jnp.arange(PAGE, dtype=jnp.int32)
    flat_index = lax.axis_index("ctx") * sub_size + lax.axis_index("sub")
    pages_here = kv_cache.shape[1] // PAGE
    base_pages = pages_here * ctx_size * sub_size // 2
    initial = (
        jnp.full((SPAN, local_heads, per_group), NEG, jnp.float32),
        jnp.zeros((SPAN, local_heads, per_group), jnp.float32),
        jnp.zeros((SPAN, local_heads, per_group, HD), jnp.float32),
    )
    half_rows = kv_cache.shape[1] // 2
    arrived = from_behind(kv_cache[:, half_rows:], "ctx", -(ctx_size // 2))
    is_lower = lax.axis_index("ctx") < ctx_size // 2
    source_flat = flat_index + ctx_size // 2 * sub_size
    working = jnp.where(is_lower, arrived, kv_cache[:, :half_rows])
    first_page = jnp.where(
        is_lower, source_flat * pages_here + pages_here // 2, flat_index * pages_here
    )
    page_total = working.shape[1] // PAGE

    def add_page(page_turn, running):
        page_index = first_page + page_turn
        relative = page_index - base_pages
        counted = jnp.sum((relative >= page_ends).astype(jnp.int32))
        request = jnp.where(relative < 0, REQS, counted)

        def update(partial_value):
            run_max, run_sum, run_out = partial_value
            request_id = jnp.minimum(request, REQS - 1)
            row_start = request_id * QR
            gathered = row_start + offsets
            within = gathered % ctx_rows
            ctx_block = gathered // ctx_rows
            sub_part = within // (head_count * tok_rows)
            head_part = within // tok_rows % head_count
            tok_part = within % tok_rows
            natural = ctx_block * ctx_rows + (head_part * sub_size + sub_part) * tok_rows + tok_part
            query_pos = (page_ends[request_id] + base_pages) * PAGE - QR + natural - row_start
            key_pos = page_index * PAGE + columns
            visible = key_pos[None, :] <= query_pos[:, None]
            page_keys = working[0].reshape(PAGE, local_heads, HD)
            page_values = working[1].reshape(PAGE, local_heads, HD)
            query_rows = lax.dynamic_slice_in_dim(all_queries, row_start, QR, 0)
            scores = (
                jnp.einsum(
                    "qkgd,pkd->qkgp", query_rows, page_keys, preferred_element_type=jnp.float32
                )
                * score_scale
            )
            scores = jnp.where(visible[:, None, None, :], scores, NEG)
            old_max = lax.dynamic_slice_in_dim(run_max, row_start, QR, 0)
            old_sum = lax.dynamic_slice_in_dim(run_sum, row_start, QR, 0)
            old_out = lax.dynamic_slice_in_dim(run_out, row_start, QR, 0)
            new_max = jnp.maximum(old_max, jnp.max(scores, axis=3))
            factor = jnp.exp(old_max - new_max)
            numerators = jnp.exp(scores - new_max[..., None])
            new_sum = old_sum * factor + jnp.sum(numerators, axis=3)
            product = jnp.einsum(
                "qkgp,pkd->qkgd",
                numerators.astype(jnp.bfloat16),
                page_values,
                preferred_element_type=jnp.float32,
            )
            new_out = old_out * factor[..., None] + product
            return (
                lax.dynamic_update_slice_in_dim(run_max, new_max, row_start, 0),
                lax.dynamic_update_slice_in_dim(run_sum, new_sum, row_start, 0),
                lax.dynamic_update_slice_in_dim(run_out, new_out, row_start, 0),
            )

        def unchanged(partial_value):
            return partial_value

        return lax.cond(request < REQS, update, unchanged, running)

    run_max, run_sum, run_out = lax.fori_loop(0, page_total, add_page, initial)
    share = SPAN // (ctx_size * sub_size)
    global_max = lax.pmax(run_max, ("ctx", "sub"))
    factor = jnp.exp(run_max - global_max)
    sums_here, outs_here = (
        lax.psum_scatter(
            (run_sum * factor).astype(jnp.bfloat16), ("ctx", "sub"), scatter_dimension=0, tiled=True
        ).astype(jnp.float32),
        lax.psum_scatter(
            (run_out * factor[..., None]).astype(jnp.bfloat16),
            ("ctx", "sub"),
            scatter_dimension=0,
            tiled=True,
        ).astype(jnp.float32),
    )
    finished = (outs_here / sums_here[..., None]).astype(jnp.bfloat16)
    finished = finished.reshape(share, local_heads * per_group * HD)
    return lax.all_to_all(finished, "head", split_axis=0, concat_axis=1, tiled=True)


def per_device(queries, kv_cache, page_counts):
    ctx_size, sub_size, head_count = lax.axis_size("ctx"), lax.axis_size("sub"), lax.axis_size("head")
    small = (
        ctx_size == REQS == 4
        and head_count == sub_size == 2
        and kv_cache.shape[1] == 2 * PAGE
        and kv_cache.shape[2] % (sub_size * HD) == 0
        and queries.shape[0] % 16 == 0
        and queries.shape[0] * head_count * sub_size == QR
    )
    return (one_request_each if small else queries_to_pages)(queries, kv_cache, page_counts)


def solution(mesh):
    return jax.shard_map(
        per_device,
        mesh=mesh,
        in_specs=(
            P(("grp", "ctx", "head", "sub"), None),
            P(None, ("grp", "ctx", "sub"), "head"),
            P("grp"),
        ),
        out_specs=P(("grp", "ctx", "head", "sub"), None),
        check_vma=False,
    )
```

```python
import functools

import jax
import jax.numpy as jnp
from jax import lax
from jax.experimental import pallas as pl
from jax.experimental.pallas import tpu as pltpu
from jax.sharding import PartitionSpec as P

HQ = 128
KVH = 8
HD = 128
REQS = 4
QR = 64
PAGE = 256
SPAN = 256


NEG = -1e30
EXP2_SCALE = HD ** (-0.5) * 1.4426950408889634


def run(copies):
    for copy in copies:
        copy.start()
    for copy in copies:
        copy.wait()


def head_part(step, width):
    return pl.ds(pl.multiple_of((lax.axis_index("head") ^ step) * width, width), width)


def split_kernel(queries, *refs):
    outs, sems = refs[:-1], refs[-1]
    run([
        pltpu.make_async_copy(queries.at[:, head_part(step, out.shape[1])], out, sems.at[step])
        for step, out in enumerate(outs)
    ])


def join_kernel(step, sub_count, *refs):
    pieces, (out, sems) = refs[:sub_count], refs[-2:]
    for source, piece in enumerate(pieces):
        @pl.when(lax.axis_index("sub") == source)
        def _():
            run([pltpu.make_async_copy(piece, out.at[:, head_part(step, piece.shape[1])], sems.at[0])])


def worker_places(low_ctx):
    return (0, 0), (low_ctx, 1), (low_ctx + 1, 0), (low_ctx + 1, 1)


def own_request(low_ctx):
    ctx, sub = lax.axis_index("ctx"), lax.axis_index("sub")
    found = jnp.int32(-1)
    for request, place in enumerate(worker_places(low_ctx)):
        found = jnp.where((ctx == place[0]) & (sub == place[1]), request, found)
    return found


def gather_kernel(low_ctx, counts, own, near, far, out, sems):
    local_kv, most_pages = out.shape[:2]
    request = own_request(low_ctx)

    @pl.when(request >= 0)
    def _():
        start = jnp.int32(0)
        for r in range(REQS):
            start = start + jnp.where(r < request, counts[r], 0)
        count = counts[request]
        near_pair = jnp.where(request == 0, 1, request ^ 1)
        home_pair = jnp.where(request == 0, -1, request)

        def of_page(p):
            page = start + p
            page_rows = pl.ds(pl.multiple_of(lax.rem(page, 2) * PAGE, PAGE), PAGE)
            return page // 2, page_rows

        def home_copies(p, page_rows):
            return [
                pltpu.make_async_copy(own.at[i, page_rows, pl.ds(g * HD, HD)], out.at[g, p, i], sems.at[g, p, i])
                for g in range(local_kv) for i in range(2)
            ]

        for p in range(most_pages):
            pair, page_rows = of_page(p)
            @pl.when((p < count) & (pair == home_pair))
            def _():
                for copy in home_copies(p, page_rows):
                    copy.start()
        for p in range(most_pages):
            pair, page_rows = of_page(p)
            for ref, chosen in ((near, pair == near_pair), (far, (pair != near_pair) & (pair != home_pair))):
                @pl.when((p < count) & chosen)
                def _():
                    for g in range(local_kv):
                        for i in range(2):
                            out[g, p, i] = ref[i, page_rows, g * HD:(g + 1) * HD]
        for p in range(most_pages):
            pair, page_rows = of_page(p)
            @pl.when((p < count) & (pair == home_pair))
            def _():
                for copy in home_copies(p, page_rows):
                    copy.wait()


def attend_kernel(low_ctx, sub_count, step, waits, counts, pages_in, *refs):
    queries, outs = refs[:sub_count], refs[sub_count + waits:]
    head = lax.axis_index("head")
    tokens, width = queries[0].shape
    local_kv, most_pages = pages_in.shape[:2]
    span = width // local_kv
    per_group = span // HD
    piece_rows = per_group * tokens
    rows = sub_count * piece_rows
    first_token = (head ^ step) * sub_count * tokens

    def attend(pages):
        row = lax.broadcasted_iota(jnp.int32, (rows, PAGE), 0)
        token = first_token + row // piece_rows * tokens + lax.rem(row, tokens)
        column = lax.broadcasted_iota(jnp.int32, (rows, PAGE), 1)
        visible = column <= PAGE - QR + token

        def scores_of(g):
            q_blocks = [ref[:, g * span:(g + 1) * span] for ref in queries]
            q_rows = jnp.concatenate([q[:, j * HD:(j + 1) * HD] for q in q_blocks for j in range(per_group)], axis=0)
            for p in range(pages):
                scores = lax.dot_general(
                    q_rows, pages_in[g, p, 0], (((1,), (1,)), ((), ())), preferred_element_type=jnp.float32
                )
                yield jnp.where(visible, scores, NEG) if p == pages - 1 else scores

        scores = list(scores_of(0))
        for g in range(local_kv):
            following = scores_of(g + 1) if g + 1 < local_kv else iter(())
            later = []
            top = jnp.max(functools.reduce(jnp.maximum, scores), axis=1, keepdims=True)
            totals, product = None, None
            for p in range(pages):
                later += [s for _, s in zip(range(1), following)]
                numerators = jnp.exp2((scores[p] - top) * EXP2_SCALE)
                part = jnp.dot(
                    numerators.astype(jnp.bfloat16), pages_in[g, p, 1], preferred_element_type=jnp.float32
                )
                totals = numerators if p == 0 else totals + numerators
                product = part if p == 0 else product + part
            totals = jnp.sum(totals, axis=1, keepdims=True)
            done = (product / totals).astype(jnp.bfloat16)
            for i, out in enumerate(outs):
                start = i * piece_rows
                out[:, g * span:(g + 1) * span] = jnp.concatenate(
                    [done[start + j * tokens:start + (j + 1) * tokens] for j in range(per_group)], axis=1
                )
            scores = later

    request = own_request(low_ctx)

    @pl.when(request >= 0)
    def _():
        count = counts[request]
        for pages in [*range(1, most_pages - REQS + 3), most_pages]:
            @pl.when(count == pages)
            def _():
                attend(pages)


def one_request_each(queries, kv_cache, page_counts):
    ctx_size, sub_size = lax.axis_size("ctx"), lax.axis_size("sub")
    head_count = lax.axis_size("head")
    low_ctx = ctx_size // 2
    most_pages = kv_cache.shape[1] // PAGE * ctx_size * sub_size // 4
    local_kv = kv_cache.shape[2] // HD
    tokens, width = queries.shape[0], queries.shape[1] // head_count
    anywhere = pl.BlockSpec(memory_space=pl.ANY)
    in_vmem = pl.BlockSpec(memory_space=pltpu.VMEM)
    q_piece = pltpu.VMEM((tokens, width), queries.dtype)

    def vmem(array):
        return pltpu.with_memory_space_constraint(array, pltpu.VMEM)

    def hbm(array):
        return pltpu.with_memory_space_constraint(array, pltpu.HBM)

    def moved(array, routes):
        def flat(place):
            return (place[0] * head_count + place[1]) * sub_size + place[2]

        return lax.ppermute(array, ("ctx", "head", "sub"), [(flat(a), flat(b)) for a, b in routes])

    def worker(request, head):
        ctx, sub = worker_places(low_ctx)[request]
        return ctx, head, sub

    heads = range(head_count)
    q_out = pl.pallas_call(
        split_kernel,
        out_shape=[q_piece] * head_count,
        in_specs=[anywhere],
        out_specs=[anywhere] * head_count,
        scratch_shapes=[pltpu.SemaphoreType.DMA((head_count,))],
        compiler_params=pltpu.CompilerParams(vmem_limit_bytes=2**20),
        name="split",
    )(hbm(queries))
    routes = {
        (step, s): [((r, h, s), worker(r, h ^ step)) for r in range(ctx_size) for h in heads]
        for step in heads[::-1] for s in range(sub_size)
    }
    q_in = {key: moved(q_out[key[0]], pairs) for key, pairs in routes.items()}

    pairs = [(low_ctx + n // 2, n % 2) for n in range(4)]
    workers = worker_places(low_ctx)
    near, far = (
        moved(kv_cache, [((*a[:1], h, *a[1:]), (*b[:1], h, *b[1:])) for a, b in sends for h in heads])
        for sends in (
            [(pairs[0], workers[1]), (pairs[1], workers[0]), (pairs[2], workers[3]), (pairs[3], workers[2])],
            [(pairs[0], workers[0]), (pairs[1], workers[2]), (pairs[2], workers[1])],
        )
    )
    gathered = pl.pallas_call(
        functools.partial(gather_kernel, low_ctx),
        out_shape=pltpu.VMEM((local_kv, most_pages, 2, PAGE, HD), kv_cache.dtype),
        in_specs=[pl.BlockSpec(memory_space=pltpu.SMEM), anywhere] + [in_vmem] * 2,
        out_specs=in_vmem,
        scratch_shapes=[pltpu.SemaphoreType.DMA((local_kv, most_pages, 2))],
        compiler_params=pltpu.CompilerParams(vmem_limit_bytes=2**20),
        name="gather",
    )(page_counts, hbm(kv_cache), vmem(near), vmem(far))

    back = {}
    after = []
    for step in heads[::-1]:
        subs = range(sub_size)
        outs = pl.pallas_call(
            functools.partial(attend_kernel, low_ctx, sub_size, step, len(after)),
            out_shape=[q_piece] * sub_size,
            in_specs=[pl.BlockSpec(memory_space=pltpu.SMEM)] + [in_vmem] * (1 + sub_size) + [anywhere] * len(after),
            out_specs=[in_vmem] * sub_size,
            compiler_params=pltpu.CompilerParams(vmem_limit_bytes=12 * 2**20),
            cost_estimate=pl.CostEstimate(flops=10**10, bytes_accessed=2**22, transcendentals=10**6),
            name=f"attend_{step}",
        )(page_counts, vmem(gathered), *[vmem(q_in[step, s]) for s in subs], *after)
        for s in subs:
            back[step, s] = moved(outs[s], [(b, a) for a, b in routes[step, s]])
        after = [outs[0]]

    joined = []
    for step in heads[::-1]:
        joined = [
            pl.pallas_call(
                functools.partial(join_kernel, step, sub_size),
                out_shape=pltpu.HBM(queries.shape, queries.dtype),
                in_specs=[anywhere] * (sub_size + len(joined)),
                out_specs=anywhere,
                scratch_shapes=[pltpu.SemaphoreType.DMA((1,))],
                input_output_aliases={sub_size: 0} if joined else {},
                compiler_params=pltpu.CompilerParams(vmem_limit_bytes=2**20),
                name=f"join_{step}",
            )(*[vmem(back[step, s]) for s in range(sub_size)], *map(hbm, joined))
        ]
    return joined[0]


def from_behind(array, axis, by):
    count = lax.axis_size(axis)
    pairs = [(i, i + by) for i in range(count) if 0 <= i + by < count]
    return lax.ppermute(array, axis, pairs)


def queries_to_pages(queries, kv_cache, page_counts):
    per_group = HQ // KVH
    local_heads = kv_cache.shape[2] // HD
    ctx_size = lax.axis_size("ctx")
    sub_size = lax.axis_size("sub")
    head_count = lax.axis_size("head")
    tok_rows = queries.shape[0]
    score_scale = HD ** (-0.5)
    regrouped = lax.all_to_all(queries, "head", split_axis=1, concat_axis=0, tiled=True)
    all_queries = lax.all_gather(regrouped, ("ctx", "sub"), axis=0, tiled=True)
    all_queries = all_queries.reshape(SPAN, local_heads, per_group, HD)
    page_ends = jnp.cumsum(page_counts)
    ctx_rows = SPAN // ctx_size
    offsets = jnp.arange(QR, dtype=jnp.int32)
    columns = jnp.arange(PAGE, dtype=jnp.int32)
    flat_index = lax.axis_index("ctx") * sub_size + lax.axis_index("sub")
    pages_here = kv_cache.shape[1] // PAGE
    base_pages = pages_here * ctx_size * sub_size // 2
    initial = (
        jnp.full((SPAN, local_heads, per_group), NEG, jnp.float32),
        jnp.zeros((SPAN, local_heads, per_group), jnp.float32),
        jnp.zeros((SPAN, local_heads, per_group, HD), jnp.float32),
    )
    half_rows = kv_cache.shape[1] // 2
    arrived = from_behind(kv_cache[:, half_rows:], "ctx", -(ctx_size // 2))
    is_lower = lax.axis_index("ctx") < ctx_size // 2
    source_flat = flat_index + ctx_size // 2 * sub_size
    working = jnp.where(is_lower, arrived, kv_cache[:, :half_rows])
    first_page = jnp.where(
        is_lower, source_flat * pages_here + pages_here // 2, flat_index * pages_here
    )
    page_total = working.shape[1] // PAGE

    def add_page(page_turn, running):
        page_index = first_page + page_turn
        relative = page_index - base_pages
        counted = jnp.sum((relative >= page_ends).astype(jnp.int32))
        request = jnp.where(relative < 0, REQS, counted)

        def update(partial_value):
            run_max, run_sum, run_out = partial_value
            request_id = jnp.minimum(request, REQS - 1)
            row_start = request_id * QR
            gathered = row_start + offsets
            within = gathered % ctx_rows
            ctx_block = gathered // ctx_rows
            sub_part = within // (head_count * tok_rows)
            head_part = within // tok_rows % head_count
            tok_part = within % tok_rows
            natural = ctx_block * ctx_rows + (head_part * sub_size + sub_part) * tok_rows + tok_part
            query_pos = (page_ends[request_id] + base_pages) * PAGE - QR + natural - row_start
            key_pos = page_index * PAGE + columns
            visible = key_pos[None, :] <= query_pos[:, None]
            page_keys = working[0].reshape(PAGE, local_heads, HD)
            page_values = working[1].reshape(PAGE, local_heads, HD)
            query_rows = lax.dynamic_slice_in_dim(all_queries, row_start, QR, 0)
            scores = (
                jnp.einsum(
                    "qkgd,pkd->qkgp", query_rows, page_keys, preferred_element_type=jnp.float32
                )
                * score_scale
            )
            scores = jnp.where(visible[:, None, None, :], scores, NEG)
            old_max = lax.dynamic_slice_in_dim(run_max, row_start, QR, 0)
            old_sum = lax.dynamic_slice_in_dim(run_sum, row_start, QR, 0)
            old_out = lax.dynamic_slice_in_dim(run_out, row_start, QR, 0)
            new_max = jnp.maximum(old_max, jnp.max(scores, axis=3))
            factor = jnp.exp(old_max - new_max)
            numerators = jnp.exp(scores - new_max[..., None])
            new_sum = old_sum * factor + jnp.sum(numerators, axis=3)
            product = jnp.einsum(
                "qkgp,pkd->qkgd",
                numerators.astype(jnp.bfloat16),
                page_values,
                preferred_element_type=jnp.float32,
            )
            new_out = old_out * factor[..., None] + product
            return (
                lax.dynamic_update_slice_in_dim(run_max, new_max, row_start, 0),
                lax.dynamic_update_slice_in_dim(run_sum, new_sum, row_start, 0),
                lax.dynamic_update_slice_in_dim(run_out, new_out, row_start, 0),
            )

        def unchanged(partial_value):
            return partial_value

        return lax.cond(request < REQS, update, unchanged, running)

    run_max, run_sum, run_out = lax.fori_loop(0, page_total, add_page, initial)
    share = SPAN // (ctx_size * sub_size)
    global_max = lax.pmax(run_max, ("ctx", "sub"))
    factor = jnp.exp(run_max - global_max)
    sums_here, outs_here = (
        lax.psum_scatter(
            (run_sum * factor).astype(jnp.bfloat16), ("ctx", "sub"), scatter_dimension=0, tiled=True
        ).astype(jnp.float32),
        lax.psum_scatter(
            (run_out * factor[..., None]).astype(jnp.bfloat16),
            ("ctx", "sub"),
            scatter_dimension=0,
            tiled=True,
        ).astype(jnp.float32),
    )
    finished = (outs_here / sums_here[..., None]).astype(jnp.bfloat16)
    finished = finished.reshape(share, local_heads * per_group * HD)
    return lax.all_to_all(finished, "head", split_axis=0, concat_axis=1, tiled=True)


def per_device(queries, kv_cache, page_counts):
    ctx_size, sub_size, head_count = lax.axis_size("ctx"), lax.axis_size("sub"), lax.axis_size("head")
    small = (
        ctx_size == REQS == 4
        and head_count == sub_size == 2
        and kv_cache.shape[1] == 2 * PAGE
        and kv_cache.shape[2] % (sub_size * HD) == 0
        and queries.shape[0] % 16 == 0
        and queries.shape[0] * head_count * sub_size == QR
    )
    return (one_request_each if small else queries_to_pages)(queries, kv_cache, page_counts)


def solution(mesh):
    return jax.shard_map(
        per_device,
        mesh=mesh,
        in_specs=(
            P(("grp", "ctx", "head", "sub"), None),
            P(None, ("grp", "ctx", "sub"), "head"),
            P("grp"),
        ),
        out_specs=P(("grp", "ctx", "head", "sub"), None),
        check_vma=False,
    )
```

```python
import functools

import jax
import jax.numpy as jnp
from jax import lax
from jax.experimental import pallas as pl
from jax.experimental.pallas import tpu as pltpu
from jax.sharding import PartitionSpec as P

HQ = 128
KVH = 8
HD = 128
REQS = 4
QR = 64
PAGE = 256
SPAN = 256


NEG = -1e30
EXP2_SCALE = HD ** (-0.5) * 1.4426950408889634


def run(copies):
    for copy in copies:
        copy.start()
    for copy in copies:
        copy.wait()


def head_part(step, width):
    return pl.ds(pl.multiple_of((lax.axis_index("head") ^ step) * width, width), width)


def split_kernel(queries, *refs):
    outs, sems = refs[:-1], refs[-1]
    run([
        pltpu.make_async_copy(queries.at[:, head_part(step, out.shape[1])], out, sems.at[step])
        for step, out in enumerate(outs)
    ])


def join_kernel(step, sub_count, *refs):
    pieces, (out, sems) = refs[:sub_count], refs[-2:]
    for source, piece in enumerate(pieces):
        @pl.when(lax.axis_index("sub") == source)
        def _():
            run([pltpu.make_async_copy(piece, out.at[:, head_part(step, piece.shape[1])], sems.at[0])])


def worker_places(low_ctx):
    return (0, 0), (low_ctx, 1), (low_ctx + 1, 0), (low_ctx + 1, 1)


def own_request(low_ctx):
    ctx, sub = lax.axis_index("ctx"), lax.axis_index("sub")
    found = jnp.int32(-1)
    for request, place in enumerate(worker_places(low_ctx)):
        found = jnp.where((ctx == place[0]) & (sub == place[1]), request, found)
    return found


def gather_kernel(low_ctx, counts, own, near, far, after, out, sems):
    local_kv, most_pages = out.shape[:2]
    request = own_request(low_ctx)

    @pl.when(request >= 0)
    def _():
        start = jnp.int32(0)
        for r in range(REQS):
            start = start + jnp.where(r < request, counts[r], 0)
        count = counts[request]
        near_pair = jnp.where(request == 0, 1, request ^ 1)
        home_pair = jnp.where(request == 0, -1, request)

        def of_page(p):
            page = start + p
            page_rows = pl.ds(pl.multiple_of(lax.rem(page, 2) * PAGE, PAGE), PAGE)
            return page // 2, page_rows

        def home_copies(p, page_rows):
            return [
                pltpu.make_async_copy(own.at[i, page_rows, pl.ds(g * HD, HD)], out.at[g, p, i], sems.at[g, p, i])
                for g in range(local_kv) for i in range(2)
            ]

        for p in range(most_pages):
            pair, page_rows = of_page(p)
            @pl.when((p < count) & (pair == home_pair))
            def _():
                for copy in home_copies(p, page_rows):
                    copy.start()
        for p in range(most_pages):
            pair, page_rows = of_page(p)
            for ref, chosen in ((near, pair == near_pair), (far, (pair != near_pair) & (pair != home_pair))):
                @pl.when((p < count) & chosen)
                def _():
                    for g in range(local_kv):
                        for i in range(2):
                            out[g, p, i] = ref[i, page_rows, g * HD:(g + 1) * HD]
        for p in range(most_pages):
            pair, page_rows = of_page(p)
            @pl.when((p < count) & (pair == home_pair))
            def _():
                for copy in home_copies(p, page_rows):
                    copy.wait()


def attend_kernel(low_ctx, sub_count, step, waits, counts, pages_in, *refs):
    queries, outs = refs[:sub_count], refs[sub_count + waits:]
    head = lax.axis_index("head")
    tokens, width = queries[0].shape
    local_kv, most_pages = pages_in.shape[:2]
    span = width // local_kv
    per_group = span // HD
    piece_rows = per_group * tokens
    rows = sub_count * piece_rows
    first_token = (head ^ step) * sub_count * tokens

    def attend(pages):
        row = lax.broadcasted_iota(jnp.int32, (rows, PAGE), 0)
        token = first_token + row // piece_rows * tokens + lax.rem(row, tokens)
        column = lax.broadcasted_iota(jnp.int32, (rows, PAGE), 1)
        visible = column <= PAGE - QR + token

        def scores_of(g):
            q_blocks = [ref[:, g * span:(g + 1) * span] for ref in queries]
            q_rows = jnp.concatenate([q[:, j * HD:(j + 1) * HD] for q in q_blocks for j in range(per_group)], axis=0)
            for p in range(pages):
                scores = lax.dot_general(
                    q_rows, pages_in[g, p, 0], (((1,), (1,)), ((), ())), preferred_element_type=jnp.float32
                )
                yield jnp.where(visible, scores, NEG) if p == pages - 1 else scores

        scores = list(scores_of(0))
        for g in range(local_kv):
            following = scores_of(g + 1) if g + 1 < local_kv else iter(())
            later = []
            top = jnp.max(functools.reduce(jnp.maximum, scores), axis=1, keepdims=True)
            totals, product = None, None
            for p in range(pages):
                later += [s for _, s in zip(range(1), following)]
                numerators = jnp.exp2((scores[p] - top) * EXP2_SCALE)
                part = jnp.dot(
                    numerators.astype(jnp.bfloat16), pages_in[g, p, 1], preferred_element_type=jnp.float32
                )
                totals = numerators if p == 0 else totals + numerators
                product = part if p == 0 else product + part
            totals = jnp.sum(totals, axis=1, keepdims=True)
            done = (product / totals).astype(jnp.bfloat16)
            for i, out in enumerate(outs):
                start = i * piece_rows
                out[:, g * span:(g + 1) * span] = jnp.concatenate(
                    [done[start + j * tokens:start + (j + 1) * tokens] for j in range(per_group)], axis=1
                )
            scores = later

    request = own_request(low_ctx)

    @pl.when(request >= 0)
    def _():
        count = counts[request]
        for pages in [*range(1, most_pages - REQS + 3), most_pages]:
            @pl.when(count == pages)
            def _():
                attend(pages)


def one_request_each(queries, kv_cache, page_counts):
    ctx_size, sub_size = lax.axis_size("ctx"), lax.axis_size("sub")
    head_count = lax.axis_size("head")
    low_ctx = ctx_size // 2
    most_pages = kv_cache.shape[1] // PAGE * ctx_size * sub_size // 4
    local_kv = kv_cache.shape[2] // HD
    tokens, width = queries.shape[0], queries.shape[1] // head_count
    anywhere = pl.BlockSpec(memory_space=pl.ANY)
    in_vmem = pl.BlockSpec(memory_space=pltpu.VMEM)
    q_piece = pltpu.VMEM((tokens, width), queries.dtype)

    def vmem(array):
        return pltpu.with_memory_space_constraint(array, pltpu.VMEM)

    def hbm(array):
        return pltpu.with_memory_space_constraint(array, pltpu.HBM)

    def moved(array, routes):
        def flat(place):
            return (place[0] * head_count + place[1]) * sub_size + place[2]

        return lax.ppermute(array, ("ctx", "head", "sub"), [(flat(a), flat(b)) for a, b in routes])

    def worker(request, head):
        ctx, sub = worker_places(low_ctx)[request]
        return ctx, head, sub

    heads = range(head_count)
    q_out = pl.pallas_call(
        split_kernel,
        out_shape=[q_piece] * head_count,
        in_specs=[anywhere],
        out_specs=[anywhere] * head_count,
        scratch_shapes=[pltpu.SemaphoreType.DMA((head_count,))],
        compiler_params=pltpu.CompilerParams(vmem_limit_bytes=2**20),
        name="split",
    )(hbm(queries))
    routes = {
        (step, s): [((r, h, s), worker(r, h ^ step)) for r in range(ctx_size) for h in heads]
        for step in heads[::-1] for s in range(sub_size)
    }
    q_in = {key: moved(q_out[key[0]], pairs) for key, pairs in routes.items()}

    pairs = [(low_ctx + n // 2, n % 2) for n in range(4)]
    workers = worker_places(low_ctx)
    near, far = (
        moved(kv_cache, [((*a[:1], h, *a[1:]), (*b[:1], h, *b[1:])) for a, b in sends for h in heads])
        for sends in (
            [(pairs[0], workers[1]), (pairs[1], workers[0]), (pairs[2], workers[3]), (pairs[3], workers[2])],
            [(pairs[0], workers[0]), (pairs[1], workers[2]), (pairs[2], workers[1])],
        )
    )
    first_here = pl.pallas_call(
        lambda *refs: None,
        out_shape=pltpu.VMEM((8, HD), jnp.float32),
        in_specs=[anywhere],
        out_specs=anywhere,
        compiler_params=pltpu.CompilerParams(vmem_limit_bytes=2**20),
        name="first_here",
    )(vmem(q_in[list(routes)[0]]))
    gathered = pl.pallas_call(
        functools.partial(gather_kernel, low_ctx),
        out_shape=pltpu.VMEM((local_kv, most_pages, 2, PAGE, HD), kv_cache.dtype),
        in_specs=[pl.BlockSpec(memory_space=pltpu.SMEM), anywhere] + [in_vmem] * 2 + [anywhere],
        out_specs=in_vmem,
        scratch_shapes=[pltpu.SemaphoreType.DMA((local_kv, most_pages, 2))],
        compiler_params=pltpu.CompilerParams(vmem_limit_bytes=2**20),
        name="gather",
    )(hbm(page_counts), hbm(kv_cache), vmem(near), vmem(far), vmem(first_here))

    back = {}
    after = []
    for step in heads[::-1]:
        subs = range(sub_size)
        outs = pl.pallas_call(
            functools.partial(attend_kernel, low_ctx, sub_size, step, len(after)),
            out_shape=[q_piece] * sub_size,
            in_specs=[pl.BlockSpec(memory_space=pltpu.SMEM)] + [in_vmem] * (1 + sub_size) + [anywhere] * len(after),
            out_specs=[in_vmem] * sub_size,
            compiler_params=pltpu.CompilerParams(vmem_limit_bytes=12 * 2**20),
            cost_estimate=pl.CostEstimate(flops=10**10, bytes_accessed=2**22, transcendentals=10**6),
            name=f"attend_{step}",
        )(hbm(page_counts), vmem(gathered), *[vmem(q_in[step, s]) for s in subs], *after)
        for s in subs:
            back[step, s] = moved(outs[s], [(b, a) for a, b in routes[step, s]])
        after = [outs[0]]

    joined = []
    for step in heads[::-1]:
        joined = [
            pl.pallas_call(
                functools.partial(join_kernel, step, sub_size),
                out_shape=pltpu.HBM(queries.shape, queries.dtype),
                in_specs=[anywhere] * (sub_size + len(joined)),
                out_specs=anywhere,
                scratch_shapes=[pltpu.SemaphoreType.DMA((1,))],
                input_output_aliases={sub_size: 0} if joined else {},
                compiler_params=pltpu.CompilerParams(vmem_limit_bytes=2**20),
                name=f"join_{step}",
            )(*[vmem(back[step, s]) for s in range(sub_size)], *map(hbm, joined))
        ]
    return joined[0]


def from_behind(array, axis, by):
    count = lax.axis_size(axis)
    pairs = [(i, i + by) for i in range(count) if 0 <= i + by < count]
    return lax.ppermute(array, axis, pairs)


def queries_to_pages(queries, kv_cache, page_counts):
    per_group = HQ // KVH
    local_heads = kv_cache.shape[2] // HD
    ctx_size = lax.axis_size("ctx")
    sub_size = lax.axis_size("sub")
    head_count = lax.axis_size("head")
    tok_rows = queries.shape[0]
    score_scale = HD ** (-0.5)
    regrouped = lax.all_to_all(queries, "head", split_axis=1, concat_axis=0, tiled=True)
    all_queries = lax.all_gather(regrouped, ("ctx", "sub"), axis=0, tiled=True)
    all_queries = all_queries.reshape(SPAN, local_heads, per_group, HD)
    page_ends = jnp.cumsum(page_counts)
    ctx_rows = SPAN // ctx_size
    offsets = jnp.arange(QR, dtype=jnp.int32)
    columns = jnp.arange(PAGE, dtype=jnp.int32)
    flat_index = lax.axis_index("ctx") * sub_size + lax.axis_index("sub")
    pages_here = kv_cache.shape[1] // PAGE
    base_pages = pages_here * ctx_size * sub_size // 2
    initial = (
        jnp.full((SPAN, local_heads, per_group), NEG, jnp.float32),
        jnp.zeros((SPAN, local_heads, per_group), jnp.float32),
        jnp.zeros((SPAN, local_heads, per_group, HD), jnp.float32),
    )
    half_rows = kv_cache.shape[1] // 2
    arrived = from_behind(kv_cache[:, half_rows:], "ctx", -(ctx_size // 2))
    is_lower = lax.axis_index("ctx") < ctx_size // 2
    source_flat = flat_index + ctx_size // 2 * sub_size
    working = jnp.where(is_lower, arrived, kv_cache[:, :half_rows])
    first_page = jnp.where(
        is_lower, source_flat * pages_here + pages_here // 2, flat_index * pages_here
    )
    page_total = working.shape[1] // PAGE

    def add_page(page_turn, running):
        page_index = first_page + page_turn
        relative = page_index - base_pages
        counted = jnp.sum((relative >= page_ends).astype(jnp.int32))
        request = jnp.where(relative < 0, REQS, counted)

        def update(partial_value):
            run_max, run_sum, run_out = partial_value
            request_id = jnp.minimum(request, REQS - 1)
            row_start = request_id * QR
            gathered = row_start + offsets
            within = gathered % ctx_rows
            ctx_block = gathered // ctx_rows
            sub_part = within // (head_count * tok_rows)
            head_part = within // tok_rows % head_count
            tok_part = within % tok_rows
            natural = ctx_block * ctx_rows + (head_part * sub_size + sub_part) * tok_rows + tok_part
            query_pos = (page_ends[request_id] + base_pages) * PAGE - QR + natural - row_start
            key_pos = page_index * PAGE + columns
            visible = key_pos[None, :] <= query_pos[:, None]
            page_keys = working[0].reshape(PAGE, local_heads, HD)
            page_values = working[1].reshape(PAGE, local_heads, HD)
            query_rows = lax.dynamic_slice_in_dim(all_queries, row_start, QR, 0)
            scores = (
                jnp.einsum(
                    "qkgd,pkd->qkgp", query_rows, page_keys, preferred_element_type=jnp.float32
                )
                * score_scale
            )
            scores = jnp.where(visible[:, None, None, :], scores, NEG)
            old_max = lax.dynamic_slice_in_dim(run_max, row_start, QR, 0)
            old_sum = lax.dynamic_slice_in_dim(run_sum, row_start, QR, 0)
            old_out = lax.dynamic_slice_in_dim(run_out, row_start, QR, 0)
            new_max = jnp.maximum(old_max, jnp.max(scores, axis=3))
            factor = jnp.exp(old_max - new_max)
            numerators = jnp.exp(scores - new_max[..., None])
            new_sum = old_sum * factor + jnp.sum(numerators, axis=3)
            product = jnp.einsum(
                "qkgp,pkd->qkgd",
                numerators.astype(jnp.bfloat16),
                page_values,
                preferred_element_type=jnp.float32,
            )
            new_out = old_out * factor[..., None] + product
            return (
                lax.dynamic_update_slice_in_dim(run_max, new_max, row_start, 0),
                lax.dynamic_update_slice_in_dim(run_sum, new_sum, row_start, 0),
                lax.dynamic_update_slice_in_dim(run_out, new_out, row_start, 0),
            )

        def unchanged(partial_value):
            return partial_value

        return lax.cond(request < REQS, update, unchanged, running)

    run_max, run_sum, run_out = lax.fori_loop(0, page_total, add_page, initial)
    share = SPAN // (ctx_size * sub_size)
    global_max = lax.pmax(run_max, ("ctx", "sub"))
    factor = jnp.exp(run_max - global_max)
    sums_here, outs_here = (
        lax.psum_scatter(
            (run_sum * factor).astype(jnp.bfloat16), ("ctx", "sub"), scatter_dimension=0, tiled=True
        ).astype(jnp.float32),
        lax.psum_scatter(
            (run_out * factor[..., None]).astype(jnp.bfloat16),
            ("ctx", "sub"),
            scatter_dimension=0,
            tiled=True,
        ).astype(jnp.float32),
    )
    finished = (outs_here / sums_here[..., None]).astype(jnp.bfloat16)
    finished = finished.reshape(share, local_heads * per_group * HD)
    return lax.all_to_all(finished, "head", split_axis=0, concat_axis=1, tiled=True)


def per_device(queries, kv_cache, page_counts):
    ctx_size, sub_size, head_count = lax.axis_size("ctx"), lax.axis_size("sub"), lax.axis_size("head")
    small = (
        ctx_size == REQS == 4
        and head_count == sub_size == 2
        and kv_cache.shape[1] == 2 * PAGE
        and kv_cache.shape[2] % (sub_size * HD) == 0
        and queries.shape[0] % 16 == 0
        and queries.shape[0] * head_count * sub_size == QR
    )
    return (one_request_each if small else queries_to_pages)(queries, kv_cache, page_counts)


def solution(mesh):
    return jax.shard_map(
        per_device,
        mesh=mesh,
        in_specs=(
            P(("grp", "ctx", "head", "sub"), None),
            P(None, ("grp", "ctx", "sub"), "head"),
            P("grp"),
        ),
        out_specs=P(("grp", "ctx", "head", "sub"), None),
        check_vma=False,
    )
```

```python
import functools

import jax
import jax.numpy as jnp
from jax import lax
from jax.experimental import pallas as pl
from jax.experimental.pallas import tpu as pltpu
from jax.sharding import PartitionSpec as P

HQ = 128
KVH = 8
HD = 128
REQS = 4
QR = 64
PAGE = 256
SPAN = 256


NEG = -1e30
EXP2_SCALE = HD ** (-0.5) * 1.4426950408889634


def run(copies):
    for copy in copies:
        copy.start()
    for copy in copies:
        copy.wait()


def head_part(step, width):
    return pl.ds(pl.multiple_of((lax.axis_index("head") ^ step) * width, width), width)


def split_kernel(queries, *refs):
    outs, sems = refs[:-1], refs[-1]
    run([
        pltpu.make_async_copy(queries.at[:, head_part(step, out.shape[1])], out, sems.at[step])
        for step, out in enumerate(outs)
    ])


def join_kernel(keys, *refs):
    out, sems = refs[-2:]
    for i, (step, source) in enumerate(keys):
        @pl.when(lax.axis_index("sub") == source)
        def _():
            run([pltpu.make_async_copy(refs[i], out.at[:, head_part(step, refs[i].shape[1])], sems.at[0])])


def worker_places(low_ctx):
    return (low_ctx, 0), (low_ctx, 1), (low_ctx + 1, 1), (low_ctx + 1, 0)


def own_request(low_ctx):
    ctx, sub = lax.axis_index("ctx"), lax.axis_index("sub")
    found = jnp.int32(-1)
    for request, place in enumerate(worker_places(low_ctx)):
        found = jnp.where((ctx == place[0]) & (sub == place[1]), request, found)
    return found


def gather_kernel(low_ctx, sub_count, counts, own, far, paired, after, out):
    local_kv, most_pages = out.shape[:2]
    request = own_request(low_ctx)
    home_pair = (lax.axis_index("ctx") - low_ctx) * sub_count + lax.axis_index("sub")

    @pl.when(request >= 0)
    def _():
        start = jnp.int32(0)
        for r in range(REQS):
            start = start + jnp.where(r < request, counts[r], 0)
        count = counts[request]
        for p in range(most_pages):
            page = start + p
            pair = page // 2
            which = jnp.where(pair == home_pair, 0, jnp.where(pair == (home_pair ^ 1), 1, 2))
            page_rows = pl.ds(pl.multiple_of(lax.rem(page, 2) * PAGE, PAGE), PAGE)
            for n, ref in enumerate((own, paired, far)):
                @pl.when((p < count) & (which == n))
                def _():
                    for g in range(local_kv):
                        for i in range(2):
                            out[g, p, i] = ref[i, page_rows, g * HD:(g + 1) * HD]


def attend_kernel(low_ctx, sub_count, step, source_sub, waits, counts, pages_in, queries, *refs):
    out = refs[waits]
    head = lax.axis_index("head")
    tokens, width = queries.shape
    local_kv, most_pages = pages_in.shape[:2]
    span = width // local_kv
    per_group = span // HD
    rows = per_group * tokens
    first_token = ((head ^ step) * sub_count + source_sub) * tokens

    def attend(pages):
        token = lax.rem(lax.broadcasted_iota(jnp.int32, (rows, PAGE), 0), tokens)
        column = lax.broadcasted_iota(jnp.int32, (rows, PAGE), 1)
        visible = column <= PAGE - QR + first_token + token

        def scores_of(g):
            q_block = queries[:, g * span:(g + 1) * span]
            q_rows = jnp.concatenate([q_block[:, j * HD:(j + 1) * HD] for j in range(per_group)], axis=0)
            for p in range(pages):
                scores = lax.dot_general(
                    q_rows, pages_in[g, p, 0], (((1,), (1,)), ((), ())), preferred_element_type=jnp.float32
                )
                yield jnp.where(visible, scores, NEG) if p == pages - 1 else scores

        scores = list(scores_of(0))
        for g in range(local_kv):
            following = scores_of(g + 1) if g + 1 < local_kv else iter(())
            later = []
            top = jnp.max(functools.reduce(jnp.maximum, scores), axis=1, keepdims=True)
            totals, product = None, None
            for p in range(pages):
                later += [s for _, s in zip(range(1), following)]
                numerators = jnp.exp2((scores[p] - top) * EXP2_SCALE)
                part = jnp.dot(
                    numerators.astype(jnp.bfloat16), pages_in[g, p, 1], preferred_element_type=jnp.float32
                )
                totals = numerators if p == 0 else totals + numerators
                product = part if p == 0 else product + part
            totals = jnp.sum(totals, axis=1, keepdims=True)
            done = (product / totals).astype(jnp.bfloat16)
            out[:, g * span:(g + 1) * span] = jnp.concatenate(
                [done[j * tokens:(j + 1) * tokens] for j in range(per_group)], axis=1
            )
            scores = later

    request = own_request(low_ctx)

    @pl.when(request >= 0)
    def _():
        count = counts[request]
        for pages in [*range(1, most_pages - REQS + 3), most_pages]:
            @pl.when(count == pages)
            def _():
                attend(pages)


def one_request_each(queries, kv_cache, page_counts):
    ctx_size, sub_size = lax.axis_size("ctx"), lax.axis_size("sub")
    head_count = lax.axis_size("head")
    low_ctx = ctx_size // 2
    most_pages = kv_cache.shape[1] // PAGE * ctx_size * sub_size // 4
    local_kv = kv_cache.shape[2] // HD
    tokens, width = queries.shape[0], queries.shape[1] // head_count
    anywhere = pl.BlockSpec(memory_space=pl.ANY)
    in_vmem = pl.BlockSpec(memory_space=pltpu.VMEM)
    q_piece = pltpu.VMEM((tokens, width), queries.dtype)

    def vmem(array):
        return pltpu.with_memory_space_constraint(array, pltpu.VMEM)

    def hbm(array):
        return pltpu.with_memory_space_constraint(array, pltpu.HBM)

    def moved(array, routes):
        def flat(place):
            return (place[0] * head_count + place[1]) * sub_size + place[2]

        return lax.ppermute(array, ("ctx", "head", "sub"), [(flat(a), flat(b)) for a, b in routes])

    def worker(request, head):
        ctx, sub = worker_places(low_ctx)[request]
        return ctx, head, sub

    heads = range(head_count)
    q_out = pl.pallas_call(
        split_kernel,
        out_shape=[q_piece] * head_count,
        in_specs=[anywhere],
        out_specs=[anywhere] * head_count,
        scratch_shapes=[pltpu.SemaphoreType.DMA((head_count,))],
        compiler_params=pltpu.CompilerParams(vmem_limit_bytes=2**20),
        name="split",
    )(hbm(queries))
    routes = {
        (step, s): [((r, h, s), worker(r, h ^ step)) for r in range(ctx_size) for h in heads]
        for step in heads[::-1] for s in range(sub_size)
    }
    q_in = {key: moved(q_out[key[0]], pairs) for key, pairs in routes.items()}
    first = list(routes)[0]

    sends = [((low_ctx, sub_size - 1), worker_places(low_ctx)[2]), ((low_ctx + 1, 0), worker_places(low_ctx)[1])]
    far = moved(kv_cache, [((a[0], h, a[1]), (b[0], h, b[1])) for a, b in sends for h in heads])
    paired = moved(
        kv_cache, [((c, h, s), (c, h, 1 - s)) for c in range(low_ctx, ctx_size) for h in heads for s in range(sub_size)]
    )
    first_here = pl.pallas_call(
        lambda *refs: None,
        out_shape=pltpu.VMEM((8, HD), jnp.float32),
        in_specs=[anywhere] * 2,
        out_specs=anywhere,
        cost_estimate=pl.CostEstimate(flops=2 * 10**10, bytes_accessed=2**20, transcendentals=0),
        compiler_params=pltpu.CompilerParams(vmem_limit_bytes=2**20),
        name="first_here",
    )(vmem(q_in[first]), vmem(far))
    gathered = pl.pallas_call(
        functools.partial(gather_kernel, low_ctx, sub_size),
        out_shape=pltpu.VMEM((local_kv, most_pages, 2, PAGE, HD), kv_cache.dtype),
        in_specs=[pl.BlockSpec(memory_space=pltpu.SMEM)] + [in_vmem] * 3 + [anywhere],
        out_specs=in_vmem,
        compiler_params=pltpu.CompilerParams(vmem_limit_bytes=2**20),
        name="gather",
    )(page_counts, vmem(kv_cache), vmem(far), vmem(paired), vmem(first_here))

    back = {}
    after = []
    for step, s in routes:
        out = pl.pallas_call(
            functools.partial(attend_kernel, low_ctx, sub_size, step, s, len(after)),
            out_shape=q_piece,
            in_specs=[pl.BlockSpec(memory_space=pltpu.SMEM)] + [in_vmem] * 2 + [anywhere] * len(after),
            out_specs=in_vmem,
            compiler_params=pltpu.CompilerParams(vmem_limit_bytes=12 * 2**20),
            cost_estimate=pl.CostEstimate(flops=6 * 10**9, bytes_accessed=2**22, transcendentals=10**6),
            name=f"attend_{step}{s}",
        )(page_counts, vmem(gathered), vmem(q_in[step, s]), *after)
        back[step, s] = moved(out, [(b, a) for a, b in routes[step, s]])
        after = [out]

    joined = []
    for keys in [[key for key in routes if key[0]]] + [[key] for key in routes if not key[0]]:
        joined = [
            pl.pallas_call(
                functools.partial(join_kernel, keys),
                out_shape=pltpu.HBM(queries.shape, queries.dtype),
                in_specs=[anywhere] * (len(keys) + len(joined)),
                out_specs=anywhere,
                scratch_shapes=[pltpu.SemaphoreType.DMA((1,))],
                input_output_aliases={len(keys): 0} if joined else {},
                compiler_params=pltpu.CompilerParams(vmem_limit_bytes=2**20),
                name="join",
            )(*[vmem(back[key]) for key in keys], *map(hbm, joined))
        ]
    return joined[0]


def from_behind(array, axis, by):
    count = lax.axis_size(axis)
    pairs = [(i, i + by) for i in range(count) if 0 <= i + by < count]
    return lax.ppermute(array, axis, pairs)


def queries_to_pages(queries, kv_cache, page_counts):
    per_group = HQ // KVH
    local_heads = kv_cache.shape[2] // HD
    ctx_size = lax.axis_size("ctx")
    sub_size = lax.axis_size("sub")
    head_count = lax.axis_size("head")
    tok_rows = queries.shape[0]
    score_scale = HD ** (-0.5)
    regrouped = lax.all_to_all(queries, "head", split_axis=1, concat_axis=0, tiled=True)
    all_queries = lax.all_gather(regrouped, ("ctx", "sub"), axis=0, tiled=True)
    all_queries = all_queries.reshape(SPAN, local_heads, per_group, HD)
    page_ends = jnp.cumsum(page_counts)
    ctx_rows = SPAN // ctx_size
    offsets = jnp.arange(QR, dtype=jnp.int32)
    columns = jnp.arange(PAGE, dtype=jnp.int32)
    flat_index = lax.axis_index("ctx") * sub_size + lax.axis_index("sub")
    pages_here = kv_cache.shape[1] // PAGE
    base_pages = pages_here * ctx_size * sub_size // 2
    initial = (
        jnp.full((SPAN, local_heads, per_group), NEG, jnp.float32),
        jnp.zeros((SPAN, local_heads, per_group), jnp.float32),
        jnp.zeros((SPAN, local_heads, per_group, HD), jnp.float32),
    )
    half_rows = kv_cache.shape[1] // 2
    arrived = from_behind(kv_cache[:, half_rows:], "ctx", -(ctx_size // 2))
    is_lower = lax.axis_index("ctx") < ctx_size // 2
    source_flat = flat_index + ctx_size // 2 * sub_size
    working = jnp.where(is_lower, arrived, kv_cache[:, :half_rows])
    first_page = jnp.where(
        is_lower, source_flat * pages_here + pages_here // 2, flat_index * pages_here
    )
    page_total = working.shape[1] // PAGE

    def add_page(page_turn, running):
        page_index = first_page + page_turn
        relative = page_index - base_pages
        counted = jnp.sum((relative >= page_ends).astype(jnp.int32))
        request = jnp.where(relative < 0, REQS, counted)

        def update(partial_value):
            run_max, run_sum, run_out = partial_value
            request_id = jnp.minimum(request, REQS - 1)
            row_start = request_id * QR
            gathered = row_start + offsets
            within = gathered % ctx_rows
            ctx_block = gathered // ctx_rows
            sub_part = within // (head_count * tok_rows)
            head_part = within // tok_rows % head_count
            tok_part = within % tok_rows
            natural = ctx_block * ctx_rows + (head_part * sub_size + sub_part) * tok_rows + tok_part
            query_pos = (page_ends[request_id] + base_pages) * PAGE - QR + natural - row_start
            key_pos = page_index * PAGE + columns
            visible = key_pos[None, :] <= query_pos[:, None]
            page_keys = working[0].reshape(PAGE, local_heads, HD)
            page_values = working[1].reshape(PAGE, local_heads, HD)
            query_rows = lax.dynamic_slice_in_dim(all_queries, row_start, QR, 0)
            scores = (
                jnp.einsum(
                    "qkgd,pkd->qkgp", query_rows, page_keys, preferred_element_type=jnp.float32
                )
                * score_scale
            )
            scores = jnp.where(visible[:, None, None, :], scores, NEG)
            old_max = lax.dynamic_slice_in_dim(run_max, row_start, QR, 0)
            old_sum = lax.dynamic_slice_in_dim(run_sum, row_start, QR, 0)
            old_out = lax.dynamic_slice_in_dim(run_out, row_start, QR, 0)
            new_max = jnp.maximum(old_max, jnp.max(scores, axis=3))
            factor = jnp.exp(old_max - new_max)
            numerators = jnp.exp(scores - new_max[..., None])
            new_sum = old_sum * factor + jnp.sum(numerators, axis=3)
            product = jnp.einsum(
                "qkgp,pkd->qkgd",
                numerators.astype(jnp.bfloat16),
                page_values,
                preferred_element_type=jnp.float32,
            )
            new_out = old_out * factor[..., None] + product
            return (
                lax.dynamic_update_slice_in_dim(run_max, new_max, row_start, 0),
                lax.dynamic_update_slice_in_dim(run_sum, new_sum, row_start, 0),
                lax.dynamic_update_slice_in_dim(run_out, new_out, row_start, 0),
            )

        def unchanged(partial_value):
            return partial_value

        return lax.cond(request < REQS, update, unchanged, running)

    run_max, run_sum, run_out = lax.fori_loop(0, page_total, add_page, initial)
    share = SPAN // (ctx_size * sub_size)
    global_max = lax.pmax(run_max, ("ctx", "sub"))
    factor = jnp.exp(run_max - global_max)
    sums_here, outs_here = (
        lax.psum_scatter(
            (run_sum * factor).astype(jnp.bfloat16), ("ctx", "sub"), scatter_dimension=0, tiled=True
        ).astype(jnp.float32),
        lax.psum_scatter(
            (run_out * factor[..., None]).astype(jnp.bfloat16),
            ("ctx", "sub"),
            scatter_dimension=0,
            tiled=True,
        ).astype(jnp.float32),
    )
    finished = (outs_here / sums_here[..., None]).astype(jnp.bfloat16)
    finished = finished.reshape(share, local_heads * per_group * HD)
    return lax.all_to_all(finished, "head", split_axis=0, concat_axis=1, tiled=True)


def per_device(queries, kv_cache, page_counts):
    ctx_size, sub_size, head_count = lax.axis_size("ctx"), lax.axis_size("sub"), lax.axis_size("head")
    small = (
        ctx_size == REQS == 4
        and head_count == sub_size == 2
        and kv_cache.shape[1] == 2 * PAGE
        and kv_cache.shape[2] % (sub_size * HD) == 0
        and queries.shape[0] % 16 == 0
        and queries.shape[0] * head_count * sub_size == QR
    )
    return (one_request_each if small else queries_to_pages)(queries, kv_cache, page_counts)


def solution(mesh):
    return jax.shard_map(
        per_device,
        mesh=mesh,
        in_specs=(
            P(("grp", "ctx", "head", "sub"), None),
            P(None, ("grp", "ctx", "sub"), "head"),
            P("grp"),
        ),
        out_specs=P(("grp", "ctx", "head", "sub"), None),
        check_vma=False,
    )
```

```python
import functools

import jax
import jax.numpy as jnp
from jax import lax
from jax.experimental import pallas as pl
from jax.experimental.pallas import tpu as pltpu
from jax.sharding import PartitionSpec as P

HQ = 128
KVH = 8
HD = 128
REQS = 4
QR = 64
PAGE = 256
SPAN = 256


NEG = -1e30
EXP2_SCALE = HD ** (-0.5) * 1.4426950408889634


def run(copies):
    for copy in copies:
        copy.start()
    for copy in copies:
        copy.wait()


def head_part(step, width):
    return pl.ds(pl.multiple_of((lax.axis_index("head") ^ step) * width, width), width)


def split_kernel(queries, *refs):
    outs, sems = refs[:-1], refs[-1]
    run([
        pltpu.make_async_copy(queries.at[:, head_part(step, out.shape[1])], out, sems.at[step])
        for step, out in enumerate(outs)
    ])


def join_kernel(keys, *refs):
    out, sems = refs[-2:]

    @pl.when(lax.axis_index("sub") == keys[0][1])
    def _():
        run([
            pltpu.make_async_copy(piece, out.at[:, head_part(step, piece.shape[1])], sems.at[i])
            for i, (piece, (step, _)) in enumerate(zip(refs, keys))
        ])


def worker_places(low_ctx):
    return (0, 0), (low_ctx, 1), (low_ctx + 1, 0), (low_ctx + 1, 1)


def own_request(low_ctx):
    ctx, sub = lax.axis_index("ctx"), lax.axis_index("sub")
    found = jnp.int32(-1)
    for request, place in enumerate(worker_places(low_ctx)):
        found = jnp.where((ctx == place[0]) & (sub == place[1]), request, found)
    return found


def gather_kernel(low_ctx, counts, own, near, far, after, out, sems):
    local_kv, most_pages = out.shape[:2]
    request = own_request(low_ctx)

    @pl.when(request >= 0)
    def _():
        start = jnp.int32(0)
        for r in range(REQS):
            start = start + jnp.where(r < request, counts[r], 0)
        count = counts[request]
        near_pair = jnp.where(request == 0, 1, request ^ 1)
        home_pair = jnp.where(request == 0, -1, request)

        def of_page(p):
            page = start + p
            page_rows = pl.ds(pl.multiple_of(lax.rem(page, 2) * PAGE, PAGE), PAGE)
            return page // 2, page_rows

        def home_copies(p, page_rows):
            return [
                pltpu.make_async_copy(own.at[i, page_rows, pl.ds(g * HD, HD)], out.at[g, p, i], sems.at[g, p, i])
                for g in range(local_kv) for i in range(2)
            ]

        for p in range(most_pages):
            pair, page_rows = of_page(p)
            @pl.when((p < count) & (pair == home_pair))
            def _():
                for copy in home_copies(p, page_rows):
                    copy.start()
        for p in range(most_pages):
            pair, page_rows = of_page(p)
            for ref, chosen in ((near, pair == near_pair), (far, (pair != near_pair) & (pair != home_pair))):
                @pl.when((p < count) & chosen)
                def _():
                    for g in range(local_kv):
                        for i in range(2):
                            out[g, p, i] = ref[i, page_rows, g * HD:(g + 1) * HD]
        for p in range(most_pages):
            pair, page_rows = of_page(p)
            @pl.when((p < count) & (pair == home_pair))
            def _():
                for copy in home_copies(p, page_rows):
                    copy.wait()


def attend_kernel(low_ctx, sub_count, keys, waits, counts, pages_in, *refs):
    queries, outs = refs[:len(keys)], refs[len(keys) + waits:]
    head = lax.axis_index("head")
    tokens, width = queries[0].shape
    local_kv, most_pages = pages_in.shape[:2]
    span = width // local_kv
    per_group = span // HD
    piece_rows = per_group * tokens
    rows = len(keys) * piece_rows

    def attend(pages):
        row = lax.broadcasted_iota(jnp.int32, (rows, PAGE), 0)
        token = lax.rem(row, tokens)
        for i, (step, source) in enumerate(keys):
            first_token = ((head ^ step) * sub_count + source) * tokens
            token = jnp.where(row // piece_rows == i, token + first_token, token)
        column = lax.broadcasted_iota(jnp.int32, (rows, PAGE), 1)
        visible = column <= PAGE - QR + token

        def scores_of(g):
            q_blocks = [ref[:, g * span:(g + 1) * span] for ref in queries]
            q_rows = jnp.concatenate([q[:, j * HD:(j + 1) * HD] for q in q_blocks for j in range(per_group)], axis=0)
            for p in range(pages):
                scores = lax.dot_general(
                    q_rows, pages_in[g, p, 0], (((1,), (1,)), ((), ())), preferred_element_type=jnp.float32
                )
                yield jnp.where(visible, scores, NEG) if p == pages - 1 else scores

        scores = list(scores_of(0))
        for g in range(local_kv):
            following = scores_of(g + 1) if g + 1 < local_kv else iter(())
            later = []
            top = jnp.max(functools.reduce(jnp.maximum, scores), axis=1, keepdims=True)
            totals, product = None, None
            for p in range(pages):
                later += [s for _, s in zip(range(1), following)]
                numerators = jnp.exp2((scores[p] - top) * EXP2_SCALE)
                part = jnp.dot(
                    numerators.astype(jnp.bfloat16), pages_in[g, p, 1], preferred_element_type=jnp.float32
                )
                totals = numerators if p == 0 else totals + numerators
                product = part if p == 0 else product + part
            totals = jnp.sum(totals, axis=1, keepdims=True)
            done = (product / totals).astype(jnp.bfloat16)
            for i, out in enumerate(outs):
                start = i * piece_rows
                out[:, g * span:(g + 1) * span] = jnp.concatenate(
                    [done[start + j * tokens:start + (j + 1) * tokens] for j in range(per_group)], axis=1
                )
            scores = later

    request = own_request(low_ctx)

    @pl.when(request >= 0)
    def _():
        count = counts[request]
        for pages in [*range(1, most_pages - REQS + 3), most_pages]:
            @pl.when(count == pages)
            def _():
                attend(pages)


def one_request_each(queries, kv_cache, page_counts):
    ctx_size, sub_size = lax.axis_size("ctx"), lax.axis_size("sub")
    head_count = lax.axis_size("head")
    low_ctx = ctx_size // 2
    most_pages = kv_cache.shape[1] // PAGE * ctx_size * sub_size // 4
    local_kv = kv_cache.shape[2] // HD
    tokens, width = queries.shape[0], queries.shape[1] // head_count
    anywhere = pl.BlockSpec(memory_space=pl.ANY)
    in_vmem = pl.BlockSpec(memory_space=pltpu.VMEM)
    q_piece = pltpu.VMEM((tokens, width), queries.dtype)

    def vmem(array):
        return pltpu.with_memory_space_constraint(array, pltpu.VMEM)

    def hbm(array):
        return pltpu.with_memory_space_constraint(array, pltpu.HBM)

    def moved(array, routes):
        def flat(place):
            return (place[0] * head_count + place[1]) * sub_size + place[2]

        return lax.ppermute(array, ("ctx", "head", "sub"), [(flat(a), flat(b)) for a, b in routes])

    def worker(request, head):
        ctx, sub = worker_places(low_ctx)[request]
        return ctx, head, sub

    heads = range(head_count)
    q_out = pl.pallas_call(
        split_kernel,
        out_shape=[q_piece] * head_count,
        in_specs=[anywhere],
        out_specs=[anywhere] * head_count,
        scratch_shapes=[pltpu.SemaphoreType.DMA((head_count,))],
        compiler_params=pltpu.CompilerParams(vmem_limit_bytes=2**20),
        name="split",
    )(hbm(queries))
    routes = {
        (step, s): [((r, h, s), worker(r, h ^ step)) for r in range(ctx_size) for h in heads]
        for s in range(sub_size) for step in heads[::-1]
    }
    q_in = {key: moved(q_out[key[0]], pairs) for key, pairs in routes.items()}

    pairs = [(low_ctx + n // 2, n % 2) for n in range(4)]
    workers = worker_places(low_ctx)
    near, far = (
        moved(kv_cache, [((*a[:1], h, *a[1:]), (*b[:1], h, *b[1:])) for a, b in sends for h in heads])
        for sends in (
            [(pairs[0], workers[1]), (pairs[1], workers[0]), (pairs[2], workers[3]), (pairs[3], workers[2])],
            [(pairs[0], workers[0]), (pairs[1], workers[2]), (pairs[2], workers[1])],
        )
    )
    first_here = pl.pallas_call(
        lambda *refs: None,
        out_shape=pltpu.VMEM((8, HD), jnp.float32),
        in_specs=[anywhere],
        out_specs=anywhere,
        compiler_params=pltpu.CompilerParams(vmem_limit_bytes=2**20),
        name="first_here",
    )(vmem(q_in[list(routes)[0]]))
    gathered = pl.pallas_call(
        functools.partial(gather_kernel, low_ctx),
        out_shape=pltpu.VMEM((local_kv, most_pages, 2, PAGE, HD), kv_cache.dtype),
        in_specs=[pl.BlockSpec(memory_space=pltpu.SMEM), anywhere] + [in_vmem] * 2 + [anywhere],
        out_specs=in_vmem,
        scratch_shapes=[pltpu.SemaphoreType.DMA((local_kv, most_pages, 2))],
        compiler_params=pltpu.CompilerParams(vmem_limit_bytes=2**20),
        name="gather",
    )(hbm(page_counts), hbm(kv_cache), vmem(near), vmem(far), vmem(first_here))

    back = {}
    after = []
    groups = [[(step, s) for step in heads[::-1]] for s in range(sub_size)]
    for keys in groups:
        outs = pl.pallas_call(
            functools.partial(attend_kernel, low_ctx, sub_size, keys, len(after)),
            out_shape=[q_piece] * len(keys),
            in_specs=[pl.BlockSpec(memory_space=pltpu.SMEM)] + [in_vmem] * (1 + len(keys)) + [anywhere] * len(after),
            out_specs=[in_vmem] * len(keys),
            compiler_params=pltpu.CompilerParams(vmem_limit_bytes=12 * 2**20),
            cost_estimate=pl.CostEstimate(flops=10**10, bytes_accessed=2**22, transcendentals=10**6),
            name=f"attend_{keys[0][1]}",
        )(hbm(page_counts), vmem(gathered), *[vmem(q_in[key]) for key in keys], *after)
        for key, out in zip(keys, outs):
            back[key] = moved(out, [(b, a) for a, b in routes[key]])
        after = [outs[0]]

    joined = []
    for keys in groups:
        joined = [
            pl.pallas_call(
                functools.partial(join_kernel, keys),
                out_shape=pltpu.HBM(queries.shape, queries.dtype),
                in_specs=[anywhere] * (len(keys) + len(joined)),
                out_specs=anywhere,
                scratch_shapes=[pltpu.SemaphoreType.DMA((len(keys),))],
                input_output_aliases={len(keys): 0} if joined else {},
                compiler_params=pltpu.CompilerParams(vmem_limit_bytes=2**20),
                name=f"join_{keys[0][1]}",
            )(*[vmem(back[key]) for key in keys], *map(hbm, joined))
        ]
    return joined[0]


def from_behind(array, axis, by):
    count = lax.axis_size(axis)
    pairs = [(i, i + by) for i in range(count) if 0 <= i + by < count]
    return lax.ppermute(array, axis, pairs)


def queries_to_pages(queries, kv_cache, page_counts):
    per_group = HQ // KVH
    local_heads = kv_cache.shape[2] // HD
    ctx_size = lax.axis_size("ctx")
    sub_size = lax.axis_size("sub")
    head_count = lax.axis_size("head")
    tok_rows = queries.shape[0]
    score_scale = HD ** (-0.5)
    regrouped = lax.all_to_all(queries, "head", split_axis=1, concat_axis=0, tiled=True)
    all_queries = lax.all_gather(regrouped, ("ctx", "sub"), axis=0, tiled=True)
    all_queries = all_queries.reshape(SPAN, local_heads, per_group, HD)
    page_ends = jnp.cumsum(page_counts)
    ctx_rows = SPAN // ctx_size
    offsets = jnp.arange(QR, dtype=jnp.int32)
    columns = jnp.arange(PAGE, dtype=jnp.int32)
    flat_index = lax.axis_index("ctx") * sub_size + lax.axis_index("sub")
    pages_here = kv_cache.shape[1] // PAGE
    base_pages = pages_here * ctx_size * sub_size // 2
    initial = (
        jnp.full((SPAN, local_heads, per_group), NEG, jnp.float32),
        jnp.zeros((SPAN, local_heads, per_group), jnp.float32),
        jnp.zeros((SPAN, local_heads, per_group, HD), jnp.float32),
    )
    half_rows = kv_cache.shape[1] // 2
    arrived = from_behind(kv_cache[:, half_rows:], "ctx", -(ctx_size // 2))
    is_lower = lax.axis_index("ctx") < ctx_size // 2
    source_flat = flat_index + ctx_size // 2 * sub_size
    working = jnp.where(is_lower, arrived, kv_cache[:, :half_rows])
    first_page = jnp.where(
        is_lower, source_flat * pages_here + pages_here // 2, flat_index * pages_here
    )
    page_total = working.shape[1] // PAGE

    def add_page(page_turn, running):
        page_index = first_page + page_turn
        relative = page_index - base_pages
        counted = jnp.sum((relative >= page_ends).astype(jnp.int32))
        request = jnp.where(relative < 0, REQS, counted)

        def update(partial_value):
            run_max, run_sum, run_out = partial_value
            request_id = jnp.minimum(request, REQS - 1)
            row_start = request_id * QR
            gathered = row_start + offsets
            within = gathered % ctx_rows
            ctx_block = gathered // ctx_rows
            sub_part = within // (head_count * tok_rows)
            head_part = within // tok_rows % head_count
            tok_part = within % tok_rows
            natural = ctx_block * ctx_rows + (head_part * sub_size + sub_part) * tok_rows + tok_part
            query_pos = (page_ends[request_id] + base_pages) * PAGE - QR + natural - row_start
            key_pos = page_index * PAGE + columns
            visible = key_pos[None, :] <= query_pos[:, None]
            page_keys = working[0].reshape(PAGE, local_heads, HD)
            page_values = working[1].reshape(PAGE, local_heads, HD)
            query_rows = lax.dynamic_slice_in_dim(all_queries, row_start, QR, 0)
            scores = (
                jnp.einsum(
                    "qkgd,pkd->qkgp", query_rows, page_keys, preferred_element_type=jnp.float32
                )
                * score_scale
            )
            scores = jnp.where(visible[:, None, None, :], scores, NEG)
            old_max = lax.dynamic_slice_in_dim(run_max, row_start, QR, 0)
            old_sum = lax.dynamic_slice_in_dim(run_sum, row_start, QR, 0)
            old_out = lax.dynamic_slice_in_dim(run_out, row_start, QR, 0)
            new_max = jnp.maximum(old_max, jnp.max(scores, axis=3))
            factor = jnp.exp(old_max - new_max)
            numerators = jnp.exp(scores - new_max[..., None])
            new_sum = old_sum * factor + jnp.sum(numerators, axis=3)
            product = jnp.einsum(
                "qkgp,pkd->qkgd",
                numerators.astype(jnp.bfloat16),
                page_values,
                preferred_element_type=jnp.float32,
            )
            new_out = old_out * factor[..., None] + product
            return (
                lax.dynamic_update_slice_in_dim(run_max, new_max, row_start, 0),
                lax.dynamic_update_slice_in_dim(run_sum, new_sum, row_start, 0),
                lax.dynamic_update_slice_in_dim(run_out, new_out, row_start, 0),
            )

        def unchanged(partial_value):
            return partial_value

        return lax.cond(request < REQS, update, unchanged, running)

    run_max, run_sum, run_out = lax.fori_loop(0, page_total, add_page, initial)
    share = SPAN // (ctx_size * sub_size)
    global_max = lax.pmax(run_max, ("ctx", "sub"))
    factor = jnp.exp(run_max - global_max)
    sums_here, outs_here = (
        lax.psum_scatter(
            (run_sum * factor).astype(jnp.bfloat16), ("ctx", "sub"), scatter_dimension=0, tiled=True
        ).astype(jnp.float32),
        lax.psum_scatter(
            (run_out * factor[..., None]).astype(jnp.bfloat16),
            ("ctx", "sub"),
            scatter_dimension=0,
            tiled=True,
        ).astype(jnp.float32),
    )
    finished = (outs_here / sums_here[..., None]).astype(jnp.bfloat16)
    finished = finished.reshape(share, local_heads * per_group * HD)
    return lax.all_to_all(finished, "head", split_axis=0, concat_axis=1, tiled=True)


def per_device(queries, kv_cache, page_counts):
    ctx_size, sub_size, head_count = lax.axis_size("ctx"), lax.axis_size("sub"), lax.axis_size("head")
    small = (
        ctx_size == REQS == 4
        and head_count == sub_size == 2
        and kv_cache.shape[1] == 2 * PAGE
        and kv_cache.shape[2] % (sub_size * HD) == 0
        and queries.shape[0] % 16 == 0
        and queries.shape[0] * head_count * sub_size == QR
    )
    return (one_request_each if small else queries_to_pages)(queries, kv_cache, page_counts)


def solution(mesh):
    return jax.shard_map(
        per_device,
        mesh=mesh,
        in_specs=(
            P(("grp", "ctx", "head", "sub"), None),
            P(None, ("grp", "ctx", "sub"), "head"),
            P("grp"),
        ),
        out_specs=P(("grp", "ctx", "head", "sub"), None),
        check_vma=False,
    )
```

```python
import functools

import jax
import jax.numpy as jnp
from jax import lax
from jax.experimental import pallas as pl
from jax.experimental.pallas import tpu as pltpu
from jax.sharding import PartitionSpec as P

HQ = 128
KVH = 8
HD = 128
REQS = 4
QR = 64
PAGE = 256
SPAN = 256


NEG = -1e30
EXP2_SCALE = HD ** (-0.5) * 1.4426950408889634


def run(copies):
    for copy in copies:
        copy.start()
    for copy in copies:
        copy.wait()


def head_part(step, width):
    return pl.ds(pl.multiple_of((lax.axis_index("head") ^ step) * width, width), width)


def split_kernel(halves, queries, kv, *refs):
    outs, sems = refs[:-1], refs[-1]
    copies = []
    for i, out in enumerate(outs):
        if i < halves:
            source = kv.at[:, :, pl.ds(i * out.shape[2], out.shape[2])]
        else:
            source = queries.at[:, head_part(i - halves, out.shape[1])]
        copies.append(pltpu.make_async_copy(source, out, sems.at[i]))
    run(copies)


def join_kernel(keys, *refs):
    out, sems = refs[-2:]

    @pl.when(lax.axis_index("sub") == keys[0][1])
    def _():
        run([
            pltpu.make_async_copy(piece, out.at[:, head_part(step, piece.shape[1])], sems.at[i])
            for i, (piece, (step, _)) in enumerate(zip(refs, keys))
        ])


def worker_places(low_ctx):
    return (0, 0), (low_ctx, 1), (low_ctx + 1, 0), (low_ctx + 1, 1)


def own_request(low_ctx):
    ctx, sub = lax.axis_index("ctx"), lax.axis_index("sub")
    found = jnp.int32(-1)
    for request, place in enumerate(worker_places(low_ctx)):
        found = jnp.where((ctx == place[0]) & (sub == place[1]), request, found)
    return found


def gather_kernel(low_ctx, counts, own, near, far, after, out):
    local_kv, most_pages = out.shape[:2]
    request = own_request(low_ctx)

    @pl.when(request >= 0)
    def _():
        start = jnp.int32(0)
        for r in range(REQS):
            start = start + jnp.where(r < request, counts[r], 0)
        count = counts[request]
        near_pair = jnp.where(request == 0, 1, request ^ 1)
        home_pair = jnp.where(request == 0, -1, request)
        for p in range(most_pages):
            page = start + p
            pair = page // 2
            which = jnp.where(pair == home_pair, 0, jnp.where(pair == near_pair, 1, 2))
            page_rows = pl.ds(pl.multiple_of(lax.rem(page, 2) * PAGE, PAGE), PAGE)
            for n, ref in enumerate((own, near, far)):
                @pl.when((p < count) & (which == n))
                def _():
                    for g in range(local_kv):
                        for i in range(2):
                            out[g, p, i] = ref[i, page_rows, g * HD:(g + 1) * HD]


def attend_kernel(low_ctx, sub_count, keys, first_head, waits, counts, pages_in, *refs):
    queries, outs = refs[:len(keys)], refs[len(keys) + waits:]
    head = lax.axis_index("head")
    tokens, width = queries[0].shape
    local_kv, most_pages = pages_in.shape[:2]
    per_group = HQ // KVH
    span = per_group * HD
    piece_rows = per_group * tokens
    rows = len(keys) * piece_rows

    def attend(pages):
        row = lax.broadcasted_iota(jnp.int32, (rows, PAGE), 0)
        token = lax.rem(row, tokens)
        for i, (step, source) in enumerate(keys):
            first_token = ((head ^ step) * sub_count + source) * tokens
            token = jnp.where(row // piece_rows == i, token + first_token, token)
        column = lax.broadcasted_iota(jnp.int32, (rows, PAGE), 1)
        visible = column <= PAGE - QR + token

        def scores_of(g):
            q_blocks = [ref[:, (first_head + g) * span:(first_head + g + 1) * span] for ref in queries]
            q_rows = jnp.concatenate([q[:, j * HD:(j + 1) * HD] for q in q_blocks for j in range(per_group)], axis=0)
            for p in range(pages):
                scores = lax.dot_general(
                    q_rows, pages_in[g, p, 0], (((1,), (1,)), ((), ())), preferred_element_type=jnp.float32
                )
                yield jnp.where(visible, scores, NEG) if p == pages - 1 else scores

        scores = list(scores_of(0))
        for g in range(local_kv):
            following = scores_of(g + 1) if g + 1 < local_kv else iter(())
            later = []
            top = jnp.max(functools.reduce(jnp.maximum, scores), axis=1, keepdims=True)
            totals, product = None, None
            for p in range(pages):
                later += [s for _, s in zip(range(1), following)]
                numerators = jnp.exp2((scores[p] - top) * EXP2_SCALE)
                part = jnp.dot(
                    numerators.astype(jnp.bfloat16), pages_in[g, p, 1], preferred_element_type=jnp.float32
                )
                totals = numerators if p == 0 else totals + numerators
                product = part if p == 0 else product + part
            totals = jnp.sum(totals, axis=1, keepdims=True)
            done = (product / totals).astype(jnp.bfloat16)
            for i, out in enumerate(outs):
                start = i * piece_rows
                out[:, (first_head + g) * span:(first_head + g + 1) * span] = jnp.concatenate(
                    [done[start + j * tokens:start + (j + 1) * tokens] for j in range(per_group)], axis=1
                )
            scores = later

    request = own_request(low_ctx)

    @pl.when(request >= 0)
    def _():
        count = counts[request]
        for pages in [*range(1, most_pages - REQS + 3), most_pages]:
            @pl.when(count == pages)
            def _():
                attend(pages)


def one_request_each(queries, kv_cache, page_counts):
    ctx_size, sub_size = lax.axis_size("ctx"), lax.axis_size("sub")
    head_count = lax.axis_size("head")
    low_ctx = ctx_size // 2
    most_pages = kv_cache.shape[1] // PAGE * ctx_size * sub_size // 4
    local_kv = kv_cache.shape[2] // HD
    tokens, width = queries.shape[0], queries.shape[1] // head_count
    anywhere = pl.BlockSpec(memory_space=pl.ANY)
    in_vmem = pl.BlockSpec(memory_space=pltpu.VMEM)
    q_piece = pltpu.VMEM((tokens, width), queries.dtype)

    def vmem(array):
        return pltpu.with_memory_space_constraint(array, pltpu.VMEM)

    def hbm(array):
        return pltpu.with_memory_space_constraint(array, pltpu.HBM)

    def moved(array, routes):
        def flat(place):
            return (place[0] * head_count + place[1]) * sub_size + place[2]

        return lax.ppermute(array, ("ctx", "head", "sub"), [(flat(a), flat(b)) for a, b in routes])

    def worker(request, head):
        ctx, sub = worker_places(low_ctx)[request]
        return ctx, head, sub

    heads = range(head_count)
    halves = 2
    half = kv_cache.shape[2] // halves
    kv_piece = pltpu.VMEM((*kv_cache.shape[:2], half), kv_cache.dtype)
    parts = pl.pallas_call(
        functools.partial(split_kernel, halves),
        out_shape=[kv_piece] * halves + [q_piece] * head_count,
        in_specs=[anywhere] * 2,
        out_specs=[anywhere] * (halves + head_count),
        scratch_shapes=[pltpu.SemaphoreType.DMA((halves + head_count,))],
        compiler_params=pltpu.CompilerParams(vmem_limit_bytes=2**20),
        name="split",
    )(hbm(queries), hbm(kv_cache))
    kv_halves, q_out = parts[:halves], parts[halves:]
    routes = {
        (step, s): [((r, h, s), worker(r, h ^ step)) for r in range(ctx_size) for h in heads]
        for s in range(sub_size) for step in heads[::-1]
    }
    pairs = [(low_ctx + n // 2, n % 2) for n in range(4)]
    workers = worker_places(low_ctx)
    sends = (
        [(pairs[0], workers[1]), (pairs[1], workers[0]), (pairs[2], workers[3]), (pairs[3], workers[2])],
        [(pairs[0], workers[0]), (pairs[1], workers[2]), (pairs[2], workers[1])],
    )
    near_far = [
        [moved(part, [((*a[:1], h, *a[1:]), (*b[:1], h, *b[1:])) for a, b in some for h in heads]) for some in sends]
        for part in kv_halves
    ]
    *q_later, near_far[0][0] = lax.optimization_barrier((*q_out, near_far[0][0]))
    q_in = {(step, s): moved((q_later if s else q_out)[step], pairs) for (step, s), pairs in routes.items()}
    first_here = pl.pallas_call(
        lambda *refs: None,
        out_shape=pltpu.VMEM((8, HD), jnp.float32),
        in_specs=[anywhere],
        out_specs=anywhere,
        compiler_params=pltpu.CompilerParams(vmem_limit_bytes=2**20),
        name="first_here",
    )(vmem(q_in[list(routes)[0]]))
    groups = [[(step, s) for step in heads[::-1]] for s in range(sub_size)]
    back = {}
    outs = [[]] * len(groups)
    for i in range(halves):
        gathered = pl.pallas_call(
            functools.partial(gather_kernel, low_ctx),
            out_shape=pltpu.VMEM((local_kv // halves, most_pages, 2, PAGE, HD), kv_cache.dtype),
            in_specs=[pl.BlockSpec(memory_space=pltpu.SMEM)] + [in_vmem] * 3 + [anywhere],
            out_specs=in_vmem,
            compiler_params=pltpu.CompilerParams(vmem_limit_bytes=2**20),
            name=f"gather_{i}",
        )(hbm(page_counts), vmem(kv_halves[i]), *map(vmem, near_far[i]), vmem(outs[-1][0] if i else first_here))
        for n, keys in enumerate(groups):
            waits = [vmem(out) for out in outs[n]]
            outs[n] = pl.pallas_call(
                functools.partial(attend_kernel, low_ctx, sub_size, keys, i * local_kv // halves, len(waits)),
                out_shape=[q_piece] * len(keys),
                in_specs=(
                    [pl.BlockSpec(memory_space=pltpu.SMEM)] + [in_vmem] * (1 + len(keys)) + [anywhere] * len(waits)
                ),
                out_specs=[in_vmem] * len(keys),
                input_output_aliases={2 + len(keys) + k: k for k in range(len(waits))},
                compiler_params=pltpu.CompilerParams(vmem_limit_bytes=12 * 2**20),
                cost_estimate=pl.CostEstimate(flops=5 * 10**9, bytes_accessed=2**22, transcendentals=10**6),
                name=f"attend_{i}{n}",
            )(hbm(page_counts), vmem(gathered), *[vmem(q_in[key]) for key in keys], *waits)
            if i == halves - 1:
                for key, out in zip(keys, outs[n]):
                    back[key] = moved(out, [(b, a) for a, b in routes[key]])

    joined = []
    for keys in groups:
        joined = [
            pl.pallas_call(
                functools.partial(join_kernel, keys),
                out_shape=pltpu.HBM(queries.shape, queries.dtype),
                in_specs=[anywhere] * (len(keys) + len(joined)),
                out_specs=anywhere,
                scratch_shapes=[pltpu.SemaphoreType.DMA((len(keys),))],
                input_output_aliases={len(keys): 0} if joined else {},
                compiler_params=pltpu.CompilerParams(vmem_limit_bytes=2**20),
                name=f"join_{keys[0][1]}",
            )(*[vmem(back[key]) for key in keys], *map(hbm, joined))
        ]
    return joined[0]


def from_behind(array, axis, by):
    count = lax.axis_size(axis)
    pairs = [(i, i + by) for i in range(count) if 0 <= i + by < count]
    return lax.ppermute(array, axis, pairs)


def queries_to_pages(queries, kv_cache, page_counts):
    per_group = HQ // KVH
    local_heads = kv_cache.shape[2] // HD
    ctx_size = lax.axis_size("ctx")
    sub_size = lax.axis_size("sub")
    head_count = lax.axis_size("head")
    tok_rows = queries.shape[0]
    score_scale = HD ** (-0.5)
    regrouped = lax.all_to_all(queries, "head", split_axis=1, concat_axis=0, tiled=True)
    all_queries = lax.all_gather(regrouped, ("ctx", "sub"), axis=0, tiled=True)
    all_queries = all_queries.reshape(SPAN, local_heads, per_group, HD)
    page_ends = jnp.cumsum(page_counts)
    ctx_rows = SPAN // ctx_size
    offsets = jnp.arange(QR, dtype=jnp.int32)
    columns = jnp.arange(PAGE, dtype=jnp.int32)
    flat_index = lax.axis_index("ctx") * sub_size + lax.axis_index("sub")
    pages_here = kv_cache.shape[1] // PAGE
    base_pages = pages_here * ctx_size * sub_size // 2
    initial = (
        jnp.full((SPAN, local_heads, per_group), NEG, jnp.float32),
        jnp.zeros((SPAN, local_heads, per_group), jnp.float32),
        jnp.zeros((SPAN, local_heads, per_group, HD), jnp.float32),
    )
    half_rows = kv_cache.shape[1] // 2
    arrived = from_behind(kv_cache[:, half_rows:], "ctx", -(ctx_size // 2))
    is_lower = lax.axis_index("ctx") < ctx_size // 2
    source_flat = flat_index + ctx_size // 2 * sub_size
    working = jnp.where(is_lower, arrived, kv_cache[:, :half_rows])
    first_page = jnp.where(
        is_lower, source_flat * pages_here + pages_here // 2, flat_index * pages_here
    )
    page_total = working.shape[1] // PAGE

    def add_page(page_turn, running):
        page_index = first_page + page_turn
        relative = page_index - base_pages
        counted = jnp.sum((relative >= page_ends).astype(jnp.int32))
        request = jnp.where(relative < 0, REQS, counted)

        def update(partial_value):
            run_max, run_sum, run_out = partial_value
            request_id = jnp.minimum(request, REQS - 1)
            row_start = request_id * QR
            gathered = row_start + offsets
            within = gathered % ctx_rows
            ctx_block = gathered // ctx_rows
            sub_part = within // (head_count * tok_rows)
            head_part = within // tok_rows % head_count
            tok_part = within % tok_rows
            natural = ctx_block * ctx_rows + (head_part * sub_size + sub_part) * tok_rows + tok_part
            query_pos = (page_ends[request_id] + base_pages) * PAGE - QR + natural - row_start
            key_pos = page_index * PAGE + columns
            visible = key_pos[None, :] <= query_pos[:, None]
            page_keys = working[0].reshape(PAGE, local_heads, HD)
            page_values = working[1].reshape(PAGE, local_heads, HD)
            query_rows = lax.dynamic_slice_in_dim(all_queries, row_start, QR, 0)
            scores = (
                jnp.einsum(
                    "qkgd,pkd->qkgp", query_rows, page_keys, preferred_element_type=jnp.float32
                )
                * score_scale
            )
            scores = jnp.where(visible[:, None, None, :], scores, NEG)
            old_max = lax.dynamic_slice_in_dim(run_max, row_start, QR, 0)
            old_sum = lax.dynamic_slice_in_dim(run_sum, row_start, QR, 0)
            old_out = lax.dynamic_slice_in_dim(run_out, row_start, QR, 0)
            new_max = jnp.maximum(old_max, jnp.max(scores, axis=3))
            factor = jnp.exp(old_max - new_max)
            numerators = jnp.exp(scores - new_max[..., None])
            new_sum = old_sum * factor + jnp.sum(numerators, axis=3)
            product = jnp.einsum(
                "qkgp,pkd->qkgd",
                numerators.astype(jnp.bfloat16),
                page_values,
                preferred_element_type=jnp.float32,
            )
            new_out = old_out * factor[..., None] + product
            return (
                lax.dynamic_update_slice_in_dim(run_max, new_max, row_start, 0),
                lax.dynamic_update_slice_in_dim(run_sum, new_sum, row_start, 0),
                lax.dynamic_update_slice_in_dim(run_out, new_out, row_start, 0),
            )

        def unchanged(partial_value):
            return partial_value

        return lax.cond(request < REQS, update, unchanged, running)

    run_max, run_sum, run_out = lax.fori_loop(0, page_total, add_page, initial)
    share = SPAN // (ctx_size * sub_size)
    global_max = lax.pmax(run_max, ("ctx", "sub"))
    factor = jnp.exp(run_max - global_max)
    sums_here, outs_here = (
        lax.psum_scatter(
            (run_sum * factor).astype(jnp.bfloat16), ("ctx", "sub"), scatter_dimension=0, tiled=True
        ).astype(jnp.float32),
        lax.psum_scatter(
            (run_out * factor[..., None]).astype(jnp.bfloat16),
            ("ctx", "sub"),
            scatter_dimension=0,
            tiled=True,
        ).astype(jnp.float32),
    )
    finished = (outs_here / sums_here[..., None]).astype(jnp.bfloat16)
    finished = finished.reshape(share, local_heads * per_group * HD)
    return lax.all_to_all(finished, "head", split_axis=0, concat_axis=1, tiled=True)


def per_device(queries, kv_cache, page_counts):
    ctx_size, sub_size, head_count = lax.axis_size("ctx"), lax.axis_size("sub"), lax.axis_size("head")
    small = (
        ctx_size == REQS == 4
        and head_count == sub_size == 2
        and kv_cache.shape[1] == 2 * PAGE
        and kv_cache.shape[2] % (sub_size * HD) == 0
        and queries.shape[0] % 16 == 0
        and queries.shape[0] * head_count * sub_size == QR
    )
    return (one_request_each if small else queries_to_pages)(queries, kv_cache, page_counts)


def solution(mesh):
    return jax.shard_map(
        per_device,
        mesh=mesh,
        in_specs=(
            P(("grp", "ctx", "head", "sub"), None),
            P(None, ("grp", "ctx", "sub"), "head"),
            P("grp"),
        ),
        out_specs=P(("grp", "ctx", "head", "sub"), None),
        check_vma=False,
    )
```

```python
import functools

import jax
import jax.numpy as jnp
from jax import lax
from jax.experimental import pallas as pl
from jax.experimental.pallas import tpu as pltpu
from jax.sharding import PartitionSpec as P

HQ = 128
KVH = 8
HD = 128
REQS = 4
QR = 64
PAGE = 256
SPAN = 256


NEG = -1e30
EXP2_SCALE = HD ** (-0.5) * 1.4426950408889634


def run(copies):
    for copy in copies:
        copy.start()
    for copy in copies:
        copy.wait()


def head_part(step, width):
    return pl.ds(pl.multiple_of((lax.axis_index("head") ^ step) * width, width), width)


def split_kernel(halves, queries, kv, *refs):
    outs, sems = refs[:-1], refs[-1]
    copies = []
    for i, out in enumerate(outs):
        if i < halves:
            source = kv.at[:, :, pl.ds(i * out.shape[2], out.shape[2])]
        else:
            source = queries.at[:, head_part(i - halves, out.shape[1])]
        copies.append(pltpu.make_async_copy(source, out, sems.at[i]))
    run(copies)


def join_kernel(keys, *refs):
    out, sems = refs[-2:]

    @pl.when(lax.axis_index("sub") == keys[0][1])
    def _():
        run([
            pltpu.make_async_copy(piece, out.at[:, head_part(step, piece.shape[1])], sems.at[i])
            for i, (piece, (step, _)) in enumerate(zip(refs, keys))
        ])


def worker_places(low_ctx):
    return (0, 0), (low_ctx, 1), (low_ctx + 1, 0), (low_ctx + 1, 1)


def own_request(low_ctx):
    ctx, sub = lax.axis_index("ctx"), lax.axis_index("sub")
    found = jnp.int32(-1)
    for request, place in enumerate(worker_places(low_ctx)):
        found = jnp.where((ctx == place[0]) & (sub == place[1]), request, found)
    return found


def gather_kernel(low_ctx, counts, own, near, far, after, out):
    local_kv, most_pages = out.shape[:2]
    request = own_request(low_ctx)

    @pl.when(request >= 0)
    def _():
        start = jnp.int32(0)
        for r in range(REQS):
            start = start + jnp.where(r < request, counts[r], 0)
        count = counts[request]
        near_pair = jnp.where(request == 0, 1, request ^ 1)
        home_pair = jnp.where(request == 0, -1, request)
        for p in range(most_pages):
            page = start + p
            pair = page // 2
            which = jnp.where(pair == home_pair, 0, jnp.where(pair == near_pair, 1, 2))
            page_rows = pl.ds(pl.multiple_of(lax.rem(page, 2) * PAGE, PAGE), PAGE)
            for n, ref in enumerate((own, near, far)):
                @pl.when((p < count) & (which == n))
                def _():
                    for g in range(local_kv):
                        for i in range(2):
                            out[g, p, i] = ref[i, page_rows, g * HD:(g + 1) * HD]


def attend_kernel(low_ctx, sub_count, keys, first_head, waits, counts, pages_in, *refs):
    queries, outs = refs[:len(keys)], refs[len(keys) + waits:]
    head = lax.axis_index("head")
    tokens, width = queries[0].shape
    local_kv, most_pages = pages_in.shape[:2]
    per_group = HQ // KVH
    span = per_group * HD
    piece_rows = per_group * tokens
    rows = len(keys) * piece_rows

    def attend(pages):
        row = lax.broadcasted_iota(jnp.int32, (rows, PAGE), 0)
        token = lax.rem(row, tokens)
        for i, (step, source) in enumerate(keys):
            first_token = ((head ^ step) * sub_count + source) * tokens
            token = jnp.where(row // piece_rows == i, token + first_token, token)
        column = lax.broadcasted_iota(jnp.int32, (rows, PAGE), 1)
        visible = column <= PAGE - QR + token

        def scores_of(g):
            q_blocks = [ref[:, (first_head + g) * span:(first_head + g + 1) * span] for ref in queries]
            q_rows = jnp.concatenate([q[:, j * HD:(j + 1) * HD] for q in q_blocks for j in range(per_group)], axis=0)
            for p in range(pages):
                scores = lax.dot_general(
                    q_rows, pages_in[g, p, 0], (((1,), (1,)), ((), ())), preferred_element_type=jnp.float32
                )
                yield jnp.where(visible, scores, NEG) if p == pages - 1 else scores

        scores = list(scores_of(0))
        for g in range(local_kv):
            following = scores_of(g + 1) if g + 1 < local_kv else iter(())
            later = []
            top = jnp.max(functools.reduce(jnp.maximum, scores), axis=1, keepdims=True)
            totals, product = None, None
            for p in range(pages):
                later += [s for _, s in zip(range(1), following)]
                numerators = jnp.exp2((scores[p] - top) * EXP2_SCALE)
                part = jnp.dot(
                    numerators.astype(jnp.bfloat16), pages_in[g, p, 1], preferred_element_type=jnp.float32
                )
                totals = numerators if p == 0 else totals + numerators
                product = part if p == 0 else product + part
            totals = jnp.sum(totals, axis=1, keepdims=True)
            done = (product / totals).astype(jnp.bfloat16)
            for i, out in enumerate(outs):
                start = i * piece_rows
                out[:, (first_head + g) * span:(first_head + g + 1) * span] = jnp.concatenate(
                    [done[start + j * tokens:start + (j + 1) * tokens] for j in range(per_group)], axis=1
                )
            scores = later

    request = own_request(low_ctx)

    @pl.when(request >= 0)
    def _():
        count = counts[request]
        for pages in [*range(1, most_pages - REQS + 3), most_pages]:
            @pl.when(count == pages)
            def _():
                attend(pages)


def one_request_each(queries, kv_cache, page_counts):
    ctx_size, sub_size = lax.axis_size("ctx"), lax.axis_size("sub")
    head_count = lax.axis_size("head")
    low_ctx = ctx_size // 2
    most_pages = kv_cache.shape[1] // PAGE * ctx_size * sub_size // 4
    local_kv = kv_cache.shape[2] // HD
    tokens, width = queries.shape[0], queries.shape[1] // head_count
    anywhere = pl.BlockSpec(memory_space=pl.ANY)
    in_vmem = pl.BlockSpec(memory_space=pltpu.VMEM)
    q_piece = pltpu.VMEM((tokens, width), queries.dtype)

    def vmem(array):
        return pltpu.with_memory_space_constraint(array, pltpu.VMEM)

    def hbm(array):
        return pltpu.with_memory_space_constraint(array, pltpu.HBM)

    def moved(array, routes):
        def flat(place):
            return (place[0] * head_count + place[1]) * sub_size + place[2]

        return lax.ppermute(array, ("ctx", "head", "sub"), [(flat(a), flat(b)) for a, b in routes])

    def worker(request, head):
        ctx, sub = worker_places(low_ctx)[request]
        return ctx, head, sub

    heads = range(head_count)
    halves = 2
    half = kv_cache.shape[2] // halves
    kv_piece = pltpu.VMEM((*kv_cache.shape[:2], half), kv_cache.dtype)
    parts = pl.pallas_call(
        functools.partial(split_kernel, halves),
        out_shape=[kv_piece] * halves + [q_piece] * head_count,
        in_specs=[anywhere] * 2,
        out_specs=[anywhere] * (halves + head_count),
        scratch_shapes=[pltpu.SemaphoreType.DMA((halves + head_count,))],
        compiler_params=pltpu.CompilerParams(vmem_limit_bytes=2**20),
        name="split",
    )(hbm(queries), hbm(kv_cache))
    kv_halves, q_out = parts[:halves], parts[halves:]
    routes = {
        (step, s): [((r, h, s), worker(r, h ^ step)) for r in range(ctx_size) for h in heads]
        for s in range(sub_size) for step in heads[::-1]
    }
    pairs = [(low_ctx + n // 2, n % 2) for n in range(4)]
    workers = worker_places(low_ctx)
    sends = (
        [(pairs[0], workers[1]), (pairs[1], workers[0]), (pairs[2], workers[3]), (pairs[3], workers[2])],
        [(pairs[0], workers[0]), (pairs[1], workers[2]), (pairs[2], workers[1])],
    )
    near_far = [
        [moved(part, [((*a[:1], h, *a[1:]), (*b[:1], h, *b[1:])) for a, b in some for h in heads]) for some in sends]
        for part in kv_halves
    ]
    q_in = {key: moved(q_out[key[0]], pairs) for key, pairs in routes.items()}
    first_here = pl.pallas_call(
        lambda *refs: None,
        out_shape=pltpu.VMEM((8, HD), jnp.float32),
        in_specs=[anywhere],
        out_specs=anywhere,
        compiler_params=pltpu.CompilerParams(vmem_limit_bytes=2**20),
        name="first_here",
    )(vmem(q_in[list(routes)[0]]))
    groups = [[(step, s) for step in heads[::-1]] for s in range(sub_size)]
    back = {}
    outs = [[]] * len(groups)
    for i in range(halves):
        gathered = pl.pallas_call(
            functools.partial(gather_kernel, low_ctx),
            out_shape=pltpu.VMEM((local_kv // halves, most_pages, 2, PAGE, HD), kv_cache.dtype),
            in_specs=[pl.BlockSpec(memory_space=pltpu.SMEM)] + [in_vmem] * 3 + [anywhere],
            out_specs=in_vmem,
            compiler_params=pltpu.CompilerParams(vmem_limit_bytes=2**20),
            name=f"gather_{i}",
        )(hbm(page_counts), vmem(kv_halves[i]), *map(vmem, near_far[i]), vmem(outs[-1][0] if i else first_here))
        for n, keys in enumerate(groups):
            waits = [vmem(out) for out in outs[n]]
            outs[n] = pl.pallas_call(
                functools.partial(attend_kernel, low_ctx, sub_size, keys, i * local_kv // halves, len(waits)),
                out_shape=[q_piece] * len(keys),
                in_specs=(
                    [pl.BlockSpec(memory_space=pltpu.SMEM)] + [in_vmem] * (1 + len(keys)) + [anywhere] * len(waits)
                ),
                out_specs=[in_vmem] * len(keys),
                input_output_aliases={2 + len(keys) + k: k for k in range(len(waits))},
                compiler_params=pltpu.CompilerParams(vmem_limit_bytes=12 * 2**20),
                cost_estimate=pl.CostEstimate(flops=5 * 10**9, bytes_accessed=2**22, transcendentals=10**6),
                name=f"attend_{i}{n}",
            )(hbm(page_counts), vmem(gathered), *[vmem(q_in[key]) for key in keys], *waits)
            if i == halves - 1:
                for key, out in zip(keys, outs[n]):
                    back[key] = moved(out, [(b, a) for a, b in routes[key]])

    joined = []
    for keys in groups:
        joined = [
            pl.pallas_call(
                functools.partial(join_kernel, keys),
                out_shape=pltpu.HBM(queries.shape, queries.dtype),
                in_specs=[anywhere] * (len(keys) + len(joined)),
                out_specs=anywhere,
                scratch_shapes=[pltpu.SemaphoreType.DMA((len(keys),))],
                input_output_aliases={len(keys): 0} if joined else {},
                compiler_params=pltpu.CompilerParams(vmem_limit_bytes=2**20),
                name=f"join_{keys[0][1]}",
            )(*[vmem(back[key]) for key in keys], *map(hbm, joined))
        ]
    return joined[0]


def from_behind(array, axis, by):
    count = lax.axis_size(axis)
    pairs = [(i, i + by) for i in range(count) if 0 <= i + by < count]
    return lax.ppermute(array, axis, pairs)


def queries_to_pages(queries, kv_cache, page_counts):
    per_group = HQ // KVH
    local_heads = kv_cache.shape[2] // HD
    ctx_size = lax.axis_size("ctx")
    sub_size = lax.axis_size("sub")
    head_count = lax.axis_size("head")
    tok_rows = queries.shape[0]
    score_scale = HD ** (-0.5)
    regrouped = lax.all_to_all(queries, "head", split_axis=1, concat_axis=0, tiled=True)
    all_queries = lax.all_gather(regrouped, ("ctx", "sub"), axis=0, tiled=True)
    all_queries = all_queries.reshape(SPAN, local_heads, per_group, HD)
    page_ends = jnp.cumsum(page_counts)
    ctx_rows = SPAN // ctx_size
    offsets = jnp.arange(QR, dtype=jnp.int32)
    columns = jnp.arange(PAGE, dtype=jnp.int32)
    flat_index = lax.axis_index("ctx") * sub_size + lax.axis_index("sub")
    pages_here = kv_cache.shape[1] // PAGE
    base_pages = pages_here * ctx_size * sub_size // 2
    initial = (
        jnp.full((SPAN, local_heads, per_group), NEG, jnp.float32),
        jnp.zeros((SPAN, local_heads, per_group), jnp.float32),
        jnp.zeros((SPAN, local_heads, per_group, HD), jnp.float32),
    )
    half_rows = kv_cache.shape[1] // 2
    arrived = from_behind(kv_cache[:, half_rows:], "ctx", -(ctx_size // 2))
    is_lower = lax.axis_index("ctx") < ctx_size // 2
    source_flat = flat_index + ctx_size // 2 * sub_size
    working = jnp.where(is_lower, arrived, kv_cache[:, :half_rows])
    first_page = jnp.where(
        is_lower, source_flat * pages_here + pages_here // 2, flat_index * pages_here
    )
    page_total = working.shape[1] // PAGE

    def add_page(page_turn, running):
        page_index = first_page + page_turn
        relative = page_index - base_pages
        counted = jnp.sum((relative >= page_ends).astype(jnp.int32))
        request = jnp.where(relative < 0, REQS, counted)

        def update(partial_value):
            run_max, run_sum, run_out = partial_value
            request_id = jnp.minimum(request, REQS - 1)
            row_start = request_id * QR
            gathered = row_start + offsets
            within = gathered % ctx_rows
            ctx_block = gathered // ctx_rows
            sub_part = within // (head_count * tok_rows)
            head_part = within // tok_rows % head_count
            tok_part = within % tok_rows
            natural = ctx_block * ctx_rows + (head_part * sub_size + sub_part) * tok_rows + tok_part
            query_pos = (page_ends[request_id] + base_pages) * PAGE - QR + natural - row_start
            key_pos = page_index * PAGE + columns
            visible = key_pos[None, :] <= query_pos[:, None]
            page_keys = working[0].reshape(PAGE, local_heads, HD)
            page_values = working[1].reshape(PAGE, local_heads, HD)
            query_rows = lax.dynamic_slice_in_dim(all_queries, row_start, QR, 0)
            scores = (
                jnp.einsum(
                    "qkgd,pkd->qkgp", query_rows, page_keys, preferred_element_type=jnp.float32
                )
                * score_scale
            )
            scores = jnp.where(visible[:, None, None, :], scores, NEG)
            old_max = lax.dynamic_slice_in_dim(run_max, row_start, QR, 0)
            old_sum = lax.dynamic_slice_in_dim(run_sum, row_start, QR, 0)
            old_out = lax.dynamic_slice_in_dim(run_out, row_start, QR, 0)
            new_max = jnp.maximum(old_max, jnp.max(scores, axis=3))
            factor = jnp.exp(old_max - new_max)
            numerators = jnp.exp(scores - new_max[..., None])
            new_sum = old_sum * factor + jnp.sum(numerators, axis=3)
            product = jnp.einsum(
                "qkgp,pkd->qkgd",
                numerators.astype(jnp.bfloat16),
                page_values,
                preferred_element_type=jnp.float32,
            )
            new_out = old_out * factor[..., None] + product
            return (
                lax.dynamic_update_slice_in_dim(run_max, new_max, row_start, 0),
                lax.dynamic_update_slice_in_dim(run_sum, new_sum, row_start, 0),
                lax.dynamic_update_slice_in_dim(run_out, new_out, row_start, 0),
            )

        def unchanged(partial_value):
            return partial_value

        return lax.cond(request < REQS, update, unchanged, running)

    run_max, run_sum, run_out = lax.fori_loop(0, page_total, add_page, initial)
    share = SPAN // (ctx_size * sub_size)
    global_max = lax.pmax(run_max, ("ctx", "sub"))
    factor = jnp.exp(run_max - global_max)
    sums_here, outs_here = (
        lax.psum_scatter(
            (run_sum * factor).astype(jnp.bfloat16), ("ctx", "sub"), scatter_dimension=0, tiled=True
        ).astype(jnp.float32),
        lax.psum_scatter(
            (run_out * factor[..., None]).astype(jnp.bfloat16),
            ("ctx", "sub"),
            scatter_dimension=0,
            tiled=True,
        ).astype(jnp.float32),
    )
    finished = (outs_here / sums_here[..., None]).astype(jnp.bfloat16)
    finished = finished.reshape(share, local_heads * per_group * HD)
    return lax.all_to_all(finished, "head", split_axis=0, concat_axis=1, tiled=True)


def per_device(queries, kv_cache, page_counts):
    ctx_size, sub_size, head_count = lax.axis_size("ctx"), lax.axis_size("sub"), lax.axis_size("head")
    small = (
        ctx_size == REQS == 4
        and head_count == sub_size == 2
        and kv_cache.shape[1] == 2 * PAGE
        and kv_cache.shape[2] % (sub_size * HD) == 0
        and queries.shape[0] % 16 == 0
        and queries.shape[0] * head_count * sub_size == QR
    )
    return (one_request_each if small else queries_to_pages)(queries, kv_cache, page_counts)


def solution(mesh):
    return jax.shard_map(
        per_device,
        mesh=mesh,
        in_specs=(
            P(("grp", "ctx", "head", "sub"), None),
            P(None, ("grp", "ctx", "sub"), "head"),
            P("grp"),
        ),
        out_specs=P(("grp", "ctx", "head", "sub"), None),
        check_vma=False,
    )
```

```python
import functools

import jax
import jax.numpy as jnp
from jax import lax
from jax.experimental import pallas as pl
from jax.experimental.pallas import tpu as pltpu
from jax.sharding import PartitionSpec as P

HQ = 128
KVH = 8
HD = 128
REQS = 4
QR = 64
PAGE = 256
SPAN = 256


NEG = -1e30
EXP2_SCALE = HD ** (-0.5) * 1.4426950408889634


def run(copies):
    for copy in copies:
        copy.start()
    for copy in copies:
        copy.wait()


def head_part(step, width):
    return pl.ds(pl.multiple_of((lax.axis_index("head") ^ step) * width, width), width)


def split_kernel(queries, *refs):
    outs, sems = refs[:-1], refs[-1]
    run([
        pltpu.make_async_copy(queries.at[:, head_part(step, out.shape[1])], out, sems.at[step])
        for step, out in enumerate(outs)
    ])


def join_kernel(keys, *refs):
    out, sems = refs[-2:]

    @pl.when(lax.axis_index("sub") == keys[0][1])
    def _():
        run([
            pltpu.make_async_copy(piece, out.at[:, head_part(step, piece.shape[1])], sems.at[i])
            for i, (piece, (step, _)) in enumerate(zip(refs, keys))
        ])


def worker_places(low_ctx):
    return (0, 0), (low_ctx, 1), (low_ctx + 1, 0), (low_ctx + 1, 1)


def own_request(low_ctx):
    ctx, sub = lax.axis_index("ctx"), lax.axis_index("sub")
    found = jnp.int32(-1)
    for request, place in enumerate(worker_places(low_ctx)):
        found = jnp.where((ctx == place[0]) & (sub == place[1]), request, found)
    return found


def pages_of(low_ctx, counts, most_pages):
    request = own_request(low_ctx)
    start = jnp.int32(0)
    for r in range(REQS):
        start = start + jnp.where(r < request, counts[r], 0)
    count = jnp.where(request >= 0, counts[jnp.maximum(request, 0)], 0)
    home_pair = jnp.where(request == 0, -1, request)
    near_pair = jnp.where(request == 0, 1, request ^ 1)
    for p in range(most_pages):
        page = start + p
        pair = page // 2
        which = jnp.where(pair == home_pair, 0, jnp.where(pair == near_pair, 1, 2))
        yield p, p < count, which, pl.ds(pl.multiple_of(lax.rem(page, 2) * PAGE, PAGE), PAGE)


def gather_home_kernel(low_ctx, counts, counts_in, own, after, out, counts_out, sems, counts_sem):
    local_kv, most_pages = out.shape[:2]
    counts_copy = pltpu.make_async_copy(counts_in, counts_out, counts_sem)
    counts_copy.start()
    plan = [
        (here & (which == 0), [
            pltpu.make_async_copy(own.at[i, rows, pl.ds(g * HD, HD)], out.at[g, p, i], sems.at[g, p, i])
            for g in range(local_kv) for i in range(2)
        ])
        for p, here, which, rows in pages_of(low_ctx, counts, most_pages)
    ]
    for here, copies in plan:
        @pl.when(here)
        def _():
            for copy in copies:
                copy.start()
    for here, copies in plan:
        @pl.when(here)
        def _():
            for copy in copies:
                copy.wait()
    counts_copy.wait()


def gather_rest_kernel(low_ctx, counts, near, far, home, out):
    local_kv, most_pages = out.shape[:2]
    for p, here, which, rows in pages_of(low_ctx, counts, most_pages):
        for n, ref in enumerate((near, far)):
            @pl.when(here & (which == n + 1))
            def _():
                for g in range(local_kv):
                    for i in range(2):
                        out[g, p, i] = ref[i, rows, g * HD:(g + 1) * HD]


def attend_kernel(low_ctx, sub_count, groups, waits, counts, pages_in, *refs):
    keys = [key for group in groups for key in group]
    queries, outs = dict(zip(keys, refs)), dict(zip(keys, refs[len(keys) + waits:]))
    head = lax.axis_index("head")
    tokens, width = refs[0].shape
    local_kv, most_pages = pages_in.shape[:2]
    span = width // local_kv
    per_group = span // HD
    piece_rows = per_group * tokens
    rows = len(groups[0]) * piece_rows

    def visible_of(group):
        row = lax.broadcasted_iota(jnp.int32, (rows, PAGE), 0)
        token = lax.rem(row, tokens)
        for i, (step, source) in enumerate(group):
            first_token = ((head ^ step) * sub_count + source) * tokens
            token = jnp.where(row // piece_rows == i, token + first_token, token)
        return lax.broadcasted_iota(jnp.int32, (rows, PAGE), 1) <= PAGE - QR + token

    def attend(pages):
        def scores_of(group, g):
            q_blocks = [queries[key][:, g * span:(g + 1) * span] for key in group]
            q_rows = jnp.concatenate([q[:, j * HD:(j + 1) * HD] for q in q_blocks for j in range(per_group)], axis=0)
            for p in range(pages):
                scores = lax.dot_general(
                    q_rows, pages_in[g, p, 0], (((1,), (1,)), ((), ())), preferred_element_type=jnp.float32
                )
                yield jnp.where(visible_of(group), scores, NEG) if p == pages - 1 else scores

        units = [(group, g) for group in groups for g in range(local_kv)]
        scores = list(scores_of(*units[0]))
        for n, (group, g) in enumerate(units):
            following = scores_of(*units[n + 1]) if n + 1 < len(units) else iter(())
            later = []
            top = jnp.max(functools.reduce(jnp.maximum, scores), axis=1, keepdims=True)
            totals, product = None, None
            for p in range(pages):
                later += [s for _, s in zip(range(1), following)]
                numerators = jnp.exp2((scores[p] - top) * EXP2_SCALE)
                part = jnp.dot(
                    numerators.astype(jnp.bfloat16), pages_in[g, p, 1], preferred_element_type=jnp.float32
                )
                totals = numerators if p == 0 else totals + numerators
                product = part if p == 0 else product + part
            totals = jnp.sum(totals, axis=1, keepdims=True)
            done = (product / totals).astype(jnp.bfloat16)
            for i, key in enumerate(group):
                start = i * piece_rows
                outs[key][:, g * span:(g + 1) * span] = jnp.concatenate(
                    [done[start + j * tokens:start + (j + 1) * tokens] for j in range(per_group)], axis=1
                )
            scores = later

    request = own_request(low_ctx)

    @pl.when(request >= 0)
    def _():
        count = counts[request]
        for pages in [*range(1, most_pages - REQS + 3), most_pages]:
            @pl.when(count == pages)
            def _():
                attend(pages)


def one_request_each(queries, kv_cache, page_counts):
    ctx_size, sub_size = lax.axis_size("ctx"), lax.axis_size("sub")
    head_count = lax.axis_size("head")
    low_ctx = ctx_size // 2
    most_pages = kv_cache.shape[1] // PAGE * ctx_size * sub_size // 4
    local_kv = kv_cache.shape[2] // HD
    tokens, width = queries.shape[0], queries.shape[1] // head_count
    anywhere = pl.BlockSpec(memory_space=pl.ANY)
    in_vmem = pl.BlockSpec(memory_space=pltpu.VMEM)
    q_piece = pltpu.VMEM((tokens, width), queries.dtype)

    def vmem(array):
        return pltpu.with_memory_space_constraint(array, pltpu.VMEM)

    def hbm(array):
        return pltpu.with_memory_space_constraint(array, pltpu.HBM)

    def moved(array, routes):
        def flat(place):
            return (place[0] * head_count + place[1]) * sub_size + place[2]

        return lax.ppermute(array, ("ctx", "head", "sub"), [(flat(a), flat(b)) for a, b in routes])

    def worker(request, head):
        ctx, sub = worker_places(low_ctx)[request]
        return ctx, head, sub

    heads = range(head_count)
    q_out = pl.pallas_call(
        split_kernel,
        out_shape=[q_piece] * head_count,
        in_specs=[anywhere],
        out_specs=[anywhere] * head_count,
        scratch_shapes=[pltpu.SemaphoreType.DMA((head_count,))],
        compiler_params=pltpu.CompilerParams(vmem_limit_bytes=2**20),
        name="split",
    )(hbm(queries))
    routes = {
        (step, s): [((r, h, s), worker(r, h ^ step)) for r in range(ctx_size) for h in heads]
        for s in range(sub_size) for step in heads[::-1]
    }
    first, last = list(routes)[0], list(routes)[-1]
    q_in = {first: moved(q_out[first[0]], routes[first])}
    home, counts = pl.pallas_call(
        functools.partial(gather_home_kernel, low_ctx),
        out_shape=[
            pltpu.VMEM((local_kv, most_pages, 2, PAGE, HD), kv_cache.dtype),
            pltpu.VMEM(page_counts.shape, page_counts.dtype),
        ],
        in_specs=[pl.BlockSpec(memory_space=pltpu.SMEM)] + [anywhere] * 3,
        out_specs=[anywhere] * 2,
        scratch_shapes=[pltpu.SemaphoreType.DMA((local_kv, most_pages, 2)), pltpu.SemaphoreType.DMA],
        compiler_params=pltpu.CompilerParams(vmem_limit_bytes=2**20),
        name="gather_home",
    )(hbm(page_counts), hbm(page_counts), hbm(kv_cache), vmem(q_in[first]))
    q_last, counts = lax.optimization_barrier((q_out[last[0]], counts))
    for key in list(routes)[1:]:
        q_in[key] = moved(q_last if key == last else q_out[key[0]], routes[key])

    pairs = [(low_ctx + n // 2, n % 2) for n in range(4)]
    workers = worker_places(low_ctx)
    near, far = (
        moved(kv_cache, [((*a[:1], h, *a[1:]), (*b[:1], h, *b[1:])) for a, b in sends for h in heads])
        for sends in (
            [(pairs[0], workers[1]), (pairs[1], workers[0]), (pairs[2], workers[3]), (pairs[3], workers[2])],
            [(pairs[0], workers[0]), (pairs[1], workers[2]), (pairs[2], workers[1])],
        )
    )
    gathered = pl.pallas_call(
        functools.partial(gather_rest_kernel, low_ctx),
        out_shape=pltpu.VMEM(home.shape, home.dtype),
        in_specs=[pl.BlockSpec(memory_space=pltpu.SMEM)] + [in_vmem] * 2 + [anywhere],
        out_specs=in_vmem,
        input_output_aliases={3: 0},
        compiler_params=pltpu.CompilerParams(vmem_limit_bytes=2**20),
        name="gather_rest",
    )(vmem(counts), vmem(near), vmem(far), vmem(home))

    groups = [[(step, s) for step in heads[::-1]] for s in range(sub_size)]
    back = {}
    after = []
    for keys in groups:
        outs = pl.pallas_call(
            functools.partial(attend_kernel, low_ctx, sub_size, [keys], len(after)),
            out_shape=[q_piece] * len(keys),
            in_specs=[pl.BlockSpec(memory_space=pltpu.SMEM)] + [in_vmem] * (1 + len(keys)) + [anywhere] * len(after),
            out_specs=[in_vmem] * len(keys),
            compiler_params=pltpu.CompilerParams(vmem_limit_bytes=12 * 2**20),
            cost_estimate=pl.CostEstimate(flops=10**10, bytes_accessed=2**22, transcendentals=10**6),
            name=f"attend_{keys[0][1]}",
        )(vmem(counts), vmem(gathered), *[vmem(q_in[key]) for key in keys], *after)
        for key, out in zip(keys, outs):
            back[key] = moved(out, [(b, a) for a, b in routes[key]])
        after = [outs[0]]

    joined = []
    for keys in groups:
        joined = [
            pl.pallas_call(
                functools.partial(join_kernel, keys),
                out_shape=pltpu.HBM(queries.shape, queries.dtype),
                in_specs=[anywhere] * (len(keys) + len(joined)),
                out_specs=anywhere,
                scratch_shapes=[pltpu.SemaphoreType.DMA((len(keys),))],
                input_output_aliases={len(keys): 0} if joined else {},
                compiler_params=pltpu.CompilerParams(vmem_limit_bytes=2**20),
                name=f"join_{keys[0][1]}",
            )(*[vmem(back[key]) for key in keys], *map(hbm, joined))
        ]
    return joined[0]


def from_behind(array, axis, by):
    count = lax.axis_size(axis)
    pairs = [(i, i + by) for i in range(count) if 0 <= i + by < count]
    return lax.ppermute(array, axis, pairs)


def queries_to_pages(queries, kv_cache, page_counts):
    per_group = HQ // KVH
    local_heads = kv_cache.shape[2] // HD
    ctx_size = lax.axis_size("ctx")
    sub_size = lax.axis_size("sub")
    head_count = lax.axis_size("head")
    tok_rows = queries.shape[0]
    score_scale = HD ** (-0.5)
    regrouped = lax.all_to_all(queries, "head", split_axis=1, concat_axis=0, tiled=True)
    all_queries = lax.all_gather(regrouped, ("ctx", "sub"), axis=0, tiled=True)
    all_queries = all_queries.reshape(SPAN, local_heads, per_group, HD)
    page_ends = jnp.cumsum(page_counts)
    ctx_rows = SPAN // ctx_size
    offsets = jnp.arange(QR, dtype=jnp.int32)
    columns = jnp.arange(PAGE, dtype=jnp.int32)
    flat_index = lax.axis_index("ctx") * sub_size + lax.axis_index("sub")
    pages_here = kv_cache.shape[1] // PAGE
    base_pages = pages_here * ctx_size * sub_size // 2
    initial = (
        jnp.full((SPAN, local_heads, per_group), NEG, jnp.float32),
        jnp.zeros((SPAN, local_heads, per_group), jnp.float32),
        jnp.zeros((SPAN, local_heads, per_group, HD), jnp.float32),
    )
    half_rows = kv_cache.shape[1] // 2
    arrived = from_behind(kv_cache[:, half_rows:], "ctx", -(ctx_size // 2))
    is_lower = lax.axis_index("ctx") < ctx_size // 2
    source_flat = flat_index + ctx_size // 2 * sub_size
    working = jnp.where(is_lower, arrived, kv_cache[:, :half_rows])
    first_page = jnp.where(
        is_lower, source_flat * pages_here + pages_here // 2, flat_index * pages_here
    )
    page_total = working.shape[1] // PAGE

    def add_page(page_turn, running):
        page_index = first_page + page_turn
        relative = page_index - base_pages
        counted = jnp.sum((relative >= page_ends).astype(jnp.int32))
        request = jnp.where(relative < 0, REQS, counted)

        def update(partial_value):
            run_max, run_sum, run_out = partial_value
            request_id = jnp.minimum(request, REQS - 1)
            row_start = request_id * QR
            gathered = row_start + offsets
            within = gathered % ctx_rows
            ctx_block = gathered // ctx_rows
            sub_part = within // (head_count * tok_rows)
            head_part = within // tok_rows % head_count
            tok_part = within % tok_rows
            natural = ctx_block * ctx_rows + (head_part * sub_size + sub_part) * tok_rows + tok_part
            query_pos = (page_ends[request_id] + base_pages) * PAGE - QR + natural - row_start
            key_pos = page_index * PAGE + columns
            visible = key_pos[None, :] <= query_pos[:, None]
            page_keys = working[0].reshape(PAGE, local_heads, HD)
            page_values = working[1].reshape(PAGE, local_heads, HD)
            query_rows = lax.dynamic_slice_in_dim(all_queries, row_start, QR, 0)
            scores = (
                jnp.einsum(
                    "qkgd,pkd->qkgp", query_rows, page_keys, preferred_element_type=jnp.float32
                )
                * score_scale
            )
            scores = jnp.where(visible[:, None, None, :], scores, NEG)
            old_max = lax.dynamic_slice_in_dim(run_max, row_start, QR, 0)
            old_sum = lax.dynamic_slice_in_dim(run_sum, row_start, QR, 0)
            old_out = lax.dynamic_slice_in_dim(run_out, row_start, QR, 0)
            new_max = jnp.maximum(old_max, jnp.max(scores, axis=3))
            factor = jnp.exp(old_max - new_max)
            numerators = jnp.exp(scores - new_max[..., None])
            new_sum = old_sum * factor + jnp.sum(numerators, axis=3)
            product = jnp.einsum(
                "qkgp,pkd->qkgd",
                numerators.astype(jnp.bfloat16),
                page_values,
                preferred_element_type=jnp.float32,
            )
            new_out = old_out * factor[..., None] + product
            return (
                lax.dynamic_update_slice_in_dim(run_max, new_max, row_start, 0),
                lax.dynamic_update_slice_in_dim(run_sum, new_sum, row_start, 0),
                lax.dynamic_update_slice_in_dim(run_out, new_out, row_start, 0),
            )

        def unchanged(partial_value):
            return partial_value

        return lax.cond(request < REQS, update, unchanged, running)

    run_max, run_sum, run_out = lax.fori_loop(0, page_total, add_page, initial)
    share = SPAN // (ctx_size * sub_size)
    global_max = lax.pmax(run_max, ("ctx", "sub"))
    factor = jnp.exp(run_max - global_max)
    sums_here, outs_here = (
        lax.psum_scatter(
            (run_sum * factor).astype(jnp.bfloat16), ("ctx", "sub"), scatter_dimension=0, tiled=True
        ).astype(jnp.float32),
        lax.psum_scatter(
            (run_out * factor[..., None]).astype(jnp.bfloat16),
            ("ctx", "sub"),
            scatter_dimension=0,
            tiled=True,
        ).astype(jnp.float32),
    )
    finished = (outs_here / sums_here[..., None]).astype(jnp.bfloat16)
    finished = finished.reshape(share, local_heads * per_group * HD)
    return lax.all_to_all(finished, "head", split_axis=0, concat_axis=1, tiled=True)


def per_device(queries, kv_cache, page_counts):
    ctx_size, sub_size, head_count = lax.axis_size("ctx"), lax.axis_size("sub"), lax.axis_size("head")
    small = (
        ctx_size == REQS == 4
        and head_count == sub_size == 2
        and kv_cache.shape[1] == 2 * PAGE
        and kv_cache.shape[2] % (sub_size * HD) == 0
        and queries.shape[0] % 16 == 0
        and queries.shape[0] * head_count * sub_size == QR
    )
    return (one_request_each if small else queries_to_pages)(queries, kv_cache, page_counts)


def solution(mesh):
    return jax.shard_map(
        per_device,
        mesh=mesh,
        in_specs=(
            P(("grp", "ctx", "head", "sub"), None),
            P(None, ("grp", "ctx", "sub"), "head"),
            P("grp"),
        ),
        out_specs=P(("grp", "ctx", "head", "sub"), None),
        check_vma=False,
    )
```

```python
import functools

import jax
import jax.numpy as jnp
from jax import lax
from jax.experimental import pallas as pl
from jax.experimental.pallas import tpu as pltpu
from jax.sharding import PartitionSpec as P

HQ = 128
KVH = 8
HD = 128
REQS = 4
QR = 64
PAGE = 256
SPAN = 256


NEG = -1e30
EXP2_SCALE = HD ** (-0.5) * 1.4426950408889634


def run(copies):
    for copy in copies:
        copy.start()
    for copy in copies:
        copy.wait()


def head_part(step, width):
    return pl.ds(pl.multiple_of((lax.axis_index("head") ^ step) * width, width), width)


def split_kernel(queries, *refs):
    outs, sems = refs[:-1], refs[-1]
    run([
        pltpu.make_async_copy(queries.at[:, head_part(step, out.shape[1])], out, sems.at[step])
        for step, out in enumerate(outs)
    ])


def join_kernel(keys, *refs):
    out, sems = refs[-2:]

    @pl.when(lax.axis_index("sub") == keys[0][1])
    def _():
        run([
            pltpu.make_async_copy(piece, out.at[:, head_part(step, piece.shape[1])], sems.at[i])
            for i, (piece, (step, _)) in enumerate(zip(refs, keys))
        ])


def worker_places(low_ctx):
    return (0, 0), (low_ctx, 1), (low_ctx + 1, 1), (low_ctx + 1, 0)


def own_request(low_ctx):
    ctx, sub = lax.axis_index("ctx"), lax.axis_index("sub")
    found = jnp.int32(-1)
    for request, place in enumerate(worker_places(low_ctx)):
        found = jnp.where((ctx == place[0]) & (sub == place[1]), request, found)
    return found


def pages_of(low_ctx, counts, most_pages):
    request = own_request(low_ctx)
    start = jnp.int32(0)
    for r in range(REQS):
        start = start + jnp.where(r < request, counts[r], 0)
    count = jnp.where(request >= 0, counts[jnp.maximum(request, 0)], 0)
    home_pair = jnp.where(request == 0, -1, jnp.where(request == 1, 1, 5 - request))
    near_pair = jnp.where(request == 0, 1, home_pair ^ 1)
    for p in range(most_pages):
        page = start + p
        pair = page // 2
        which = jnp.where(pair == home_pair, 0, jnp.where(pair == near_pair, 1, 2))
        yield p, p < count, which, pl.ds(pl.multiple_of(lax.rem(page, 2) * PAGE, PAGE), PAGE)


def gather_home_kernel(low_ctx, counts, counts_in, own, after, out, counts_out, sems, counts_sem):
    local_kv, most_pages = out.shape[:2]
    counts_copy = pltpu.make_async_copy(counts_in, counts_out, counts_sem)
    counts_copy.start()
    plan = [
        (here & (which == 0), [
            pltpu.make_async_copy(own.at[i, rows, pl.ds(g * HD, HD)], out.at[g, p, i], sems.at[g, p, i])
            for g in range(local_kv) for i in range(2)
        ])
        for p, here, which, rows in pages_of(low_ctx, counts, most_pages)
    ]
    for here, copies in plan:
        @pl.when(here)
        def _():
            for copy in copies:
                copy.start()
    for here, copies in plan:
        @pl.when(here)
        def _():
            for copy in copies:
                copy.wait()
    counts_copy.wait()


def gather_rest_kernel(low_ctx, counts, near, far, home, out):
    local_kv, most_pages = out.shape[:2]
    for p, here, which, rows in pages_of(low_ctx, counts, most_pages):
        for n, ref in enumerate((near, far)):
            @pl.when(here & (which == n + 1))
            def _():
                for g in range(local_kv):
                    for i in range(2):
                        out[g, p, i] = ref[i, rows, g * HD:(g + 1) * HD]


def attend_kernel(low_ctx, sub_count, groups, waits, counts, pages_in, *refs):
    keys = [key for group in groups for key in group]
    queries, outs = dict(zip(keys, refs)), dict(zip(keys, refs[len(keys) + waits:]))
    head = lax.axis_index("head")
    tokens, width = refs[0].shape
    local_kv, most_pages = pages_in.shape[:2]
    span = width // local_kv
    per_group = span // HD
    piece_rows = per_group * tokens
    rows = len(groups[0]) * piece_rows

    def visible_of(group):
        row = lax.broadcasted_iota(jnp.int32, (rows, PAGE), 0)
        token = lax.rem(row, tokens)
        for i, (step, source) in enumerate(group):
            first_token = ((head ^ step) * sub_count + source) * tokens
            token = jnp.where(row // piece_rows == i, token + first_token, token)
        return lax.broadcasted_iota(jnp.int32, (rows, PAGE), 1) <= PAGE - QR + token

    def attend(pages):
        def scores_of(group, g):
            q_blocks = [queries[key][:, g * span:(g + 1) * span] for key in group]
            q_rows = jnp.concatenate([q[:, j * HD:(j + 1) * HD] for q in q_blocks for j in range(per_group)], axis=0)
            for p in range(pages):
                scores = lax.dot_general(
                    q_rows, pages_in[g, p, 0], (((1,), (1,)), ((), ())), preferred_element_type=jnp.float32
                )
                yield jnp.where(visible_of(group), scores, NEG) if p == pages - 1 else scores

        units = [(group, g) for group in groups for g in range(local_kv)]
        scores = list(scores_of(*units[0]))
        for n, (group, g) in enumerate(units):
            following = scores_of(*units[n + 1]) if n + 1 < len(units) else iter(())
            later = []
            top = jnp.max(functools.reduce(jnp.maximum, scores), axis=1, keepdims=True)
            totals, product = None, None
            for p in range(pages):
                later += [s for _, s in zip(range(1), following)]
                numerators = jnp.exp2((scores[p] - top) * EXP2_SCALE)
                part = jnp.dot(
                    numerators.astype(jnp.bfloat16), pages_in[g, p, 1], preferred_element_type=jnp.float32
                )
                totals = numerators if p == 0 else totals + numerators
                product = part if p == 0 else product + part
            totals = jnp.sum(totals, axis=1, keepdims=True)
            done = (product / totals).astype(jnp.bfloat16)
            for i, key in enumerate(group):
                start = i * piece_rows
                outs[key][:, g * span:(g + 1) * span] = jnp.concatenate(
                    [done[start + j * tokens:start + (j + 1) * tokens] for j in range(per_group)], axis=1
                )
            scores = later

    request = own_request(low_ctx)

    @pl.when(request >= 0)
    def _():
        count = counts[request]
        for pages in [*range(1, most_pages - REQS + 3), most_pages]:
            @pl.when(count == pages)
            def _():
                attend(pages)


def one_request_each(queries, kv_cache, page_counts):
    ctx_size, sub_size = lax.axis_size("ctx"), lax.axis_size("sub")
    head_count = lax.axis_size("head")
    low_ctx = ctx_size // 2
    most_pages = kv_cache.shape[1] // PAGE * ctx_size * sub_size // 4
    local_kv = kv_cache.shape[2] // HD
    tokens, width = queries.shape[0], queries.shape[1] // head_count
    anywhere = pl.BlockSpec(memory_space=pl.ANY)
    in_vmem = pl.BlockSpec(memory_space=pltpu.VMEM)
    q_piece = pltpu.VMEM((tokens, width), queries.dtype)

    def vmem(array):
        return pltpu.with_memory_space_constraint(array, pltpu.VMEM)

    def hbm(array):
        return pltpu.with_memory_space_constraint(array, pltpu.HBM)

    def moved(array, routes):
        def flat(place):
            return (place[0] * head_count + place[1]) * sub_size + place[2]

        return lax.ppermute(array, ("ctx", "head", "sub"), [(flat(a), flat(b)) for a, b in routes])

    def worker(request, head):
        ctx, sub = worker_places(low_ctx)[request]
        return ctx, head, sub

    heads = range(head_count)
    q_out = pl.pallas_call(
        split_kernel,
        out_shape=[q_piece] * head_count,
        in_specs=[anywhere],
        out_specs=[anywhere] * head_count,
        scratch_shapes=[pltpu.SemaphoreType.DMA((head_count,))],
        compiler_params=pltpu.CompilerParams(vmem_limit_bytes=2**20),
        name="split",
    )(hbm(queries))
    routes = {
        (step, s): [((r, h, s), worker(r, h ^ step)) for r in range(ctx_size) for h in heads]
        for s in range(sub_size) for step in heads[::-1]
    }
    first, last = list(routes)[0], list(routes)[-1]
    q_in = {first: moved(q_out[first[0]], routes[first])}
    home, counts = pl.pallas_call(
        functools.partial(gather_home_kernel, low_ctx),
        out_shape=[
            pltpu.VMEM((local_kv, most_pages, 2, PAGE, HD), kv_cache.dtype),
            pltpu.VMEM(page_counts.shape, page_counts.dtype),
        ],
        in_specs=[pl.BlockSpec(memory_space=pltpu.SMEM)] + [anywhere] * 3,
        out_specs=[anywhere] * 2,
        scratch_shapes=[pltpu.SemaphoreType.DMA((local_kv, most_pages, 2)), pltpu.SemaphoreType.DMA],
        compiler_params=pltpu.CompilerParams(vmem_limit_bytes=2**20),
        name="gather_home",
    )(hbm(page_counts), hbm(page_counts), hbm(kv_cache), vmem(q_in[first]))
    q_last, counts = lax.optimization_barrier((q_out[last[0]], counts))
    for key in list(routes)[1:]:
        q_in[key] = moved(q_last if key == last else q_out[key[0]], routes[key])

    pairs = [(low_ctx + n // 2, n % 2) for n in range(4)]
    workers = worker_places(low_ctx)
    near, far = (
        moved(kv_cache, [((*a[:1], h, *a[1:]), (*b[:1], h, *b[1:])) for a, b in sends for h in heads])
        for sends in (
            [(pairs[0], workers[1]), (pairs[1], workers[0]), (pairs[2], workers[2]), (pairs[3], workers[3])],
            [(pairs[0], workers[0]), (pairs[1], workers[2]), (pairs[2], workers[1])],
        )
    )
    gathered = pl.pallas_call(
        functools.partial(gather_rest_kernel, low_ctx),
        out_shape=pltpu.VMEM(home.shape, home.dtype),
        in_specs=[pl.BlockSpec(memory_space=pltpu.SMEM)] + [in_vmem] * 2 + [anywhere],
        out_specs=in_vmem,
        input_output_aliases={3: 0},
        compiler_params=pltpu.CompilerParams(vmem_limit_bytes=2**20),
        name="gather_rest",
    )(vmem(counts), vmem(near), vmem(far), vmem(home))

    groups = [[(step, s) for step in heads[::-1]] for s in range(sub_size)]
    back = {}
    after = []
    for keys in groups:
        outs = pl.pallas_call(
            functools.partial(attend_kernel, low_ctx, sub_size, [keys], len(after)),
            out_shape=[q_piece] * len(keys),
            in_specs=[pl.BlockSpec(memory_space=pltpu.SMEM)] + [in_vmem] * (1 + len(keys)) + [anywhere] * len(after),
            out_specs=[in_vmem] * len(keys),
            compiler_params=pltpu.CompilerParams(vmem_limit_bytes=12 * 2**20),
            cost_estimate=pl.CostEstimate(flops=10**10, bytes_accessed=2**22, transcendentals=10**6),
            name=f"attend_{keys[0][1]}",
        )(vmem(counts), vmem(gathered), *[vmem(q_in[key]) for key in keys], *after)
        for key, out in zip(keys, outs):
            back[key] = moved(out, [(b, a) for a, b in routes[key]])
        after = [outs[0]]

    joined = []
    for keys in groups:
        joined = [
            pl.pallas_call(
                functools.partial(join_kernel, keys),
                out_shape=pltpu.HBM(queries.shape, queries.dtype),
                in_specs=[anywhere] * (len(keys) + len(joined)),
                out_specs=anywhere,
                scratch_shapes=[pltpu.SemaphoreType.DMA((len(keys),))],
                input_output_aliases={len(keys): 0} if joined else {},
                compiler_params=pltpu.CompilerParams(vmem_limit_bytes=2**20),
                name=f"join_{keys[0][1]}",
            )(*[vmem(back[key]) for key in keys], *map(hbm, joined))
        ]
    return joined[0]


def from_behind(array, axis, by):
    count = lax.axis_size(axis)
    pairs = [(i, i + by) for i in range(count) if 0 <= i + by < count]
    return lax.ppermute(array, axis, pairs)


def queries_to_pages(queries, kv_cache, page_counts):
    per_group = HQ // KVH
    local_heads = kv_cache.shape[2] // HD
    ctx_size = lax.axis_size("ctx")
    sub_size = lax.axis_size("sub")
    head_count = lax.axis_size("head")
    tok_rows = queries.shape[0]
    score_scale = HD ** (-0.5)
    regrouped = lax.all_to_all(queries, "head", split_axis=1, concat_axis=0, tiled=True)
    all_queries = lax.all_gather(regrouped, ("ctx", "sub"), axis=0, tiled=True)
    all_queries = all_queries.reshape(SPAN, local_heads, per_group, HD)
    page_ends = jnp.cumsum(page_counts)
    ctx_rows = SPAN // ctx_size
    offsets = jnp.arange(QR, dtype=jnp.int32)
    columns = jnp.arange(PAGE, dtype=jnp.int32)
    flat_index = lax.axis_index("ctx") * sub_size + lax.axis_index("sub")
    pages_here = kv_cache.shape[1] // PAGE
    base_pages = pages_here * ctx_size * sub_size // 2
    initial = (
        jnp.full((SPAN, local_heads, per_group), NEG, jnp.float32),
        jnp.zeros((SPAN, local_heads, per_group), jnp.float32),
        jnp.zeros((SPAN, local_heads, per_group, HD), jnp.float32),
    )
    half_rows = kv_cache.shape[1] // 2
    arrived = from_behind(kv_cache[:, half_rows:], "ctx", -(ctx_size // 2))
    is_lower = lax.axis_index("ctx") < ctx_size // 2
    source_flat = flat_index + ctx_size // 2 * sub_size
    working = jnp.where(is_lower, arrived, kv_cache[:, :half_rows])
    first_page = jnp.where(
        is_lower, source_flat * pages_here + pages_here // 2, flat_index * pages_here
    )
    page_total = working.shape[1] // PAGE

    def add_page(page_turn, running):
        page_index = first_page + page_turn
        relative = page_index - base_pages
        counted = jnp.sum((relative >= page_ends).astype(jnp.int32))
        request = jnp.where(relative < 0, REQS, counted)

        def update(partial_value):
            run_max, run_sum, run_out = partial_value
            request_id = jnp.minimum(request, REQS - 1)
            row_start = request_id * QR
            gathered = row_start + offsets
            within = gathered % ctx_rows
            ctx_block = gathered // ctx_rows
            sub_part = within // (head_count * tok_rows)
            head_part = within // tok_rows % head_count
            tok_part = within % tok_rows
            natural = ctx_block * ctx_rows + (head_part * sub_size + sub_part) * tok_rows + tok_part
            query_pos = (page_ends[request_id] + base_pages) * PAGE - QR + natural - row_start
            key_pos = page_index * PAGE + columns
            visible = key_pos[None, :] <= query_pos[:, None]
            page_keys = working[0].reshape(PAGE, local_heads, HD)
            page_values = working[1].reshape(PAGE, local_heads, HD)
            query_rows = lax.dynamic_slice_in_dim(all_queries, row_start, QR, 0)
            scores = (
                jnp.einsum(
                    "qkgd,pkd->qkgp", query_rows, page_keys, preferred_element_type=jnp.float32
                )
                * score_scale
            )
            scores = jnp.where(visible[:, None, None, :], scores, NEG)
            old_max = lax.dynamic_slice_in_dim(run_max, row_start, QR, 0)
            old_sum = lax.dynamic_slice_in_dim(run_sum, row_start, QR, 0)
            old_out = lax.dynamic_slice_in_dim(run_out, row_start, QR, 0)
            new_max = jnp.maximum(old_max, jnp.max(scores, axis=3))
            factor = jnp.exp(old_max - new_max)
            numerators = jnp.exp(scores - new_max[..., None])
            new_sum = old_sum * factor + jnp.sum(numerators, axis=3)
            product = jnp.einsum(
                "qkgp,pkd->qkgd",
                numerators.astype(jnp.bfloat16),
                page_values,
                preferred_element_type=jnp.float32,
            )
            new_out = old_out * factor[..., None] + product
            return (
                lax.dynamic_update_slice_in_dim(run_max, new_max, row_start, 0),
                lax.dynamic_update_slice_in_dim(run_sum, new_sum, row_start, 0),
                lax.dynamic_update_slice_in_dim(run_out, new_out, row_start, 0),
            )

        def unchanged(partial_value):
            return partial_value

        return lax.cond(request < REQS, update, unchanged, running)

    run_max, run_sum, run_out = lax.fori_loop(0, page_total, add_page, initial)
    share = SPAN // (ctx_size * sub_size)
    global_max = lax.pmax(run_max, ("ctx", "sub"))
    factor = jnp.exp(run_max - global_max)
    sums_here, outs_here = (
        lax.psum_scatter(
            (run_sum * factor).astype(jnp.bfloat16), ("ctx", "sub"), scatter_dimension=0, tiled=True
        ).astype(jnp.float32),
        lax.psum_scatter(
            (run_out * factor[..., None]).astype(jnp.bfloat16),
            ("ctx", "sub"),
            scatter_dimension=0,
            tiled=True,
        ).astype(jnp.float32),
    )
    finished = (outs_here / sums_here[..., None]).astype(jnp.bfloat16)
    finished = finished.reshape(share, local_heads * per_group * HD)
    return lax.all_to_all(finished, "head", split_axis=0, concat_axis=1, tiled=True)


def per_device(queries, kv_cache, page_counts):
    ctx_size, sub_size, head_count = lax.axis_size("ctx"), lax.axis_size("sub"), lax.axis_size("head")
    small = (
        ctx_size == REQS == 4
        and head_count == sub_size == 2
        and kv_cache.shape[1] == 2 * PAGE
        and kv_cache.shape[2] % (sub_size * HD) == 0
        and queries.shape[0] % 16 == 0
        and queries.shape[0] * head_count * sub_size == QR
    )
    return (one_request_each if small else queries_to_pages)(queries, kv_cache, page_counts)


def solution(mesh):
    return jax.shard_map(
        per_device,
        mesh=mesh,
        in_specs=(
            P(("grp", "ctx", "head", "sub"), None),
            P(None, ("grp", "ctx", "sub"), "head"),
            P("grp"),
        ),
        out_specs=P(("grp", "ctx", "head", "sub"), None),
        check_vma=False,
    )
```

```python
import functools

import jax
import jax.numpy as jnp
from jax import lax
from jax.experimental import pallas as pl
from jax.experimental.pallas import tpu as pltpu
from jax.sharding import PartitionSpec as P

HQ = 128
KVH = 8
HD = 128
REQS = 4
QR = 64
PAGE = 256
SPAN = 256


NEG = -1e30
EXP2_SCALE = HD ** (-0.5) * 1.4426950408889634


def run(copies):
    for copy in copies:
        copy.start()
    for copy in copies:
        copy.wait()


def head_part(step, width):
    return pl.ds(pl.multiple_of((lax.axis_index("head") ^ step) * width, width), width)


def split_kernel(queries, *refs):
    outs, sems = refs[:-1], refs[-1]
    run([
        pltpu.make_async_copy(queries.at[:, head_part(step, out.shape[1])], out, sems.at[step])
        for step, out in enumerate(outs)
    ])


def join_kernel(keys, *refs):
    out, sems = refs[-2:]

    @pl.when(lax.axis_index("sub") == keys[0][1])
    def _():
        run([
            pltpu.make_async_copy(piece, out.at[:, head_part(step, piece.shape[1])], sems.at[i])
            for i, (piece, (step, _)) in enumerate(zip(refs, keys))
        ])


def worker_places(low_ctx):
    return (0, 0), (low_ctx, 1), (low_ctx + 1, 1), (low_ctx + 1, 0)


def own_request(low_ctx):
    ctx, sub = lax.axis_index("ctx"), lax.axis_index("sub")
    found = jnp.int32(-1)
    for request, place in enumerate(worker_places(low_ctx)):
        found = jnp.where((ctx == place[0]) & (sub == place[1]), request, found)
    return found


def pages_of(low_ctx, counts, most_pages):
    request = own_request(low_ctx)
    start = jnp.int32(0)
    for r in range(REQS):
        start = start + jnp.where(r < request, counts[r], 0)
    count = jnp.where(request >= 0, counts[jnp.maximum(request, 0)], 0)
    home_pair = jnp.where(request == 0, -1, jnp.where(request == 1, 1, 5 - request))
    near_pair = jnp.where(request == 0, 1, home_pair ^ 1)
    for p in range(most_pages):
        page = start + p
        pair = page // 2
        which = jnp.where(pair == home_pair, 0, jnp.where(pair == near_pair, 1, 2))
        yield p, p < count, which, pl.ds(pl.multiple_of(lax.rem(page, 2) * PAGE, PAGE), PAGE)


def gather_home_kernel(low_ctx, counts, counts_in, own, after, out, counts_out, sems, counts_sem):
    local_kv, most_pages = out.shape[:2]
    counts_copy = pltpu.make_async_copy(counts_in, counts_out, counts_sem)
    counts_copy.start()
    plan = [
        (here & (which == 0), [
            pltpu.make_async_copy(own.at[i, rows, pl.ds(g * HD, HD)], out.at[g, p, i], sems.at[g, p, i])
            for g in range(local_kv) for i in range(2)
        ])
        for p, here, which, rows in pages_of(low_ctx, counts, most_pages)
    ]
    for here, copies in plan:
        @pl.when(here)
        def _():
            for copy in copies:
                copy.start()
    for here, copies in plan:
        @pl.when(here)
        def _():
            for copy in copies:
                copy.wait()
    counts_copy.wait()


def gather_rest(low_ctx, counts, home, far, near, out):
    local_kv, most_pages = out.shape[:2]
    for p, here, which, rows in pages_of(low_ctx, counts, most_pages):
        @pl.when(here & (which == 0))
        def _():
            for g in range(local_kv):
                out[g, p] = home[g, p]
        for n, ref in enumerate((near, far)):
            @pl.when(here & (which == n + 1))
            def _():
                for g in range(local_kv):
                    for i in range(2):
                        out[g, p, i] = ref[i, rows, g * HD:(g + 1) * HD]


def attend_kernel(low_ctx, sub_count, groups, others, counts, home, *refs):
    keys = [key for group in groups for key in group]
    queries, outs = dict(zip(keys, refs)), dict(zip(keys, refs[len(keys) + others:]))
    pages_in = home
    if others:
        pages_in = refs[-1]
        gather_rest(low_ctx, counts, home, *refs[len(keys):len(keys) + others], pages_in)
    head = lax.axis_index("head")
    tokens, width = refs[0].shape
    local_kv, most_pages = pages_in.shape[:2]
    span = width // local_kv
    per_group = span // HD
    piece_rows = per_group * tokens
    rows = len(groups[0]) * piece_rows

    def visible_of(group):
        row = lax.broadcasted_iota(jnp.int32, (rows, PAGE), 0)
        token = lax.rem(row, tokens)
        for i, (step, source) in enumerate(group):
            first_token = ((head ^ step) * sub_count + source) * tokens
            token = jnp.where(row // piece_rows == i, token + first_token, token)
        return lax.broadcasted_iota(jnp.int32, (rows, PAGE), 1) <= PAGE - QR + token

    def attend(pages):
        def scores_of(group, g):
            q_blocks = [queries[key][:, g * span:(g + 1) * span] for key in group]
            q_rows = jnp.concatenate([q[:, j * HD:(j + 1) * HD] for q in q_blocks for j in range(per_group)], axis=0)
            for p in range(pages):
                scores = lax.dot_general(
                    q_rows, pages_in[g, p, 0], (((1,), (1,)), ((), ())), preferred_element_type=jnp.float32
                )
                yield jnp.where(visible_of(group), scores, NEG) if p == pages - 1 else scores

        units = [(group, g) for group in groups for g in range(local_kv)]
        scores = list(scores_of(*units[0]))
        for n, (group, g) in enumerate(units):
            following = scores_of(*units[n + 1]) if n + 1 < len(units) else iter(())
            later = []
            top = jnp.max(functools.reduce(jnp.maximum, scores), axis=1, keepdims=True)
            totals, product = None, None
            for p in range(pages):
                later += [s for _, s in zip(range(1), following)]
                numerators = jnp.exp2((scores[p] - top) * EXP2_SCALE)
                part = jnp.dot(
                    numerators.astype(jnp.bfloat16), pages_in[g, p, 1], preferred_element_type=jnp.float32
                )
                totals = numerators if p == 0 else totals + numerators
                product = part if p == 0 else product + part
            totals = jnp.sum(totals, axis=1, keepdims=True)
            done = (product / totals).astype(jnp.bfloat16)
            for i, key in enumerate(group):
                start = i * piece_rows
                outs[key][:, g * span:(g + 1) * span] = jnp.concatenate(
                    [done[start + j * tokens:start + (j + 1) * tokens] for j in range(per_group)], axis=1
                )
            scores = later

    request = own_request(low_ctx)

    @pl.when(request >= 0)
    def _():
        count = counts[request]
        for pages in [*range(1, most_pages - REQS + 3), most_pages]:
            @pl.when(count == pages)
            def _():
                attend(pages)


def one_request_each(queries, kv_cache, page_counts):
    ctx_size, sub_size = lax.axis_size("ctx"), lax.axis_size("sub")
    head_count = lax.axis_size("head")
    low_ctx = ctx_size // 2
    most_pages = kv_cache.shape[1] // PAGE * ctx_size * sub_size // 4
    local_kv = kv_cache.shape[2] // HD
    tokens, width = queries.shape[0], queries.shape[1] // head_count
    anywhere = pl.BlockSpec(memory_space=pl.ANY)
    in_vmem = pl.BlockSpec(memory_space=pltpu.VMEM)
    q_piece = pltpu.VMEM((tokens, width), queries.dtype)

    def vmem(array):
        return pltpu.with_memory_space_constraint(array, pltpu.VMEM)

    def hbm(array):
        return pltpu.with_memory_space_constraint(array, pltpu.HBM)

    def moved(array, routes):
        def flat(place):
            return (place[0] * head_count + place[1]) * sub_size + place[2]

        return lax.ppermute(array, ("ctx", "head", "sub"), [(flat(a), flat(b)) for a, b in routes])

    def worker(request, head):
        ctx, sub = worker_places(low_ctx)[request]
        return ctx, head, sub

    heads = range(head_count)
    q_out = pl.pallas_call(
        split_kernel,
        out_shape=[q_piece] * head_count,
        in_specs=[anywhere],
        out_specs=[anywhere] * head_count,
        scratch_shapes=[pltpu.SemaphoreType.DMA((head_count,))],
        compiler_params=pltpu.CompilerParams(vmem_limit_bytes=2**20),
        name="split",
    )(hbm(queries))
    routes = {
        (step, s): [((r, h, s), worker(r, h ^ step)) for r in range(ctx_size) for h in heads]
        for s in range(sub_size) for step in heads[::-1]
    }
    first, last = list(routes)[0], list(routes)[-1]
    q_in = {first: moved(q_out[first[0]], routes[first])}
    home, counts = pl.pallas_call(
        functools.partial(gather_home_kernel, low_ctx),
        out_shape=[
            pltpu.VMEM((local_kv, most_pages, 2, PAGE, HD), kv_cache.dtype),
            pltpu.VMEM(page_counts.shape, page_counts.dtype),
        ],
        in_specs=[pl.BlockSpec(memory_space=pltpu.SMEM)] + [anywhere] * 3,
        out_specs=[anywhere] * 2,
        scratch_shapes=[pltpu.SemaphoreType.DMA((local_kv, most_pages, 2)), pltpu.SemaphoreType.DMA],
        compiler_params=pltpu.CompilerParams(vmem_limit_bytes=2**20),
        name="gather_home",
    )(hbm(page_counts), hbm(page_counts), hbm(kv_cache), vmem(q_in[first]))
    q_last, counts = lax.optimization_barrier((q_out[last[0]], counts))
    for key in list(routes)[1:]:
        q_in[key] = moved(q_last if key == last else q_out[key[0]], routes[key])

    pairs = [(low_ctx + n // 2, n % 2) for n in range(4)]
    workers = worker_places(low_ctx)
    near, far = (
        moved(kv_cache, [((*a[:1], h, *a[1:]), (*b[:1], h, *b[1:])) for a, b in sends for h in heads])
        for sends in (
            [(pairs[0], workers[1]), (pairs[1], workers[0]), (pairs[2], workers[2]), (pairs[3], workers[3])],
            [(pairs[0], workers[0]), (pairs[1], workers[2]), (pairs[2], workers[1])],
        )
    )
    groups = [[(step, s) for step in heads[::-1]] for s in range(sub_size)]
    back = {}
    pages, others = home, [vmem(far), vmem(near)]
    for keys in groups:
        outs = pl.pallas_call(
            functools.partial(attend_kernel, low_ctx, sub_size, [keys], len(others)),
            out_shape=[q_piece] * len(keys) + [pltpu.VMEM(home.shape, home.dtype)] * bool(others),
            in_specs=[pl.BlockSpec(memory_space=pltpu.SMEM)] + [in_vmem] * (1 + len(keys) + len(others)),
            out_specs=[in_vmem] * (len(keys) + bool(others)),
            compiler_params=pltpu.CompilerParams(vmem_limit_bytes=12 * 2**20),
            cost_estimate=pl.CostEstimate(flops=10**10, bytes_accessed=2**22, transcendentals=10**6),
            name=f"attend_{keys[0][1]}",
        )(vmem(counts), vmem(pages), *[vmem(q_in[key]) for key in keys], *others)
        for key, out in zip(keys, outs):
            back[key] = moved(out, [(b, a) for a, b in routes[key]])
        if others:
            pages, others = outs[-1], []

    joined = []
    for keys in groups:
        joined = [
            pl.pallas_call(
                functools.partial(join_kernel, keys),
                out_shape=pltpu.HBM(queries.shape, queries.dtype),
                in_specs=[anywhere] * (len(keys) + len(joined)),
                out_specs=anywhere,
                scratch_shapes=[pltpu.SemaphoreType.DMA((len(keys),))],
                input_output_aliases={len(keys): 0} if joined else {},
                compiler_params=pltpu.CompilerParams(vmem_limit_bytes=2**20),
                name=f"join_{keys[0][1]}",
            )(*[vmem(back[key]) for key in keys], *map(hbm, joined))
        ]
    return joined[0]


def from_behind(array, axis, by):
    count = lax.axis_size(axis)
    pairs = [(i, i + by) for i in range(count) if 0 <= i + by < count]
    return lax.ppermute(array, axis, pairs)


def queries_to_pages(queries, kv_cache, page_counts):
    per_group = HQ // KVH
    local_heads = kv_cache.shape[2] // HD
    ctx_size = lax.axis_size("ctx")
    sub_size = lax.axis_size("sub")
    head_count = lax.axis_size("head")
    tok_rows = queries.shape[0]
    score_scale = HD ** (-0.5)
    regrouped = lax.all_to_all(queries, "head", split_axis=1, concat_axis=0, tiled=True)
    all_queries = lax.all_gather(regrouped, ("ctx", "sub"), axis=0, tiled=True)
    all_queries = all_queries.reshape(SPAN, local_heads, per_group, HD)
    page_ends = jnp.cumsum(page_counts)
    ctx_rows = SPAN // ctx_size
    offsets = jnp.arange(QR, dtype=jnp.int32)
    columns = jnp.arange(PAGE, dtype=jnp.int32)
    flat_index = lax.axis_index("ctx") * sub_size + lax.axis_index("sub")
    pages_here = kv_cache.shape[1] // PAGE
    base_pages = pages_here * ctx_size * sub_size // 2
    initial = (
        jnp.full((SPAN, local_heads, per_group), NEG, jnp.float32),
        jnp.zeros((SPAN, local_heads, per_group), jnp.float32),
        jnp.zeros((SPAN, local_heads, per_group, HD), jnp.float32),
    )
    half_rows = kv_cache.shape[1] // 2
    arrived = from_behind(kv_cache[:, half_rows:], "ctx", -(ctx_size // 2))
    is_lower = lax.axis_index("ctx") < ctx_size // 2
    source_flat = flat_index + ctx_size // 2 * sub_size
    working = jnp.where(is_lower, arrived, kv_cache[:, :half_rows])
    first_page = jnp.where(
        is_lower, source_flat * pages_here + pages_here // 2, flat_index * pages_here
    )
    page_total = working.shape[1] // PAGE

    def add_page(page_turn, running):
        page_index = first_page + page_turn
        relative = page_index - base_pages
        counted = jnp.sum((relative >= page_ends).astype(jnp.int32))
        request = jnp.where(relative < 0, REQS, counted)

        def update(partial_value):
            run_max, run_sum, run_out = partial_value
            request_id = jnp.minimum(request, REQS - 1)
            row_start = request_id * QR
            gathered = row_start + offsets
            within = gathered % ctx_rows
            ctx_block = gathered // ctx_rows
            sub_part = within // (head_count * tok_rows)
            head_part = within // tok_rows % head_count
            tok_part = within % tok_rows
            natural = ctx_block * ctx_rows + (head_part * sub_size + sub_part) * tok_rows + tok_part
            query_pos = (page_ends[request_id] + base_pages) * PAGE - QR + natural - row_start
            key_pos = page_index * PAGE + columns
            visible = key_pos[None, :] <= query_pos[:, None]
            page_keys = working[0].reshape(PAGE, local_heads, HD)
            page_values = working[1].reshape(PAGE, local_heads, HD)
            query_rows = lax.dynamic_slice_in_dim(all_queries, row_start, QR, 0)
            scores = (
                jnp.einsum(
                    "qkgd,pkd->qkgp", query_rows, page_keys, preferred_element_type=jnp.float32
                )
                * score_scale
            )
            scores = jnp.where(visible[:, None, None, :], scores, NEG)
            old_max = lax.dynamic_slice_in_dim(run_max, row_start, QR, 0)
            old_sum = lax.dynamic_slice_in_dim(run_sum, row_start, QR, 0)
            old_out = lax.dynamic_slice_in_dim(run_out, row_start, QR, 0)
            new_max = jnp.maximum(old_max, jnp.max(scores, axis=3))
            factor = jnp.exp(old_max - new_max)
            numerators = jnp.exp(scores - new_max[..., None])
            new_sum = old_sum * factor + jnp.sum(numerators, axis=3)
            product = jnp.einsum(
                "qkgp,pkd->qkgd",
                numerators.astype(jnp.bfloat16),
                page_values,
                preferred_element_type=jnp.float32,
            )
            new_out = old_out * factor[..., None] + product
            return (
                lax.dynamic_update_slice_in_dim(run_max, new_max, row_start, 0),
                lax.dynamic_update_slice_in_dim(run_sum, new_sum, row_start, 0),
                lax.dynamic_update_slice_in_dim(run_out, new_out, row_start, 0),
            )

        def unchanged(partial_value):
            return partial_value

        return lax.cond(request < REQS, update, unchanged, running)

    run_max, run_sum, run_out = lax.fori_loop(0, page_total, add_page, initial)
    share = SPAN // (ctx_size * sub_size)
    global_max = lax.pmax(run_max, ("ctx", "sub"))
    factor = jnp.exp(run_max - global_max)
    sums_here, outs_here = (
        lax.psum_scatter(
            (run_sum * factor).astype(jnp.bfloat16), ("ctx", "sub"), scatter_dimension=0, tiled=True
        ).astype(jnp.float32),
        lax.psum_scatter(
            (run_out * factor[..., None]).astype(jnp.bfloat16),
            ("ctx", "sub"),
            scatter_dimension=0,
            tiled=True,
        ).astype(jnp.float32),
    )
    finished = (outs_here / sums_here[..., None]).astype(jnp.bfloat16)
    finished = finished.reshape(share, local_heads * per_group * HD)
    return lax.all_to_all(finished, "head", split_axis=0, concat_axis=1, tiled=True)


def per_device(queries, kv_cache, page_counts):
    ctx_size, sub_size, head_count = lax.axis_size("ctx"), lax.axis_size("sub"), lax.axis_size("head")
    small = (
        ctx_size == REQS == 4
        and head_count == sub_size == 2
        and kv_cache.shape[1] == 2 * PAGE
        and kv_cache.shape[2] % (sub_size * HD) == 0
        and queries.shape[0] % 16 == 0
        and queries.shape[0] * head_count * sub_size == QR
    )
    return (one_request_each if small else queries_to_pages)(queries, kv_cache, page_counts)


def solution(mesh):
    return jax.shard_map(
        per_device,
        mesh=mesh,
        in_specs=(
            P(("grp", "ctx", "head", "sub"), None),
            P(None, ("grp", "ctx", "sub"), "head"),
            P("grp"),
        ),
        out_specs=P(("grp", "ctx", "head", "sub"), None),
        check_vma=False,
    )
```

```python
import functools

import jax
import jax.numpy as jnp
from jax import lax
from jax.experimental import pallas as pl
from jax.experimental.pallas import tpu as pltpu
from jax.sharding import PartitionSpec as P

HQ = 128
KVH = 8
HD = 128
REQS = 4
QR = 64
PAGE = 256
SPAN = 256


NEG = -1e30
EXP2_SCALE = HD ** (-0.5) * 1.4426950408889634


def run(copies):
    for copy in copies:
        copy.start()
    for copy in copies:
        copy.wait()


def head_part(step, width):
    return pl.ds(pl.multiple_of((lax.axis_index("head") ^ step) * width, width), width)


def split_kernel(queries, *refs):
    outs, sems = refs[:-1], refs[-1]
    run([
        pltpu.make_async_copy(queries.at[:, head_part(step, out.shape[1])], out, sems.at[step])
        for step, out in enumerate(outs)
    ])


def join_kernel(keys, *refs):
    out, sems = refs[-2:]

    @pl.when(lax.axis_index("sub") == keys[0][1])
    def _():
        run([
            pltpu.make_async_copy(piece, out.at[:, head_part(step, piece.shape[1])], sems.at[i])
            for i, (piece, (step, _)) in enumerate(zip(refs, keys))
        ])


def worker_places(low_ctx):
    return (0, 0), (low_ctx, 1), (low_ctx + 1, 1), (low_ctx + 1, 0)


def own_request(low_ctx):
    ctx, sub = lax.axis_index("ctx"), lax.axis_index("sub")
    found = jnp.int32(-1)
    for request, place in enumerate(worker_places(low_ctx)):
        found = jnp.where((ctx == place[0]) & (sub == place[1]), request, found)
    return found


def pages_of(low_ctx, counts, most_pages):
    request = own_request(low_ctx)
    start = jnp.int32(0)
    for r in range(REQS):
        start = start + jnp.where(r < request, counts[r], 0)
    count = jnp.where(request >= 0, counts[jnp.maximum(request, 0)], 0)
    home_pair = jnp.where(request == 0, -1, jnp.where(request == 1, 1, 5 - request))
    near_pair = jnp.where(request == 0, 1, home_pair ^ 1)
    for p in range(most_pages):
        page = start + p
        pair = page // 2
        which = jnp.where(pair == home_pair, 0, jnp.where(pair == near_pair, 1, 2))
        yield p, p < count, which, pl.ds(pl.multiple_of(lax.rem(page, 2) * PAGE, PAGE), PAGE)


def gather_home_kernel(low_ctx, counts, counts_in, own, after, out, counts_out, sems, counts_sem):
    local_kv, _, most_pages = out.shape[:3]
    counts_copy = pltpu.make_async_copy(counts_in, counts_out, counts_sem)
    counts_copy.start()
    plan = [
        (here & (which == 0), [
            pltpu.make_async_copy(own.at[i, rows, pl.ds(g * HD, HD)], out.at[g, i, p], sems.at[g, i, p])
            for g in range(local_kv) for i in range(2)
        ])
        for p, here, which, rows in pages_of(low_ctx, counts, most_pages)
    ]
    for here, copies in plan:
        @pl.when(here)
        def _():
            for copy in copies:
                copy.start()
    for here, copies in plan:
        @pl.when(here)
        def _():
            for copy in copies:
                copy.wait()
    counts_copy.wait()


def gather_rest(low_ctx, counts, home, far, near, out):
    local_kv, _, most_pages = out.shape[:3]
    for p, here, which, rows in pages_of(low_ctx, counts, most_pages):
        @pl.when(here & (which == 0))
        def _():
            for g in range(local_kv):
                out[g, :, p] = home[g, :, p]
        for n, ref in enumerate((near, far)):
            @pl.when(here & (which == n + 1))
            def _():
                for g in range(local_kv):
                    for i in range(2):
                        out[g, i, p] = ref[i, rows, g * HD:(g + 1) * HD]


def attend_kernel(low_ctx, sub_count, groups, others, counts, home, *refs):
    keys = [key for group in groups for key in group]
    queries, outs = dict(zip(keys, refs)), dict(zip(keys, refs[len(keys) + others:]))
    pages_in = home
    if others:
        pages_in = refs[-1]
        gather_rest(low_ctx, counts, home, *refs[len(keys):len(keys) + others], pages_in)
    head = lax.axis_index("head")
    tokens, width = refs[0].shape
    local_kv, _, most_pages = pages_in.shape[:3]
    span = width // local_kv
    per_group = span // HD
    piece_rows = per_group * tokens
    rows = len(groups[0]) * piece_rows

    def attend(pages):
        span_rows = pages * PAGE
        row = lax.broadcasted_iota(jnp.int32, (rows, PAGE), 0)
        column = lax.broadcasted_iota(jnp.int32, (rows, PAGE), 1)

        def visible_of(group):
            token = lax.rem(row, tokens)
            for i, (step, source) in enumerate(group):
                first_token = ((head ^ step) * sub_count + source) * tokens
                token = jnp.where(row // piece_rows == i, token + first_token, token)
            return column <= PAGE - QR + token

        def of_pages(g, i):
            return pages_in[g, i, 0:pages].reshape(span_rows, HD)

        def scores_of(group, g):
            q_blocks = [queries[key][:, g * span:(g + 1) * span] for key in group]
            q_rows = jnp.concatenate([q[:, j * HD:(j + 1) * HD] for q in q_blocks for j in range(per_group)], axis=0)
            scores = lax.dot_general(
                q_rows, of_pages(g, 0), (((1,), (1,)), ((), ())), preferred_element_type=jnp.float32
            )
            scores = [scores[:, p * PAGE:(p + 1) * PAGE] for p in range(pages)]
            scores[-1] = jnp.where(visible_of(group), scores[-1], NEG)
            return scores

        units = [(group, g) for group in groups for g in range(local_kv)]
        scores = scores_of(*units[0])
        for n, (group, g) in enumerate(units):
            later = scores_of(*units[n + 1]) if n + 1 < len(units) else None
            top = jnp.max(functools.reduce(jnp.maximum, scores), axis=1, keepdims=True)
            numerators = [jnp.exp2((s - top) * EXP2_SCALE) for s in scores]
            totals = jnp.sum(functools.reduce(jnp.add, numerators), axis=1, keepdims=True)
            weights = jnp.concatenate([s.astype(jnp.bfloat16) for s in numerators], axis=1)
            product = jnp.dot(weights, of_pages(g, 1), preferred_element_type=jnp.float32)
            done = (product / totals).astype(jnp.bfloat16)
            for i, key in enumerate(group):
                start = i * piece_rows
                outs[key][:, g * span:(g + 1) * span] = jnp.concatenate(
                    [done[start + j * tokens:start + (j + 1) * tokens] for j in range(per_group)], axis=1
                )
            scores = later

    request = own_request(low_ctx)

    @pl.when(request >= 0)
    def _():
        count = counts[request]
        for pages in [*range(1, most_pages - REQS + 3), most_pages]:
            @pl.when(count == pages)
            def _():
                attend(pages)


def one_request_each(queries, kv_cache, page_counts):
    ctx_size, sub_size = lax.axis_size("ctx"), lax.axis_size("sub")
    head_count = lax.axis_size("head")
    low_ctx = ctx_size // 2
    most_pages = kv_cache.shape[1] // PAGE * ctx_size * sub_size // 4
    local_kv = kv_cache.shape[2] // HD
    tokens, width = queries.shape[0], queries.shape[1] // head_count
    anywhere = pl.BlockSpec(memory_space=pl.ANY)
    in_vmem = pl.BlockSpec(memory_space=pltpu.VMEM)
    q_piece = pltpu.VMEM((tokens, width), queries.dtype)

    def vmem(array):
        return pltpu.with_memory_space_constraint(array, pltpu.VMEM)

    def hbm(array):
        return pltpu.with_memory_space_constraint(array, pltpu.HBM)

    def moved(array, routes):
        def flat(place):
            return (place[0] * head_count + place[1]) * sub_size + place[2]

        return lax.ppermute(array, ("ctx", "head", "sub"), [(flat(a), flat(b)) for a, b in routes])

    def worker(request, head):
        ctx, sub = worker_places(low_ctx)[request]
        return ctx, head, sub

    heads = range(head_count)
    q_out = pl.pallas_call(
        split_kernel,
        out_shape=[q_piece] * head_count,
        in_specs=[anywhere],
        out_specs=[anywhere] * head_count,
        scratch_shapes=[pltpu.SemaphoreType.DMA((head_count,))],
        compiler_params=pltpu.CompilerParams(vmem_limit_bytes=2**20),
        name="split",
    )(hbm(queries))
    routes = {
        (step, s): [((r, h, s), worker(r, h ^ step)) for r in range(ctx_size) for h in heads]
        for s in range(sub_size) for step in heads[::-1]
    }
    first, last = list(routes)[0], list(routes)[-1]
    q_in = {first: moved(q_out[first[0]], routes[first])}
    home, counts = pl.pallas_call(
        functools.partial(gather_home_kernel, low_ctx),
        out_shape=[
            pltpu.VMEM((local_kv, 2, most_pages, PAGE, HD), kv_cache.dtype),
            pltpu.VMEM(page_counts.shape, page_counts.dtype),
        ],
        in_specs=[pl.BlockSpec(memory_space=pltpu.SMEM)] + [anywhere] * 3,
        out_specs=[anywhere] * 2,
        scratch_shapes=[pltpu.SemaphoreType.DMA((local_kv, 2, most_pages)), pltpu.SemaphoreType.DMA],
        compiler_params=pltpu.CompilerParams(vmem_limit_bytes=2**20),
        name="gather_home",
    )(hbm(page_counts), hbm(page_counts), hbm(kv_cache), vmem(q_in[first]))
    q_last, counts = lax.optimization_barrier((q_out[last[0]], counts))
    for key in list(routes)[1:]:
        q_in[key] = moved(q_last if key == last else q_out[key[0]], routes[key])

    pairs = [(low_ctx + n // 2, n % 2) for n in range(4)]
    workers = worker_places(low_ctx)
    near, far = (
        moved(kv_cache, [((*a[:1], h, *a[1:]), (*b[:1], h, *b[1:])) for a, b in sends for h in heads])
        for sends in (
            [(pairs[0], workers[1]), (pairs[1], workers[0]), (pairs[2], workers[2]), (pairs[3], workers[3])],
            [(pairs[0], workers[0]), (pairs[1], workers[2]), (pairs[2], workers[1])],
        )
    )
    groups = [[(step, s) for step in heads[::-1]] for s in range(sub_size)]
    back = {}
    pages, others = home, [vmem(far), vmem(near)]
    for keys in groups:
        outs = pl.pallas_call(
            functools.partial(attend_kernel, low_ctx, sub_size, [keys], len(others)),
            out_shape=[q_piece] * len(keys) + [pltpu.VMEM(home.shape, home.dtype)] * bool(others),
            in_specs=[pl.BlockSpec(memory_space=pltpu.SMEM)] + [in_vmem] * (1 + len(keys) + len(others)),
            out_specs=[in_vmem] * (len(keys) + bool(others)),
            compiler_params=pltpu.CompilerParams(vmem_limit_bytes=12 * 2**20),
            cost_estimate=pl.CostEstimate(flops=10**10, bytes_accessed=2**22, transcendentals=10**6),
            name=f"attend_{keys[0][1]}",
        )(vmem(counts), vmem(pages), *[vmem(q_in[key]) for key in keys], *others)
        for key, out in zip(keys, outs):
            back[key] = moved(out, [(b, a) for a, b in routes[key]])
        if others:
            pages, others = outs[-1], []

    joined = []
    for keys in groups:
        joined = [
            pl.pallas_call(
                functools.partial(join_kernel, keys),
                out_shape=pltpu.HBM(queries.shape, queries.dtype),
                in_specs=[anywhere] * (len(keys) + len(joined)),
                out_specs=anywhere,
                scratch_shapes=[pltpu.SemaphoreType.DMA((len(keys),))],
                input_output_aliases={len(keys): 0} if joined else {},
                compiler_params=pltpu.CompilerParams(vmem_limit_bytes=2**20),
                name=f"join_{keys[0][1]}",
            )(*[vmem(back[key]) for key in keys], *map(hbm, joined))
        ]
    return joined[0]


def from_behind(array, axis, by):
    count = lax.axis_size(axis)
    pairs = [(i, i + by) for i in range(count) if 0 <= i + by < count]
    return lax.ppermute(array, axis, pairs)


def queries_to_pages(queries, kv_cache, page_counts):
    per_group = HQ // KVH
    local_heads = kv_cache.shape[2] // HD
    ctx_size = lax.axis_size("ctx")
    sub_size = lax.axis_size("sub")
    head_count = lax.axis_size("head")
    tok_rows = queries.shape[0]
    score_scale = HD ** (-0.5)
    regrouped = lax.all_to_all(queries, "head", split_axis=1, concat_axis=0, tiled=True)
    all_queries = lax.all_gather(regrouped, ("ctx", "sub"), axis=0, tiled=True)
    all_queries = all_queries.reshape(SPAN, local_heads, per_group, HD)
    page_ends = jnp.cumsum(page_counts)
    ctx_rows = SPAN // ctx_size
    offsets = jnp.arange(QR, dtype=jnp.int32)
    columns = jnp.arange(PAGE, dtype=jnp.int32)
    flat_index = lax.axis_index("ctx") * sub_size + lax.axis_index("sub")
    pages_here = kv_cache.shape[1] // PAGE
    base_pages = pages_here * ctx_size * sub_size // 2
    initial = (
        jnp.full((SPAN, local_heads, per_group), NEG, jnp.float32),
        jnp.zeros((SPAN, local_heads, per_group), jnp.float32),
        jnp.zeros((SPAN, local_heads, per_group, HD), jnp.float32),
    )
    half_rows = kv_cache.shape[1] // 2
    arrived = from_behind(kv_cache[:, half_rows:], "ctx", -(ctx_size // 2))
    is_lower = lax.axis_index("ctx") < ctx_size // 2
    source_flat = flat_index + ctx_size // 2 * sub_size
    working = jnp.where(is_lower, arrived, kv_cache[:, :half_rows])
    first_page = jnp.where(
        is_lower, source_flat * pages_here + pages_here // 2, flat_index * pages_here
    )
    page_total = working.shape[1] // PAGE

    def add_page(page_turn, running):
        page_index = first_page + page_turn
        relative = page_index - base_pages
        counted = jnp.sum((relative >= page_ends).astype(jnp.int32))
        request = jnp.where(relative < 0, REQS, counted)

        def update(partial_value):
            run_max, run_sum, run_out = partial_value
            request_id = jnp.minimum(request, REQS - 1)
            row_start = request_id * QR
            gathered = row_start + offsets
            within = gathered % ctx_rows
            ctx_block = gathered // ctx_rows
            sub_part = within // (head_count * tok_rows)
            head_part = within // tok_rows % head_count
            tok_part = within % tok_rows
            natural = ctx_block * ctx_rows + (head_part * sub_size + sub_part) * tok_rows + tok_part
            query_pos = (page_ends[request_id] + base_pages) * PAGE - QR + natural - row_start
            key_pos = page_index * PAGE + columns
            visible = key_pos[None, :] <= query_pos[:, None]
            page_keys = working[0].reshape(PAGE, local_heads, HD)
            page_values = working[1].reshape(PAGE, local_heads, HD)
            query_rows = lax.dynamic_slice_in_dim(all_queries, row_start, QR, 0)
            scores = (
                jnp.einsum(
                    "qkgd,pkd->qkgp", query_rows, page_keys, preferred_element_type=jnp.float32
                )
                * score_scale
            )
            scores = jnp.where(visible[:, None, None, :], scores, NEG)
            old_max = lax.dynamic_slice_in_dim(run_max, row_start, QR, 0)
            old_sum = lax.dynamic_slice_in_dim(run_sum, row_start, QR, 0)
            old_out = lax.dynamic_slice_in_dim(run_out, row_start, QR, 0)
            new_max = jnp.maximum(old_max, jnp.max(scores, axis=3))
            factor = jnp.exp(old_max - new_max)
            numerators = jnp.exp(scores - new_max[..., None])
            new_sum = old_sum * factor + jnp.sum(numerators, axis=3)
            product = jnp.einsum(
                "qkgp,pkd->qkgd",
                numerators.astype(jnp.bfloat16),
                page_values,
                preferred_element_type=jnp.float32,
            )
            new_out = old_out * factor[..., None] + product
            return (
                lax.dynamic_update_slice_in_dim(run_max, new_max, row_start, 0),
                lax.dynamic_update_slice_in_dim(run_sum, new_sum, row_start, 0),
                lax.dynamic_update_slice_in_dim(run_out, new_out, row_start, 0),
            )

        def unchanged(partial_value):
            return partial_value

        return lax.cond(request < REQS, update, unchanged, running)

    run_max, run_sum, run_out = lax.fori_loop(0, page_total, add_page, initial)
    share = SPAN // (ctx_size * sub_size)
    global_max = lax.pmax(run_max, ("ctx", "sub"))
    factor = jnp.exp(run_max - global_max)
    sums_here, outs_here = (
        lax.psum_scatter(
            (run_sum * factor).astype(jnp.bfloat16), ("ctx", "sub"), scatter_dimension=0, tiled=True
        ).astype(jnp.float32),
        lax.psum_scatter(
            (run_out * factor[..., None]).astype(jnp.bfloat16),
            ("ctx", "sub"),
            scatter_dimension=0,
            tiled=True,
        ).astype(jnp.float32),
    )
    finished = (outs_here / sums_here[..., None]).astype(jnp.bfloat16)
    finished = finished.reshape(share, local_heads * per_group * HD)
    return lax.all_to_all(finished, "head", split_axis=0, concat_axis=1, tiled=True)


def per_device(queries, kv_cache, page_counts):
    ctx_size, sub_size, head_count = lax.axis_size("ctx"), lax.axis_size("sub"), lax.axis_size("head")
    small = (
        ctx_size == REQS == 4
        and head_count == sub_size == 2
        and kv_cache.shape[1] == 2 * PAGE
        and kv_cache.shape[2] % (sub_size * HD) == 0
        and queries.shape[0] % 16 == 0
        and queries.shape[0] * head_count * sub_size == QR
    )
    return (one_request_each if small else queries_to_pages)(queries, kv_cache, page_counts)


def solution(mesh):
    return jax.shard_map(
        per_device,
        mesh=mesh,
        in_specs=(
            P(("grp", "ctx", "head", "sub"), None),
            P(None, ("grp", "ctx", "sub"), "head"),
            P("grp"),
        ),
        out_specs=P(("grp", "ctx", "head", "sub"), None),
        check_vma=False,
    )
```

```python
import functools

import jax
import jax.numpy as jnp
from jax import lax
from jax.experimental import pallas as pl
from jax.experimental.pallas import tpu as pltpu
from jax.sharding import PartitionSpec as P

HQ = 128
KVH = 8
HD = 128
REQS = 4
QR = 64
PAGE = 256
SPAN = 256


NEG = -1e30
EXP2_SCALE = HD ** (-0.5) * 1.4426950408889634


def run(copies):
    for copy in copies:
        copy.start()
    for copy in copies:
        copy.wait()


def head_part(step, width):
    return pl.ds(pl.multiple_of((lax.axis_index("head") ^ step) * width, width), width)


def split_kernel(queries, *refs):
    outs, sems = refs[:-1], refs[-1]
    run([
        pltpu.make_async_copy(queries.at[:, head_part(step, out.shape[1])], out, sems.at[step])
        for step, out in enumerate(outs)
    ])


def join_kernel(keys, *refs):
    out, sems = refs[-2:]

    @pl.when(lax.axis_index("sub") == keys[0][1])
    def _():
        run([
            pltpu.make_async_copy(piece, out.at[:, head_part(step, piece.shape[1])], sems.at[i])
            for i, (piece, (step, _)) in enumerate(zip(refs, keys))
        ])


def worker_places(low_ctx):
    return (0, 0), (low_ctx, 1), (low_ctx + 1, 1), (low_ctx + 1, 0)


def own_request(low_ctx):
    ctx, sub = lax.axis_index("ctx"), lax.axis_index("sub")
    found = jnp.int32(-1)
    for request, place in enumerate(worker_places(low_ctx)):
        found = jnp.where((ctx == place[0]) & (sub == place[1]), request, found)
    return found


def pages_of(low_ctx, counts, most_pages):
    request = own_request(low_ctx)
    start = jnp.int32(0)
    for r in range(REQS):
        start = start + jnp.where(r < request, counts[r], 0)
    count = jnp.where(request >= 0, counts[jnp.maximum(request, 0)], 0)
    home_pair = jnp.where(request == 0, -1, jnp.where(request == 1, 1, 5 - request))
    near_pair = jnp.where(request == 0, 1, home_pair ^ 1)
    for p in range(most_pages):
        page = start + p
        pair = page // 2
        which = jnp.where(pair == home_pair, 0, jnp.where(pair == near_pair, 1, 2))
        yield p, p < count, which, pl.ds(pl.multiple_of(lax.rem(page, 2) * PAGE, PAGE), PAGE)


def gather_home_kernel(low_ctx, counts, counts_in, own, after, out, counts_out, sems, counts_sem):
    local_kv, _, most_pages = out.shape[:3]
    counts_copy = pltpu.make_async_copy(counts_in, counts_out, counts_sem)
    counts_copy.start()
    plan = [
        (here & (which == 0), [
            pltpu.make_async_copy(own.at[i, rows, pl.ds(g * HD, HD)], out.at[g, i, p], sems.at[g, i, p])
            for g in range(local_kv) for i in range(2)
        ])
        for p, here, which, rows in pages_of(low_ctx, counts, most_pages)
    ]
    for here, copies in plan:
        @pl.when(here)
        def _():
            for copy in copies:
                copy.start()
    for here, copies in plan:
        @pl.when(here)
        def _():
            for copy in copies:
                copy.wait()
    counts_copy.wait()


def gather_rest(low_ctx, counts, home, far, near, out):
    local_kv, _, most_pages = out.shape[:3]
    for p, here, which, rows in pages_of(low_ctx, counts, most_pages):
        @pl.when(here & (which == 0))
        def _():
            for g in range(local_kv):
                out[g, :, p] = home[g, :, p]
        for n, ref in enumerate((near, far)):
            @pl.when(here & (which == n + 1))
            def _():
                for g in range(local_kv):
                    for i in range(2):
                        out[g, i, p] = ref[i, rows, g * HD:(g + 1) * HD]


def attend_kernel(low_ctx, sub_count, groups, others, counts, home, *refs):
    keys = [key for group in groups for key in group]
    queries, outs = dict(zip(keys, refs)), dict(zip(keys, refs[len(keys) + others:]))
    pages_in = home
    if others:
        pages_in = refs[-1]
        gather_rest(low_ctx, counts, home, *refs[len(keys):len(keys) + others], pages_in)
    head = lax.axis_index("head")
    tokens, width = refs[0].shape
    local_kv, _, most_pages = pages_in.shape[:3]
    span = width // local_kv
    per_group = span // HD
    piece_rows = per_group * tokens
    rows = len(groups[0]) * piece_rows

    def attend(pages):
        span_rows = pages * PAGE
        row = lax.broadcasted_iota(jnp.int32, (rows, PAGE), 0)
        column = lax.broadcasted_iota(jnp.int32, (rows, PAGE), 1)

        def visible_of(group):
            token = lax.rem(row, tokens)
            for i, (step, source) in enumerate(group):
                first_token = ((head ^ step) * sub_count + source) * tokens
                token = jnp.where(row // piece_rows == i, token + first_token, token)
            return column <= PAGE - QR + token

        def of_pages(g, i):
            return pages_in[g, i, 0:pages].reshape(span_rows, HD)

        def scores_of(group, g):
            q_blocks = [queries[key][:, g * span:(g + 1) * span] for key in group]
            q_rows = jnp.concatenate([q[:, j * HD:(j + 1) * HD] for q in q_blocks for j in range(per_group)], axis=0)
            scores = lax.dot_general(
                q_rows, of_pages(g, 0), (((1,), (1,)), ((), ())), preferred_element_type=jnp.float32
            )
            scores = [scores[:, p * PAGE:(p + 1) * PAGE] for p in range(pages)]
            scores[-1] = jnp.where(visible_of(group), scores[-1], NEG)
            return scores

        units = [(group, g) for group in groups for g in range(local_kv)]
        scores = scores_of(*units[0])
        for n, (group, g) in enumerate(units):
            later = scores_of(*units[n + 1]) if n + 1 < len(units) else None
            top = jnp.max(functools.reduce(jnp.maximum, scores), axis=1, keepdims=True)
            weights = [jnp.exp2(((s - top) * EXP2_SCALE).astype(jnp.bfloat16)) for s in scores]
            values = jnp.concatenate([of_pages(g, 1), jnp.ones((span_rows, HD), jnp.bfloat16)], axis=1)
            product = jnp.dot(jnp.concatenate(weights, axis=1), values, preferred_element_type=jnp.float32)
            done = (product[:, :HD] / product[:, HD:]).astype(jnp.bfloat16)
            for i, key in enumerate(group):
                start = i * piece_rows
                outs[key][:, g * span:(g + 1) * span] = jnp.concatenate(
                    [done[start + j * tokens:start + (j + 1) * tokens] for j in range(per_group)], axis=1
                )
            scores = later

    request = own_request(low_ctx)

    @pl.when(request >= 0)
    def _():
        count = counts[request]
        for pages in [*range(1, most_pages - REQS + 3), most_pages]:
            @pl.when(count == pages)
            def _():
                attend(pages)


def one_request_each(queries, kv_cache, page_counts):
    ctx_size, sub_size = lax.axis_size("ctx"), lax.axis_size("sub")
    head_count = lax.axis_size("head")
    low_ctx = ctx_size // 2
    most_pages = kv_cache.shape[1] // PAGE * ctx_size * sub_size // 4
    local_kv = kv_cache.shape[2] // HD
    tokens, width = queries.shape[0], queries.shape[1] // head_count
    anywhere = pl.BlockSpec(memory_space=pl.ANY)
    in_vmem = pl.BlockSpec(memory_space=pltpu.VMEM)
    q_piece = pltpu.VMEM((tokens, width), queries.dtype)

    def vmem(array):
        return pltpu.with_memory_space_constraint(array, pltpu.VMEM)

    def hbm(array):
        return pltpu.with_memory_space_constraint(array, pltpu.HBM)

    def moved(array, routes):
        def flat(place):
            return (place[0] * head_count + place[1]) * sub_size + place[2]

        return lax.ppermute(array, ("ctx", "head", "sub"), [(flat(a), flat(b)) for a, b in routes])

    def worker(request, head):
        ctx, sub = worker_places(low_ctx)[request]
        return ctx, head, sub

    heads = range(head_count)
    q_out = pl.pallas_call(
        split_kernel,
        out_shape=[q_piece] * head_count,
        in_specs=[anywhere],
        out_specs=[anywhere] * head_count,
        scratch_shapes=[pltpu.SemaphoreType.DMA((head_count,))],
        compiler_params=pltpu.CompilerParams(vmem_limit_bytes=2**20),
        name="split",
    )(hbm(queries))
    routes = {
        (step, s): [((r, h, s), worker(r, h ^ step)) for r in range(ctx_size) for h in heads]
        for s in range(sub_size) for step in heads[::-1]
    }
    first, last = list(routes)[0], list(routes)[-1]
    q_in = {first: moved(q_out[first[0]], routes[first])}
    home, counts = pl.pallas_call(
        functools.partial(gather_home_kernel, low_ctx),
        out_shape=[
            pltpu.VMEM((local_kv, 2, most_pages, PAGE, HD), kv_cache.dtype),
            pltpu.VMEM(page_counts.shape, page_counts.dtype),
        ],
        in_specs=[pl.BlockSpec(memory_space=pltpu.SMEM)] + [anywhere] * 3,
        out_specs=[anywhere] * 2,
        scratch_shapes=[pltpu.SemaphoreType.DMA((local_kv, 2, most_pages)), pltpu.SemaphoreType.DMA],
        compiler_params=pltpu.CompilerParams(vmem_limit_bytes=2**20),
        name="gather_home",
    )(hbm(page_counts), hbm(page_counts), hbm(kv_cache), vmem(q_in[first]))
    q_last, counts = lax.optimization_barrier((q_out[last[0]], counts))
    for key in list(routes)[1:]:
        q_in[key] = moved(q_last if key == last else q_out[key[0]], routes[key])

    pairs = [(low_ctx + n // 2, n % 2) for n in range(4)]
    workers = worker_places(low_ctx)
    near, far = (
        moved(kv_cache, [((*a[:1], h, *a[1:]), (*b[:1], h, *b[1:])) for a, b in sends for h in heads])
        for sends in (
            [(pairs[0], workers[1]), (pairs[1], workers[0]), (pairs[2], workers[2]), (pairs[3], workers[3])],
            [(pairs[0], workers[0]), (pairs[1], workers[2]), (pairs[2], workers[1])],
        )
    )
    groups = [[(step, s) for step in heads[::-1]] for s in range(sub_size)]
    back = {}
    pages, others = home, [vmem(far), vmem(near)]
    for keys in groups:
        outs = pl.pallas_call(
            functools.partial(attend_kernel, low_ctx, sub_size, [keys], len(others)),
            out_shape=[q_piece] * len(keys) + [pltpu.VMEM(home.shape, home.dtype)] * bool(others),
            in_specs=[pl.BlockSpec(memory_space=pltpu.SMEM)] + [in_vmem] * (1 + len(keys) + len(others)),
            out_specs=[in_vmem] * (len(keys) + bool(others)),
            compiler_params=pltpu.CompilerParams(vmem_limit_bytes=12 * 2**20),
            cost_estimate=pl.CostEstimate(flops=10**10, bytes_accessed=2**22, transcendentals=10**6),
            name=f"attend_{keys[0][1]}",
        )(vmem(counts), vmem(pages), *[vmem(q_in[key]) for key in keys], *others)
        for key, out in zip(keys, outs):
            back[key] = moved(out, [(b, a) for a, b in routes[key]])
        if others:
            pages, others = outs[-1], []

    joined = []
    for keys in groups:
        joined = [
            pl.pallas_call(
                functools.partial(join_kernel, keys),
                out_shape=pltpu.HBM(queries.shape, queries.dtype),
                in_specs=[anywhere] * (len(keys) + len(joined)),
                out_specs=anywhere,
                scratch_shapes=[pltpu.SemaphoreType.DMA((len(keys),))],
                input_output_aliases={len(keys): 0} if joined else {},
                compiler_params=pltpu.CompilerParams(vmem_limit_bytes=2**20),
                name=f"join_{keys[0][1]}",
            )(*[vmem(back[key]) for key in keys], *map(hbm, joined))
        ]
    return joined[0]


def from_behind(array, axis, by):
    count = lax.axis_size(axis)
    pairs = [(i, i + by) for i in range(count) if 0 <= i + by < count]
    return lax.ppermute(array, axis, pairs)


def queries_to_pages(queries, kv_cache, page_counts):
    per_group = HQ // KVH
    local_heads = kv_cache.shape[2] // HD
    ctx_size = lax.axis_size("ctx")
    sub_size = lax.axis_size("sub")
    head_count = lax.axis_size("head")
    tok_rows = queries.shape[0]
    score_scale = HD ** (-0.5)
    regrouped = lax.all_to_all(queries, "head", split_axis=1, concat_axis=0, tiled=True)
    all_queries = lax.all_gather(regrouped, ("ctx", "sub"), axis=0, tiled=True)
    all_queries = all_queries.reshape(SPAN, local_heads, per_group, HD)
    page_ends = jnp.cumsum(page_counts)
    ctx_rows = SPAN // ctx_size
    offsets = jnp.arange(QR, dtype=jnp.int32)
    columns = jnp.arange(PAGE, dtype=jnp.int32)
    flat_index = lax.axis_index("ctx") * sub_size + lax.axis_index("sub")
    pages_here = kv_cache.shape[1] // PAGE
    base_pages = pages_here * ctx_size * sub_size // 2
    initial = (
        jnp.full((SPAN, local_heads, per_group), NEG, jnp.float32),
        jnp.zeros((SPAN, local_heads, per_group), jnp.float32),
        jnp.zeros((SPAN, local_heads, per_group, HD), jnp.float32),
    )
    half_rows = kv_cache.shape[1] // 2
    arrived = from_behind(kv_cache[:, half_rows:], "ctx", -(ctx_size // 2))
    is_lower = lax.axis_index("ctx") < ctx_size // 2
    source_flat = flat_index + ctx_size // 2 * sub_size
    working = jnp.where(is_lower, arrived, kv_cache[:, :half_rows])
    first_page = jnp.where(
        is_lower, source_flat * pages_here + pages_here // 2, flat_index * pages_here
    )
    page_total = working.shape[1] // PAGE

    def add_page(page_turn, running):
        page_index = first_page + page_turn
        relative = page_index - base_pages
        counted = jnp.sum((relative >= page_ends).astype(jnp.int32))
        request = jnp.where(relative < 0, REQS, counted)

        def update(partial_value):
            run_max, run_sum, run_out = partial_value
            request_id = jnp.minimum(request, REQS - 1)
            row_start = request_id * QR
            gathered = row_start + offsets
            within = gathered % ctx_rows
            ctx_block = gathered // ctx_rows
            sub_part = within // (head_count * tok_rows)
            head_part = within // tok_rows % head_count
            tok_part = within % tok_rows
            natural = ctx_block * ctx_rows + (head_part * sub_size + sub_part) * tok_rows + tok_part
            query_pos = (page_ends[request_id] + base_pages) * PAGE - QR + natural - row_start
            key_pos = page_index * PAGE + columns
            visible = key_pos[None, :] <= query_pos[:, None]
            page_keys = working[0].reshape(PAGE, local_heads, HD)
            page_values = working[1].reshape(PAGE, local_heads, HD)
            query_rows = lax.dynamic_slice_in_dim(all_queries, row_start, QR, 0)
            scores = (
                jnp.einsum(
                    "qkgd,pkd->qkgp", query_rows, page_keys, preferred_element_type=jnp.float32
                )
                * score_scale
            )
            scores = jnp.where(visible[:, None, None, :], scores, NEG)
            old_max = lax.dynamic_slice_in_dim(run_max, row_start, QR, 0)
            old_sum = lax.dynamic_slice_in_dim(run_sum, row_start, QR, 0)
            old_out = lax.dynamic_slice_in_dim(run_out, row_start, QR, 0)
            new_max = jnp.maximum(old_max, jnp.max(scores, axis=3))
            factor = jnp.exp(old_max - new_max)
            numerators = jnp.exp(scores - new_max[..., None])
            new_sum = old_sum * factor + jnp.sum(numerators, axis=3)
            product = jnp.einsum(
                "qkgp,pkd->qkgd",
                numerators.astype(jnp.bfloat16),
                page_values,
                preferred_element_type=jnp.float32,
            )
            new_out = old_out * factor[..., None] + product
            return (
                lax.dynamic_update_slice_in_dim(run_max, new_max, row_start, 0),
                lax.dynamic_update_slice_in_dim(run_sum, new_sum, row_start, 0),
                lax.dynamic_update_slice_in_dim(run_out, new_out, row_start, 0),
            )

        def unchanged(partial_value):
            return partial_value

        return lax.cond(request < REQS, update, unchanged, running)

    run_max, run_sum, run_out = lax.fori_loop(0, page_total, add_page, initial)
    share = SPAN // (ctx_size * sub_size)
    global_max = lax.pmax(run_max, ("ctx", "sub"))
    factor = jnp.exp(run_max - global_max)
    sums_here, outs_here = (
        lax.psum_scatter(
            (run_sum * factor).astype(jnp.bfloat16), ("ctx", "sub"), scatter_dimension=0, tiled=True
        ).astype(jnp.float32),
        lax.psum_scatter(
            (run_out * factor[..., None]).astype(jnp.bfloat16),
            ("ctx", "sub"),
            scatter_dimension=0,
            tiled=True,
        ).astype(jnp.float32),
    )
    finished = (outs_here / sums_here[..., None]).astype(jnp.bfloat16)
    finished = finished.reshape(share, local_heads * per_group * HD)
    return lax.all_to_all(finished, "head", split_axis=0, concat_axis=1, tiled=True)


def per_device(queries, kv_cache, page_counts):
    ctx_size, sub_size, head_count = lax.axis_size("ctx"), lax.axis_size("sub"), lax.axis_size("head")
    small = (
        ctx_size == REQS == 4
        and head_count == sub_size == 2
        and kv_cache.shape[1] == 2 * PAGE
        and kv_cache.shape[2] % (sub_size * HD) == 0
        and queries.shape[0] % 16 == 0
        and queries.shape[0] * head_count * sub_size == QR
    )
    return (one_request_each if small else queries_to_pages)(queries, kv_cache, page_counts)


def solution(mesh):
    return jax.shard_map(
        per_device,
        mesh=mesh,
        in_specs=(
            P(("grp", "ctx", "head", "sub"), None),
            P(None, ("grp", "ctx", "sub"), "head"),
            P("grp"),
        ),
        out_specs=P(("grp", "ctx", "head", "sub"), None),
        check_vma=False,
    )
```

```python
import functools

import jax
import jax.numpy as jnp
from jax import lax
from jax.experimental import pallas as pl
from jax.experimental.pallas import tpu as pltpu
from jax.sharding import PartitionSpec as P

HQ = 128
KVH = 8
HD = 128
REQS = 4
QR = 64
PAGE = 256
SPAN = 256


NEG = -1e30
EXP2_SCALE = HD ** (-0.5) * 1.4426950408889634


def run(copies):
    for copy in copies:
        copy.start()
    for copy in copies:
        copy.wait()


def head_part(step, width):
    return pl.ds(pl.multiple_of((lax.axis_index("head") ^ step) * width, width), width)


def split_kernel(queries, *refs):
    outs, sems = refs[:-1], refs[-1]
    run([
        pltpu.make_async_copy(queries.at[:, head_part(step, out.shape[1])], out, sems.at[step])
        for step, out in enumerate(outs)
    ])


def join_kernel(keys, *refs):
    out, sems = refs[-2:]

    @pl.when(lax.axis_index("sub") == keys[0][1])
    def _():
        run([
            pltpu.make_async_copy(piece, out.at[:, head_part(step, piece.shape[1])], sems.at[i])
            for i, (piece, (step, _)) in enumerate(zip(refs, keys))
        ])


def worker_places(low_ctx):
    return (0, 0), (low_ctx, 1), (low_ctx + 1, 1), (low_ctx + 1, 0)


def own_request(low_ctx):
    ctx, sub = lax.axis_index("ctx"), lax.axis_index("sub")
    found = jnp.int32(-1)
    for request, place in enumerate(worker_places(low_ctx)):
        found = jnp.where((ctx == place[0]) & (sub == place[1]), request, found)
    return found


def pages_of(low_ctx, counts, most_pages):
    request = own_request(low_ctx)
    start = jnp.int32(0)
    for r in range(REQS):
        start = start + jnp.where(r < request, counts[r], 0)
    count = jnp.where(request >= 0, counts[jnp.maximum(request, 0)], 0)
    home_pair = jnp.where(request == 0, -1, jnp.where(request == 1, 1, 5 - request))
    near_pair = jnp.where(request == 0, 1, home_pair ^ 1)
    for p in range(most_pages):
        page = start + p
        pair = page // 2
        which = jnp.where(pair == home_pair, 0, jnp.where(pair == near_pair, 1, 2))
        yield p, p < count, which, pl.ds(pl.multiple_of(lax.rem(page, 2) * PAGE, PAGE), PAGE)


def gather_home_kernel(low_ctx, counts, counts_in, own, after, out, counts_out, sems, counts_sem):
    local_kv, _, most_pages = out.shape[:3]
    counts_copy = pltpu.make_async_copy(counts_in, counts_out, counts_sem)
    counts_copy.start()
    plan = [
        (here & (which == 0), [
            pltpu.make_async_copy(own.at[i, rows, pl.ds(g * HD, HD)], out.at[g, i, p], sems.at[g, i, p])
            for g in range(local_kv) for i in range(2)
        ])
        for p, here, which, rows in pages_of(low_ctx, counts, most_pages)
    ]
    for here, copies in plan:
        @pl.when(here)
        def _():
            for copy in copies:
                copy.start()
    for here, copies in plan:
        @pl.when(here)
        def _():
            for copy in copies:
                copy.wait()
    counts_copy.wait()


def gather_rest(low_ctx, counts, home, near, far, out):
    local_kv, _, most_pages = out.shape[:3]
    for p, here, which, rows in pages_of(low_ctx, counts, most_pages):
        @pl.when(here & (which == 0))
        def _():
            for g in range(local_kv):
                out[g, :, p] = home[g, :, p]
        for n, ref in enumerate((near, far)):
            @pl.when(here & (which == n + 1))
            def _():
                for g in range(local_kv):
                    for i in range(2):
                        out[g, i, p] = ref[i, rows, g * HD:(g + 1) * HD]


def attend_kernel(low_ctx, sub_count, groups, others, counts, home, *refs):
    keys = [key for group in groups for key in group]
    queries, outs = dict(zip(keys, refs)), dict(zip(keys, refs[len(keys) + others:]))
    pages_in = home
    if others:
        pages_in = refs[-1]
        gather_rest(low_ctx, counts, home, *refs[len(keys):len(keys) + others], pages_in)
    head = lax.axis_index("head")
    tokens, width = refs[0].shape
    local_kv, _, most_pages = pages_in.shape[:3]
    span = width // local_kv
    per_group = span // HD
    piece_rows = per_group * tokens
    rows = len(groups[0]) * piece_rows

    def attend(pages):
        span_rows = pages * PAGE
        row = lax.broadcasted_iota(jnp.int32, (rows, PAGE), 0)
        column = lax.broadcasted_iota(jnp.int32, (rows, PAGE), 1)

        def visible_of(group):
            token = lax.rem(row, tokens)
            for i, (step, source) in enumerate(group):
                first_token = ((head ^ step) * sub_count + source) * tokens
                token = jnp.where(row // piece_rows == i, token + first_token, token)
            return column <= PAGE - QR + token

        def of_pages(g, i):
            return pages_in[g, i, 0:pages].reshape(span_rows, HD)

        def scores_of(group, g):
            q_blocks = [queries[key][:, g * span:(g + 1) * span] for key in group]
            q_rows = jnp.concatenate([q[:, j * HD:(j + 1) * HD] for q in q_blocks for j in range(per_group)], axis=0)
            scores = lax.dot_general(
                q_rows, of_pages(g, 0), (((1,), (1,)), ((), ())), preferred_element_type=jnp.float32
            )
            scores = [scores[:, p * PAGE:(p + 1) * PAGE] for p in range(pages)]
            scores[-1] = jnp.where(visible_of(group), scores[-1], NEG)
            return scores

        units = [(group, g) for group in groups for g in range(local_kv)]
        scores = scores_of(*units[0])
        for n, (group, g) in enumerate(units):
            later = scores_of(*units[n + 1]) if n + 1 < len(units) else None
            top = jnp.max(functools.reduce(jnp.maximum, scores), axis=1, keepdims=True)
            numerators = [jnp.exp2((s - top) * EXP2_SCALE) for s in scores]
            totals = jnp.sum(functools.reduce(jnp.add, numerators), axis=1, keepdims=True)
            weights = jnp.concatenate([s.astype(jnp.bfloat16) for s in numerators], axis=1)
            product = jnp.dot(weights, of_pages(g, 1), preferred_element_type=jnp.float32)
            done = (product / totals).astype(jnp.bfloat16)
            for i, key in enumerate(group):
                start = i * piece_rows
                outs[key][:, g * span:(g + 1) * span] = jnp.concatenate(
                    [done[start + j * tokens:start + (j + 1) * tokens] for j in range(per_group)], axis=1
                )
            scores = later

    request = own_request(low_ctx)

    @pl.when(request >= 0)
    def _():
        count = counts[request]
        for pages in [*range(1, most_pages - REQS + 3), most_pages]:
            @pl.when(count == pages)
            def _():
                attend(pages)


def one_request_each(queries, kv_cache, page_counts):
    ctx_size, sub_size = lax.axis_size("ctx"), lax.axis_size("sub")
    head_count = lax.axis_size("head")
    low_ctx = ctx_size // 2
    most_pages = kv_cache.shape[1] // PAGE * ctx_size * sub_size // 4
    local_kv = kv_cache.shape[2] // HD
    tokens, width = queries.shape[0], queries.shape[1] // head_count
    anywhere = pl.BlockSpec(memory_space=pl.ANY)
    in_vmem = pl.BlockSpec(memory_space=pltpu.VMEM)
    q_piece = pltpu.VMEM((tokens, width), queries.dtype)

    def vmem(array):
        return pltpu.with_memory_space_constraint(array, pltpu.VMEM)

    def hbm(array):
        return pltpu.with_memory_space_constraint(array, pltpu.HBM)

    def moved(array, routes):
        def flat(place):
            return (place[0] * head_count + place[1]) * sub_size + place[2]

        return lax.ppermute(array, ("ctx", "head", "sub"), [(flat(a), flat(b)) for a, b in routes])

    def worker(request, head):
        ctx, sub = worker_places(low_ctx)[request]
        return ctx, head, sub

    heads = range(head_count)
    q_out = pl.pallas_call(
        split_kernel,
        out_shape=[q_piece] * head_count,
        in_specs=[anywhere],
        out_specs=[anywhere] * head_count,
        scratch_shapes=[pltpu.SemaphoreType.DMA((head_count,))],
        compiler_params=pltpu.CompilerParams(vmem_limit_bytes=2**20),
        name="split",
    )(hbm(queries))
    routes = {
        (step, s): [((r, h, s), worker(r, h ^ step)) for r in range(ctx_size) for h in heads]
        for s in range(sub_size) for step in heads[::-1]
    }
    first, last = list(routes)[0], list(routes)[-1]
    q_in = {first: moved(q_out[first[0]], routes[first])}
    home, counts = pl.pallas_call(
        functools.partial(gather_home_kernel, low_ctx),
        out_shape=[
            pltpu.VMEM((local_kv, 2, most_pages, PAGE, HD), kv_cache.dtype),
            pltpu.VMEM(page_counts.shape, page_counts.dtype),
        ],
        in_specs=[pl.BlockSpec(memory_space=pltpu.SMEM)] + [anywhere] * 3,
        out_specs=[anywhere] * 2,
        scratch_shapes=[pltpu.SemaphoreType.DMA((local_kv, 2, most_pages)), pltpu.SemaphoreType.DMA],
        compiler_params=pltpu.CompilerParams(vmem_limit_bytes=2**20),
        name="gather_home",
    )(hbm(page_counts), hbm(page_counts), hbm(kv_cache), vmem(q_in[first]))
    q_last, counts = lax.optimization_barrier((q_out[last[0]], counts))
    for key in list(routes)[1:]:
        q_in[key] = moved(q_last if key == last else q_out[key[0]], routes[key])

    pairs = [(low_ctx + n // 2, n % 2) for n in range(4)]
    workers = worker_places(low_ctx)
    near, far = (
        moved(kv_cache, [((*a[:1], h, *a[1:]), (*b[:1], h, *b[1:])) for a, b in sends for h in heads])
        for sends in (
            [(pairs[0], workers[1]), (pairs[1], workers[0]), (pairs[2], workers[2]), (pairs[3], workers[3])],
            [(pairs[0], workers[0]), (pairs[1], workers[2]), (pairs[2], workers[1])],
        )
    )
    groups = [[(step, s) for step in heads[::-1]] for s in range(sub_size)]
    back = {}
    pages, others = home, [vmem(near), vmem(far)]
    for keys in groups:
        outs = pl.pallas_call(
            functools.partial(attend_kernel, low_ctx, sub_size, [keys], len(others)),
            out_shape=[q_piece] * len(keys) + [pltpu.VMEM(home.shape, home.dtype)] * bool(others),
            in_specs=[pl.BlockSpec(memory_space=pltpu.SMEM)] + [in_vmem] * (1 + len(keys) + len(others)),
            out_specs=[in_vmem] * (len(keys) + bool(others)),
            compiler_params=pltpu.CompilerParams(vmem_limit_bytes=12 * 2**20),
            cost_estimate=pl.CostEstimate(flops=10**10, bytes_accessed=2**22, transcendentals=10**6),
            name=f"attend_{keys[0][1]}",
        )(vmem(counts), vmem(pages), *[vmem(q_in[key]) for key in keys], *others)
        for key, out in zip(keys, outs):
            back[key] = moved(out, [(b, a) for a, b in routes[key]])
        if others:
            pages, others = outs[-1], []

    joined = []
    for keys in groups:
        joined = [
            pl.pallas_call(
                functools.partial(join_kernel, keys),
                out_shape=pltpu.HBM(queries.shape, queries.dtype),
                in_specs=[anywhere] * (len(keys) + len(joined)),
                out_specs=anywhere,
                scratch_shapes=[pltpu.SemaphoreType.DMA((len(keys),))],
                input_output_aliases={len(keys): 0} if joined else {},
                compiler_params=pltpu.CompilerParams(vmem_limit_bytes=2**20),
                name=f"join_{keys[0][1]}",
            )(*[vmem(back[key]) for key in keys], *map(hbm, joined))
        ]
    return joined[0]


def from_behind(array, axis, by):
    count = lax.axis_size(axis)
    pairs = [(i, i + by) for i in range(count) if 0 <= i + by < count]
    return lax.ppermute(array, axis, pairs)


def queries_to_pages(queries, kv_cache, page_counts):
    per_group = HQ // KVH
    local_heads = kv_cache.shape[2] // HD
    ctx_size = lax.axis_size("ctx")
    sub_size = lax.axis_size("sub")
    head_count = lax.axis_size("head")
    tok_rows = queries.shape[0]
    score_scale = HD ** (-0.5)
    regrouped = lax.all_to_all(queries, "head", split_axis=1, concat_axis=0, tiled=True)
    all_queries = lax.all_gather(regrouped, ("ctx", "sub"), axis=0, tiled=True)
    all_queries = all_queries.reshape(SPAN, local_heads, per_group, HD)
    page_ends = jnp.cumsum(page_counts)
    ctx_rows = SPAN // ctx_size
    offsets = jnp.arange(QR, dtype=jnp.int32)
    columns = jnp.arange(PAGE, dtype=jnp.int32)
    flat_index = lax.axis_index("ctx") * sub_size + lax.axis_index("sub")
    pages_here = kv_cache.shape[1] // PAGE
    base_pages = pages_here * ctx_size * sub_size // 2
    initial = (
        jnp.full((SPAN, local_heads, per_group), NEG, jnp.float32),
        jnp.zeros((SPAN, local_heads, per_group), jnp.float32),
        jnp.zeros((SPAN, local_heads, per_group, HD), jnp.float32),
    )
    half_rows = kv_cache.shape[1] // 2
    arrived = from_behind(kv_cache[:, half_rows:], "ctx", -(ctx_size // 2))
    is_lower = lax.axis_index("ctx") < ctx_size // 2
    source_flat = flat_index + ctx_size // 2 * sub_size
    working = jnp.where(is_lower, arrived, kv_cache[:, :half_rows])
    first_page = jnp.where(
        is_lower, source_flat * pages_here + pages_here // 2, flat_index * pages_here
    )
    page_total = working.shape[1] // PAGE

    def add_page(page_turn, running):
        page_index = first_page + page_turn
        relative = page_index - base_pages
        counted = jnp.sum((relative >= page_ends).astype(jnp.int32))
        request = jnp.where(relative < 0, REQS, counted)

        def update(partial_value):
            run_max, run_sum, run_out = partial_value
            request_id = jnp.minimum(request, REQS - 1)
            row_start = request_id * QR
            gathered = row_start + offsets
            within = gathered % ctx_rows
            ctx_block = gathered // ctx_rows
            sub_part = within // (head_count * tok_rows)
            head_part = within // tok_rows % head_count
            tok_part = within % tok_rows
            natural = ctx_block * ctx_rows + (head_part * sub_size + sub_part) * tok_rows + tok_part
            query_pos = (page_ends[request_id] + base_pages) * PAGE - QR + natural - row_start
            key_pos = page_index * PAGE + columns
            visible = key_pos[None, :] <= query_pos[:, None]
            page_keys = working[0].reshape(PAGE, local_heads, HD)
            page_values = working[1].reshape(PAGE, local_heads, HD)
            query_rows = lax.dynamic_slice_in_dim(all_queries, row_start, QR, 0)
            scores = (
                jnp.einsum(
                    "qkgd,pkd->qkgp", query_rows, page_keys, preferred_element_type=jnp.float32
                )
                * score_scale
            )
            scores = jnp.where(visible[:, None, None, :], scores, NEG)
            old_max = lax.dynamic_slice_in_dim(run_max, row_start, QR, 0)
            old_sum = lax.dynamic_slice_in_dim(run_sum, row_start, QR, 0)
            old_out = lax.dynamic_slice_in_dim(run_out, row_start, QR, 0)
            new_max = jnp.maximum(old_max, jnp.max(scores, axis=3))
            factor = jnp.exp(old_max - new_max)
            numerators = jnp.exp(scores - new_max[..., None])
            new_sum = old_sum * factor + jnp.sum(numerators, axis=3)
            product = jnp.einsum(
                "qkgp,pkd->qkgd",
                numerators.astype(jnp.bfloat16),
                page_values,
                preferred_element_type=jnp.float32,
            )
            new_out = old_out * factor[..., None] + product
            return (
                lax.dynamic_update_slice_in_dim(run_max, new_max, row_start, 0),
                lax.dynamic_update_slice_in_dim(run_sum, new_sum, row_start, 0),
                lax.dynamic_update_slice_in_dim(run_out, new_out, row_start, 0),
            )

        def unchanged(partial_value):
            return partial_value

        return lax.cond(request < REQS, update, unchanged, running)

    run_max, run_sum, run_out = lax.fori_loop(0, page_total, add_page, initial)
    share = SPAN // (ctx_size * sub_size)
    global_max = lax.pmax(run_max, ("ctx", "sub"))
    factor = jnp.exp(run_max - global_max)
    sums_here, outs_here = (
        lax.psum_scatter(
            (run_sum * factor).astype(jnp.bfloat16), ("ctx", "sub"), scatter_dimension=0, tiled=True
        ).astype(jnp.float32),
        lax.psum_scatter(
            (run_out * factor[..., None]).astype(jnp.bfloat16),
            ("ctx", "sub"),
            scatter_dimension=0,
            tiled=True,
        ).astype(jnp.float32),
    )
    finished = (outs_here / sums_here[..., None]).astype(jnp.bfloat16)
    finished = finished.reshape(share, local_heads * per_group * HD)
    return lax.all_to_all(finished, "head", split_axis=0, concat_axis=1, tiled=True)


def per_device(queries, kv_cache, page_counts):
    ctx_size, sub_size, head_count = lax.axis_size("ctx"), lax.axis_size("sub"), lax.axis_size("head")
    small = (
        ctx_size == REQS == 4
        and head_count == sub_size == 2
        and kv_cache.shape[1] == 2 * PAGE
        and kv_cache.shape[2] % (sub_size * HD) == 0
        and queries.shape[0] % 16 == 0
        and queries.shape[0] * head_count * sub_size == QR
    )
    return (one_request_each if small else queries_to_pages)(queries, kv_cache, page_counts)


def solution(mesh):
    return jax.shard_map(
        per_device,
        mesh=mesh,
        in_specs=(
            P(("grp", "ctx", "head", "sub"), None),
            P(None, ("grp", "ctx", "sub"), "head"),
            P("grp"),
        ),
        out_specs=P(("grp", "ctx", "head", "sub"), None),
        check_vma=False,
    )
```

```python
import functools

import jax
import jax.numpy as jnp
from jax import lax
from jax.experimental import pallas as pl
from jax.experimental.pallas import tpu as pltpu
from jax.sharding import PartitionSpec as P

HQ = 128
KVH = 8
HD = 128
REQS = 4
QR = 64
PAGE = 256
SPAN = 256


NEG = -1e30
EXP2_SCALE = HD ** (-0.5) * 1.4426950408889634


def run(copies):
    for copy in copies:
        copy.start()
    for copy in copies:
        copy.wait()


def head_part(step, width):
    return pl.ds(pl.multiple_of((lax.axis_index("head") ^ step) * width, width), width)


def split_kernel(queries, *refs):
    outs, sems = refs[:-1], refs[-1]
    run([
        pltpu.make_async_copy(queries.at[:, head_part(step, out.shape[1])], out, sems.at[step])
        for step, out in enumerate(outs)
    ])


def join_kernel(keys, *refs):
    out, sems = refs[-2:]

    @pl.when(lax.axis_index("sub") == keys[0][1])
    def _():
        run([
            pltpu.make_async_copy(piece, out.at[:, head_part(step, piece.shape[1])], sems.at[i])
            for i, (piece, (step, _)) in enumerate(zip(refs, keys))
        ])


def worker_places(low_ctx):
    return (0, 0), (low_ctx, 1), (low_ctx + 1, 1), (low_ctx + 1, 0)


def own_request(low_ctx):
    ctx, sub = lax.axis_index("ctx"), lax.axis_index("sub")
    found = jnp.int32(-1)
    for request, place in enumerate(worker_places(low_ctx)):
        found = jnp.where((ctx == place[0]) & (sub == place[1]), request, found)
    return found


def pages_of(low_ctx, counts, most_pages):
    request = own_request(low_ctx)
    start = jnp.int32(0)
    for r in range(REQS):
        start = start + jnp.where(r < request, counts[r], 0)
    count = jnp.where(request >= 0, counts[jnp.maximum(request, 0)], 0)
    home_pair = jnp.where(request == 0, -1, jnp.where(request == 1, 1, 5 - request))
    near_pair = jnp.where(request == 0, 1, home_pair ^ 1)
    for p in range(most_pages):
        page = start + p
        pair = page // 2
        which = jnp.where(pair == home_pair, 0, jnp.where(pair == near_pair, 1, 2))
        yield p, p < count, which, pl.ds(pl.multiple_of(lax.rem(page, 2) * PAGE, PAGE), PAGE)


def gather_home_kernel(low_ctx, counts, counts_in, own, after, out, counts_out, sems, counts_sem):
    local_kv, _, most_pages = out.shape[:3]
    counts_copy = pltpu.make_async_copy(counts_in, counts_out, counts_sem)
    counts_copy.start()
    plan = [
        (here & (which == 0), [
            pltpu.make_async_copy(own.at[i, rows, pl.ds(g * HD, HD)], out.at[g, i, p], sems.at[g, i, p])
            for g in range(local_kv) for i in range(2)
        ])
        for p, here, which, rows in pages_of(low_ctx, counts, most_pages)
    ]
    for here, copies in plan:
        @pl.when(here)
        def _():
            for copy in copies:
                copy.start()
    for here, copies in plan:
        @pl.when(here)
        def _():
            for copy in copies:
                copy.wait()
    counts_copy.wait()


def gather_rest(low_ctx, counts, home, far, near, out):
    local_kv, _, most_pages = out.shape[:3]
    for p, here, which, rows in pages_of(low_ctx, counts, most_pages):
        @pl.when(here & (which == 0))
        def _():
            for g in range(local_kv):
                out[g, :, p] = home[g, :, p]
        for n, ref in enumerate((near, far)):
            @pl.when(here & (which == n + 1))
            def _():
                for g in range(local_kv):
                    for i in range(2):
                        out[g, i, p] = ref[i, rows, g * HD:(g + 1) * HD]


def attend_kernel(low_ctx, sub_count, groups, others, counts, home, *refs):
    keys = [key for group in groups for key in group]
    queries, outs = dict(zip(keys, refs)), dict(zip(keys, refs[len(keys) + others:]))
    pages_in = home
    if others:
        pages_in = refs[-1]
        gather_rest(low_ctx, counts, home, *refs[len(keys):len(keys) + others], pages_in)
    head = lax.axis_index("head")
    tokens, width = refs[0].shape
    local_kv, _, most_pages = pages_in.shape[:3]
    span = width // local_kv
    per_group = span // HD
    piece_rows = per_group * tokens
    rows = len(groups[0]) * piece_rows

    def attend(pages):
        span_rows = pages * PAGE
        row = lax.broadcasted_iota(jnp.int32, (rows, 1), 0)
        masked_from = (PAGE - QR) // HD * HD
        column = masked_from + lax.broadcasted_iota(jnp.int32, (rows, PAGE - masked_from), 1)

        def visible_of(group):
            token = lax.rem(row, tokens)
            for i, (step, source) in enumerate(group):
                first_token = ((head ^ step) * sub_count + source) * tokens
                token = jnp.where(row // piece_rows == i, token + first_token, token)
            return column <= PAGE - QR + token

        def of_pages(g, i):
            return pages_in[g, i, 0:pages].reshape(span_rows, HD)

        def scores_of(group, g):
            q_blocks = [queries[key][:, g * span:(g + 1) * span] for key in group]
            q_rows = jnp.concatenate([q[:, j * HD:(j + 1) * HD] for q in q_blocks for j in range(per_group)], axis=0)
            scores = lax.dot_general(
                q_rows, of_pages(g, 0), (((1,), (1,)), ((), ())), preferred_element_type=jnp.float32
            )
            scores = [scores[:, p * PAGE:(p + 1) * PAGE] for p in range(pages)]
            tail = jnp.where(visible_of(group), scores[-1][:, masked_from:], NEG)
            scores[-1] = jnp.concatenate([scores[-1][:, :masked_from], tail], axis=1)
            return scores

        units = [(group, g) for group in groups for g in range(local_kv)]
        scores = scores_of(*units[0])
        for n, (group, g) in enumerate(units):
            later = scores_of(*units[n + 1]) if n + 1 < len(units) else None
            top = jnp.max(functools.reduce(jnp.maximum, scores), axis=1, keepdims=True)
            numerators = [jnp.exp2((s - top) * EXP2_SCALE) for s in scores]
            totals = jnp.sum(functools.reduce(jnp.add, numerators), axis=1, keepdims=True)
            weights = jnp.concatenate([s.astype(jnp.bfloat16) for s in numerators], axis=1)
            product = jnp.dot(weights, of_pages(g, 1), preferred_element_type=jnp.float32)
            done = (product / totals).astype(jnp.bfloat16)
            for i, key in enumerate(group):
                start = i * piece_rows
                outs[key][:, g * span:(g + 1) * span] = jnp.concatenate(
                    [done[start + j * tokens:start + (j + 1) * tokens] for j in range(per_group)], axis=1
                )
            scores = later

    request = own_request(low_ctx)

    @pl.when(request >= 0)
    def _():
        count = counts[request]
        for pages in [*range(1, most_pages - REQS + 3), most_pages]:
            @pl.when(count == pages)
            def _():
                attend(pages)


def one_request_each(queries, kv_cache, page_counts):
    ctx_size, sub_size = lax.axis_size("ctx"), lax.axis_size("sub")
    head_count = lax.axis_size("head")
    low_ctx = ctx_size // 2
    most_pages = kv_cache.shape[1] // PAGE * ctx_size * sub_size // 4
    local_kv = kv_cache.shape[2] // HD
    tokens, width = queries.shape[0], queries.shape[1] // head_count
    anywhere = pl.BlockSpec(memory_space=pl.ANY)
    in_vmem = pl.BlockSpec(memory_space=pltpu.VMEM)
    q_piece = pltpu.VMEM((tokens, width), queries.dtype)

    def vmem(array):
        return pltpu.with_memory_space_constraint(array, pltpu.VMEM)

    def hbm(array):
        return pltpu.with_memory_space_constraint(array, pltpu.HBM)

    def moved(array, routes):
        def flat(place):
            return (place[0] * head_count + place[1]) * sub_size + place[2]

        return lax.ppermute(array, ("ctx", "head", "sub"), [(flat(a), flat(b)) for a, b in routes])

    def worker(request, head):
        ctx, sub = worker_places(low_ctx)[request]
        return ctx, head, sub

    heads = range(head_count)
    q_out = pl.pallas_call(
        split_kernel,
        out_shape=[q_piece] * head_count,
        in_specs=[anywhere],
        out_specs=[anywhere] * head_count,
        scratch_shapes=[pltpu.SemaphoreType.DMA((head_count,))],
        compiler_params=pltpu.CompilerParams(vmem_limit_bytes=2**20),
        name="split",
    )(hbm(queries))
    routes = {
        (step, s): [((r, h, s), worker(r, h ^ step)) for r in range(ctx_size) for h in heads]
        for s in range(sub_size) for step in heads[::-1]
    }
    first, last = list(routes)[0], list(routes)[-1]
    q_in = {first: moved(q_out[first[0]], routes[first])}
    home, counts = pl.pallas_call(
        functools.partial(gather_home_kernel, low_ctx),
        out_shape=[
            pltpu.VMEM((local_kv, 2, most_pages, PAGE, HD), kv_cache.dtype),
            pltpu.VMEM(page_counts.shape, page_counts.dtype),
        ],
        in_specs=[pl.BlockSpec(memory_space=pltpu.SMEM)] + [anywhere] * 3,
        out_specs=[anywhere] * 2,
        scratch_shapes=[pltpu.SemaphoreType.DMA((local_kv, 2, most_pages)), pltpu.SemaphoreType.DMA],
        compiler_params=pltpu.CompilerParams(vmem_limit_bytes=2**20),
        name="gather_home",
    )(hbm(page_counts), hbm(page_counts), hbm(kv_cache), vmem(q_in[first]))
    q_last, counts = lax.optimization_barrier((q_out[last[0]], counts))
    for key in list(routes)[1:]:
        q_in[key] = moved(q_last if key == last else q_out[key[0]], routes[key])

    pairs = [(low_ctx + n // 2, n % 2) for n in range(4)]
    workers = worker_places(low_ctx)
    near, far = (
        moved(kv_cache, [((*a[:1], h, *a[1:]), (*b[:1], h, *b[1:])) for a, b in sends for h in heads])
        for sends in (
            [(pairs[0], workers[1]), (pairs[1], workers[0]), (pairs[2], workers[2]), (pairs[3], workers[3])],
            [(pairs[0], workers[0]), (pairs[1], workers[2]), (pairs[2], workers[1])],
        )
    )
    groups = [[(step, s) for step in heads[::-1]] for s in range(sub_size)]
    back = {}
    pages, others = home, [vmem(far), vmem(near)]
    for keys in groups:
        outs = pl.pallas_call(
            functools.partial(attend_kernel, low_ctx, sub_size, [keys], len(others)),
            out_shape=[q_piece] * len(keys) + [pltpu.VMEM(home.shape, home.dtype)] * bool(others),
            in_specs=[pl.BlockSpec(memory_space=pltpu.SMEM)] + [in_vmem] * (1 + len(keys) + len(others)),
            out_specs=[in_vmem] * (len(keys) + bool(others)),
            compiler_params=pltpu.CompilerParams(vmem_limit_bytes=12 * 2**20),
            cost_estimate=pl.CostEstimate(flops=10**10, bytes_accessed=2**22, transcendentals=10**6),
            name=f"attend_{keys[0][1]}",
        )(vmem(counts), vmem(pages), *[vmem(q_in[key]) for key in keys], *others)
        for key, out in zip(keys, outs):
            back[key] = moved(out, [(b, a) for a, b in routes[key]])
        if others:
            pages, others = outs[-1], []

    joined = []
    for keys in groups:
        joined = [
            pl.pallas_call(
                functools.partial(join_kernel, keys),
                out_shape=pltpu.HBM(queries.shape, queries.dtype),
                in_specs=[anywhere] * (len(keys) + len(joined)),
                out_specs=anywhere,
                scratch_shapes=[pltpu.SemaphoreType.DMA((len(keys),))],
                input_output_aliases={len(keys): 0} if joined else {},
                compiler_params=pltpu.CompilerParams(vmem_limit_bytes=2**20),
                name=f"join_{keys[0][1]}",
            )(*[vmem(back[key]) for key in keys], *map(hbm, joined))
        ]
    return joined[0]


def from_behind(array, axis, by):
    count = lax.axis_size(axis)
    pairs = [(i, i + by) for i in range(count) if 0 <= i + by < count]
    return lax.ppermute(array, axis, pairs)


def queries_to_pages(queries, kv_cache, page_counts):
    per_group = HQ // KVH
    local_heads = kv_cache.shape[2] // HD
    ctx_size = lax.axis_size("ctx")
    sub_size = lax.axis_size("sub")
    head_count = lax.axis_size("head")
    tok_rows = queries.shape[0]
    score_scale = HD ** (-0.5)
    regrouped = lax.all_to_all(queries, "head", split_axis=1, concat_axis=0, tiled=True)
    all_queries = lax.all_gather(regrouped, ("ctx", "sub"), axis=0, tiled=True)
    all_queries = all_queries.reshape(SPAN, local_heads, per_group, HD)
    page_ends = jnp.cumsum(page_counts)
    ctx_rows = SPAN // ctx_size
    offsets = jnp.arange(QR, dtype=jnp.int32)
    columns = jnp.arange(PAGE, dtype=jnp.int32)
    flat_index = lax.axis_index("ctx") * sub_size + lax.axis_index("sub")
    pages_here = kv_cache.shape[1] // PAGE
    base_pages = pages_here * ctx_size * sub_size // 2
    initial = (
        jnp.full((SPAN, local_heads, per_group), NEG, jnp.float32),
        jnp.zeros((SPAN, local_heads, per_group), jnp.float32),
        jnp.zeros((SPAN, local_heads, per_group, HD), jnp.float32),
    )
    half_rows = kv_cache.shape[1] // 2
    arrived = from_behind(kv_cache[:, half_rows:], "ctx", -(ctx_size // 2))
    is_lower = lax.axis_index("ctx") < ctx_size // 2
    source_flat = flat_index + ctx_size // 2 * sub_size
    working = jnp.where(is_lower, arrived, kv_cache[:, :half_rows])
    first_page = jnp.where(
        is_lower, source_flat * pages_here + pages_here // 2, flat_index * pages_here
    )
    page_total = working.shape[1] // PAGE

    def add_page(page_turn, running):
        page_index = first_page + page_turn
        relative = page_index - base_pages
        counted = jnp.sum((relative >= page_ends).astype(jnp.int32))
        request = jnp.where(relative < 0, REQS, counted)

        def update(partial_value):
            run_max, run_sum, run_out = partial_value
            request_id = jnp.minimum(request, REQS - 1)
            row_start = request_id * QR
            gathered = row_start + offsets
            within = gathered % ctx_rows
            ctx_block = gathered // ctx_rows
            sub_part = within // (head_count * tok_rows)
            head_part = within // tok_rows % head_count
            tok_part = within % tok_rows
            natural = ctx_block * ctx_rows + (head_part * sub_size + sub_part) * tok_rows + tok_part
            query_pos = (page_ends[request_id] + base_pages) * PAGE - QR + natural - row_start
            key_pos = page_index * PAGE + columns
            visible = key_pos[None, :] <= query_pos[:, None]
            page_keys = working[0].reshape(PAGE, local_heads, HD)
            page_values = working[1].reshape(PAGE, local_heads, HD)
            query_rows = lax.dynamic_slice_in_dim(all_queries, row_start, QR, 0)
            scores = (
                jnp.einsum(
                    "qkgd,pkd->qkgp", query_rows, page_keys, preferred_element_type=jnp.float32
                )
                * score_scale
            )
            scores = jnp.where(visible[:, None, None, :], scores, NEG)
            old_max = lax.dynamic_slice_in_dim(run_max, row_start, QR, 0)
            old_sum = lax.dynamic_slice_in_dim(run_sum, row_start, QR, 0)
            old_out = lax.dynamic_slice_in_dim(run_out, row_start, QR, 0)
            new_max = jnp.maximum(old_max, jnp.max(scores, axis=3))
            factor = jnp.exp(old_max - new_max)
            numerators = jnp.exp(scores - new_max[..., None])
            new_sum = old_sum * factor + jnp.sum(numerators, axis=3)
            product = jnp.einsum(
                "qkgp,pkd->qkgd",
                numerators.astype(jnp.bfloat16),
                page_values,
                preferred_element_type=jnp.float32,
            )
            new_out = old_out * factor[..., None] + product
            return (
                lax.dynamic_update_slice_in_dim(run_max, new_max, row_start, 0),
                lax.dynamic_update_slice_in_dim(run_sum, new_sum, row_start, 0),
                lax.dynamic_update_slice_in_dim(run_out, new_out, row_start, 0),
            )

        def unchanged(partial_value):
            return partial_value

        return lax.cond(request < REQS, update, unchanged, running)

    run_max, run_sum, run_out = lax.fori_loop(0, page_total, add_page, initial)
    share = SPAN // (ctx_size * sub_size)
    global_max = lax.pmax(run_max, ("ctx", "sub"))
    factor = jnp.exp(run_max - global_max)
    sums_here, outs_here = (
        lax.psum_scatter(
            (run_sum * factor).astype(jnp.bfloat16), ("ctx", "sub"), scatter_dimension=0, tiled=True
        ).astype(jnp.float32),
        lax.psum_scatter(
            (run_out * factor[..., None]).astype(jnp.bfloat16),
            ("ctx", "sub"),
            scatter_dimension=0,
            tiled=True,
        ).astype(jnp.float32),
    )
    finished = (outs_here / sums_here[..., None]).astype(jnp.bfloat16)
    finished = finished.reshape(share, local_heads * per_group * HD)
    return lax.all_to_all(finished, "head", split_axis=0, concat_axis=1, tiled=True)


def per_device(queries, kv_cache, page_counts):
    ctx_size, sub_size, head_count = lax.axis_size("ctx"), lax.axis_size("sub"), lax.axis_size("head")
    small = (
        ctx_size == REQS == 4
        and head_count == sub_size == 2
        and kv_cache.shape[1] == 2 * PAGE
        and kv_cache.shape[2] % (sub_size * HD) == 0
        and queries.shape[0] % 16 == 0
        and queries.shape[0] * head_count * sub_size == QR
    )
    return (one_request_each if small else queries_to_pages)(queries, kv_cache, page_counts)


def solution(mesh):
    return jax.shard_map(
        per_device,
        mesh=mesh,
        in_specs=(
            P(("grp", "ctx", "head", "sub"), None),
            P(None, ("grp", "ctx", "sub"), "head"),
            P("grp"),
        ),
        out_specs=P(("grp", "ctx", "head", "sub"), None),
        check_vma=False,
    )
```

```python
import functools

import jax
import jax.numpy as jnp
from jax import lax
from jax.experimental import pallas as pl
from jax.experimental.pallas import tpu as pltpu
from jax.sharding import PartitionSpec as P

HQ = 128
KVH = 8
HD = 128
REQS = 4
QR = 64
PAGE = 256
SPAN = 256


NEG = -1e30
EXP2_SCALE = HD ** (-0.5) * 1.4426950408889634


def run(copies):
    for copy in copies:
        copy.start()
    for copy in copies:
        copy.wait()


def head_part(step, width):
    return pl.ds(pl.multiple_of((lax.axis_index("head") ^ step) * width, width), width)


def split_kernel(queries, *refs):
    outs, sems = refs[:-1], refs[-1]
    run([
        pltpu.make_async_copy(queries.at[:, head_part(step, out.shape[1])], out, sems.at[step])
        for step, out in enumerate(outs)
    ])


def join_kernel(keys, *refs):
    out, sems = refs[-2:]

    @pl.when(lax.axis_index("sub") == keys[0][1])
    def _():
        run([
            pltpu.make_async_copy(piece, out.at[:, head_part(step, piece.shape[1])], sems.at[i])
            for i, (piece, (step, _)) in enumerate(zip(refs, keys))
        ])


def worker_places(low_ctx):
    return (0, 0), (low_ctx, 1), (low_ctx + 1, 1), (low_ctx + 1, 0)


def own_request(low_ctx):
    ctx, sub = lax.axis_index("ctx"), lax.axis_index("sub")
    found = jnp.int32(-1)
    for request, place in enumerate(worker_places(low_ctx)):
        found = jnp.where((ctx == place[0]) & (sub == place[1]), request, found)
    return found


def pages_of(low_ctx, counts, most_pages):
    request = own_request(low_ctx)
    start = jnp.int32(0)
    for r in range(REQS):
        start = start + jnp.where(r < request, counts[r], 0)
    count = jnp.where(request >= 0, counts[jnp.maximum(request, 0)], 0)
    home_pair = jnp.where(request == 0, -1, jnp.where(request == 1, 1, 5 - request))
    near_pair = jnp.where(request == 0, 1, home_pair ^ 1)
    for p in range(most_pages):
        page = start + p
        pair = page // 2
        which = jnp.where(pair == home_pair, 0, jnp.where(pair == near_pair, 1, 2))
        yield p, p < count, which, pl.ds(pl.multiple_of(lax.rem(page, 2) * PAGE, PAGE), PAGE)


def gather_home_kernel(low_ctx, counts, counts_in, own, after, out, counts_out, sems, counts_sem):
    local_kv, _, most_pages = out.shape[:3]
    counts_copy = pltpu.make_async_copy(counts_in, counts_out, counts_sem)
    counts_copy.start()
    plan = [
        (here & (which == 0), [
            pltpu.make_async_copy(own.at[i, rows, pl.ds(g * HD, HD)], out.at[g, i, p], sems.at[g, i, p])
            for g in range(local_kv) for i in range(2)
        ])
        for p, here, which, rows in pages_of(low_ctx, counts, most_pages)
    ]
    for here, copies in plan:
        @pl.when(here)
        def _():
            for copy in copies:
                copy.start()
    for here, copies in plan:
        @pl.when(here)
        def _():
            for copy in copies:
                copy.wait()
    counts_copy.wait()


def gather_rest(low_ctx, counts, home, far, near, keys_out, values_out):
    local_kv, most_pages = values_out.shape[:2]

    def put(g, p, keys, values):
        keys_out[g, :, p * PAGE:(p + 1) * PAGE] = keys.T
        values_out[g, p] = values

    for p, here, which, rows in pages_of(low_ctx, counts, most_pages):
        @pl.when(here & (which == 0))
        def _():
            for g in range(local_kv):
                put(g, p, home[g, 0, p], home[g, 1, p])
        for n, ref in enumerate((near, far)):
            @pl.when(here & (which == n + 1))
            def _():
                for g in range(local_kv):
                    part = slice(g * HD, (g + 1) * HD)
                    put(g, p, ref[0, rows, part], ref[1, rows, part])


def attend_kernel(low_ctx, sub_count, groups, others, counts, *refs):
    keys = [key for group in groups for key in group]
    before = 1 if others else 2
    after = before + len(keys) + others
    queries, outs = dict(zip(keys, refs[before:])), dict(zip(keys, refs[after:]))
    keys_in, values_in = refs[-2:] if others else refs[:2]
    if others:
        gather_rest(low_ctx, counts, refs[0], *refs[after - others:after], keys_in, values_in)
    head = lax.axis_index("head")
    tokens, width = queries[keys[0]].shape
    local_kv, most_pages = values_in.shape[:2]
    span = width // local_kv
    per_group = span // HD
    piece_rows = per_group * tokens
    rows = len(groups[0]) * piece_rows

    def attend(pages):
        span_rows = pages * PAGE
        row = lax.broadcasted_iota(jnp.int32, (rows, 1), 0)
        masked_from = (PAGE - QR) // HD * HD
        column = masked_from + lax.broadcasted_iota(jnp.int32, (rows, PAGE - masked_from), 1)

        def visible_of(group):
            token = lax.rem(row, tokens)
            for i, (step, source) in enumerate(group):
                first_token = ((head ^ step) * sub_count + source) * tokens
                token = jnp.where(row // piece_rows == i, token + first_token, token)
            return column <= PAGE - QR + token

        def scores_of(group, g):
            q_blocks = [queries[key][:, g * span:(g + 1) * span] for key in group]
            q_rows = jnp.concatenate([q[:, j * HD:(j + 1) * HD] for q in q_blocks for j in range(per_group)], axis=0)
            scores = jnp.dot(q_rows, keys_in[g, :, 0:span_rows], preferred_element_type=jnp.float32)
            scores = [scores[:, p * PAGE:(p + 1) * PAGE] for p in range(pages)]
            tail = jnp.where(visible_of(group), scores[-1][:, masked_from:], NEG)
            scores[-1] = jnp.concatenate([scores[-1][:, :masked_from], tail], axis=1)
            return scores

        units = [(group, g) for group in groups for g in range(local_kv)]
        scores = scores_of(*units[0])
        for n, (group, g) in enumerate(units):
            later = scores_of(*units[n + 1]) if n + 1 < len(units) else None
            top = jnp.max(functools.reduce(jnp.maximum, scores), axis=1, keepdims=True)
            numerators = [jnp.exp2((s - top) * EXP2_SCALE) for s in scores]
            totals = jnp.sum(functools.reduce(jnp.add, numerators), axis=1, keepdims=True)
            weights = jnp.concatenate([s.astype(jnp.bfloat16) for s in numerators], axis=1)
            product = jnp.dot(weights, values_in[g, 0:pages].reshape(span_rows, HD), preferred_element_type=jnp.float32)
            done = (product / totals).astype(jnp.bfloat16)
            for i, key in enumerate(group):
                start = i * piece_rows
                outs[key][:, g * span:(g + 1) * span] = jnp.concatenate(
                    [done[start + j * tokens:start + (j + 1) * tokens] for j in range(per_group)], axis=1
                )
            scores = later

    request = own_request(low_ctx)

    @pl.when(request >= 0)
    def _():
        count = counts[request]
        for pages in [*range(1, most_pages - REQS + 3), most_pages]:
            @pl.when(count == pages)
            def _():
                attend(pages)


def one_request_each(queries, kv_cache, page_counts):
    ctx_size, sub_size = lax.axis_size("ctx"), lax.axis_size("sub")
    head_count = lax.axis_size("head")
    low_ctx = ctx_size // 2
    most_pages = kv_cache.shape[1] // PAGE * ctx_size * sub_size // 4
    local_kv = kv_cache.shape[2] // HD
    tokens, width = queries.shape[0], queries.shape[1] // head_count
    anywhere = pl.BlockSpec(memory_space=pl.ANY)
    in_vmem = pl.BlockSpec(memory_space=pltpu.VMEM)
    q_piece = pltpu.VMEM((tokens, width), queries.dtype)

    def vmem(array):
        return pltpu.with_memory_space_constraint(array, pltpu.VMEM)

    def hbm(array):
        return pltpu.with_memory_space_constraint(array, pltpu.HBM)

    def moved(array, routes):
        def flat(place):
            return (place[0] * head_count + place[1]) * sub_size + place[2]

        return lax.ppermute(array, ("ctx", "head", "sub"), [(flat(a), flat(b)) for a, b in routes])

    def worker(request, head):
        ctx, sub = worker_places(low_ctx)[request]
        return ctx, head, sub

    heads = range(head_count)
    q_out = pl.pallas_call(
        split_kernel,
        out_shape=[q_piece] * head_count,
        in_specs=[anywhere],
        out_specs=[anywhere] * head_count,
        scratch_shapes=[pltpu.SemaphoreType.DMA((head_count,))],
        compiler_params=pltpu.CompilerParams(vmem_limit_bytes=2**20),
        name="split",
    )(hbm(queries))
    routes = {
        (step, s): [((r, h, s), worker(r, h ^ step)) for r in range(ctx_size) for h in heads]
        for s in range(sub_size) for step in heads[::-1]
    }
    first, last = list(routes)[0], list(routes)[-1]
    q_in = {first: moved(q_out[first[0]], routes[first])}
    home, counts = pl.pallas_call(
        functools.partial(gather_home_kernel, low_ctx),
        out_shape=[
            pltpu.VMEM((local_kv, 2, most_pages, PAGE, HD), kv_cache.dtype),
            pltpu.VMEM(page_counts.shape, page_counts.dtype),
        ],
        in_specs=[pl.BlockSpec(memory_space=pltpu.SMEM)] + [anywhere] * 3,
        out_specs=[anywhere] * 2,
        scratch_shapes=[pltpu.SemaphoreType.DMA((local_kv, 2, most_pages)), pltpu.SemaphoreType.DMA],
        compiler_params=pltpu.CompilerParams(vmem_limit_bytes=2**20),
        name="gather_home",
    )(hbm(page_counts), hbm(page_counts), hbm(kv_cache), vmem(q_in[first]))
    q_last, counts = lax.optimization_barrier((q_out[last[0]], counts))
    for key in list(routes)[1:]:
        q_in[key] = moved(q_last if key == last else q_out[key[0]], routes[key])

    pairs = [(low_ctx + n // 2, n % 2) for n in range(4)]
    workers = worker_places(low_ctx)
    near, far = (
        moved(kv_cache, [((*a[:1], h, *a[1:]), (*b[:1], h, *b[1:])) for a, b in sends for h in heads])
        for sends in (
            [(pairs[0], workers[1]), (pairs[1], workers[0]), (pairs[2], workers[2]), (pairs[3], workers[3])],
            [(pairs[0], workers[0]), (pairs[1], workers[2]), (pairs[2], workers[1])],
        )
    )
    groups = [[(step, s) for step in heads[::-1]] for s in range(sub_size)]
    back = {}
    pages, others = [vmem(home)], [vmem(far), vmem(near)]
    gathered = [
        pltpu.VMEM((local_kv, HD, most_pages * PAGE), kv_cache.dtype),
        pltpu.VMEM((local_kv, most_pages, PAGE, HD), kv_cache.dtype),
    ]
    for keys in groups:
        outs = pl.pallas_call(
            functools.partial(attend_kernel, low_ctx, sub_size, [keys], len(others)),
            out_shape=[q_piece] * len(keys) + gathered * bool(others),
            in_specs=[pl.BlockSpec(memory_space=pltpu.SMEM)] + [in_vmem] * (len(pages) + len(keys) + len(others)),
            out_specs=[in_vmem] * (len(keys) + len(gathered) * bool(others)),
            compiler_params=pltpu.CompilerParams(vmem_limit_bytes=12 * 2**20),
            cost_estimate=pl.CostEstimate(flops=10**10, bytes_accessed=2**22, transcendentals=10**6),
            name=f"attend_{keys[0][1]}",
        )(vmem(counts), *pages, *[vmem(q_in[key]) for key in keys], *others)
        for key, out in zip(keys, outs):
            back[key] = moved(out, [(b, a) for a, b in routes[key]])
        if others:
            pages, others = [vmem(out) for out in outs[len(keys):]], []

    joined = []
    for keys in groups:
        joined = [
            pl.pallas_call(
                functools.partial(join_kernel, keys),
                out_shape=pltpu.HBM(queries.shape, queries.dtype),
                in_specs=[anywhere] * (len(keys) + len(joined)),
                out_specs=anywhere,
                scratch_shapes=[pltpu.SemaphoreType.DMA((len(keys),))],
                input_output_aliases={len(keys): 0} if joined else {},
                compiler_params=pltpu.CompilerParams(vmem_limit_bytes=2**20),
                name=f"join_{keys[0][1]}",
            )(*[vmem(back[key]) for key in keys], *map(hbm, joined))
        ]
    return joined[0]


def from_behind(array, axis, by):
    count = lax.axis_size(axis)
    pairs = [(i, i + by) for i in range(count) if 0 <= i + by < count]
    return lax.ppermute(array, axis, pairs)


def queries_to_pages(queries, kv_cache, page_counts):
    per_group = HQ // KVH
    local_heads = kv_cache.shape[2] // HD
    ctx_size = lax.axis_size("ctx")
    sub_size = lax.axis_size("sub")
    head_count = lax.axis_size("head")
    tok_rows = queries.shape[0]
    score_scale = HD ** (-0.5)
    regrouped = lax.all_to_all(queries, "head", split_axis=1, concat_axis=0, tiled=True)
    all_queries = lax.all_gather(regrouped, ("ctx", "sub"), axis=0, tiled=True)
    all_queries = all_queries.reshape(SPAN, local_heads, per_group, HD)
    page_ends = jnp.cumsum(page_counts)
    ctx_rows = SPAN // ctx_size
    offsets = jnp.arange(QR, dtype=jnp.int32)
    columns = jnp.arange(PAGE, dtype=jnp.int32)
    flat_index = lax.axis_index("ctx") * sub_size + lax.axis_index("sub")
    pages_here = kv_cache.shape[1] // PAGE
    base_pages = pages_here * ctx_size * sub_size // 2
    initial = (
        jnp.full((SPAN, local_heads, per_group), NEG, jnp.float32),
        jnp.zeros((SPAN, local_heads, per_group), jnp.float32),
        jnp.zeros((SPAN, local_heads, per_group, HD), jnp.float32),
    )
    half_rows = kv_cache.shape[1] // 2
    arrived = from_behind(kv_cache[:, half_rows:], "ctx", -(ctx_size // 2))
    is_lower = lax.axis_index("ctx") < ctx_size // 2
    source_flat = flat_index + ctx_size // 2 * sub_size
    working = jnp.where(is_lower, arrived, kv_cache[:, :half_rows])
    first_page = jnp.where(
        is_lower, source_flat * pages_here + pages_here // 2, flat_index * pages_here
    )
    page_total = working.shape[1] // PAGE

    def add_page(page_turn, running):
        page_index = first_page + page_turn
        relative = page_index - base_pages
        counted = jnp.sum((relative >= page_ends).astype(jnp.int32))
        request = jnp.where(relative < 0, REQS, counted)

        def update(partial_value):
            run_max, run_sum, run_out = partial_value
            request_id = jnp.minimum(request, REQS - 1)
            row_start = request_id * QR
            gathered = row_start + offsets
            within = gathered % ctx_rows
            ctx_block = gathered // ctx_rows
            sub_part = within // (head_count * tok_rows)
            head_part = within // tok_rows % head_count
            tok_part = within % tok_rows
            natural = ctx_block * ctx_rows + (head_part * sub_size + sub_part) * tok_rows + tok_part
            query_pos = (page_ends[request_id] + base_pages) * PAGE - QR + natural - row_start
            key_pos = page_index * PAGE + columns
            visible = key_pos[None, :] <= query_pos[:, None]
            page_keys = working[0].reshape(PAGE, local_heads, HD)
            page_values = working[1].reshape(PAGE, local_heads, HD)
            query_rows = lax.dynamic_slice_in_dim(all_queries, row_start, QR, 0)
            scores = (
                jnp.einsum(
                    "qkgd,pkd->qkgp", query_rows, page_keys, preferred_element_type=jnp.float32
                )
                * score_scale
            )
            scores = jnp.where(visible[:, None, None, :], scores, NEG)
            old_max = lax.dynamic_slice_in_dim(run_max, row_start, QR, 0)
            old_sum = lax.dynamic_slice_in_dim(run_sum, row_start, QR, 0)
            old_out = lax.dynamic_slice_in_dim(run_out, row_start, QR, 0)
            new_max = jnp.maximum(old_max, jnp.max(scores, axis=3))
            factor = jnp.exp(old_max - new_max)
            numerators = jnp.exp(scores - new_max[..., None])
            new_sum = old_sum * factor + jnp.sum(numerators, axis=3)
            product = jnp.einsum(
                "qkgp,pkd->qkgd",
                numerators.astype(jnp.bfloat16),
                page_values,
                preferred_element_type=jnp.float32,
            )
            new_out = old_out * factor[..., None] + product
            return (
                lax.dynamic_update_slice_in_dim(run_max, new_max, row_start, 0),
                lax.dynamic_update_slice_in_dim(run_sum, new_sum, row_start, 0),
                lax.dynamic_update_slice_in_dim(run_out, new_out, row_start, 0),
            )

        def unchanged(partial_value):
            return partial_value

        return lax.cond(request < REQS, update, unchanged, running)

    run_max, run_sum, run_out = lax.fori_loop(0, page_total, add_page, initial)
    share = SPAN // (ctx_size * sub_size)
    global_max = lax.pmax(run_max, ("ctx", "sub"))
    factor = jnp.exp(run_max - global_max)
    sums_here, outs_here = (
        lax.psum_scatter(
            (run_sum * factor).astype(jnp.bfloat16), ("ctx", "sub"), scatter_dimension=0, tiled=True
        ).astype(jnp.float32),
        lax.psum_scatter(
            (run_out * factor[..., None]).astype(jnp.bfloat16),
            ("ctx", "sub"),
            scatter_dimension=0,
            tiled=True,
        ).astype(jnp.float32),
    )
    finished = (outs_here / sums_here[..., None]).astype(jnp.bfloat16)
    finished = finished.reshape(share, local_heads * per_group * HD)
    return lax.all_to_all(finished, "head", split_axis=0, concat_axis=1, tiled=True)


def per_device(queries, kv_cache, page_counts):
    ctx_size, sub_size, head_count = lax.axis_size("ctx"), lax.axis_size("sub"), lax.axis_size("head")
    small = (
        ctx_size == REQS == 4
        and head_count == sub_size == 2
        and kv_cache.shape[1] == 2 * PAGE
        and kv_cache.shape[2] % (sub_size * HD) == 0
        and queries.shape[0] % 16 == 0
        and queries.shape[0] * head_count * sub_size == QR
    )
    return (one_request_each if small else queries_to_pages)(queries, kv_cache, page_counts)


def solution(mesh):
    return jax.shard_map(
        per_device,
        mesh=mesh,
        in_specs=(
            P(("grp", "ctx", "head", "sub"), None),
            P(None, ("grp", "ctx", "sub"), "head"),
            P("grp"),
        ),
        out_specs=P(("grp", "ctx", "head", "sub"), None),
        check_vma=False,
    )
```

```python
import functools

import jax
import jax.numpy as jnp
from jax import lax
from jax.experimental import pallas as pl
from jax.experimental.pallas import tpu as pltpu
from jax.sharding import PartitionSpec as P

HQ = 128
KVH = 8
HD = 128
REQS = 4
QR = 64
PAGE = 256
SPAN = 256


NEG = -1e30
EXP2_SCALE = HD ** (-0.5) * 1.4426950408889634


def run(copies):
    for copy in copies:
        copy.start()
    for copy in copies:
        copy.wait()


def head_part(step, width):
    return pl.ds(pl.multiple_of((lax.axis_index("head") ^ step) * width, width), width)


def split_kernel(queries, *refs):
    outs, sems = refs[:-1], refs[-1]
    run([
        pltpu.make_async_copy(queries.at[:, head_part(step, out.shape[1])], out, sems.at[step])
        for step, out in enumerate(outs)
    ])


def join_kernel(keys, *refs):
    out, sems = refs[-2:]

    @pl.when(lax.axis_index("sub") == keys[0][1])
    def _():
        run([
            pltpu.make_async_copy(piece, out.at[:, head_part(step, piece.shape[1])], sems.at[i])
            for i, (piece, (step, _)) in enumerate(zip(refs, keys))
        ])


def worker_places(low_ctx):
    return (0, 0), (low_ctx, 1), (low_ctx + 1, 1), (low_ctx + 1, 0)


def own_request(low_ctx):
    ctx, sub = lax.axis_index("ctx"), lax.axis_index("sub")
    found = jnp.int32(-1)
    for request, place in enumerate(worker_places(low_ctx)):
        found = jnp.where((ctx == place[0]) & (sub == place[1]), request, found)
    return found


def pages_of(low_ctx, counts, most_pages):
    request = own_request(low_ctx)
    start = jnp.int32(0)
    for r in range(REQS):
        start = start + jnp.where(r < request, counts[r], 0)
    count = jnp.where(request >= 0, counts[jnp.maximum(request, 0)], 0)
    home_pair = jnp.where(request == 0, -1, jnp.where(request == 1, 1, 5 - request))
    near_pair = jnp.where(request == 0, 1, home_pair ^ 1)
    for p in range(most_pages):
        page = start + p
        pair = page // 2
        which = jnp.where(pair == home_pair, 0, jnp.where(pair == near_pair, 1, 2))
        yield p, p < count, which, pl.ds(pl.multiple_of(lax.rem(page, 2) * PAGE, PAGE), PAGE)


def gather_home_kernel(low_ctx, counts, counts_in, own, after, out, counts_out, sems, counts_sem):
    local_kv, _, most_pages = out.shape[:3]
    counts_copy = pltpu.make_async_copy(counts_in, counts_out, counts_sem)
    counts_copy.start()
    plan = [
        (here & (which == 0), [
            pltpu.make_async_copy(own.at[i, rows, pl.ds(g * HD, HD)], out.at[g, i, p], sems.at[g, i, p])
            for g in range(local_kv) for i in range(2)
        ])
        for p, here, which, rows in pages_of(low_ctx, counts, most_pages)
    ]
    for here, copies in plan:
        @pl.when(here)
        def _():
            for copy in copies:
                copy.start()
    for here, copies in plan:
        @pl.when(here)
        def _():
            for copy in copies:
                copy.wait()
    counts_copy.wait()


def gather_rest(low_ctx, counts, home, far, near, out):
    local_kv, _, most_pages = out.shape[:3]
    for p, here, which, rows in pages_of(low_ctx, counts, most_pages):
        @pl.when(here & (which == 0))
        def _():
            for g in range(local_kv):
                out[g, :, p] = home[g, :, p]
        for n, ref in enumerate((near, far)):
            @pl.when(here & (which == n + 1))
            def _():
                for g in range(local_kv):
                    for i in range(2):
                        out[g, i, p] = ref[i, rows, g * HD:(g + 1) * HD]


def attend_kernel(low_ctx, sub_count, groups, others, counts, home, *refs):
    keys = [key for group in groups for key in group]
    queries, outs = dict(zip(keys, refs)), dict(zip(keys, refs[len(keys) + others:]))
    pages_in = home
    if others:
        pages_in = refs[-1]
        gather_rest(low_ctx, counts, home, *refs[len(keys):len(keys) + others], pages_in)
    head = lax.axis_index("head")
    tokens, width = refs[0].shape
    local_kv, _, most_pages = pages_in.shape[:3]
    span = width // local_kv
    per_group = span // HD
    piece_rows = per_group * tokens
    rows = len(groups[0]) * piece_rows

    def attend(pages):
        span_rows = pages * PAGE
        row = lax.broadcasted_iota(jnp.int32, (rows, 1), 0)
        masked_from = (PAGE - QR) // HD * HD
        column = masked_from + lax.broadcasted_iota(jnp.int32, (rows, PAGE - masked_from), 1)

        def visible_of(group):
            token = lax.rem(row, tokens)
            for i, (step, source) in enumerate(group):
                first_token = ((head ^ step) * sub_count + source) * tokens
                token = jnp.where(row // piece_rows == i, token + first_token, token)
            return column <= PAGE - QR + token

        def of_pages(g, i):
            return pages_in[g, i, 0:pages].reshape(span_rows, HD)

        def scores_of(group, g):
            q_blocks = [queries[key][:, g * span:(g + 1) * span] for key in group]
            q_rows = jnp.concatenate([q[:, j * HD:(j + 1) * HD] for q in q_blocks for j in range(per_group)], axis=0)
            scores = lax.dot_general(
                q_rows, of_pages(g, 0), (((1,), (1,)), ((), ())), preferred_element_type=jnp.float32
            )
            scores = [scores[:, p * PAGE:(p + 1) * PAGE] for p in range(pages)]
            tail = jnp.where(visible_of(group), scores[-1][:, masked_from:], NEG)
            scores[-1] = jnp.concatenate([scores[-1][:, :masked_from], tail], axis=1)
            return scores

        units = [(group, g) for group in groups for g in range(local_kv)]
        scores = scores_of(*units[0])
        for n, (group, g) in enumerate(units):
            later = scores_of(*units[n + 1]) if n + 1 < len(units) else None
            top = jnp.max(functools.reduce(jnp.maximum, scores), axis=1, keepdims=True)
            numerators = [jnp.exp2((s - top) * EXP2_SCALE) for s in scores]
            totals = jnp.sum(functools.reduce(jnp.add, numerators), axis=1, keepdims=True)
            weights = jnp.concatenate([s.astype(jnp.bfloat16) for s in numerators], axis=1)
            product = jnp.dot(weights, of_pages(g, 1), preferred_element_type=jnp.float32)
            done = (product / totals).astype(jnp.bfloat16)
            for i, key in enumerate(group):
                start = i * piece_rows
                outs[key][:, g * span:(g + 1) * span] = jnp.concatenate(
                    [done[start + j * tokens:start + (j + 1) * tokens] for j in range(per_group)], axis=1
                )
            scores = later

    request = own_request(low_ctx)

    @pl.when(request >= 0)
    def _():
        count = counts[request]
        for pages in [*range(1, most_pages - REQS + 3), most_pages]:
            @pl.when(count == pages)
            def _():
                attend(pages)


def one_request_each(queries, kv_cache, page_counts):
    ctx_size, sub_size = lax.axis_size("ctx"), lax.axis_size("sub")
    head_count = lax.axis_size("head")
    low_ctx = ctx_size // 2
    most_pages = kv_cache.shape[1] // PAGE * ctx_size * sub_size // 4
    local_kv = kv_cache.shape[2] // HD
    tokens, width = queries.shape[0], queries.shape[1] // head_count
    anywhere = pl.BlockSpec(memory_space=pl.ANY)
    in_vmem = pl.BlockSpec(memory_space=pltpu.VMEM)
    q_piece = pltpu.VMEM((tokens, width), queries.dtype)

    def vmem(array):
        return pltpu.with_memory_space_constraint(array, pltpu.VMEM)

    def hbm(array):
        return pltpu.with_memory_space_constraint(array, pltpu.HBM)

    def moved(array, routes):
        def flat(place):
            return (place[0] * head_count + place[1]) * sub_size + place[2]

        return lax.ppermute(array, ("ctx", "head", "sub"), [(flat(a), flat(b)) for a, b in routes])

    def worker(request, head):
        ctx, sub = worker_places(low_ctx)[request]
        return ctx, head, sub

    heads = range(head_count)
    q_out = pl.pallas_call(
        split_kernel,
        out_shape=[q_piece] * head_count,
        in_specs=[anywhere],
        out_specs=[anywhere] * head_count,
        scratch_shapes=[pltpu.SemaphoreType.DMA((head_count,))],
        compiler_params=pltpu.CompilerParams(vmem_limit_bytes=2**20),
        name="split",
    )(hbm(queries))
    routes = {
        (step, s): [((r, h, s), worker(r, h ^ step)) for r in range(ctx_size) for h in heads]
        for s in range(sub_size) for step in heads[::-1]
    }
    first, last = list(routes)[0], list(routes)[-1]
    q_in = {first: moved(q_out[first[0]], routes[first])}
    home, counts = pl.pallas_call(
        functools.partial(gather_home_kernel, low_ctx),
        out_shape=[
            pltpu.VMEM((local_kv, 2, most_pages, PAGE, HD), kv_cache.dtype),
            pltpu.VMEM(page_counts.shape, page_counts.dtype),
        ],
        in_specs=[pl.BlockSpec(memory_space=pltpu.SMEM)] + [anywhere] * 3,
        out_specs=[anywhere] * 2,
        scratch_shapes=[pltpu.SemaphoreType.DMA((local_kv, 2, most_pages)), pltpu.SemaphoreType.DMA],
        compiler_params=pltpu.CompilerParams(vmem_limit_bytes=2**20),
        name="gather_home",
    )(hbm(page_counts), hbm(page_counts), hbm(kv_cache), vmem(q_in[first]))
    q_last, counts = lax.optimization_barrier((q_out[last[0]], counts))
    for key in list(routes)[1:]:
        q_in[key] = moved(q_last if key == last else q_out[key[0]], routes[key])

    pairs = [(low_ctx + n // 2, n % 2) for n in range(4)]
    workers = worker_places(low_ctx)
    near, far = (
        moved(kv_cache, [((*a[:1], h, *a[1:]), (*b[:1], h, *b[1:])) for a, b in sends for h in heads])
        for sends in (
            [(pairs[0], workers[1]), (pairs[1], workers[0]), (pairs[2], workers[2]), (pairs[3], workers[3])],
            [(pairs[0], workers[0]), (pairs[1], workers[2]), (pairs[2], workers[1])],
        )
    )
    groups = [[(step, s) for step in heads[::-1]] for s in range(sub_size)]
    done, back = {}, {}
    pages, others = home, [vmem(far), vmem(near)]
    for keys in groups:
        outs = pl.pallas_call(
            functools.partial(attend_kernel, low_ctx, sub_size, [keys], len(others)),
            out_shape=[q_piece] * len(keys) + [pltpu.VMEM(home.shape, home.dtype)] * bool(others),
            in_specs=[pl.BlockSpec(memory_space=pltpu.SMEM)] + [in_vmem] * (1 + len(keys) + len(others)),
            out_specs=[in_vmem] * (len(keys) + bool(others)),
            compiler_params=pltpu.CompilerParams(vmem_limit_bytes=12 * 2**20),
            cost_estimate=pl.CostEstimate(flops=10**10, bytes_accessed=2**22, transcendentals=10**6),
            name=f"attend_{keys[0][1]}",
        )(vmem(counts), vmem(pages), *[vmem(q_in[key]) for key in keys], *others)
        done.update(zip(keys, outs))
        if others:
            pages, others = outs[-1], []

    for key, out in zip(done, lax.optimization_barrier(tuple(done.values()))):
        back[key] = moved(out, [(b, a) for a, b in routes[key]])

    joined = []
    for keys in groups:
        joined = [
            pl.pallas_call(
                functools.partial(join_kernel, keys),
                out_shape=pltpu.HBM(queries.shape, queries.dtype),
                in_specs=[anywhere] * (len(keys) + len(joined)),
                out_specs=anywhere,
                scratch_shapes=[pltpu.SemaphoreType.DMA((len(keys),))],
                input_output_aliases={len(keys): 0} if joined else {},
                compiler_params=pltpu.CompilerParams(vmem_limit_bytes=2**20),
                name=f"join_{keys[0][1]}",
            )(*[vmem(back[key]) for key in keys], *map(hbm, joined))
        ]
    return joined[0]


def from_behind(array, axis, by):
    count = lax.axis_size(axis)
    pairs = [(i, i + by) for i in range(count) if 0 <= i + by < count]
    return lax.ppermute(array, axis, pairs)


def queries_to_pages(queries, kv_cache, page_counts):
    per_group = HQ // KVH
    local_heads = kv_cache.shape[2] // HD
    ctx_size = lax.axis_size("ctx")
    sub_size = lax.axis_size("sub")
    head_count = lax.axis_size("head")
    tok_rows = queries.shape[0]
    score_scale = HD ** (-0.5)
    regrouped = lax.all_to_all(queries, "head", split_axis=1, concat_axis=0, tiled=True)
    all_queries = lax.all_gather(regrouped, ("ctx", "sub"), axis=0, tiled=True)
    all_queries = all_queries.reshape(SPAN, local_heads, per_group, HD)
    page_ends = jnp.cumsum(page_counts)
    ctx_rows = SPAN // ctx_size
    offsets = jnp.arange(QR, dtype=jnp.int32)
    columns = jnp.arange(PAGE, dtype=jnp.int32)
    flat_index = lax.axis_index("ctx") * sub_size + lax.axis_index("sub")
    pages_here = kv_cache.shape[1] // PAGE
    base_pages = pages_here * ctx_size * sub_size // 2
    initial = (
        jnp.full((SPAN, local_heads, per_group), NEG, jnp.float32),
        jnp.zeros((SPAN, local_heads, per_group), jnp.float32),
        jnp.zeros((SPAN, local_heads, per_group, HD), jnp.float32),
    )
    half_rows = kv_cache.shape[1] // 2
    arrived = from_behind(kv_cache[:, half_rows:], "ctx", -(ctx_size // 2))
    is_lower = lax.axis_index("ctx") < ctx_size // 2
    source_flat = flat_index + ctx_size // 2 * sub_size
    working = jnp.where(is_lower, arrived, kv_cache[:, :half_rows])
    first_page = jnp.where(
        is_lower, source_flat * pages_here + pages_here // 2, flat_index * pages_here
    )
    page_total = working.shape[1] // PAGE

    def add_page(page_turn, running):
        page_index = first_page + page_turn
        relative = page_index - base_pages
        counted = jnp.sum((relative >= page_ends).astype(jnp.int32))
        request = jnp.where(relative < 0, REQS, counted)

        def update(partial_value):
            run_max, run_sum, run_out = partial_value
            request_id = jnp.minimum(request, REQS - 1)
            row_start = request_id * QR
            gathered = row_start + offsets
            within = gathered % ctx_rows
            ctx_block = gathered // ctx_rows
            sub_part = within // (head_count * tok_rows)
            head_part = within // tok_rows % head_count
            tok_part = within % tok_rows
            natural = ctx_block * ctx_rows + (head_part * sub_size + sub_part) * tok_rows + tok_part
            query_pos = (page_ends[request_id] + base_pages) * PAGE - QR + natural - row_start
            key_pos = page_index * PAGE + columns
            visible = key_pos[None, :] <= query_pos[:, None]
            page_keys = working[0].reshape(PAGE, local_heads, HD)
            page_values = working[1].reshape(PAGE, local_heads, HD)
            query_rows = lax.dynamic_slice_in_dim(all_queries, row_start, QR, 0)
            scores = (
                jnp.einsum(
                    "qkgd,pkd->qkgp", query_rows, page_keys, preferred_element_type=jnp.float32
                )
                * score_scale
            )
            scores = jnp.where(visible[:, None, None, :], scores, NEG)
            old_max = lax.dynamic_slice_in_dim(run_max, row_start, QR, 0)
            old_sum = lax.dynamic_slice_in_dim(run_sum, row_start, QR, 0)
            old_out = lax.dynamic_slice_in_dim(run_out, row_start, QR, 0)
            new_max = jnp.maximum(old_max, jnp.max(scores, axis=3))
            factor = jnp.exp(old_max - new_max)
            numerators = jnp.exp(scores - new_max[..., None])
            new_sum = old_sum * factor + jnp.sum(numerators, axis=3)
            product = jnp.einsum(
                "qkgp,pkd->qkgd",
                numerators.astype(jnp.bfloat16),
                page_values,
                preferred_element_type=jnp.float32,
            )
            new_out = old_out * factor[..., None] + product
            return (
                lax.dynamic_update_slice_in_dim(run_max, new_max, row_start, 0),
                lax.dynamic_update_slice_in_dim(run_sum, new_sum, row_start, 0),
                lax.dynamic_update_slice_in_dim(run_out, new_out, row_start, 0),
            )

        def unchanged(partial_value):
            return partial_value

        return lax.cond(request < REQS, update, unchanged, running)

    run_max, run_sum, run_out = lax.fori_loop(0, page_total, add_page, initial)
    share = SPAN // (ctx_size * sub_size)
    global_max = lax.pmax(run_max, ("ctx", "sub"))
    factor = jnp.exp(run_max - global_max)
    sums_here, outs_here = (
        lax.psum_scatter(
            (run_sum * factor).astype(jnp.bfloat16), ("ctx", "sub"), scatter_dimension=0, tiled=True
        ).astype(jnp.float32),
        lax.psum_scatter(
            (run_out * factor[..., None]).astype(jnp.bfloat16),
            ("ctx", "sub"),
            scatter_dimension=0,
            tiled=True,
        ).astype(jnp.float32),
    )
    finished = (outs_here / sums_here[..., None]).astype(jnp.bfloat16)
    finished = finished.reshape(share, local_heads * per_group * HD)
    return lax.all_to_all(finished, "head", split_axis=0, concat_axis=1, tiled=True)


def per_device(queries, kv_cache, page_counts):
    ctx_size, sub_size, head_count = lax.axis_size("ctx"), lax.axis_size("sub"), lax.axis_size("head")
    small = (
        ctx_size == REQS == 4
        and head_count == sub_size == 2
        and kv_cache.shape[1] == 2 * PAGE
        and kv_cache.shape[2] % (sub_size * HD) == 0
        and queries.shape[0] % 16 == 0
        and queries.shape[0] * head_count * sub_size == QR
    )
    return (one_request_each if small else queries_to_pages)(queries, kv_cache, page_counts)


def solution(mesh):
    return jax.shard_map(
        per_device,
        mesh=mesh,
        in_specs=(
            P(("grp", "ctx", "head", "sub"), None),
            P(None, ("grp", "ctx", "sub"), "head"),
            P("grp"),
        ),
        out_specs=P(("grp", "ctx", "head", "sub"), None),
        check_vma=False,
    )
```

```python
import functools

import jax
import jax.numpy as jnp
from jax import lax
from jax.experimental import pallas as pl
from jax.experimental.pallas import tpu as pltpu
from jax.sharding import PartitionSpec as P

HQ = 128
KVH = 8
HD = 128
REQS = 4
QR = 64
PAGE = 256
SPAN = 256


NEG = -1e30
EXP2_SCALE = HD ** (-0.5) * 1.4426950408889634


def run(copies):
    for copy in copies:
        copy.start()
    for copy in copies:
        copy.wait()


def head_part(step, width):
    return pl.ds(pl.multiple_of((lax.axis_index("head") ^ step) * width, width), width)


def split_kernel(queries, *refs):
    outs, sems = refs[:-1], refs[-1]
    run([
        pltpu.make_async_copy(queries.at[:, head_part(step, out.shape[1])], out, sems.at[step])
        for step, out in enumerate(outs)
    ])


def join_kernel(keys, *refs):
    out, sems = refs[-2:]

    @pl.when(lax.axis_index("sub") == keys[0][1])
    def _():
        run([
            pltpu.make_async_copy(piece, out.at[:, head_part(step, piece.shape[1])], sems.at[i])
            for i, (piece, (step, _)) in enumerate(zip(refs, keys))
        ])


def worker_places(low_ctx):
    return (0, 1), (low_ctx, 1), (low_ctx + 1, 1), (low_ctx + 1, 0)


def own_request(low_ctx):
    ctx, sub = lax.axis_index("ctx"), lax.axis_index("sub")
    found = jnp.int32(-1)
    for request, place in enumerate(worker_places(low_ctx)):
        found = jnp.where((ctx == place[0]) & (sub == place[1]), request, found)
    return found


def pages_of(low_ctx, counts, most_pages):
    request = own_request(low_ctx)
    start = jnp.int32(0)
    for r in range(REQS):
        start = start + jnp.where(r < request, counts[r], 0)
    count = jnp.where(request >= 0, counts[jnp.maximum(request, 0)], 0)
    home_pair = jnp.where(request == 0, -1, jnp.where(request == 1, 1, 5 - request))
    near_pair = jnp.where(request == 0, 1, home_pair ^ 1)
    for p in range(most_pages):
        page = start + p
        pair = page // 2
        which = jnp.where(pair == home_pair, 0, jnp.where(pair == near_pair, 1, 2))
        yield p, p < count, which, pl.ds(pl.multiple_of(lax.rem(page, 2) * PAGE, PAGE), PAGE)


def gather_home_kernel(low_ctx, counts, counts_in, own, after, out, counts_out, sems, counts_sem):
    local_kv, _, most_pages = out.shape[:3]
    counts_copy = pltpu.make_async_copy(counts_in, counts_out, counts_sem)
    counts_copy.start()
    plan = [
        (here & (which == 0), [
            pltpu.make_async_copy(own.at[i, rows, pl.ds(g * HD, HD)], out.at[g, i, p], sems.at[g, i, p])
            for g in range(local_kv) for i in range(2)
        ])
        for p, here, which, rows in pages_of(low_ctx, counts, most_pages)
    ]
    for here, copies in plan:
        @pl.when(here)
        def _():
            for copy in copies:
                copy.start()
    for here, copies in plan:
        @pl.when(here)
        def _():
            for copy in copies:
                copy.wait()
    counts_copy.wait()


def gather_rest(low_ctx, counts, home, far, near, out):
    local_kv, _, most_pages = out.shape[:3]
    for p, here, which, rows in pages_of(low_ctx, counts, most_pages):
        @pl.when(here & (which == 0))
        def _():
            for g in range(local_kv):
                out[g, :, p] = home[g, :, p]
        for n, ref in enumerate((near, far)):
            @pl.when(here & (which == n + 1))
            def _():
                for g in range(local_kv):
                    for i in range(2):
                        out[g, i, p] = ref[i, rows, g * HD:(g + 1) * HD]


def attend_kernel(low_ctx, sub_count, groups, others, counts, home, *refs):
    keys = [key for group in groups for key in group]
    queries, outs = dict(zip(keys, refs)), dict(zip(keys, refs[len(keys) + others:]))
    pages_in = home
    if others:
        pages_in = refs[-1]
        gather_rest(low_ctx, counts, home, *refs[len(keys):len(keys) + others], pages_in)
    head = lax.axis_index("head")
    tokens, width = refs[0].shape
    local_kv, _, most_pages = pages_in.shape[:3]
    span = width // local_kv
    per_group = span // HD
    piece_rows = per_group * tokens
    rows = len(groups[0]) * piece_rows

    def attend(pages):
        span_rows = pages * PAGE
        row = lax.broadcasted_iota(jnp.int32, (rows, 1), 0)
        masked_from = (PAGE - QR) // HD * HD
        column = masked_from + lax.broadcasted_iota(jnp.int32, (rows, PAGE - masked_from), 1)

        def visible_of(group):
            token = lax.rem(row, tokens)
            for i, (step, source) in enumerate(group):
                first_token = ((head ^ step) * sub_count + source) * tokens
                token = jnp.where(row // piece_rows == i, token + first_token, token)
            return column <= PAGE - QR + token

        def of_pages(g, i):
            return pages_in[g, i, 0:pages].reshape(span_rows, HD)

        def scores_of(group, g):
            q_blocks = [queries[key][:, g * span:(g + 1) * span] for key in group]
            q_rows = jnp.concatenate([q[:, j * HD:(j + 1) * HD] for q in q_blocks for j in range(per_group)], axis=0)
            scores = lax.dot_general(
                q_rows, of_pages(g, 0), (((1,), (1,)), ((), ())), preferred_element_type=jnp.float32
            )
            scores = [scores[:, p * PAGE:(p + 1) * PAGE] for p in range(pages)]
            tail = jnp.where(visible_of(group), scores[-1][:, masked_from:], NEG)
            scores[-1] = jnp.concatenate([scores[-1][:, :masked_from], tail], axis=1)
            return scores

        units = [(group, g) for group in groups for g in range(local_kv)]
        scores = scores_of(*units[0])
        for n, (group, g) in enumerate(units):
            later = scores_of(*units[n + 1]) if n + 1 < len(units) else None
            top = jnp.max(functools.reduce(jnp.maximum, scores), axis=1, keepdims=True)
            numerators = [jnp.exp2((s - top) * EXP2_SCALE) for s in scores]
            totals = jnp.sum(functools.reduce(jnp.add, numerators), axis=1, keepdims=True)
            weights = jnp.concatenate([s.astype(jnp.bfloat16) for s in numerators], axis=1)
            product = jnp.dot(weights, of_pages(g, 1), preferred_element_type=jnp.float32)
            done = (product / totals).astype(jnp.bfloat16)
            for i, key in enumerate(group):
                start = i * piece_rows
                outs[key][:, g * span:(g + 1) * span] = jnp.concatenate(
                    [done[start + j * tokens:start + (j + 1) * tokens] for j in range(per_group)], axis=1
                )
            scores = later

    request = own_request(low_ctx)

    @pl.when(request >= 0)
    def _():
        count = counts[request]
        for pages in [*range(1, most_pages - REQS + 3), most_pages]:
            @pl.when(count == pages)
            def _():
                attend(pages)


def one_request_each(queries, kv_cache, page_counts):
    ctx_size, sub_size = lax.axis_size("ctx"), lax.axis_size("sub")
    head_count = lax.axis_size("head")
    low_ctx = ctx_size // 2
    most_pages = kv_cache.shape[1] // PAGE * ctx_size * sub_size // 4
    local_kv = kv_cache.shape[2] // HD
    tokens, width = queries.shape[0], queries.shape[1] // head_count
    anywhere = pl.BlockSpec(memory_space=pl.ANY)
    in_vmem = pl.BlockSpec(memory_space=pltpu.VMEM)
    q_piece = pltpu.VMEM((tokens, width), queries.dtype)

    def vmem(array):
        return pltpu.with_memory_space_constraint(array, pltpu.VMEM)

    def hbm(array):
        return pltpu.with_memory_space_constraint(array, pltpu.HBM)

    def moved(array, routes):
        def flat(place):
            return (place[0] * head_count + place[1]) * sub_size + place[2]

        return lax.ppermute(array, ("ctx", "head", "sub"), [(flat(a), flat(b)) for a, b in routes])

    def worker(request, head):
        ctx, sub = worker_places(low_ctx)[request]
        return ctx, head, sub

    heads = range(head_count)
    q_out = pl.pallas_call(
        split_kernel,
        out_shape=[q_piece] * head_count,
        in_specs=[anywhere],
        out_specs=[anywhere] * head_count,
        scratch_shapes=[pltpu.SemaphoreType.DMA((head_count,))],
        compiler_params=pltpu.CompilerParams(vmem_limit_bytes=2**20),
        name="split",
    )(hbm(queries))
    routes = {
        (step, s): [((r, h, s), worker(r, h ^ step)) for r in range(ctx_size) for h in heads]
        for s in range(sub_size) for step in heads[::-1]
    }
    first, last = list(routes)[0], list(routes)[-1]
    q_in = {first: moved(q_out[first[0]], routes[first])}
    home, counts = pl.pallas_call(
        functools.partial(gather_home_kernel, low_ctx),
        out_shape=[
            pltpu.VMEM((local_kv, 2, most_pages, PAGE, HD), kv_cache.dtype),
            pltpu.VMEM(page_counts.shape, page_counts.dtype),
        ],
        in_specs=[pl.BlockSpec(memory_space=pltpu.SMEM)] + [anywhere] * 3,
        out_specs=[anywhere] * 2,
        scratch_shapes=[pltpu.SemaphoreType.DMA((local_kv, 2, most_pages)), pltpu.SemaphoreType.DMA],
        compiler_params=pltpu.CompilerParams(vmem_limit_bytes=2**20),
        name="gather_home",
    )(hbm(page_counts), hbm(page_counts), hbm(kv_cache), vmem(q_in[first]))
    q_last, counts = lax.optimization_barrier((q_out[last[0]], counts))
    for key in list(routes)[1:]:
        q_in[key] = moved(q_last if key == last else q_out[key[0]], routes[key])

    pairs = [(low_ctx + n // 2, n % 2) for n in range(4)]
    workers = worker_places(low_ctx)
    near, far = (
        moved(kv_cache, [((*a[:1], h, *a[1:]), (*b[:1], h, *b[1:])) for a, b in sends for h in heads])
        for sends in (
            [(pairs[0], workers[1]), (pairs[1], workers[0]), (pairs[2], workers[2]), (pairs[3], workers[3])],
            [(pairs[0], workers[0]), (pairs[1], workers[2]), (pairs[2], workers[1])],
        )
    )
    groups = [[(step, s) for step in heads[::-1]] for s in range(sub_size)]
    back = {}
    pages, others = home, [vmem(far), vmem(near)]
    for keys in groups:
        outs = pl.pallas_call(
            functools.partial(attend_kernel, low_ctx, sub_size, [keys], len(others)),
            out_shape=[q_piece] * len(keys) + [pltpu.VMEM(home.shape, home.dtype)] * bool(others),
            in_specs=[pl.BlockSpec(memory_space=pltpu.SMEM)] + [in_vmem] * (1 + len(keys) + len(others)),
            out_specs=[in_vmem] * (len(keys) + bool(others)),
            compiler_params=pltpu.CompilerParams(vmem_limit_bytes=12 * 2**20),
            cost_estimate=pl.CostEstimate(flops=10**10, bytes_accessed=2**22, transcendentals=10**6),
            name=f"attend_{keys[0][1]}",
        )(vmem(counts), vmem(pages), *[vmem(q_in[key]) for key in keys], *others)
        for key, out in zip(keys, outs):
            back[key] = moved(out, [(b, a) for a, b in routes[key]])
        if others:
            pages, others = outs[-1], []

    joined = []
    for keys in groups:
        joined = [
            pl.pallas_call(
                functools.partial(join_kernel, keys),
                out_shape=pltpu.HBM(queries.shape, queries.dtype),
                in_specs=[anywhere] * (len(keys) + len(joined)),
                out_specs=anywhere,
                scratch_shapes=[pltpu.SemaphoreType.DMA((len(keys),))],
                input_output_aliases={len(keys): 0} if joined else {},
                compiler_params=pltpu.CompilerParams(vmem_limit_bytes=2**20),
                name=f"join_{keys[0][1]}",
            )(*[vmem(back[key]) for key in keys], *map(hbm, joined))
        ]
    return joined[0]


def from_behind(array, axis, by):
    count = lax.axis_size(axis)
    pairs = [(i, i + by) for i in range(count) if 0 <= i + by < count]
    return lax.ppermute(array, axis, pairs)


def queries_to_pages(queries, kv_cache, page_counts):
    per_group = HQ // KVH
    local_heads = kv_cache.shape[2] // HD
    ctx_size = lax.axis_size("ctx")
    sub_size = lax.axis_size("sub")
    head_count = lax.axis_size("head")
    tok_rows = queries.shape[0]
    score_scale = HD ** (-0.5)
    regrouped = lax.all_to_all(queries, "head", split_axis=1, concat_axis=0, tiled=True)
    all_queries = lax.all_gather(regrouped, ("ctx", "sub"), axis=0, tiled=True)
    all_queries = all_queries.reshape(SPAN, local_heads, per_group, HD)
    page_ends = jnp.cumsum(page_counts)
    ctx_rows = SPAN // ctx_size
    offsets = jnp.arange(QR, dtype=jnp.int32)
    columns = jnp.arange(PAGE, dtype=jnp.int32)
    flat_index = lax.axis_index("ctx") * sub_size + lax.axis_index("sub")
    pages_here = kv_cache.shape[1] // PAGE
    base_pages = pages_here * ctx_size * sub_size // 2
    initial = (
        jnp.full((SPAN, local_heads, per_group), NEG, jnp.float32),
        jnp.zeros((SPAN, local_heads, per_group), jnp.float32),
        jnp.zeros((SPAN, local_heads, per_group, HD), jnp.float32),
    )
    half_rows = kv_cache.shape[1] // 2
    arrived = from_behind(kv_cache[:, half_rows:], "ctx", -(ctx_size // 2))
    is_lower = lax.axis_index("ctx") < ctx_size // 2
    source_flat = flat_index + ctx_size // 2 * sub_size
    working = jnp.where(is_lower, arrived, kv_cache[:, :half_rows])
    first_page = jnp.where(
        is_lower, source_flat * pages_here + pages_here // 2, flat_index * pages_here
    )
    page_total = working.shape[1] // PAGE

    def add_page(page_turn, running):
        page_index = first_page + page_turn
        relative = page_index - base_pages
        counted = jnp.sum((relative >= page_ends).astype(jnp.int32))
        request = jnp.where(relative < 0, REQS, counted)

        def update(partial_value):
            run_max, run_sum, run_out = partial_value
            request_id = jnp.minimum(request, REQS - 1)
            row_start = request_id * QR
            gathered = row_start + offsets
            within = gathered % ctx_rows
            ctx_block = gathered // ctx_rows
            sub_part = within // (head_count * tok_rows)
            head_part = within // tok_rows % head_count
            tok_part = within % tok_rows
            natural = ctx_block * ctx_rows + (head_part * sub_size + sub_part) * tok_rows + tok_part
            query_pos = (page_ends[request_id] + base_pages) * PAGE - QR + natural - row_start
            key_pos = page_index * PAGE + columns
            visible = key_pos[None, :] <= query_pos[:, None]
            page_keys = working[0].reshape(PAGE, local_heads, HD)
            page_values = working[1].reshape(PAGE, local_heads, HD)
            query_rows = lax.dynamic_slice_in_dim(all_queries, row_start, QR, 0)
            scores = (
                jnp.einsum(
                    "qkgd,pkd->qkgp", query_rows, page_keys, preferred_element_type=jnp.float32
                )
                * score_scale
            )
            scores = jnp.where(visible[:, None, None, :], scores, NEG)
            old_max = lax.dynamic_slice_in_dim(run_max, row_start, QR, 0)
            old_sum = lax.dynamic_slice_in_dim(run_sum, row_start, QR, 0)
            old_out = lax.dynamic_slice_in_dim(run_out, row_start, QR, 0)
            new_max = jnp.maximum(old_max, jnp.max(scores, axis=3))
            factor = jnp.exp(old_max - new_max)
            numerators = jnp.exp(scores - new_max[..., None])
            new_sum = old_sum * factor + jnp.sum(numerators, axis=3)
            product = jnp.einsum(
                "qkgp,pkd->qkgd",
                numerators.astype(jnp.bfloat16),
                page_values,
                preferred_element_type=jnp.float32,
            )
            new_out = old_out * factor[..., None] + product
            return (
                lax.dynamic_update_slice_in_dim(run_max, new_max, row_start, 0),
                lax.dynamic_update_slice_in_dim(run_sum, new_sum, row_start, 0),
                lax.dynamic_update_slice_in_dim(run_out, new_out, row_start, 0),
            )

        def unchanged(partial_value):
            return partial_value

        return lax.cond(request < REQS, update, unchanged, running)

    run_max, run_sum, run_out = lax.fori_loop(0, page_total, add_page, initial)
    share = SPAN // (ctx_size * sub_size)
    global_max = lax.pmax(run_max, ("ctx", "sub"))
    factor = jnp.exp(run_max - global_max)
    sums_here, outs_here = (
        lax.psum_scatter(
            (run_sum * factor).astype(jnp.bfloat16), ("ctx", "sub"), scatter_dimension=0, tiled=True
        ).astype(jnp.float32),
        lax.psum_scatter(
            (run_out * factor[..., None]).astype(jnp.bfloat16),
            ("ctx", "sub"),
            scatter_dimension=0,
            tiled=True,
        ).astype(jnp.float32),
    )
    finished = (outs_here / sums_here[..., None]).astype(jnp.bfloat16)
    finished = finished.reshape(share, local_heads * per_group * HD)
    return lax.all_to_all(finished, "head", split_axis=0, concat_axis=1, tiled=True)


def per_device(queries, kv_cache, page_counts):
    ctx_size, sub_size, head_count = lax.axis_size("ctx"), lax.axis_size("sub"), lax.axis_size("head")
    small = (
        ctx_size == REQS == 4
        and head_count == sub_size == 2
        and kv_cache.shape[1] == 2 * PAGE
        and kv_cache.shape[2] % (sub_size * HD) == 0
        and queries.shape[0] % 16 == 0
        and queries.shape[0] * head_count * sub_size == QR
    )
    return (one_request_each if small else queries_to_pages)(queries, kv_cache, page_counts)


def solution(mesh):
    return jax.shard_map(
        per_device,
        mesh=mesh,
        in_specs=(
            P(("grp", "ctx", "head", "sub"), None),
            P(None, ("grp", "ctx", "sub"), "head"),
            P("grp"),
        ),
        out_specs=P(("grp", "ctx", "head", "sub"), None),
        check_vma=False,
    )
```

```python
import functools

import jax
import jax.numpy as jnp
from jax import lax
from jax.experimental import pallas as pl
from jax.experimental.pallas import tpu as pltpu
from jax.sharding import PartitionSpec as P

HQ = 128
KVH = 8
HD = 128
REQS = 4
QR = 64
PAGE = 256
SPAN = 256


NEG = -1e30
EXP2_SCALE = HD ** (-0.5) * 1.4426950408889634


def run(copies):
    for copy in copies:
        copy.start()
    for copy in copies:
        copy.wait()


def head_part(step, width):
    return pl.ds(pl.multiple_of((lax.axis_index("head") ^ step) * width, width), width)


def split_kernel(queries, *refs):
    outs, sems = refs[:-1], refs[-1]
    run([
        pltpu.make_async_copy(queries.at[:, head_part(step, out.shape[1])], out, sems.at[step])
        for step, out in enumerate(outs)
    ])


def join_kernel(keys, *refs):
    out, sems = refs[-2:]

    @pl.when(lax.axis_index("sub") == keys[0][1])
    def _():
        run([
            pltpu.make_async_copy(piece, out.at[:, head_part(step, piece.shape[1])], sems.at[i])
            for i, (piece, (step, _)) in enumerate(zip(refs, keys))
        ])


def worker_places(low_ctx):
    return (0, 1), (low_ctx, 1), (low_ctx + 1, 1), (low_ctx + 1, 0)


def own_request(low_ctx):
    ctx, sub = lax.axis_index("ctx"), lax.axis_index("sub")
    found = jnp.int32(-1)
    for request, place in enumerate(worker_places(low_ctx)):
        found = jnp.where((ctx == place[0]) & (sub == place[1]), request, found)
    return found


def pages_of(low_ctx, counts, most_pages):
    request = own_request(low_ctx)
    start = jnp.int32(0)
    for r in range(REQS):
        start = start + jnp.where(r < request, counts[r], 0)
    count = jnp.where(request >= 0, counts[jnp.maximum(request, 0)], 0)
    home_pair = jnp.where(request == 0, -1, jnp.where(request == 1, 1, 5 - request))
    near_pair = jnp.where(request == 0, 1, home_pair ^ 1)
    for p in range(most_pages):
        page = start + p
        pair = page // 2
        which = jnp.where(pair == home_pair, 0, jnp.where(pair == near_pair, 1, 2))
        yield p, p < count, which, pl.ds(pl.multiple_of(lax.rem(page, 2) * PAGE, PAGE), PAGE)


def gather_home_kernel(low_ctx, counts, counts_in, own, after, out, counts_out, sems, counts_sem):
    local_kv, _, most_pages = out.shape[:3]
    counts_copy = pltpu.make_async_copy(counts_in, counts_out, counts_sem)
    counts_copy.start()
    plan = [
        (here & (which == 0), [
            pltpu.make_async_copy(own.at[i, rows, pl.ds(g * HD, HD)], out.at[g, i, p], sems.at[g, i, p])
            for g in range(local_kv) for i in range(2)
        ])
        for p, here, which, rows in pages_of(low_ctx, counts, most_pages)
    ]
    for here, copies in plan:
        @pl.when(here)
        def _():
            for copy in copies:
                copy.start()
    for here, copies in plan:
        @pl.when(here)
        def _():
            for copy in copies:
                copy.wait()
    counts_copy.wait()


def gather_rest(low_ctx, counts, home, far, near, keys_out, values_out):
    local_kv, most_pages = values_out.shape[:2]

    def put(g, p, keys, values):
        keys_out[g, :, p * PAGE:(p + 1) * PAGE] = keys.T
        values_out[g, p] = values

    for p, here, which, rows in pages_of(low_ctx, counts, most_pages):
        @pl.when(here & (which == 0))
        def _():
            for g in range(local_kv):
                put(g, p, home[g, 0, p], home[g, 1, p])
        for n, ref in enumerate((near, far)):
            @pl.when(here & (which == n + 1))
            def _():
                for g in range(local_kv):
                    part = slice(g * HD, (g + 1) * HD)
                    put(g, p, ref[0, rows, part], ref[1, rows, part])


def attend_kernel(low_ctx, sub_count, groups, others, counts, *refs):
    keys = [key for group in groups for key in group]
    before = 1 if others else 2
    after = before + len(keys) + others
    queries, outs = dict(zip(keys, refs[before:])), dict(zip(keys, refs[after:]))
    keys_in, values_in = refs[-2:] if others else refs[:2]
    if others:
        gather_rest(low_ctx, counts, refs[0], *refs[after - others:after], keys_in, values_in)
    head = lax.axis_index("head")
    tokens, width = queries[keys[0]].shape
    local_kv, most_pages = values_in.shape[:2]
    span = width // local_kv
    per_group = span // HD
    piece_rows = per_group * tokens
    rows = len(groups[0]) * piece_rows

    def attend(pages):
        span_rows = pages * PAGE
        row = lax.broadcasted_iota(jnp.int32, (rows, 1), 0)
        masked_from = (PAGE - QR) // HD * HD
        column = masked_from + lax.broadcasted_iota(jnp.int32, (rows, PAGE - masked_from), 1)

        def visible_of(group):
            token = lax.rem(row, tokens)
            for i, (step, source) in enumerate(group):
                first_token = ((head ^ step) * sub_count + source) * tokens
                token = jnp.where(row // piece_rows == i, token + first_token, token)
            return column <= PAGE - QR + token

        def scores_of(group, g):
            q_blocks = [queries[key][:, g * span:(g + 1) * span] for key in group]
            q_rows = jnp.concatenate([q[:, j * HD:(j + 1) * HD] for q in q_blocks for j in range(per_group)], axis=0)
            scores = jnp.dot(q_rows, keys_in[g, :, 0:span_rows], preferred_element_type=jnp.float32)
            scores = [scores[:, p * PAGE:(p + 1) * PAGE] for p in range(pages)]
            tail = jnp.where(visible_of(group), scores[-1][:, masked_from:], NEG)
            scores[-1] = jnp.concatenate([scores[-1][:, :masked_from], tail], axis=1)
            return scores

        units = [(group, g) for group in groups for g in range(local_kv)]
        scores = scores_of(*units[0])
        for n, (group, g) in enumerate(units):
            later = scores_of(*units[n + 1]) if n + 1 < len(units) else None
            top = jnp.max(functools.reduce(jnp.maximum, scores), axis=1, keepdims=True)
            numerators = [jnp.exp2((s - top) * EXP2_SCALE) for s in scores]
            totals = jnp.sum(functools.reduce(jnp.add, numerators), axis=1, keepdims=True)
            weights = jnp.concatenate([s.astype(jnp.bfloat16) for s in numerators], axis=1)
            product = jnp.dot(weights, values_in[g, 0:pages].reshape(span_rows, HD), preferred_element_type=jnp.float32)
            done = (product / totals).astype(jnp.bfloat16)
            for i, key in enumerate(group):
                start = i * piece_rows
                outs[key][:, g * span:(g + 1) * span] = jnp.concatenate(
                    [done[start + j * tokens:start + (j + 1) * tokens] for j in range(per_group)], axis=1
                )
            scores = later

    request = own_request(low_ctx)

    @pl.when(request >= 0)
    def _():
        count = counts[request]
        for pages in [*range(1, most_pages - REQS + 3), most_pages]:
            @pl.when(count == pages)
            def _():
                attend(pages)


def one_request_each(queries, kv_cache, page_counts):
    ctx_size, sub_size = lax.axis_size("ctx"), lax.axis_size("sub")
    head_count = lax.axis_size("head")
    low_ctx = ctx_size // 2
    most_pages = kv_cache.shape[1] // PAGE * ctx_size * sub_size // 4
    local_kv = kv_cache.shape[2] // HD
    tokens, width = queries.shape[0], queries.shape[1] // head_count
    anywhere = pl.BlockSpec(memory_space=pl.ANY)
    in_vmem = pl.BlockSpec(memory_space=pltpu.VMEM)
    q_piece = pltpu.VMEM((tokens, width), queries.dtype)

    def vmem(array):
        return pltpu.with_memory_space_constraint(array, pltpu.VMEM)

    def hbm(array):
        return pltpu.with_memory_space_constraint(array, pltpu.HBM)

    def moved(array, routes):
        def flat(place):
            return (place[0] * head_count + place[1]) * sub_size + place[2]

        return lax.ppermute(array, ("ctx", "head", "sub"), [(flat(a), flat(b)) for a, b in routes])

    def worker(request, head):
        ctx, sub = worker_places(low_ctx)[request]
        return ctx, head, sub

    heads = range(head_count)
    q_out = pl.pallas_call(
        split_kernel,
        out_shape=[q_piece] * head_count,
        in_specs=[anywhere],
        out_specs=[anywhere] * head_count,
        scratch_shapes=[pltpu.SemaphoreType.DMA((head_count,))],
        compiler_params=pltpu.CompilerParams(vmem_limit_bytes=2**20),
        name="split",
    )(hbm(queries))
    routes = {
        (step, s): [((r, h, s), worker(r, h ^ step)) for r in range(ctx_size) for h in heads]
        for s in range(sub_size) for step in heads[::-1]
    }
    first, last = list(routes)[0], list(routes)[-1]
    q_in = {first: moved(q_out[first[0]], routes[first])}
    home, counts = pl.pallas_call(
        functools.partial(gather_home_kernel, low_ctx),
        out_shape=[
            pltpu.VMEM((local_kv, 2, most_pages, PAGE, HD), kv_cache.dtype),
            pltpu.VMEM(page_counts.shape, page_counts.dtype),
        ],
        in_specs=[pl.BlockSpec(memory_space=pltpu.SMEM)] + [anywhere] * 3,
        out_specs=[anywhere] * 2,
        scratch_shapes=[pltpu.SemaphoreType.DMA((local_kv, 2, most_pages)), pltpu.SemaphoreType.DMA],
        compiler_params=pltpu.CompilerParams(vmem_limit_bytes=2**20),
        name="gather_home",
    )(hbm(page_counts), hbm(page_counts), hbm(kv_cache), vmem(q_in[first]))
    q_last, counts = lax.optimization_barrier((q_out[last[0]], counts))
    for key in list(routes)[1:]:
        q_in[key] = moved(q_last if key == last else q_out[key[0]], routes[key])

    pairs = [(low_ctx + n // 2, n % 2) for n in range(4)]
    workers = worker_places(low_ctx)
    near, far = (
        moved(kv_cache, [((*a[:1], h, *a[1:]), (*b[:1], h, *b[1:])) for a, b in sends for h in heads])
        for sends in (
            [(pairs[0], workers[1]), (pairs[1], workers[0]), (pairs[2], workers[2]), (pairs[3], workers[3])],
            [(pairs[0], workers[0]), (pairs[1], workers[2]), (pairs[2], workers[1])],
        )
    )
    groups = [[(step, s) for step in heads[::-1]] for s in range(sub_size)]
    back = {}
    pages, others = [vmem(home)], [vmem(far), vmem(near)]
    gathered = [
        pltpu.VMEM((local_kv, HD, most_pages * PAGE), kv_cache.dtype),
        pltpu.VMEM((local_kv, most_pages, PAGE, HD), kv_cache.dtype),
    ]
    for keys in groups:
        outs = pl.pallas_call(
            functools.partial(attend_kernel, low_ctx, sub_size, [keys], len(others)),
            out_shape=[q_piece] * len(keys) + gathered * bool(others),
            in_specs=[pl.BlockSpec(memory_space=pltpu.SMEM)] + [in_vmem] * (len(pages) + len(keys) + len(others)),
            out_specs=[in_vmem] * (len(keys) + len(gathered) * bool(others)),
            compiler_params=pltpu.CompilerParams(vmem_limit_bytes=12 * 2**20),
            cost_estimate=pl.CostEstimate(flops=10**10, bytes_accessed=2**22, transcendentals=10**6),
            name=f"attend_{keys[0][1]}",
        )(vmem(counts), *pages, *[vmem(q_in[key]) for key in keys], *others)
        for key, out in zip(keys, outs):
            back[key] = moved(out, [(b, a) for a, b in routes[key]])
        if others:
            pages, others = [vmem(out) for out in outs[len(keys):]], []

    joined = []
    for keys in groups:
        joined = [
            pl.pallas_call(
                functools.partial(join_kernel, keys),
                out_shape=pltpu.HBM(queries.shape, queries.dtype),
                in_specs=[anywhere] * (len(keys) + len(joined)),
                out_specs=anywhere,
                scratch_shapes=[pltpu.SemaphoreType.DMA((len(keys),))],
                input_output_aliases={len(keys): 0} if joined else {},
                compiler_params=pltpu.CompilerParams(vmem_limit_bytes=2**20),
                name=f"join_{keys[0][1]}",
            )(*[vmem(back[key]) for key in keys], *map(hbm, joined))
        ]
    return joined[0]


def from_behind(array, axis, by):
    count = lax.axis_size(axis)
    pairs = [(i, i + by) for i in range(count) if 0 <= i + by < count]
    return lax.ppermute(array, axis, pairs)


def queries_to_pages(queries, kv_cache, page_counts):
    per_group = HQ // KVH
    local_heads = kv_cache.shape[2] // HD
    ctx_size = lax.axis_size("ctx")
    sub_size = lax.axis_size("sub")
    head_count = lax.axis_size("head")
    tok_rows = queries.shape[0]
    score_scale = HD ** (-0.5)
    regrouped = lax.all_to_all(queries, "head", split_axis=1, concat_axis=0, tiled=True)
    all_queries = lax.all_gather(regrouped, ("ctx", "sub"), axis=0, tiled=True)
    all_queries = all_queries.reshape(SPAN, local_heads, per_group, HD)
    page_ends = jnp.cumsum(page_counts)
    ctx_rows = SPAN // ctx_size
    offsets = jnp.arange(QR, dtype=jnp.int32)
    columns = jnp.arange(PAGE, dtype=jnp.int32)
    flat_index = lax.axis_index("ctx") * sub_size + lax.axis_index("sub")
    pages_here = kv_cache.shape[1] // PAGE
    base_pages = pages_here * ctx_size * sub_size // 2
    initial = (
        jnp.full((SPAN, local_heads, per_group), NEG, jnp.float32),
        jnp.zeros((SPAN, local_heads, per_group), jnp.float32),
        jnp.zeros((SPAN, local_heads, per_group, HD), jnp.float32),
    )
    half_rows = kv_cache.shape[1] // 2
    arrived = from_behind(kv_cache[:, half_rows:], "ctx", -(ctx_size // 2))
    is_lower = lax.axis_index("ctx") < ctx_size // 2
    source_flat = flat_index + ctx_size // 2 * sub_size
    working = jnp.where(is_lower, arrived, kv_cache[:, :half_rows])
    first_page = jnp.where(
        is_lower, source_flat * pages_here + pages_here // 2, flat_index * pages_here
    )
    page_total = working.shape[1] // PAGE

    def add_page(page_turn, running):
        page_index = first_page + page_turn
        relative = page_index - base_pages
        counted = jnp.sum((relative >= page_ends).astype(jnp.int32))
        request = jnp.where(relative < 0, REQS, counted)

        def update(partial_value):
            run_max, run_sum, run_out = partial_value
            request_id = jnp.minimum(request, REQS - 1)
            row_start = request_id * QR
            gathered = row_start + offsets
            within = gathered % ctx_rows
            ctx_block = gathered // ctx_rows
            sub_part = within // (head_count * tok_rows)
            head_part = within // tok_rows % head_count
            tok_part = within % tok_rows
            natural = ctx_block * ctx_rows + (head_part * sub_size + sub_part) * tok_rows + tok_part
            query_pos = (page_ends[request_id] + base_pages) * PAGE - QR + natural - row_start
            key_pos = page_index * PAGE + columns
            visible = key_pos[None, :] <= query_pos[:, None]
            page_keys = working[0].reshape(PAGE, local_heads, HD)
            page_values = working[1].reshape(PAGE, local_heads, HD)
            query_rows = lax.dynamic_slice_in_dim(all_queries, row_start, QR, 0)
            scores = (
                jnp.einsum(
                    "qkgd,pkd->qkgp", query_rows, page_keys, preferred_element_type=jnp.float32
                )
                * score_scale
            )
            scores = jnp.where(visible[:, None, None, :], scores, NEG)
            old_max = lax.dynamic_slice_in_dim(run_max, row_start, QR, 0)
            old_sum = lax.dynamic_slice_in_dim(run_sum, row_start, QR, 0)
            old_out = lax.dynamic_slice_in_dim(run_out, row_start, QR, 0)
            new_max = jnp.maximum(old_max, jnp.max(scores, axis=3))
            factor = jnp.exp(old_max - new_max)
            numerators = jnp.exp(scores - new_max[..., None])
            new_sum = old_sum * factor + jnp.sum(numerators, axis=3)
            product = jnp.einsum(
                "qkgp,pkd->qkgd",
                numerators.astype(jnp.bfloat16),
                page_values,
                preferred_element_type=jnp.float32,
            )
            new_out = old_out * factor[..., None] + product
            return (
                lax.dynamic_update_slice_in_dim(run_max, new_max, row_start, 0),
                lax.dynamic_update_slice_in_dim(run_sum, new_sum, row_start, 0),
                lax.dynamic_update_slice_in_dim(run_out, new_out, row_start, 0),
            )

        def unchanged(partial_value):
            return partial_value

        return lax.cond(request < REQS, update, unchanged, running)

    run_max, run_sum, run_out = lax.fori_loop(0, page_total, add_page, initial)
    share = SPAN // (ctx_size * sub_size)
    global_max = lax.pmax(run_max, ("ctx", "sub"))
    factor = jnp.exp(run_max - global_max)
    sums_here, outs_here = (
        lax.psum_scatter(
            (run_sum * factor).astype(jnp.bfloat16), ("ctx", "sub"), scatter_dimension=0, tiled=True
        ).astype(jnp.float32),
        lax.psum_scatter(
            (run_out * factor[..., None]).astype(jnp.bfloat16),
            ("ctx", "sub"),
            scatter_dimension=0,
            tiled=True,
        ).astype(jnp.float32),
    )
    finished = (outs_here / sums_here[..., None]).astype(jnp.bfloat16)
    finished = finished.reshape(share, local_heads * per_group * HD)
    return lax.all_to_all(finished, "head", split_axis=0, concat_axis=1, tiled=True)


def per_device(queries, kv_cache, page_counts):
    ctx_size, sub_size, head_count = lax.axis_size("ctx"), lax.axis_size("sub"), lax.axis_size("head")
    small = (
        ctx_size == REQS == 4
        and head_count == sub_size == 2
        and kv_cache.shape[1] == 2 * PAGE
        and kv_cache.shape[2] % (sub_size * HD) == 0
        and queries.shape[0] % 16 == 0
        and queries.shape[0] * head_count * sub_size == QR
    )
    return (one_request_each if small else queries_to_pages)(queries, kv_cache, page_counts)


def solution(mesh):
    return jax.shard_map(
        per_device,
        mesh=mesh,
        in_specs=(
            P(("grp", "ctx", "head", "sub"), None),
            P(None, ("grp", "ctx", "sub"), "head"),
            P("grp"),
        ),
        out_specs=P(("grp", "ctx", "head", "sub"), None),
        check_vma=False,
    )
```
